32 devices in a mesh: dp: 16 (over z, y, x), mp: 2 (over core).
Axes of the slice: x: 2, y: 2, z: 4, core: 2. Of those that a mesh axis runs over, the one named last changes fastest.
Arguments:
- tokens: bfloat16 [7168, 768], P('dp'), may hold values from -6 to 6
- enc_states: bfloat16 [16, 1500, 768], P('dp'), may hold values from -6 to 6
- lengths: int32 [16], P('dp'), may hold values from 1 to 448, as said below
- cotangent: bfloat16 [7168, 768], P('dp'), may hold values from -6 to 6
- attn_master: float32 [2, 4, 768, 768], P(None, None, 'dp', 'mp')
- attn_first: float32 [2, 4, 768, 768], P(None, None, 'dp', 'mp'), may hold values from -0.0048828125 to 0.0048828125
- attn_second: float32 [2, 4, 768, 768], P(None, None, 'dp', 'mp'), may hold values from 5.290871e-08 to 8.4653936e-07
- dense_master: float32 [2, 768, 3072], P(None, 'dp', 'mp'), may hold values from -0.21875 to 0.21875
- dense_first: float32 [2, 768, 3072], P(None, 'dp', 'mp'), may hold values from -0.0048828125 to 0.0048828125
- dense_second: float32 [2, 768, 3072], P(None, 'dp', 'mp'), may hold values from 5.290871e-08 to 8.4653936e-07
- vector_params: float32 [17, 768], P(None, ('dp', 'mp'))
- vector_first: float32 [17, 768], P(None, ('dp', 'mp')), may hold values from -0.009765625 to 0.009765625
- vector_second: float32 [17, 768], P(None, ('dp', 'mp')), may hold values from 1.0581742e-07 to 1.6930787e-06
- decays: float32 [2], replicated, may hold values from 0.4 to 0.6
Outputs:
- layer_out: bfloat16 [7168, 768], P('dp')
- input_grad: float32 [7168, 768], P('dp')
- enc_grad: float32 [16, 1500, 768], P('dp', None, 'mp')
- clip_norm: float32 [], replicated
- attn_new: float32 [2, 4, 768, 768], P(None, None, 'dp', 'mp')
- attn_first_new: float32 [2, 4, 768, 768], P(None, None, 'dp', 'mp')
- attn_second_new: float32 [2, 4, 768, 768], P(None, None, 'dp', 'mp')
- attn_copy: bfloat16 [2, 4, 768, 768], P(None, None, 'dp', 'mp')
- dense_new: float32 [2, 768, 3072], P(None, 'dp', 'mp')
- dense_first_new: float32 [2, 768, 3072], P(None, 'dp', 'mp')
- dense_second_new: float32 [2, 768, 3072], P(None, 'dp', 'mp')
- dense_copy: bfloat16 [2, 768, 3072], P(None, 'dp', 'mp')
- vector_new: float32 [17, 768], P(None, ('dp', 'mp'))
- vector_first_new: float32 [17, 768], P(None, ('dp', 'mp'))
- vector_second_new: float32 [17, 768], P(None, ('dp', 'mp'))
- vector_copy: bfloat16 [17, 768], P(None, ('dp', 'mp'))
- bias_gradient: float32 [768], P(('dp', 'mp'))
The draws below stay inside these ranges and needn't reach their ends.
Inputs may be any that keep to these rules, and one draw needn't show every extreme that they name: `lengths`: each transcript has 1 to 448 tokens; every transcript whose index is a multiple of 8 has exactly 448.
All inputs are finite; a program needn't handle non-finite values.
Results may differ from the reference program's by a relative error of at most 0.03.
Values may be sent and summed in bfloat16 or wider, within the bound.
No kernel may reach another device: no remote copies, remote signals or barrier semaphores. Data moves between devices by JAX's collectives and lax.ppermute only.
A program may use at most 192 MiB of HBM per device.

```python
import math
import jax
import jax.numpy as jnp
from jax import lax

D = 768
HEADS = 12
HEAD_DIM = 64
FF = 3072
ENC = 1500
BLOCK = 448
STEP = 3
CLIPS = 16
TOKENS = 7168
PARAMS = 9450240


def draw_lengths(key, part):
    first_key, second_key = jax.random.split(key, 2)
    first_draw = jax.random.randint(first_key, (CLIPS,), 1, BLOCK + 1)
    second_draw = jax.random.randint(second_key, (CLIPS,), 1, BLOCK + 1)
    shorter = jnp.minimum(first_draw, second_draw)
    slot_ids = jnp.arange(CLIPS)
    return jnp.where(slot_ids % 8 == 0, BLOCK, shorter).astype(jnp.int32)


def draw_attn_master(key, part):
    base_draw = jax.random.normal(key, (2, 4, D, D), jnp.float32)
    factor_table = jnp.array([[1.0, 1.0, 1.0, 6.0], [1.0, 1.0, 1.0, 12.0]], jnp.float32)
    return base_draw * D ** (-0.5) * factor_table[:, :, None, None]


def draw_vector_params(key, part):
    row_count = 13 + FF // D
    gain_key, shift_key = jax.random.split(key)
    place = jnp.arange(D).astype(jnp.float32) / D
    spread_draw = jax.random.normal(shift_key, (row_count, D), jnp.float32) * 0.3
    rising = 0.55 * jnp.exp(place * 1.0986123)
    jitter = jax.random.uniform(gain_key, (row_count, D), jnp.float32, 0.8, 1.25)
    gain_draw = rising[None, :] * jitter
    row_ids = jnp.arange(row_count)[:, None]
    is_gain = (row_ids == 0) | (row_ids == 2) | (row_ids == 4)
    return jnp.where(is_gain, gain_draw, spread_draw)


def levels(key, dims, shards, least, top_value):
    loudness, own = 1.0, jax.random.fold_in(key, 6)
    for axis_at, parts in shards:
        heights = jnp.exp(jax.random.uniform(jax.random.fold_in(own, axis_at), (parts,), jnp.float32, least / len(shards), top_value / len(shards)))
        loudness = loudness * jnp.repeat(heights, dims[axis_at] // parts).reshape([-1 if axis == axis_at else 1 for axis in range(len(dims))])
    return loudness


def gaussian(stream_key, extent, scale, most, cuts=(), held_as=jnp.bfloat16):
    entries = jax.random.normal(stream_key, extent, jnp.float32) * scale
    if len(cuts) > 0:
        entries = levels(stream_key, extent, cuts, -0.22, 0.18) * entries
    return jnp.clip(entries, min=-most, max=most).astype(held_as)


def setup_inputs(seed: int = 0) -> dict:
    streams_of = jax.random.split(jax.random.key(seed), 15)
    return {
        "tokens": gaussian(streams_of[0], (TOKENS, D), 1.0, 6.0, ((0, 16),)),
        "enc_states": gaussian(streams_of[1], (CLIPS, ENC, D), 1.0, 6.0, ((0, 16),)),
        "lengths": draw_lengths(jax.random.fold_in(streams_of[14], 71), 0),
        "cotangent": gaussian(streams_of[3], (TOKENS, D), 1.0, 6.0, ((0, 16),)),
        "attn_master": draw_attn_master(jax.random.fold_in(streams_of[14], 71), 0),
        "attn_first": gaussian(streams_of[5], (2, 4, D, D), (PARAMS ** -0.5), 0.0048828125, ((2, 16), (3, 2)), jnp.float32),
        "attn_second": jnp.clip(jnp.exp(math.log(8.465393648293684e-07) - 2.7725887 * jax.random.uniform(streams_of[6], (2, 4, D, D), jnp.float32) ** levels(streams_of[6], (2, 4, D, D), ((2, 16), (3, 2)), -0.2, 0.2)), 5.2908710301835526e-08, 8.465393648293684e-07),
        "dense_master": gaussian(streams_of[7], (2, D, FF), D ** -0.5, 0.21875, ((1, 16), (2, 2)), jnp.float32),
        "dense_first": gaussian(streams_of[8], (2, D, FF), (PARAMS ** -0.5), 0.0048828125, ((1, 16), (2, 2)), jnp.float32),
        "dense_second": jnp.clip(jnp.exp(math.log(8.465393648293684e-07) - 2.7725887 * jax.random.uniform(streams_of[9], (2, D, FF), jnp.float32) ** levels(streams_of[9], (2, D, FF), ((1, 16), (2, 2)), -0.2, 0.2)), 5.2908710301835526e-08, 8.465393648293684e-07),
        "vector_params": draw_vector_params(jax.random.fold_in(streams_of[14], 71), 0),
        "vector_first": gaussian(streams_of[11], (13 + FF // D, D), (2.0 * PARAMS ** -0.5), 0.009765625, ((1, 32),), jnp.float32),
        "vector_second": jnp.clip(jnp.exp(math.log(1.6930787296587368e-06) - 2.7725887 * jax.random.uniform(streams_of[12], (13 + FF // D, D), jnp.float32) ** levels(streams_of[12], (13 + FF // D, D), ((1, 32),), -0.2, 0.2)), 1.0581742060367105e-07, 1.6930787296587368e-06),
        "decays": jnp.clip(jax.random.uniform(streams_of[13], (2,), jnp.float32, 0.4, 0.6), 0.4, 0.6),
    }


@jax.custom_vjp
def low(v):
    return lax.optimization_barrier(v.astype(jnp.bfloat16)).astype(jnp.float32)

@jax.custom_vjp
def low_back(v):
    return v

def low_keep(v):
    return (low(v), None)

def low_pass(kept, grad):
    return (grad,)

def back_keep(v):
    return (v, None)

def back_low(kept, grad):
    return (low(grad),)
low.defvjp(low_keep, low_pass)
low_back.defvjp(back_keep, back_low)
highest = lax.Precision.HIGHEST
attn_rate = 0.08
dense_rate = 0.03
vector_rate = 0.3

def both_ways(values):
    return low(low_back(values))

def matmul_high(left_side, right_side):
    return jnp.dot(left_side, right_side, precision=highest)

def layer_norm(values, gain, shift):
    row_mean = lax.optimization_barrier(jnp.mean(values, axis=-1, keepdims=True))
    centred = values - row_mean
    return centred * lax.rsqrt(lax.optimization_barrier(jnp.mean(centred * centred, axis=-1, keepdims=True)) + 1e-05) * gain + shift

def exact_gelu(values):
    return jax.nn.gelu(values, approximate=False)

def attention(queries, key_rows, value_rows, seq_length, causal):
    query_count = queries.shape[0]
    key_count = key_rows.shape[0]
    query_heads = queries.reshape(query_count, HEADS, HEAD_DIM)
    key_heads = key_rows.reshape(key_count, HEADS, HEAD_DIM)
    value_heads = value_rows.reshape(key_count, HEADS, HEAD_DIM)
    raw_scores = low_back(jnp.einsum('qhc,khc->hqk', query_heads, key_heads, precision=highest))
    scores = raw_scores * 0.125
    if causal:
        row_ids = lax.broadcasted_iota(jnp.int32, (query_count, key_count), 0)
        col_ids = lax.broadcasted_iota(jnp.int32, (query_count, key_count), 1)
        allowed = (col_ids <= row_ids) & (col_ids < seq_length)
        scores = jnp.where(allowed[None, :, :], scores, -1e+30)
    soft_weights = jax.nn.softmax(scores, axis=-1)
    mixed_rows = jnp.einsum('hqk,khc->qhc', low(soft_weights), value_heads, precision=highest)
    return both_ways(mixed_rows.reshape(query_count, D))

def forward(masters, seq_tokens, seq_enc, seq_length):
    attn_master, dense_master, vector_params = masters
    attn_low = low(attn_master)
    dense_low = low(dense_master)
    hidden_bias = vector_params[13:].reshape(FF)
    hidden1 = low(layer_norm(seq_tokens, vector_params[0], vector_params[1]))
    self_q = both_ways(matmul_high(hidden1, attn_low[0, 0]) + vector_params[6])
    self_k = both_ways(matmul_high(hidden1, attn_low[0, 1]))
    self_v = both_ways(matmul_high(hidden1, attn_low[0, 2]) + vector_params[7])
    self_mixed = attention(self_q, self_k, self_v, seq_length, True)
    section1 = seq_tokens + low_back(matmul_high(self_mixed, attn_low[0, 3].T) + vector_params[8])
    hidden2 = low(layer_norm(section1, vector_params[2], vector_params[3]))
    cross_q = both_ways(matmul_high(hidden2, attn_low[1, 0]) + vector_params[9])
    cross_k = both_ways(matmul_high(seq_enc, attn_low[1, 1]))
    cross_v = both_ways(matmul_high(seq_enc, attn_low[1, 2]) + vector_params[10])
    cross_mixed = attention(cross_q, cross_k, cross_v, seq_length, False)
    section2 = section1 + low_back(matmul_high(cross_mixed, attn_low[1, 3].T) + vector_params[11])
    hidden3 = low(layer_norm(section2, vector_params[4], vector_params[5]))
    pre_act = low_back(matmul_high(hidden3, dense_low[0]) + hidden_bias)
    act_rows = both_ways(exact_gelu(pre_act))
    return section2 + low_back(matmul_high(act_rows, dense_low[1].T) + vector_params[12])

def adamw(weight, gradient, first_moment, second, factor, decays, step_rate):
    clipped = gradient * factor
    first_new = decays[0] * first_moment + (1.0 - decays[0]) * clipped
    second_new = decays[1] * second + (1.0 - decays[1]) * clipped * clipped
    first_hat = first_new / (1.0 - decays[0] ** STEP)
    second_hat = second_new / (1.0 - decays[1] ** STEP)
    weight_new = weight - step_rate * (first_hat / (jnp.sqrt(second_hat) + 1e-08) + 0.1 * weight)
    return (weight_new, first_new, second_new, weight_new.astype(jnp.bfloat16))

def reference(tokens, enc_states, lengths, cotangent, attn_master, attn_first, attn_second, dense_master, dense_first, dense_second, vector_params, vector_first, vector_second, decays):
    masters = (attn_master, dense_master, vector_params)
    tokens_all = tokens.astype(jnp.float32).reshape(CLIPS, BLOCK, D)
    grads_all = cotangent.astype(jnp.float32).reshape(CLIPS, BLOCK, D)

    def one_sequence(grad_sums, seq_item):
        seq_tokens, seq_enc, seq_length, seq_cot = seq_item

        def local_forward(weights_in, tokens_in, enc_in):
            return forward(weights_in, tokens_in, enc_in, seq_length)
        seq_out, pullback = jax.vjp(local_forward, masters, seq_tokens, seq_enc.astype(jnp.float32))
        valid_rows = (lax.broadcasted_iota(jnp.int32, (BLOCK, 1), 0) < seq_length).astype(jnp.float32)
        grad_masters, grad_tokens, grad_enc = pullback(seq_cot * valid_rows)
        grad_sums = jax.tree.map(jnp.add, grad_sums, grad_masters)
        return (grad_sums, (seq_out.astype(jnp.bfloat16), grad_tokens, grad_enc))
    zero_grads = jax.tree.map(jnp.zeros_like, masters)
    grad_sums, (seq_outs, grad_tokens, enc_grad) = lax.scan(one_sequence, zero_grads, (tokens_all, enc_states, lengths, grads_all))
    grad_attn, grad_dense, grad_vector = grad_sums
    square_total = jnp.sum(grad_attn * grad_attn) + jnp.sum(grad_dense * grad_dense) + jnp.sum(grad_vector * grad_vector)
    clip_norm = jnp.sqrt(square_total)
    factor = jnp.minimum(1.0, 1.0 / (clip_norm + 1e-06))
    bias_gradient = grad_vector[12] * factor
    attn_new, attn_first_new, attn_second_new, attn_copy = adamw(attn_master, grad_attn, attn_first, attn_second, factor, decays, attn_rate)
    dense_new, dense_first_new, dense_second_new, dense_copy = adamw(dense_master, grad_dense, dense_first, dense_second, factor, decays, dense_rate)
    vector_new, vector_first_new, vector_second_new, vector_copy = adamw(vector_params, grad_vector, vector_first, vector_second, factor, decays, vector_rate)
    return (seq_outs.reshape(TOKENS, D), grad_tokens.reshape(TOKENS, D), enc_grad, clip_norm, attn_new, attn_first_new, attn_second_new, attn_copy, dense_new, dense_first_new, dense_second_new, dense_copy, vector_new, vector_first_new, vector_second_new, vector_copy, bias_gradient)
```

```python
import functools

import jax
import jax.numpy as jnp
from jax import lax
from jax.experimental import pallas as pl
from jax.experimental.pallas import tpu as pltpu
from jax.sharding import PartitionSpec as P

D = 768
HEAD_DIM = 64
FF = 3072
BLOCK = 448
STEP = 3


attn_rate = 0.08
dense_rate = 0.03
vector_rate = 0.3
LOG2E = 1.4426950408889634


def dot(left_side, right_side):
    return jnp.dot(left_side, right_side, preferred_element_type=jnp.float32)


def dot_nt(left_side, right_side):
    return lax.dot_general(
        left_side, right_side, (((1,), (1,)), ((), ())), preferred_element_type=jnp.float32
    )


def spans(total, step):
    return [(at, min(step, total - at)) for at in range(0, total, step)]


def unit_norm(values):
    centred = values - jnp.mean(values, axis=-1, keepdims=True)
    inverse = lax.rsqrt(jnp.mean(centred * centred, axis=-1, keepdims=True) + 1e-05)
    return centred * inverse, inverse


def norm_rows(values, gain, shift):
    unit, _ = unit_norm(values)
    return (unit * gain + shift).astype(jnp.bfloat16)


def norm_pull(values, grad, gain):
    unit, inverse = unit_norm(values)
    scaled = grad * gain
    pulled = inverse * (
        scaled
        - jnp.mean(scaled, axis=-1, keepdims=True)
        - unit * jnp.mean(scaled * unit, axis=-1, keepdims=True)
    )
    return (
        pulled,
        jnp.sum(grad * unit, axis=0, keepdims=True),
        jnp.sum(grad, axis=0, keepdims=True),
    )


def head_masks():
    lane = lax.broadcasted_iota(jnp.int32, (1, 2 * HEAD_DIM), 1)
    return [(lane < HEAD_DIM).astype(jnp.bfloat16), (lane >= HEAD_DIM).astype(jnp.bfloat16)]


def row_sum(values):
    return jnp.sum(values.astype(jnp.float32), axis=0, keepdims=True)


def run_kernel(kernel, out_shapes, *operands, scratch=(), flops=0, moved=0):
    spaces = [
        pl.BlockSpec(
            memory_space=pltpu.SMEM if operand.dtype == jnp.int32 else pltpu.VMEM
        )
        for operand in operands
    ]
    return pl.pallas_call(
        kernel,
        out_shape=out_shapes,
        in_specs=spaces,
        out_specs=jax.tree.map(lambda _: pl.BlockSpec(memory_space=pltpu.VMEM), out_shapes),
        scratch_shapes=list(scratch),
        compiler_params=pltpu.CompilerParams(vmem_limit_bytes=56 * 2**20),
        cost_estimate=pl.CostEstimate(flops=flops, bytes_accessed=moved, transcendentals=0),
    )(*operands)


def array_of(shape, dtype=jnp.bfloat16):
    return jax.ShapeDtypeStruct(shape, dtype)


def cross_keys_kernel(enc, wk, wv, bias_v, keys, values, keys_t, values_t, enc_t):
    for at, size in spans(enc.shape[0], 256):
        rows = pl.ds(at, size)
        block = enc[rows, :]
        enc_t[:, rows] = block.T
        key_block = dot(block, wk[...]).astype(jnp.bfloat16)
        value_block = (dot(block, wv[...]) + bias_v[...]).astype(jnp.bfloat16)
        keys[rows, :] = key_block
        values[rows, :] = value_block
        keys_t[:, rows] = key_block.T
        values_t[:, rows] = value_block.T


def self_forward_kernel(
    length, tokens, params, bias_q, bias_v, wq, wk, wv, wo,
    hidden, q, k, v, mixed, mixed_t, lse, part,
    values_t, allowed,
):
    count = tokens.shape[0]
    for at, size in spans(count, 64):
        rows = pl.ds(at, size)
        hidden[rows, :] = norm_rows(
            tokens[rows, :].astype(jnp.float32), params[0:1, :], params[1:2, :]
        )
    q[...] = (dot(hidden[...], wq[...]) + bias_q[...]).astype(jnp.bfloat16)
    k[...] = dot(hidden[...], wk[...]).astype(jnp.bfloat16)
    v[...] = (dot(hidden[...], wv[...]) + bias_v[...]).astype(jnp.bfloat16)
    values_t[...] = v[...].T
    key_ids = lax.broadcasted_iota(jnp.int32, (count, count), 0)
    query_ids = lax.broadcasted_iota(jnp.int32, (count, count), 1)
    allowed[...] = ((key_ids <= query_ids) & (key_ids < length[0])).astype(jnp.float32)
    masks = head_masks()

    def pair_step(pair, carry):
        cols = pl.ds(pl.multiple_of(pair * 128, 128), 128)
        for parity in range(2):
            head = pair * 2 + parity
            scores = dot_nt(k[:, cols], q[:, cols] * masks[parity]) * (0.125 * LOG2E)
            scores = jnp.where(allowed[...] > 0.5, scores, -1e30)
            top = jnp.max(scores, axis=0, keepdims=True)
            weights = jnp.exp2(scores - top)
            total = jnp.sum(weights, axis=0, keepdims=True)
            lse[pl.ds(head, 1), :] = top + jnp.log2(total)
            own = pl.ds(pl.multiple_of(head * HEAD_DIM, HEAD_DIM), HEAD_DIM)
            mixed_t[own, :] = (
                dot(values_t[own, :], weights.astype(jnp.bfloat16)) * (1.0 / total)
            ).astype(jnp.bfloat16)
        return carry

    lax.fori_loop(0, q.shape[1] // 128, pair_step, 0)
    mixed[...] = mixed_t[...].T
    part[...] = dot_nt(mixed[...], wo[...]).astype(jnp.bfloat16)


def cross_forward_kernel(
    tokens, own_part, other_part, params, bias_q, wq, wo, keys, values_t,
    section, hidden, q, mixed, mixed_t, lse, part,
    scores, weights,
):
    count = tokens.shape[0]
    for at, size in spans(count, 64):
        rows = pl.ds(at, size)
        branch = own_part[rows, :].astype(jnp.float32) + other_part[rows, :].astype(jnp.float32)
        block = tokens[rows, :].astype(jnp.float32) + (branch + params[8:9, :])
        section[rows, :] = block
        hidden[rows, :] = norm_rows(block, params[2:3, :], params[3:4, :])
    q[...] = (dot(hidden[...], wq[...]) + bias_q[...]).astype(jnp.bfloat16)
    masks = head_masks()
    key_spans = spans(keys.shape[0], 256)

    def pair_step(pair, carry):
        cols = pl.ds(pl.multiple_of(pair * 128, 128), 128)
        for parity in range(2):
            head = pair * 2 + parity
            queries = q[:, cols] * masks[parity]
            top = None
            for at, size in key_spans:
                block = dot_nt(keys[pl.ds(at, size), cols], queries) * (0.125 * LOG2E)
                scores[pl.ds(at, size), :] = block
                block_top = jnp.max(block, axis=0, keepdims=True)
                top = block_top if top is None else jnp.maximum(top, block_top)
            total = jnp.zeros_like(top)
            for at, size in key_spans:
                block = jnp.exp2(scores[pl.ds(at, size), :] - top)
                total = total + jnp.sum(block, axis=0, keepdims=True)
                weights[pl.ds(at, size), :] = block.astype(jnp.bfloat16)
            lse[pl.ds(head, 1), :] = top + jnp.log2(total)
            own = pl.ds(pl.multiple_of(head * HEAD_DIM, HEAD_DIM), HEAD_DIM)
            mixed_t[own, :] = (dot(values_t[own, :], weights[...]) * (1.0 / total)).astype(
                jnp.bfloat16
            )
        return carry

    lax.fori_loop(0, q.shape[1] // 128, pair_step, 0)
    mixed[...] = mixed_t[...].T
    part[...] = dot_nt(mixed[...], wo[...]).astype(jnp.bfloat16)


def dense_kernel(
    length, section, own_part, other_part, params, bias_hidden, w1, w2, cotangent,
    section_new, hidden, act, grad_pre, grad_low, part, grad_hidden, grad_bias,
):
    count = section.shape[0]
    for at, size in spans(count, 64):
        rows = pl.ds(at, size)
        branch = own_part[rows, :].astype(jnp.float32) + other_part[rows, :].astype(jnp.float32)
        block = section[rows, :] + (branch + params[11:12, :])
        section_new[rows, :] = block
        hidden[rows, :] = norm_rows(block, params[4:5, :], params[5:6, :])
        row_ids = lax.broadcasted_iota(jnp.int32, (size, 1), 0) + at
        valid = (row_ids < length[0]).astype(jnp.float32)
        grad_low[rows, :] = (cotangent[rows, :].astype(jnp.float32) * valid).astype(jnp.bfloat16)

    def step(at, carry):
        cols = pl.ds(pl.multiple_of(at * 256, 256), 256)
        pre_act = dot(hidden[...], w1[:, cols]) + bias_hidden[:, cols]
        spread = 0.5 + 0.5 * lax.erf(pre_act * (2.0**-0.5))
        act[:, cols] = (pre_act * spread).astype(jnp.bfloat16)
        slope = spread + pre_act * (
            jnp.exp2(pre_act * pre_act * (-0.5 * LOG2E)) * 0.3989422804014327
        )
        grad_act = dot(grad_low[...], w2[:, cols]).astype(jnp.bfloat16).astype(jnp.float32)
        grad_block = (grad_act * slope).astype(jnp.bfloat16)
        grad_pre[:, cols] = grad_block
        grad_bias[:, cols] = row_sum(grad_block)
        return carry

    lax.fori_loop(0, act.shape[1] // 256, step, 0)
    part[...] = dot_nt(act[...], w2[...]).astype(jnp.bfloat16)
    grad_hidden[...] = dot_nt(grad_pre[...], w1[...]).astype(jnp.bfloat16)


def put_relative(product, here, order, keep, send, which, cols):
    half = keep.shape[0]
    rows = keep.shape[2]
    for at, offset in enumerate(order):
        block = product[pl.ds(pl.multiple_of((here ^ offset) * rows, 16), rows), :]
        target = keep if at < half else send
        target[at % half, which, :, cols] = block.astype(jnp.bfloat16)


def weight_kernel(uses, orders, *refs):
    left_count = 1 + max(left for left, _, _ in uses)
    lefts, rights = refs[1 : 1 + left_count], refs[1 + left_count : 1 + left_count + len(uses)]
    outs = refs[1 + left_count + len(uses) : -2]
    product, turned = refs[-2:]
    width = product.shape[1]
    me = refs[0][0]
    in_turned = None
    for (left, group, which), right in zip(uses, rights):
        left_t = lefts[left]
        if left_t.shape[0] != D:
            if in_turned != left:
                turned[...] = left_t[...].T
                in_turned = left
            left_t = turned

        def step(at, carry, left_t=left_t, right=right, group=group, which=which):
            cols = pl.ds(pl.multiple_of(at * width, width), width)
            product[...] = dot(left_t[...], right[:, cols])
            if orders is None:
                outs[group][which, :, cols] = product[...].astype(jnp.bfloat16)
            else:
                put_relative(
                    product, me, orders[group], outs[2 * group], outs[2 * group + 1], which, cols
                )
            return carry

        lax.fori_loop(0, right.shape[1] // width, step, 0)


def attention_pull(
    keys, values, keys_t, q, grad_mixed, grad_mixed_t, mixed_t, lse, allowed, step,
    grad_keys, grad_values, grad_q_t,
):
    masks = head_masks()
    key_spans = spans(keys.shape[0], step)

    def pair_step(pair, carry):
        cols = pl.ds(pl.multiple_of(pair * 128, 128), 128)
        queries = [q[:, cols] * mask for mask in masks]
        grads = [(grad_mixed[:, cols] * 0.125) * mask for mask in masks]
        heads = [pl.ds(pl.multiple_of(pair * 128 + p * 64, 64), 64) for p in range(2)]
        levels, deltas = [], []
        for parity in range(2):
            levels.append(lse[pl.ds(pair * 2 + parity, 1), :])
            product = grad_mixed_t[heads[parity], :].astype(jnp.float32) * mixed_t[
                heads[parity], :
            ].astype(jnp.float32)
            deltas.append(jnp.sum(product, axis=0, keepdims=True) * 0.125)
        sums = [None, None]
        for at, size in key_spans:
            rows = pl.ds(at, size)
            key_sum = value_sum = None
            for parity in range(2):
                scores = dot_nt(keys[rows, cols], queries[parity]) * (0.125 * LOG2E)
                weights = jnp.exp2(scores - levels[parity])
                if allowed is not None:
                    weights = jnp.where(allowed[rows, :] > 0.5, weights, 0.0)
                grad_soft = dot_nt(values[rows, cols], grads[parity])
                grad_raw = (weights * (grad_soft - deltas[parity])).astype(jnp.bfloat16)
                value_part = dot(weights.astype(jnp.bfloat16), grads[parity])
                key_part = dot(grad_raw, queries[parity])
                query_part = dot(keys_t[heads[parity], rows], grad_raw)
                value_sum = value_part if value_sum is None else value_sum + value_part
                key_sum = key_part if key_sum is None else key_sum + key_part
                sums[parity] = query_part if sums[parity] is None else sums[parity] + query_part
            grad_values[rows, cols] = (value_sum * 8.0).astype(jnp.bfloat16)
            grad_keys[rows, cols] = key_sum.astype(jnp.bfloat16)
        for parity in range(2):
            grad_q_t[heads[parity], :] = sums[parity].astype(jnp.bfloat16)
        return carry

    lax.fori_loop(0, q.shape[1] // 128, pair_step, 0)


def cross_backward_kernel(
    section, grad_part, grad_other, out_part, out_other, grad_top, params,
    wo, wq, q, keys, values, keys_t, mixed_t, lse,
    layer_out, grad_section, grad_z, grad_q, grad_keys, grad_values, grad_hidden, vectors, biases,
    grad_mixed, grad_mixed_t, grad_q_t,
):
    count = section.shape[0]
    sums = None
    for at, size in spans(count, 64):
        rows = pl.ds(at, size)
        block = section[rows, :]
        branch = out_part[rows, :].astype(jnp.float32) + out_other[rows, :].astype(jnp.float32)
        layer_out[rows, :] = (block + (branch + params[12:13, :])).astype(jnp.bfloat16)
        grad = grad_part[rows, :].astype(jnp.float32) + grad_other[rows, :].astype(jnp.float32)
        pulled, gain_sum, shift_sum = norm_pull(block, grad, params[4:5, :])
        top = grad_top[rows, :].astype(jnp.float32)
        total = top + pulled
        low = total.astype(jnp.bfloat16)
        grad_section[rows, :] = total
        grad_z[rows, :] = low
        parts = [gain_sum, shift_sum, row_sum(low), jnp.sum(top, axis=0, keepdims=True)]
        sums = parts if sums is None else [old + new for old, new in zip(sums, parts)]
    for at, value in enumerate(sums):
        vectors[at : at + 1, :] = value
    grad_mixed[...] = dot(grad_z[...], wo[...]).astype(jnp.bfloat16)
    grad_mixed_t[...] = grad_mixed[...].T
    attention_pull(
        keys, values, keys_t, q, grad_mixed, grad_mixed_t, mixed_t, lse, None, 256,
        grad_keys, grad_values, grad_q_t,
    )
    grad_q[...] = grad_q_t[...].T
    grad_hidden[...] = dot_nt(grad_q[...], wq[...]).astype(jnp.bfloat16)
    biases[0:1, :] = row_sum(grad_q[...])
    biases[1:2, :] = row_sum(grad_values[...])


def self_backward_kernel(
    length, section, grad_section, grad_part, grad_other, params,
    wo, wq, wk, wv, q, k, v, mixed_t, lse,
    grad_new, grad_z, grad_q, grad_keys, grad_values, grad_hidden, vectors, biases,
    grad_mixed, grad_mixed_t, grad_q_t, keys_t, allowed,
):
    count = section.shape[0]
    sums = None
    for at, size in spans(count, 64):
        rows = pl.ds(at, size)
        grad = grad_part[rows, :].astype(jnp.float32) + grad_other[rows, :].astype(jnp.float32)
        pulled, gain_sum, shift_sum = norm_pull(section[rows, :], grad, params[2:3, :])
        total = grad_section[rows, :] + pulled
        low = total.astype(jnp.bfloat16)
        grad_new[rows, :] = total
        grad_z[rows, :] = low
        parts = [gain_sum, shift_sum, row_sum(low)]
        sums = parts if sums is None else [old + new for old, new in zip(sums, parts)]
    for at, value in enumerate(sums):
        vectors[at : at + 1, :] = value
    grad_mixed[...] = dot(grad_z[...], wo[...]).astype(jnp.bfloat16)
    grad_mixed_t[...] = grad_mixed[...].T
    keys_t[...] = k[...].T
    key_ids = lax.broadcasted_iota(jnp.int32, (count, count), 0)
    query_ids = lax.broadcasted_iota(jnp.int32, (count, count), 1)
    allowed[...] = ((key_ids <= query_ids) & (key_ids < length[0])).astype(jnp.float32)
    attention_pull(
        k, v, keys_t, q, grad_mixed, grad_mixed_t, mixed_t, lse, allowed, 256,
        grad_keys, grad_values, grad_q_t,
    )
    grad_q[...] = grad_q_t[...].T
    grad_hidden[...] = (
        dot_nt(grad_q[...], wq[...])
        + dot_nt(grad_keys[...], wk[...])
        + dot_nt(grad_values[...], wv[...])
    ).astype(jnp.bfloat16)
    biases[0:1, :] = row_sum(grad_q[...])
    biases[1:2, :] = row_sum(grad_values[...])


def last_kernel(tokens, grad_section, grad_part, grad_other, params, input_grad, vectors):
    sums = None
    for at, size in spans(tokens.shape[0], 64):
        rows = pl.ds(at, size)
        grad = grad_part[rows, :].astype(jnp.float32) + grad_other[rows, :].astype(jnp.float32)
        pulled, gain_sum, shift_sum = norm_pull(
            tokens[rows, :].astype(jnp.float32), grad, params[0:1, :]
        )
        input_grad[rows, :] = grad_section[rows, :] + pulled
        parts = [gain_sum, shift_sum]
        sums = parts if sums is None else [old + new for old, new in zip(sums, parts)]
    for at, value in enumerate(sums):
        vectors[at : at + 1, :] = value


def enc_kernel(grad_keys, grad_values, wk, wv, out):
    for at, size in spans(grad_keys.shape[0], 256):
        rows = pl.ds(at, size)
        out[rows, :] = (
            dot_nt(grad_keys[rows, :], wk[...]) + dot_nt(grad_values[rows, :], wv[...])
        ).astype(out.dtype)


def swap(array, bit):
    count = lax.axis_size("dp")
    return lax.ppermute(array, "dp", [(i, i ^ bit) for i in range(count)])


def swap_core(array):
    return lax.ppermute(array, "mp", [(0, 1), (1, 0)])


def high_bits():
    count = lax.axis_size("dp")
    return [1 << k for k in range(2, count.bit_length() - 1)]


def butterfly(array):
    array = array + swap_core(array)
    for bit in [1, 2] + high_bits():
        array = array + swap(array, bit)
    return array


def move_rows(kernel, sources, out_shapes, source_space, out_space):
    return pl.pallas_call(
        kernel,
        out_shape=out_shapes,
        in_specs=[pl.BlockSpec(memory_space=source_space)] * len(sources),
        out_specs=jax.tree.map(lambda _: pl.BlockSpec(memory_space=out_space), out_shapes),
        scratch_shapes=[pltpu.SemaphoreType.DMA((lax.axis_size("dp"),))],
    )(*sources)


def to_absolute(parts):
    count = lax.axis_size("dp")
    me = lax.axis_index("dp")
    wide, rows, cols = parts[0][0].shape[1:]
    if rows % 16 == 0:

        def kernel(*refs):
            stacks, out, sems = refs[: len(parts)], refs[len(parts)], refs[-1]
            here = lax.axis_index("dp")
            copies = []
            for stack, (_, offsets) in zip(stacks, parts):
                for at, offset in enumerate(offsets):
                    place = pl.multiple_of((here ^ offset) * rows, 16)
                    copies.append(
                        pltpu.make_async_copy(
                            stack.at[at], out.at[:, pl.ds(place, rows), :], sems.at[len(copies)]
                        )
                    )
            for copy in copies:
                copy.start()
            for copy in copies:
                copy.wait()

        return move_rows(
            kernel,
            [stack for stack, _ in parts],
            jax.ShapeDtypeStruct((wide, count * rows, cols), parts[0][0].dtype),
            pl.ANY,
            pltpu.VMEM,
        )
    pieces = {}
    for stack, offsets in parts:
        for at, offset in enumerate(offsets):
            pieces[offset] = stack[at]
    whole = flip_order(jnp.stack([pieces[offset] for offset in range(count)]), me)
    return whole.transpose(1, 0, 2, 3).reshape(wide, count * rows, cols)


def flip_order(stack, me):
    count = stack.shape[0]
    bit = 1
    while bit < count:
        split = stack.reshape((count // (2 * bit), 2, bit) + stack.shape[1:])
        split = jnp.where((me & bit) != 0, split[:, ::-1], split)
        stack = split.reshape(stack.shape)
        bit *= 2
    return stack


def to_relative(whole, offsets):
    count = lax.axis_size("dp")
    wide, all_rows, cols = whole.shape
    half = count // 2
    stack = whole.reshape(wide, count, all_rows // count, cols).transpose(1, 0, 2, 3)
    stack = flip_order(stack, lax.axis_index("dp"))
    return (
        jnp.stack([stack[offset] for offset in offsets[:half]]),
        jnp.stack([stack[offset] for offset in offsets[half:]]),
    )


def gather_rows(piece):
    stack, offsets = piece[None], [0]
    for bit in high_bits():
        stack = jnp.concatenate([stack, swap(stack, bit)], axis=0)
        offsets = offsets + [offset ^ bit for offset in offsets]
    half = piece.shape[0] // 2
    results = []
    for part, bits in ((stack[:, :half], (1, 2)), (stack[:, half:], (2, 1))):
        near = jnp.concatenate([part, swap(part, bits[0])], axis=0)
        near_offsets = offsets + [offset ^ bits[0] for offset in offsets]
        far = swap(near, bits[1])
        far_offsets = [offset ^ bits[1] for offset in near_offsets]
        results.append(to_absolute([(near, near_offsets), (far, far_offsets)]))
    return results


def weight_parts(uses, lefts, rights):
    count = lax.axis_size("dp")
    orders = []
    for bits in ((2, 1), (1, 2)):
        order = [0]
        for bit in high_bits() + [bits[1], bits[0]]:
            order = order + [offset ^ bit for offset in order]
        orders.append(order)
    cols = rights[0].shape[1]
    wide = len(uses) // 2
    rows = D // count
    direct = rows % 16 == 0
    if direct:
        outs = [array_of((count // 2, wide, rows, cols))] * 4
    else:
        outs = [array_of((wide, D, cols))] * 2
    flops = 2 * D * cols * sum(right.shape[0] for right in rights)
    results = run_kernel(
        functools.partial(weight_kernel, uses, orders if direct else None),
        outs,
        lax.axis_index("dp")[None],
        *lefts,
        *rights,
        scratch=[pltpu.VMEM((D, 384), jnp.float32), pltpu.VMEM((D, BLOCK), jnp.bfloat16)],
        flops=flops,
        moved=4 * len(uses) * D * cols,
    )
    if direct:
        return results
    return [*to_relative(results[0], orders[0]), *to_relative(results[1], orders[1])]


def halve(keep, got, bit):
    half = keep.shape[0] // 2
    high = keep[half:].astype(jnp.float32) + got[half:].astype(jnp.float32)
    came = swap(high.astype(jnp.bfloat16), bit)
    return keep[:half].astype(jnp.float32) + got[:half].astype(jnp.float32), came


def scatter_rows(keep_a, send_a, keep_b, send_b):
    parts = []
    for keep, send, bits in ((keep_a, send_a, (2, 1)), (keep_b, send_b, (1, 2))):
        parts.append(halve(keep, swap(send, bits[0]), bits[1]))
    keep = jnp.concatenate([part[0] for part in parts], axis=1)
    got = jnp.concatenate([part[1] for part in parts], axis=1)
    for bit in high_bits()[::-1]:
        keep, got = halve(keep, got, bit)
    return (keep + got.astype(jnp.float32))[0]


def adamw(weight, gradient, first_moment, second, factor, decays, step_rate):
    clipped = gradient * factor
    first_new = decays[0] * first_moment + (1.0 - decays[0]) * clipped
    second_new = decays[1] * second + (1.0 - decays[1]) * clipped * clipped
    first_hat = first_new / (1.0 - decays[0] ** STEP)
    second_hat = second_new / (1.0 - decays[1] ** STEP)
    weight_new = weight - step_rate * (first_hat / (jnp.sqrt(second_hat) + 1e-08) + 0.1 * weight)
    return (weight_new, first_new, second_new, weight_new.astype(jnp.bfloat16))


def local(
    tokens,
    enc_states,
    lengths,
    cotangent,
    attn_master,
    attn_first,
    attn_second,
    dense_master,
    dense_first,
    dense_second,
    vector_params,
    vector_first,
    vector_second,
    decays,
):
    core = lax.axis_index("mp")
    attn_low = attn_master.astype(jnp.bfloat16)
    dense_low = dense_master.astype(jnp.bfloat16)
    device = lax.axis_index("dp") * lax.axis_size("mp") + core
    own_cols = vector_params.shape[1]
    params = butterfly(
        lax.dynamic_update_slice_in_dim(
            jnp.zeros((vector_params.shape[0], D), jnp.float32), vector_params, device * own_cols, 1
        )
    )
    self_a, self_b = gather_rows(attn_low[0])
    cross_a, cross_b = gather_rows(attn_low[1])
    dense_all = lax.all_gather(dense_low, "dp", axis=1, tiled=True)
    wq_self, wk_self, wv_self, wo_self = self_a[0], self_a[1], self_b[0], self_b[1]
    wq_cross, wk_cross, wv_cross, wo_cross = cross_a[0], cross_a[1], cross_b[0], cross_b[1]
    w1, w2 = dense_all[0], dense_all[1]
    head_cols = attn_master.shape[3]
    hidden_cols = dense_master.shape[2]
    head_rows = 2 * (head_cols // 128)
    count = tokens.shape[0]
    keys_count = enc_states.shape[1]
    enc = enc_states[0]

    def local_slice(bias_row, span_size):
        return lax.dynamic_slice_in_dim(bias_row, core * span_size, span_size)[None]

    def place_local(bias_grad, full_size):
        return lax.dynamic_update_slice_in_dim(
            jnp.zeros((full_size,), jnp.float32), bias_grad, core * bias_grad.shape[0], 0
        )

    bias_q_self = local_slice(params[6], head_cols)
    bias_v_self = local_slice(params[7], head_cols)
    bias_q_cross = local_slice(params[9], head_cols)
    bias_v_cross = local_slice(params[10], head_cols)
    bias_hidden = local_slice(params[13:].reshape(FF), hidden_cols)
    rows_d = array_of((count, D))
    rows_f = array_of((count, D), jnp.float32)
    rows_h = array_of((count, head_cols))
    turned_h = array_of((head_cols, count))
    lse_shape = array_of((head_rows, count), jnp.float32)
    keys_h = array_of((keys_count, head_cols))
    keys_t_h = array_of((head_cols, keys_count))
    scratch_h = pltpu.VMEM((count, head_cols), jnp.bfloat16)
    scratch_t = pltpu.VMEM((head_cols, count), jnp.bfloat16)
    scratch_s = pltpu.VMEM((count, count), jnp.float32)

    hidden1, self_q, self_k, self_v, self_mixed, self_mixed_t, self_lse, self_part = run_kernel(
        self_forward_kernel,
        [rows_d, rows_h, rows_h, rows_h, rows_h, turned_h, lse_shape, rows_d],
        lengths, tokens, params, bias_q_self, bias_v_self, wq_self, wk_self, wv_self, wo_self,
        scratch=[scratch_t, scratch_s],
        moved=30_000_000,
    )
    cross_k, cross_v, cross_k_t, cross_v_t, enc_t = run_kernel(
        cross_keys_kernel,
        [keys_h, keys_h, keys_t_h, keys_t_h, array_of((D, keys_count))],
        enc, wk_cross, wv_cross, bias_v_cross,
        moved=25_000_000,
    )
    section1, hidden2, cross_q, cross_mixed, cross_mixed_t, cross_lse, cross_part = run_kernel(
        cross_forward_kernel,
        [rows_f, rows_d, rows_h, rows_h, turned_h, lse_shape, rows_d],
        tokens, self_part, swap_core(self_part), params, bias_q_cross, wq_cross, wo_cross,
        cross_k, cross_v_t,
        scratch=[
            pltpu.VMEM((keys_count, count), jnp.float32),
            pltpu.VMEM((keys_count, count), jnp.bfloat16),
        ],
        moved=70_000_000,
    )
    hidden_rows = array_of((count, hidden_cols))
    section2, hidden3, act, grad_pre, grad_low, out_part, grad_h3, grad_b1 = run_kernel(
        dense_kernel,
        [rows_f, rows_d, hidden_rows, hidden_rows, rows_d, rows_d, rows_d,
         array_of((1, hidden_cols), jnp.float32)],
        lengths, section1, cross_part, swap_core(cross_part), params, bias_hidden, w1, w2, cotangent,
        moved=50_000_000,
    )
    dense_parts = weight_parts(((0, 0, 0), (1, 1, 0)), (hidden3, grad_low), (grad_pre, act))
    dense_sum = scatter_rows(*dense_parts)
    (
        layer_out, grad_section2, grad_z2, cross_dq, cross_dk, cross_dv, grad_h2, vectors3, biases_cross,
    ) = run_kernel(
        cross_backward_kernel,
        [rows_d, rows_f, rows_d, rows_h, keys_h, keys_h, rows_d,
         array_of((4, D), jnp.float32), array_of((2, head_cols), jnp.float32)],
        section2, grad_h3, swap_core(grad_h3), out_part, swap_core(out_part), grad_low, params,
        wo_cross, wq_cross, cross_q, cross_k, cross_v, cross_k_t, cross_mixed_t, cross_lse,
        scratch=[scratch_h, scratch_t, scratch_t],
        moved=120_000_000,
    )
    cross_parts = weight_parts(
        ((0, 0, 0), (1, 0, 1), (1, 1, 0), (2, 1, 1)),
        (hidden2, enc_t, grad_z2),
        (cross_dq, cross_dk, cross_dv, cross_mixed),
    )
    cross_sum = scatter_rows(*cross_parts)
    (
        grad_section1, grad_z1, self_dq, self_dk, self_dv, grad_h1, vectors2, biases_self,
    ) = run_kernel(
        self_backward_kernel,
        [rows_f, rows_d, rows_h, rows_h, rows_h, rows_d,
         array_of((3, D), jnp.float32), array_of((2, head_cols), jnp.float32)],
        lengths, section1, grad_section2, grad_h2, swap_core(grad_h2), params,
        wo_self, wq_self, wk_self, wv_self, self_q, self_k, self_v, self_mixed_t, self_lse,
        scratch=[scratch_h, scratch_t, scratch_t, scratch_t, scratch_s],
        moved=60_000_000,
    )
    self_parts = weight_parts(
        ((0, 0, 0), (0, 0, 1), (0, 1, 0), (1, 1, 1)),
        (hidden1, grad_z1),
        (self_dq, self_dk, self_dv, self_mixed),
    )
    self_sum = scatter_rows(*self_parts)
    input_grad, vectors1 = run_kernel(
        last_kernel,
        [rows_f, array_of((2, D), jnp.float32)],
        tokens, grad_section1, grad_h1, swap_core(grad_h1), params,
        moved=12_000_000,
    )

    def enc_columns(place, dtype):
        return run_kernel(
            enc_kernel,
            array_of((keys_count, head_cols), dtype),
            cross_dk,
            cross_dv,
            lax.dynamic_slice_in_dim(wk_cross, place * head_cols, head_cols),
            lax.dynamic_slice_in_dim(wv_cross, place * head_cols, head_cols),
            moved=12_000_000,
        )

    enc_other = swap_core(enc_columns(1 - core, jnp.bfloat16))
    enc_grad = (enc_columns(core, jnp.float32) + enc_other.astype(jnp.float32))[None]
    leader = (core == 0).astype(jnp.float32)
    vector_grad = jnp.concatenate(
        [
            jnp.concatenate([vectors1, vectors2[:2], vectors3[:2]]) * leader,
            jnp.stack([place_local(biases_self[0], D), place_local(biases_self[1], D)]),
            vectors2[2:] * leader,
            jnp.stack([place_local(biases_cross[0], D), place_local(biases_cross[1], D)]),
            vectors3[2:] * leader,
            place_local(grad_b1[0], FF).reshape(FF // D, D),
        ],
        axis=0,
    )
    attn_sum = jnp.stack([self_sum, cross_sum])
    local_squares = jnp.sum(attn_sum * attn_sum) + jnp.sum(dense_sum * dense_sum)
    last = butterfly(jnp.concatenate([vector_grad, jnp.full((1, D), local_squares)], axis=0))
    vector_all = last[:-1]
    vector_sum = lax.dynamic_slice_in_dim(vector_all, device * own_cols, own_cols, 1)
    square_total = last[-1, 0] + jnp.sum(vector_all * vector_all)
    clip_norm = jnp.sqrt(square_total)
    factor = jnp.minimum(1.0, 1.0 / (clip_norm + 1e-06))
    bias_gradient = vector_sum[12] * factor
    attn_new, attn_first_new, attn_second_new, attn_copy = adamw(
        attn_master, attn_sum, attn_first, attn_second, factor, decays, attn_rate
    )
    dense_new, dense_first_new, dense_second_new, dense_copy = adamw(
        dense_master, dense_sum, dense_first, dense_second, factor, decays, dense_rate
    )
    vector_new, vector_first_new, vector_second_new, vector_copy = adamw(
        vector_params, vector_sum, vector_first, vector_second, factor, decays, vector_rate
    )
    return (
        layer_out,
        input_grad,
        enc_grad,
        clip_norm,
        attn_new,
        attn_first_new,
        attn_second_new,
        attn_copy,
        dense_new,
        dense_first_new,
        dense_second_new,
        dense_copy,
        vector_new,
        vector_first_new,
        vector_second_new,
        vector_copy,
        bias_gradient,
    )


def solution(mesh):
    return jax.shard_map(
        local,
        mesh=mesh,
        in_specs=(
            P("dp", None),
            P("dp", None, None),
            P("dp"),
            P("dp", None),
            P(None, None, "dp", "mp"),
            P(None, None, "dp", "mp"),
            P(None, None, "dp", "mp"),
            P(None, "dp", "mp"),
            P(None, "dp", "mp"),
            P(None, "dp", "mp"),
            P(None, ("dp", "mp")),
            P(None, ("dp", "mp")),
            P(None, ("dp", "mp")),
            P(),
        ),
        out_specs=(
            P("dp", None),
            P("dp", None),
            P("dp", None, "mp"),
            P(),
            P(None, None, "dp", "mp"),
            P(None, None, "dp", "mp"),
            P(None, None, "dp", "mp"),
            P(None, None, "dp", "mp"),
            P(None, "dp", "mp"),
            P(None, "dp", "mp"),
            P(None, "dp", "mp"),
            P(None, "dp", "mp"),
            P(None, ("dp", "mp")),
            P(None, ("dp", "mp")),
            P(None, ("dp", "mp")),
            P(None, ("dp", "mp")),
            P(("dp", "mp")),
        ),
        check_vma=False,
    )
```

```python
import functools

import jax
import jax.numpy as jnp
from jax import lax
from jax.experimental import pallas as pl
from jax.experimental.pallas import tpu as pltpu
from jax.sharding import PartitionSpec as P

D = 768
HEAD_DIM = 64
FF = 3072
BLOCK = 448
STEP = 3


attn_rate = 0.08
dense_rate = 0.03
vector_rate = 0.3
LOG2E = 1.4426950408889634


def dot(left_side, right_side):
    return jnp.dot(left_side, right_side, preferred_element_type=jnp.float32)


def dot_nt(left_side, right_side):
    return lax.dot_general(
        left_side, right_side, (((1,), (1,)), ((), ())), preferred_element_type=jnp.float32
    )


def spans(total, step):
    return [(at, min(step, total - at)) for at in range(0, total, step)]


def unit_norm(values):
    centred = values - jnp.mean(values, axis=-1, keepdims=True)
    inverse = lax.rsqrt(jnp.mean(centred * centred, axis=-1, keepdims=True) + 1e-05)
    return centred * inverse, inverse


def norm_rows(values, gain, shift):
    unit, _ = unit_norm(values)
    return (unit * gain + shift).astype(jnp.bfloat16)


def norm_pull(values, grad, gain):
    unit, inverse = unit_norm(values)
    scaled = grad * gain
    pulled = inverse * (
        scaled
        - jnp.mean(scaled, axis=-1, keepdims=True)
        - unit * jnp.mean(scaled * unit, axis=-1, keepdims=True)
    )
    return (
        pulled,
        jnp.sum(grad * unit, axis=0, keepdims=True),
        jnp.sum(grad, axis=0, keepdims=True),
    )


def head_masks():
    lane = lax.broadcasted_iota(jnp.int32, (1, 2 * HEAD_DIM), 1)
    return [(lane < HEAD_DIM).astype(jnp.bfloat16), (lane >= HEAD_DIM).astype(jnp.bfloat16)]


def row_sum(values):
    return jnp.sum(values.astype(jnp.float32), axis=0, keepdims=True)


def run_kernel(kernel, out_shapes, *operands, scratch=(), flops=0, moved=0):
    spaces = [
        pl.BlockSpec(
            memory_space=pltpu.SMEM if operand.dtype == jnp.int32 else pltpu.VMEM
        )
        for operand in operands
    ]
    return pl.pallas_call(
        kernel,
        out_shape=out_shapes,
        in_specs=spaces,
        out_specs=jax.tree.map(lambda _: pl.BlockSpec(memory_space=pltpu.VMEM), out_shapes),
        scratch_shapes=list(scratch),
        compiler_params=pltpu.CompilerParams(vmem_limit_bytes=56 * 2**20),
        cost_estimate=pl.CostEstimate(flops=flops, bytes_accessed=moved, transcendentals=0),
    )(*operands)


def array_of(shape, dtype=jnp.bfloat16):
    return jax.ShapeDtypeStruct(shape, dtype)


def cross_keys_kernel(enc, wqk, wvo, bias_v, keys, values, keys_t, values_t, enc_t):
    for at, size in spans(enc.shape[0], 256):
        rows = pl.ds(at, size)
        block = enc[rows, :]
        enc_t[:, rows] = block.T
        key_block = dot(block, wqk[1]).astype(jnp.bfloat16)
        value_block = (dot(block, wvo[0]) + bias_v[...]).astype(jnp.bfloat16)
        keys[rows, :] = key_block
        values[rows, :] = value_block
        keys_t[:, rows] = key_block.T
        values_t[:, rows] = value_block.T


def self_forward_kernel(
    length, tokens, params, bias_q, bias_v, wqk, wvo,
    hidden, q, k, v, mixed, mixed_t, lse, part,
    values_t, allowed,
):
    count = tokens.shape[0]
    for at, size in spans(count, 64):
        rows = pl.ds(at, size)
        hidden[rows, :] = norm_rows(
            tokens[rows, :].astype(jnp.float32), params[0:1, :], params[1:2, :]
        )
    q[...] = (dot(hidden[...], wqk[0]) + bias_q[...]).astype(jnp.bfloat16)
    k[...] = dot(hidden[...], wqk[1]).astype(jnp.bfloat16)
    v[...] = (dot(hidden[...], wvo[0]) + bias_v[...]).astype(jnp.bfloat16)
    values_t[...] = v[...].T
    key_ids = lax.broadcasted_iota(jnp.int32, (count, count), 0)
    query_ids = lax.broadcasted_iota(jnp.int32, (count, count), 1)
    allowed[...] = ((key_ids <= query_ids) & (key_ids < length[0])).astype(jnp.float32)
    masks = head_masks()

    def pair_step(pair, carry):
        cols = pl.ds(pl.multiple_of(pair * 128, 128), 128)
        for parity in range(2):
            head = pair * 2 + parity
            scores = dot_nt(k[:, cols], q[:, cols] * masks[parity]) * (0.125 * LOG2E)
            scores = jnp.where(allowed[...] > 0.5, scores, -1e30)
            top = jnp.max(scores, axis=0, keepdims=True)
            weights = jnp.exp2(scores - top)
            total = jnp.sum(weights, axis=0, keepdims=True)
            lse[pl.ds(head, 1), :] = top + jnp.log2(total)
            own = pl.ds(pl.multiple_of(head * HEAD_DIM, HEAD_DIM), HEAD_DIM)
            mixed_t[own, :] = (
                dot(values_t[own, :], weights.astype(jnp.bfloat16)) * (1.0 / total)
            ).astype(jnp.bfloat16)
        return carry

    lax.fori_loop(0, q.shape[1] // 128, pair_step, 0)
    mixed[...] = mixed_t[...].T
    part[...] = dot_nt(mixed[...], wvo[1]).astype(jnp.bfloat16)


def cross_forward_kernel(
    tokens, own_part, other_part, params, bias_q, wqk, wvo, keys, values_t,
    section, hidden, q, mixed, mixed_t, lse, part,
    scores, weights,
):
    count = tokens.shape[0]
    for at, size in spans(count, 64):
        rows = pl.ds(at, size)
        branch = own_part[rows, :].astype(jnp.float32) + other_part[rows, :].astype(jnp.float32)
        block = tokens[rows, :].astype(jnp.float32) + (branch + params[8:9, :])
        section[rows, :] = block
        hidden[rows, :] = norm_rows(block, params[2:3, :], params[3:4, :])
    q[...] = (dot(hidden[...], wqk[0]) + bias_q[...]).astype(jnp.bfloat16)
    masks = head_masks()
    key_spans = spans(keys.shape[0], 256)

    def pair_step(pair, carry):
        cols = pl.ds(pl.multiple_of(pair * 128, 128), 128)
        for parity in range(2):
            head = pair * 2 + parity
            queries = q[:, cols] * masks[parity]
            top = None
            for at, size in key_spans:
                block = dot_nt(keys[pl.ds(at, size), cols], queries) * (0.125 * LOG2E)
                scores[pl.ds(at, size), :] = block
                block_top = jnp.max(block, axis=0, keepdims=True)
                top = block_top if top is None else jnp.maximum(top, block_top)
            total = jnp.zeros_like(top)
            for at, size in key_spans:
                block = jnp.exp2(scores[pl.ds(at, size), :] - top)
                total = total + jnp.sum(block, axis=0, keepdims=True)
                weights[pl.ds(at, size), :] = block.astype(jnp.bfloat16)
            lse[pl.ds(head, 1), :] = top + jnp.log2(total)
            own = pl.ds(pl.multiple_of(head * HEAD_DIM, HEAD_DIM), HEAD_DIM)
            mixed_t[own, :] = (dot(values_t[own, :], weights[...]) * (1.0 / total)).astype(
                jnp.bfloat16
            )
        return carry

    lax.fori_loop(0, q.shape[1] // 128, pair_step, 0)
    mixed[...] = mixed_t[...].T
    part[...] = dot_nt(mixed[...], wvo[1]).astype(jnp.bfloat16)


def dense_kernel(
    length, section, own_part, other_part, params, bias_hidden, w1, w2, cotangent,
    section_new, hidden, act, grad_pre, grad_low, part, grad_hidden, grad_bias,
):
    count = section.shape[0]
    for at, size in spans(count, 64):
        rows = pl.ds(at, size)
        branch = own_part[rows, :].astype(jnp.float32) + other_part[rows, :].astype(jnp.float32)
        block = section[rows, :] + (branch + params[11:12, :])
        section_new[rows, :] = block
        hidden[rows, :] = norm_rows(block, params[4:5, :], params[5:6, :])
        row_ids = lax.broadcasted_iota(jnp.int32, (size, 1), 0) + at
        valid = (row_ids < length[0]).astype(jnp.float32)
        grad_low[rows, :] = (cotangent[rows, :].astype(jnp.float32) * valid).astype(jnp.bfloat16)

    def step(at, carry):
        cols = pl.ds(pl.multiple_of(at * 256, 256), 256)
        pre_act = dot(hidden[...], w1[:, cols]) + bias_hidden[:, cols]
        spread = 0.5 + 0.5 * lax.erf(pre_act * (2.0**-0.5))
        act[:, cols] = (pre_act * spread).astype(jnp.bfloat16)
        slope = spread + pre_act * (
            jnp.exp2(pre_act * pre_act * (-0.5 * LOG2E)) * 0.3989422804014327
        )
        grad_act = dot(grad_low[...], w2[:, cols]).astype(jnp.bfloat16).astype(jnp.float32)
        grad_block = (grad_act * slope).astype(jnp.bfloat16)
        grad_pre[:, cols] = grad_block
        grad_bias[:, cols] = row_sum(grad_block)
        return carry

    lax.fori_loop(0, act.shape[1] // 256, step, 0)
    part[...] = dot_nt(act[...], w2[...]).astype(jnp.bfloat16)
    grad_hidden[...] = dot_nt(grad_pre[...], w1[...]).astype(jnp.bfloat16)


def put_relative(product, here, order, keep, send, which, cols):
    half = keep.shape[0]
    rows = keep.shape[2]
    for at, (near, far) in enumerate(order):
        place = ((here ^ near) & 3) + (((here >> 2) + far) & 3) * 4
        block = product[pl.ds(pl.multiple_of(place * rows, 16), rows), :]
        target = keep if at < half else send
        target[at % half, which, :, cols] = block.astype(jnp.bfloat16)


def weight_kernel(uses, orders, *refs):
    left_count = 1 + max(left for left, _, _ in uses)
    lefts, rights = refs[1 : 1 + left_count], refs[1 + left_count : 1 + left_count + len(uses)]
    outs = refs[1 + left_count + len(uses) : -2]
    product, turned = refs[-2:]
    width = product.shape[1]
    me = refs[0][0]
    in_turned = None
    for (left, group, which), right in zip(uses, rights):
        left_t = lefts[left]
        if left_t.shape[0] != D:
            if in_turned != left:
                turned[...] = left_t[...].T
                in_turned = left
            left_t = turned

        def step(at, carry, left_t=left_t, right=right, group=group, which=which):
            cols = pl.ds(pl.multiple_of(at * width, width), width)
            product[...] = dot(left_t[...], right[:, cols])
            if orders is None:
                outs[group][which, :, cols] = product[...].astype(jnp.bfloat16)
            else:
                put_relative(
                    product, me, orders[group], outs[2 * group], outs[2 * group + 1], which, cols
                )
            return carry

        lax.fori_loop(0, right.shape[1] // width, step, 0)


def attention_pull(
    keys, values, keys_t, q, grad_mixed, grad_mixed_t, mixed_t, lse, allowed, step,
    grad_keys, grad_values, grad_q_t,
):
    masks = head_masks()
    key_spans = spans(keys.shape[0], step)

    def pair_step(pair, carry):
        cols = pl.ds(pl.multiple_of(pair * 128, 128), 128)
        queries = [q[:, cols] * mask for mask in masks]
        grads = [(grad_mixed[:, cols] * 0.125) * mask for mask in masks]
        heads = [pl.ds(pl.multiple_of(pair * 128 + p * 64, 64), 64) for p in range(2)]
        levels, deltas = [], []
        for parity in range(2):
            levels.append(lse[pl.ds(pair * 2 + parity, 1), :])
            product = grad_mixed_t[heads[parity], :].astype(jnp.float32) * mixed_t[
                heads[parity], :
            ].astype(jnp.float32)
            deltas.append(jnp.sum(product, axis=0, keepdims=True) * 0.125)
        sums = [None, None]
        for at, size in key_spans:
            rows = pl.ds(at, size)
            key_sum = value_sum = None
            for parity in range(2):
                scores = dot_nt(keys[rows, cols], queries[parity]) * (0.125 * LOG2E)
                weights = jnp.exp2(scores - levels[parity])
                if allowed is not None:
                    weights = jnp.where(allowed[rows, :] > 0.5, weights, 0.0)
                grad_soft = dot_nt(values[rows, cols], grads[parity])
                grad_raw = (weights * (grad_soft - deltas[parity])).astype(jnp.bfloat16)
                value_part = dot(weights.astype(jnp.bfloat16), grads[parity])
                key_part = dot(grad_raw, queries[parity])
                query_part = dot(keys_t[heads[parity], rows], grad_raw)
                value_sum = value_part if value_sum is None else value_sum + value_part
                key_sum = key_part if key_sum is None else key_sum + key_part
                sums[parity] = query_part if sums[parity] is None else sums[parity] + query_part
            grad_values[rows, cols] = (value_sum * 8.0).astype(jnp.bfloat16)
            grad_keys[rows, cols] = key_sum.astype(jnp.bfloat16)
        for parity in range(2):
            grad_q_t[heads[parity], :] = sums[parity].astype(jnp.bfloat16)
        return carry

    lax.fori_loop(0, q.shape[1] // 128, pair_step, 0)


def cross_backward_kernel(
    section, grad_part, grad_other, out_part, out_other, grad_top, params,
    wqk, wvo, q, keys, values, keys_t, mixed_t, lse,
    layer_out, grad_section, grad_z, grad_q, grad_keys, grad_values, grad_hidden, vectors, biases,
    grad_mixed, grad_mixed_t, grad_q_t,
):
    count = section.shape[0]
    sums = None
    for at, size in spans(count, 64):
        rows = pl.ds(at, size)
        block = section[rows, :]
        branch = out_part[rows, :].astype(jnp.float32) + out_other[rows, :].astype(jnp.float32)
        layer_out[rows, :] = (block + (branch + params[12:13, :])).astype(jnp.bfloat16)
        grad = grad_part[rows, :].astype(jnp.float32) + grad_other[rows, :].astype(jnp.float32)
        pulled, gain_sum, shift_sum = norm_pull(block, grad, params[4:5, :])
        top = grad_top[rows, :].astype(jnp.float32)
        total = top + pulled
        low = total.astype(jnp.bfloat16)
        grad_section[rows, :] = total
        grad_z[rows, :] = low
        parts = [gain_sum, shift_sum, row_sum(low), jnp.sum(top, axis=0, keepdims=True)]
        sums = parts if sums is None else [old + new for old, new in zip(sums, parts)]
    for at, value in enumerate(sums):
        vectors[at : at + 1, :] = value
    grad_mixed[...] = dot(grad_z[...], wvo[1]).astype(jnp.bfloat16)
    grad_mixed_t[...] = grad_mixed[...].T
    attention_pull(
        keys, values, keys_t, q, grad_mixed, grad_mixed_t, mixed_t, lse, None, 256,
        grad_keys, grad_values, grad_q_t,
    )
    grad_q[...] = grad_q_t[...].T
    grad_hidden[...] = dot_nt(grad_q[...], wqk[0]).astype(jnp.bfloat16)
    biases[0:1, :] = row_sum(grad_q[...])
    biases[1:2, :] = row_sum(grad_values[...])


def self_backward_kernel(
    length, section, grad_section, grad_part, grad_other, params,
    wqk, wvo, q, k, v, mixed_t, lse,
    grad_new, grad_z, grad_q, grad_keys, grad_values, grad_hidden, vectors, biases,
    grad_mixed, grad_mixed_t, grad_q_t, keys_t, allowed,
):
    count = section.shape[0]
    sums = None
    for at, size in spans(count, 64):
        rows = pl.ds(at, size)
        grad = grad_part[rows, :].astype(jnp.float32) + grad_other[rows, :].astype(jnp.float32)
        pulled, gain_sum, shift_sum = norm_pull(section[rows, :], grad, params[2:3, :])
        total = grad_section[rows, :] + pulled
        low = total.astype(jnp.bfloat16)
        grad_new[rows, :] = total
        grad_z[rows, :] = low
        parts = [gain_sum, shift_sum, row_sum(low)]
        sums = parts if sums is None else [old + new for old, new in zip(sums, parts)]
    for at, value in enumerate(sums):
        vectors[at : at + 1, :] = value
    grad_mixed[...] = dot(grad_z[...], wvo[1]).astype(jnp.bfloat16)
    grad_mixed_t[...] = grad_mixed[...].T
    keys_t[...] = k[...].T
    key_ids = lax.broadcasted_iota(jnp.int32, (count, count), 0)
    query_ids = lax.broadcasted_iota(jnp.int32, (count, count), 1)
    allowed[...] = ((key_ids <= query_ids) & (key_ids < length[0])).astype(jnp.float32)
    attention_pull(
        k, v, keys_t, q, grad_mixed, grad_mixed_t, mixed_t, lse, allowed, 256,
        grad_keys, grad_values, grad_q_t,
    )
    grad_q[...] = grad_q_t[...].T
    grad_hidden[...] = (
        dot_nt(grad_q[...], wqk[0])
        + dot_nt(grad_keys[...], wqk[1])
        + dot_nt(grad_values[...], wvo[0])
    ).astype(jnp.bfloat16)
    biases[0:1, :] = row_sum(grad_q[...])
    biases[1:2, :] = row_sum(grad_values[...])


def last_kernel(
    core, tokens, grad_section, grad_part, grad_other, params,
    vectors2, vectors3, biases_self, biases_cross, grad_b1,
    input_grad, vectors,
):
    sums = None
    for at, size in spans(tokens.shape[0], 64):
        rows = pl.ds(at, size)
        grad = grad_part[rows, :].astype(jnp.float32) + grad_other[rows, :].astype(jnp.float32)
        pulled, gain_sum, shift_sum = norm_pull(
            tokens[rows, :].astype(jnp.float32), grad, params[0:1, :]
        )
        input_grad[rows, :] = grad_section[rows, :] + pulled
        parts = [gain_sum, shift_sum]
        sums = parts if sums is None else [old + new for old, new in zip(sums, parts)]
    leader = (core[0] == 0).astype(jnp.float32)
    vectors[...] = jnp.zeros_like(vectors)
    shared = sums + [vectors2[0:1, :], vectors2[1:2, :], vectors3[0:1, :], vectors3[1:2, :]]
    shared = list(enumerate(shared)) + [(8, vectors2[2:3, :]), (11, vectors3[2:3, :]), (12, vectors3[3:4, :])]
    for at, value in shared:
        vectors[at : at + 1, :] = value * leader
    width = biases_self.shape[1]
    cols = pl.ds(pl.multiple_of(core[0] * width, 128), width)
    for at, ref in ((6, biases_self), (9, biases_cross)):
        vectors[at : at + 1, cols] = ref[0:1, :]
        vectors[at + 1 : at + 2, cols] = ref[1:2, :]
    held = grad_b1.shape[1] // D
    for at in range(held):
        vectors[pl.ds(13 + core[0] * held + at, 1), :] = grad_b1[:, at * D : at * D + D]


def enc_kernel(place, grad_keys, grad_values, wqk, wvo, *refs):
    own, out = refs[:-1], refs[-1]
    cols = pl.ds(pl.multiple_of(place[0] * wqk.shape[2], 128), wqk.shape[2])
    for at, size in spans(grad_keys.shape[0], 256):
        rows = pl.ds(at, size)
        total = dot_nt(grad_keys[rows, :], wqk[1, cols, :]) + dot_nt(
            grad_values[rows, :], wvo[0, cols, :]
        )
        if own:
            total = total + own[0][rows, :].astype(jnp.float32)
        if own:
            out[rows, 0, :] = total
        else:
            out[rows, :] = total.astype(out.dtype)


def swap(array, bit):
    count = lax.axis_size("dp")
    return lax.ppermute(array, "dp", [(i, i ^ bit) for i in range(count)])


def swap_core(array):
    return lax.ppermute(array, "mp", [(0, 1), (1, 0)])


def together(*values):
    return lax.optimization_barrier(values)


def sum_round(value, bits):
    me = lax.axis_index("dp")
    offsets = [0]
    for bit in bits:
        offsets = offsets + [offset ^ bit for offset in offsets]
    stack = [value] + [swap(value, offset) for offset in offsets[1:]]
    for bit in bits:
        flip = (me & bit) != 0
        pairs = [(stack[at], stack[at + 1]) for at in range(0, len(stack), 2)]
        stack = [jnp.where(flip, b, a) + jnp.where(flip, a, b) for a, b in pairs]
    return stack[0]


def sum_far(value):
    for bits in [(4, 8)] if lax.axis_size("dp") == 16 else high_bits():
        value = sum_round(value, bits)
    return value


def high_bits():
    return [(1 << k,) for k in range(2, lax.axis_size("dp").bit_length() - 1)]


def sum_near(value):
    value = sum_round(value, (1, 2))
    return value + swap_core(value)


FAR = [0, 4, 8, 12]


def join(stack, came):
    return jnp.concatenate([stack, came], axis=0)


def halves(stack, by_cols):
    at = 3 if by_cols else 1
    return jnp.split(stack, 2, axis=at)


def assemble(parts, split):
    wide, rows, cols = parts[0][0].shape[1:]

    def kernel(*refs):
        stacks, out, sems = refs[: len(parts)], refs[len(parts)], refs[-1]
        here = lax.axis_index("dp")
        copies = []
        for stack, (_, firsts, half) in zip(stacks, parts):
            for at in range(8):
                offset = firsts[at // 4] ^ FAR[at % 4]
                place = pl.multiple_of((here ^ offset) * rows, 16)
                target = out.at[:, pl.ds(place, rows), pl.ds(half * cols, cols)]
                copies.append(pltpu.make_async_copy(stack.at[at], target, sems.at[len(copies)]))
        for copy in copies:
            copy.start()
        for copy in copies:
            copy.wait()

    return pl.pallas_call(
        kernel,
        out_shape=array_of((wide, 16 * rows, split * cols)),
        in_specs=[pl.BlockSpec(memory_space=pl.ANY)] * len(parts),
        out_specs=pl.BlockSpec(memory_space=pltpu.VMEM),
        scratch_shapes=[pltpu.SemaphoreType.DMA((16 * split,))],
        compiler_params=pltpu.CompilerParams(vmem_limit_bytes=16 * 2**20),
        cost_estimate=pl.CostEstimate(flops=0, bytes_accessed=6_000_000, transcendentals=0),
    )(*[stack for stack, _, _ in parts])


def near_offsets(first):
    return (0, first), (3 ^ first, 3)


def weight_parts(uses, lefts, rights):
    count = lax.axis_size("dp")
    direct = count == 16
    cols = rights[0].shape[1]
    wide = len(uses) // 2
    orders = []
    for first in (2, 1):
        order = [(0, step) for step in range(4)]
        for bit in (3 ^ first, first):
            order = order + [(near ^ bit, far) for near, far in order]
        orders.append(order)
    if direct:
        outs = [array_of((8, wide, D // 16, cols))] * 4
    else:
        outs = [array_of((wide, D, cols))] * 2
    flops = 2 * D * cols * sum(right.shape[0] for right in rights)
    return run_kernel(
        functools.partial(weight_kernel, uses, orders if direct else None),
        outs,
        lax.axis_index("dp")[None],
        *lefts,
        *rights,
        scratch=[pltpu.VMEM((D, 384), jnp.float32), pltpu.VMEM((D, BLOCK), jnp.bfloat16)],
        flops=flops,
        moved=4 * len(uses) * D * cols,
    )


def fold(keep, came):
    half = keep.shape[0] // 2
    high = keep[half:].astype(jnp.float32) + came[half:].astype(jnp.float32)
    return (
        keep[:half].astype(jnp.float32) + came[:half].astype(jnp.float32),
        high.astype(jnp.bfloat16),
    )


def shift(array, pairs):
    return lax.ppermute(
        array,
        "dp",
        [(4 * a + near, 4 * b + near) for a, b in pairs for near in range(4)],
    )


def line_ready(lows, cames):
    keep = jnp.concatenate(lows, axis=1)
    came = jnp.concatenate(cames, axis=1)
    total = keep + came.astype(jnp.float32)
    level = lax.axis_index("dp") >> 2
    ends = jnp.where(level < 2, total[3], total[1]).astype(jnp.bfloat16)
    return total, ends


def line_first(ends):
    return shift(ends, [(0, 1), (3, 2)])


def line_middle(total, ends):
    return (total[2] + ends.astype(jnp.float32)).astype(jnp.bfloat16)


def line_second(middle):
    return shift(middle, [(0, 1), (1, 2)]), shift(middle, [(3, 2), (2, 1)])


def line_outer(total, up, down):
    return (
        (total[1] + up.astype(jnp.float32)).astype(jnp.bfloat16),
        (total[3] + down.astype(jnp.float32)).astype(jnp.bfloat16),
    )


def line_third(up, down):
    return shift(up, [(0, 1), (1, 2), (2, 3)]), shift(down, [(3, 2), (2, 1), (1, 0)])


def line_total(total, up, down):
    return total[0] + up.astype(jnp.float32) + down.astype(jnp.float32)


def adamw(weight, gradient, first_moment, second, factor, decays, step_rate):
    clipped = gradient * factor
    first_new = decays[0] * first_moment + (1.0 - decays[0]) * clipped
    second_new = decays[1] * second + (1.0 - decays[1]) * clipped * clipped
    first_hat = first_new / (1.0 - decays[0] ** STEP)
    second_hat = second_new / (1.0 - decays[1] ** STEP)
    weight_new = weight - step_rate * (first_hat / (jnp.sqrt(second_hat) + 1e-08) + 0.1 * weight)
    return (weight_new, first_new, second_new, weight_new.astype(jnp.bfloat16))


def local(
    tokens,
    enc_states,
    lengths,
    cotangent,
    attn_master,
    attn_first,
    attn_second,
    dense_master,
    dense_first,
    dense_second,
    vector_params,
    vector_first,
    vector_second,
    decays,
):
    core = lax.axis_index("mp")
    attn_low = attn_master.astype(jnp.bfloat16)
    dense_low = dense_master.astype(jnp.bfloat16)
    device = lax.axis_index("dp") * lax.axis_size("mp") + core
    own_cols = vector_params.shape[1]
    placed = lax.dynamic_update_slice_in_dim(
        jnp.zeros((vector_params.shape[0], D), jnp.float32), vector_params, device * own_cols, 1
    )
    fast = lax.axis_size("dp") == 16
    head_cols = attn_master.shape[3]
    hidden_cols = dense_master.shape[2]
    head_rows = 2 * (head_cols // 128)
    count = tokens.shape[0]
    keys_count = enc_states.shape[1]
    enc = enc_states[0]
    rows_d = array_of((count, D))
    rows_f = array_of((count, D), jnp.float32)
    rows_h = array_of((count, head_cols))
    turned_h = array_of((head_cols, count))
    lse_shape = array_of((head_rows, count), jnp.float32)
    keys_h = array_of((keys_count, head_cols))
    keys_t_h = array_of((head_cols, keys_count))
    scratch_h = pltpu.VMEM((count, head_cols), jnp.bfloat16)
    scratch_t = pltpu.VMEM((head_cols, count), jnp.bfloat16)
    scratch_s = pltpu.VMEM((count, count), jnp.float32)

    def local_slice(bias_row, span_size):
        return lax.dynamic_slice_in_dim(bias_row, core * span_size, span_size)[None]

    if fast:
        low_self, low_cross, low_w1, low_w2 = attn_low[0], attn_low[1], dense_low[:1], dense_low[1]
        stack, params_far = together(
            join(low_self[None], swap(low_self[None], 4)), sum_far(placed)
        )
        params, stack, low_cross, low_w1, low_w2 = together(
            sum_near(params_far), join(stack, swap(stack, 8)), low_cross, low_w1, low_w2
        )
    else:
        params = sum_near(sum_far(placed))
        attn_all = lax.all_gather(attn_low, "dp", axis=2, tiled=True)
        dense_all = lax.all_gather(dense_low, "dp", axis=1, tiled=True)
        self_qk, self_vo, cross_qk, cross_vo = (
            attn_all[0, :2], attn_all[0, 2:], attn_all[1, :2], attn_all[1, 2:],
        )
        w1, w2 = dense_all[0], dense_all[1]
    bias_q_self = local_slice(params[6], head_cols)
    bias_v_self = local_slice(params[7], head_cols)
    bias_q_cross = local_slice(params[9], head_cols)
    bias_v_cross = local_slice(params[10], head_cols)
    bias_hidden = local_slice(params[13:].reshape(FF), hidden_cols)

    if fast:
        w2 = lax.all_gather(low_w2, "dp", axis=0, tiled=True)
        part_a, part_b = halves(stack, False)
        near_a, near_b, cross_stack = together(
            join(part_a, swap(part_a, 1)),
            join(part_b, swap(part_b, 2)),
            join(low_cross[None], swap(low_cross[None], 4)),
        )
        last_a, last_b, cross_stack, low_w1, length_in = together(
            swap(near_a, 2),
            swap(near_b, 1),
            join(cross_stack, swap(cross_stack, 8)),
            low_w1,
            lengths,
        )
        first, second = near_offsets(1)
        self_qk = assemble([(near_a, first, 0), (last_a, second, 0)], 1)
        first, second = near_offsets(2)
        self_vo = assemble([(near_b, first, 0), (last_b, second, 0)], 1)
    else:
        length_in = lengths
    hidden1, self_q, self_k, self_v, self_mixed, self_mixed_t, self_lse, self_part = run_kernel(
        self_forward_kernel,
        [rows_d, rows_h, rows_h, rows_h, rows_h, turned_h, lse_shape, rows_d],
        length_in, tokens, params, bias_q_self, bias_v_self, self_qk, self_vo,
        scratch=[scratch_t, scratch_s],
        moved=30_000_000,
    )
    if fast:
        part_a, part_b = halves(cross_stack, False)
        near_a, near_b, w1_stack, self_part = together(
            join(part_a, swap(part_a, 1)),
            join(part_b, swap(part_b, 2)),
            join(low_w1[None], swap(low_w1[None], 4)),
            self_part,
        )
        last_a, last_b, w1_stack, self_other, bias_v_cross = together(
            swap(near_a, 2),
            swap(near_b, 1),
            join(w1_stack, swap(w1_stack, 8)),
            swap_core(self_part),
            bias_v_cross,
        )
        first, second = near_offsets(1)
        cross_qk = assemble([(near_a, first, 0), (last_a, second, 0)], 1)
        first, second = near_offsets(2)
        cross_vo = assemble([(near_b, first, 0), (last_b, second, 0)], 1)
    else:
        self_other = swap_core(self_part)
    cross_k, cross_v, cross_k_t, cross_v_t, enc_t = run_kernel(
        cross_keys_kernel,
        [keys_h, keys_h, keys_t_h, keys_t_h, array_of((D, keys_count))],
        enc, cross_qk, cross_vo, bias_v_cross,
        moved=25_000_000,
    )
    if fast:
        part_a, part_b = halves(w1_stack, True)
        near_a, near_b, cross_k = together(
            join(part_a, swap(part_a, 1)), join(part_b, swap(part_b, 2)), cross_k
        )
    section1, hidden2, cross_q, cross_mixed, cross_mixed_t, cross_lse, cross_part = run_kernel(
        cross_forward_kernel,
        [rows_f, rows_d, rows_h, rows_h, turned_h, lse_shape, rows_d],
        tokens, self_part, self_other, params, bias_q_cross, cross_qk, cross_vo,
        cross_k, cross_v_t,
        scratch=[
            pltpu.VMEM((keys_count, count), jnp.float32),
            pltpu.VMEM((keys_count, count), jnp.bfloat16),
        ],
        moved=70_000_000,
    )
    if fast:
        last_a, last_b, cross_part = together(swap(near_a, 2), swap(near_b, 1), cross_part)
        (first, second), (third, fourth) = near_offsets(1), near_offsets(2)
        w1 = assemble(
            [(near_a, first, 0), (last_a, second, 0), (near_b, third, 1), (last_b, fourth, 1)], 2
        )[0]
    hidden_rows = array_of((count, hidden_cols))
    section2, hidden3, act, grad_pre, grad_low, out_part, grad_h3, grad_b1 = run_kernel(
        dense_kernel,
        [rows_f, rows_d, hidden_rows, hidden_rows, rows_d, rows_d, rows_d,
         array_of((1, hidden_cols), jnp.float32)],
        lengths, section1, cross_part, swap_core(cross_part), params, bias_hidden, w1, w2, cotangent,
        moved=50_000_000,
    )
    dense_parts = weight_parts(((0, 0, 0), (1, 1, 0)), (hidden3, grad_low), (grad_pre, act))
    dense_parts, grad_h3_other, out_other = together(
        dense_parts, swap_core(grad_h3), swap_core(out_part)
    )
    (
        layer_out, grad_section2, grad_z2, cross_dq, cross_dk, cross_dv, grad_h2, vectors3, biases_cross,
    ) = run_kernel(
        cross_backward_kernel,
        [rows_d, rows_f, rows_d, rows_h, keys_h, keys_h, rows_d,
         array_of((4, D), jnp.float32), array_of((2, head_cols), jnp.float32)],
        section2, grad_h3, grad_h3_other, out_part, out_other, grad_low, params,
        cross_qk, cross_vo, cross_q, cross_k, cross_v, cross_k_t, cross_mixed_t, cross_lse,
        scratch=[scratch_h, scratch_t, scratch_t],
        moved=120_000_000,
    )
    if fast:
        keep_a, send_a, keep_b, send_b = dense_parts
        came_a, came_b, cross_dq, cross_dk, grad_h2 = together(
            swap(send_a, 2), swap(send_b, 1), cross_dq, cross_dk, grad_h2
        )
        low_a, high_a = fold(keep_a, came_a)
        low_b, high_b = fold(keep_b, came_b)
    cross_parts = weight_parts(
        ((0, 0, 0), (1, 0, 1), (1, 1, 0), (2, 1, 1)),
        (hidden2, enc_t, grad_z2),
        (cross_dq, cross_dk, cross_dv, cross_mixed),
    )
    enc_other = run_kernel(
        enc_kernel,
        array_of((keys_count, head_cols)),
        1 - core[None], cross_dk, cross_dv, cross_qk, cross_vo,
        moved=15_000_000,
    )
    grad_h2_other = swap_core(grad_h2)
    length_back = lengths
    if fast:
        came_a, came_b, cross_parts, enc_other, grad_h2_other, length_back = together(
            swap(high_a, 1), swap(high_b, 2), cross_parts, enc_other, grad_h2_other, lengths
        )
        dense_total, ends = line_ready([low_a, low_b], [came_a, came_b])
    (
        grad_section1, grad_z1, self_dq, self_dk, self_dv, grad_h1, vectors2, biases_self,
    ) = run_kernel(
        self_backward_kernel,
        [rows_f, rows_d, rows_h, rows_h, rows_h, rows_d,
         array_of((3, D), jnp.float32), array_of((2, head_cols), jnp.float32)],
        length_back, section1, grad_section2, grad_h2, grad_h2_other, params,
        self_qk, self_vo, self_q, self_k, self_v, self_mixed_t, self_lse,
        scratch=[scratch_h, scratch_t, scratch_t, scratch_t, scratch_s],
        moved=60_000_000,
    )
    enc_came = swap_core(enc_other)
    if fast:
        keep_a, send_a, keep_b, send_b = cross_parts
        came_a, came_b, ends, self_dq, grad_h1, enc_came = together(
            swap(send_a, 2), swap(send_b, 1), line_first(ends), self_dq, grad_h1, enc_came
        )
        low_a, high_a = fold(keep_a, came_a)
        low_b, high_b = fold(keep_b, came_b)
        middle = line_middle(dense_total, ends)
    self_parts = weight_parts(
        ((0, 0, 0), (0, 0, 1), (0, 1, 0), (1, 1, 1)),
        (hidden1, grad_z1),
        (self_dq, self_dk, self_dv, self_mixed),
    )
    enc_grad = run_kernel(
        enc_kernel,
        array_of((keys_count, 1, head_cols), jnp.float32),
        core[None], cross_dk, cross_dv, cross_qk, cross_vo, enc_came,
        moved=20_000_000,
    )
    grad_h1_other = swap_core(grad_h1)
    core_in = core[None]
    if fast:
        came_a, came_b, (up, down), self_parts, enc_grad, grad_h1_other, core_in = together(
            swap(high_a, 1), swap(high_b, 2), line_second(middle),
            self_parts, enc_grad, grad_h1_other, core_in,
        )
        cross_total, cross_ends = line_ready([low_a, low_b], [came_a, came_b])
        up, down = line_outer(dense_total, up, down)
    input_grad, vector_grad = run_kernel(
        last_kernel,
        [rows_f, array_of(params.shape, jnp.float32)],
        core_in, tokens, grad_section1, grad_h1, grad_h1_other, params,
        vectors2, vectors3, biases_self, biases_cross, grad_b1,
        moved=12_000_000,
    )
    if fast:
        keep_a, send_a, keep_b, send_b = self_parts
        came_a, came_b, (up, down), cross_ends, vector_grad = together(
            swap(send_a, 2), swap(send_b, 1), line_third(up, down), line_first(cross_ends),
            vector_grad,
        )
        dense_sum = line_total(dense_total, up, down)
        low_a, high_a = fold(keep_a, came_a)
        low_b, high_b = fold(keep_b, came_b)
        middle = line_middle(cross_total, cross_ends)
        came_a, came_b, (up, down), vector_all = together(
            swap(high_a, 1), swap(high_b, 2), line_second(middle), sum_near(sum_far(vector_grad))
        )
        self_total, ends = line_ready([low_a, low_b], [came_a, came_b])
        up, down = line_outer(cross_total, up, down)
        (up, down), ends = together(line_third(up, down), line_first(ends))
        cross_sum = line_total(cross_total, up, down)
        middle = line_middle(self_total, ends)
        (up, down), = together(line_second(middle))
        up, down = line_third(*line_outer(self_total, up, down))
        self_sum = line_total(self_total, up, down)
    else:
        vector_all = sum_near(sum_far(vector_grad))
        self_sum, cross_sum, dense_sum = [
            jnp.concatenate(
                [
                    lax.psum_scatter(
                        part.astype(jnp.float32), "dp", scatter_dimension=1, tiled=True
                    )
                    for part in parts
                ],
                axis=0,
            )
            for parts in (self_parts, cross_parts, dense_parts)
        ]
    enc_grad = enc_grad.transpose(1, 0, 2)
    vector_sum = lax.dynamic_slice_in_dim(vector_all, device * own_cols, own_cols, 1)
    vector_squares = jnp.sum(vector_all * vector_all)
    attn_sum = jnp.stack([self_sum, cross_sum])
    local_squares = jnp.sum(attn_sum * attn_sum) + jnp.sum(dense_sum * dense_sum)
    square_total = sum_near(sum_far(jnp.full((8, 128), local_squares)))[0, 0] + vector_squares
    clip_norm = jnp.sqrt(square_total)
    factor = jnp.minimum(1.0, 1.0 / (clip_norm + 1e-06))
    bias_gradient = vector_sum[12] * factor
    attn_new, attn_first_new, attn_second_new, attn_copy = adamw(
        attn_master, attn_sum, attn_first, attn_second, factor, decays, attn_rate
    )
    dense_new, dense_first_new, dense_second_new, dense_copy = adamw(
        dense_master, dense_sum, dense_first, dense_second, factor, decays, dense_rate
    )
    vector_new, vector_first_new, vector_second_new, vector_copy = adamw(
        vector_params, vector_sum, vector_first, vector_second, factor, decays, vector_rate
    )
    return (
        layer_out,
        input_grad,
        enc_grad,
        clip_norm,
        attn_new,
        attn_first_new,
        attn_second_new,
        attn_copy,
        dense_new,
        dense_first_new,
        dense_second_new,
        dense_copy,
        vector_new,
        vector_first_new,
        vector_second_new,
        vector_copy,
        bias_gradient,
    )


def solution(mesh):
    return jax.shard_map(
        local,
        mesh=mesh,
        in_specs=(
            P("dp", None),
            P("dp", None, None),
            P("dp"),
            P("dp", None),
            P(None, None, "dp", "mp"),
            P(None, None, "dp", "mp"),
            P(None, None, "dp", "mp"),
            P(None, "dp", "mp"),
            P(None, "dp", "mp"),
            P(None, "dp", "mp"),
            P(None, ("dp", "mp")),
            P(None, ("dp", "mp")),
            P(None, ("dp", "mp")),
            P(),
        ),
        out_specs=(
            P("dp", None),
            P("dp", None),
            P("dp", None, "mp"),
            P(),
            P(None, None, "dp", "mp"),
            P(None, None, "dp", "mp"),
            P(None, None, "dp", "mp"),
            P(None, None, "dp", "mp"),
            P(None, "dp", "mp"),
            P(None, "dp", "mp"),
            P(None, "dp", "mp"),
            P(None, "dp", "mp"),
            P(None, ("dp", "mp")),
            P(None, ("dp", "mp")),
            P(None, ("dp", "mp")),
            P(None, ("dp", "mp")),
            P(("dp", "mp")),
        ),
        check_vma=False,
    )
```

```python
import functools

import jax
import jax.numpy as jnp
from jax import lax
from jax.experimental import pallas as pl
from jax.experimental.pallas import tpu as pltpu
from jax.sharding import PartitionSpec as P

D = 768
HEAD_DIM = 64
FF = 3072
BLOCK = 448
STEP = 3


attn_rate = 0.08
dense_rate = 0.03
vector_rate = 0.3
LOG2E = 1.4426950408889634


def dot(left_side, right_side):
    return jnp.dot(left_side, right_side, preferred_element_type=jnp.float32)


def dot_nt(left_side, right_side):
    return lax.dot_general(
        left_side, right_side, (((1,), (1,)), ((), ())), preferred_element_type=jnp.float32
    )


def spans(total, step):
    return [(at, min(step, total - at)) for at in range(0, total, step)]


def unit_norm(values):
    centred = values - jnp.mean(values, axis=-1, keepdims=True)
    inverse = lax.rsqrt(jnp.mean(centred * centred, axis=-1, keepdims=True) + 1e-05)
    return centred * inverse, inverse


def norm_rows(values, gain, shift):
    unit, _ = unit_norm(values)
    return (unit * gain + shift).astype(jnp.bfloat16)


def norm_pull(values, grad, gain):
    unit, inverse = unit_norm(values)
    scaled = grad * gain
    pulled = inverse * (
        scaled
        - jnp.mean(scaled, axis=-1, keepdims=True)
        - unit * jnp.mean(scaled * unit, axis=-1, keepdims=True)
    )
    return (
        pulled,
        jnp.sum(grad * unit, axis=0, keepdims=True),
        jnp.sum(grad, axis=0, keepdims=True),
    )


def head_masks():
    lane = lax.broadcasted_iota(jnp.int32, (1, 2 * HEAD_DIM), 1)
    return [(lane < HEAD_DIM).astype(jnp.bfloat16), (lane >= HEAD_DIM).astype(jnp.bfloat16)]


def row_sum(values):
    return jnp.sum(values.astype(jnp.float32), axis=0, keepdims=True)


def run_kernel(kernel, out_shapes, *operands, scratch=(), flops=0, moved=0):
    spaces = [
        pl.BlockSpec(
            memory_space=pltpu.SMEM if operand.dtype == jnp.int32 else pltpu.VMEM
        )
        for operand in operands
    ]
    return pl.pallas_call(
        kernel,
        out_shape=out_shapes,
        in_specs=spaces,
        out_specs=jax.tree.map(lambda _: pl.BlockSpec(memory_space=pltpu.VMEM), out_shapes),
        scratch_shapes=list(scratch),
        compiler_params=pltpu.CompilerParams(vmem_limit_bytes=56 * 2**20),
        cost_estimate=pl.CostEstimate(flops=flops, bytes_accessed=moved, transcendentals=0),
    )(*operands)


def array_of(shape, dtype=jnp.bfloat16):
    return jax.ShapeDtypeStruct(shape, dtype)


def cross_keys_kernel(enc, wqk, wvo, bias_v, keys, values, keys_t, values_t, enc_t):
    for at, size in spans(enc.shape[0], 256):
        rows = pl.ds(at, size)
        block = enc[rows, :]
        enc_t[:, rows] = block.T
        key_block = dot(block, wqk[1]).astype(jnp.bfloat16)
        value_block = (dot(block, wvo[0]) + bias_v[...]).astype(jnp.bfloat16)
        keys[rows, :] = key_block
        values[rows, :] = value_block
        keys_t[:, rows] = key_block.T
        values_t[:, rows] = value_block.T


def self_forward_kernel(
    length, tokens, params, bias_q, bias_v, wqk, wvo,
    hidden, q, k, v, mixed, mixed_t, lse, part,
    values_t, allowed,
):
    count = tokens.shape[0]
    for at, size in spans(count, 64):
        rows = pl.ds(at, size)
        hidden[rows, :] = norm_rows(
            tokens[rows, :].astype(jnp.float32), params[0:1, :], params[1:2, :]
        )
    q[...] = (dot(hidden[...], wqk[0]) + bias_q[...]).astype(jnp.bfloat16)
    k[...] = dot(hidden[...], wqk[1]).astype(jnp.bfloat16)
    v[...] = (dot(hidden[...], wvo[0]) + bias_v[...]).astype(jnp.bfloat16)
    values_t[...] = v[...].T
    key_ids = lax.broadcasted_iota(jnp.int32, (count, count), 0)
    query_ids = lax.broadcasted_iota(jnp.int32, (count, count), 1)
    allowed[...] = ((key_ids <= query_ids) & (key_ids < length[0])).astype(jnp.float32)
    masks = head_masks()

    def pair_step(pair, carry):
        cols = pl.ds(pl.multiple_of(pair * 128, 128), 128)
        for parity in range(2):
            head = pair * 2 + parity
            scores = dot_nt(k[:, cols], q[:, cols] * masks[parity]) * (0.125 * LOG2E)
            scores = jnp.where(allowed[...] > 0.5, scores, -1e30)
            top = jnp.max(scores, axis=0, keepdims=True)
            weights = jnp.exp2(scores - top)
            total = jnp.sum(weights, axis=0, keepdims=True)
            lse[pl.ds(head, 1), :] = top + jnp.log2(total)
            own = pl.ds(pl.multiple_of(head * HEAD_DIM, HEAD_DIM), HEAD_DIM)
            mixed_t[own, :] = (
                dot(values_t[own, :], weights.astype(jnp.bfloat16)) * (1.0 / total)
            ).astype(jnp.bfloat16)
        return carry

    lax.fori_loop(0, q.shape[1] // 128, pair_step, 0)
    mixed[...] = mixed_t[...].T
    part[...] = dot_nt(mixed[...], wvo[1]).astype(jnp.bfloat16)


def cross_forward_kernel(
    tokens, own_part, other_part, params, bias_q, wqk, wvo, keys, values_t,
    section, hidden, q, mixed, mixed_t, lse, part,
    scores, weights,
):
    count = tokens.shape[0]
    for at, size in spans(count, 64):
        rows = pl.ds(at, size)
        branch = own_part[rows, :].astype(jnp.float32) + other_part[rows, :].astype(jnp.float32)
        block = tokens[rows, :].astype(jnp.float32) + (branch + params[8:9, :])
        section[rows, :] = block
        hidden[rows, :] = norm_rows(block, params[2:3, :], params[3:4, :])
    q[...] = (dot(hidden[...], wqk[0]) + bias_q[...]).astype(jnp.bfloat16)
    masks = head_masks()
    key_spans = spans(keys.shape[0], 256)

    def pair_step(pair, carry):
        cols = pl.ds(pl.multiple_of(pair * 128, 128), 128)
        for parity in range(2):
            head = pair * 2 + parity
            queries = q[:, cols] * masks[parity]
            top = None
            for at, size in key_spans:
                block = dot_nt(keys[pl.ds(at, size), cols], queries) * (0.125 * LOG2E)
                scores[pl.ds(at, size), :] = block
                block_top = jnp.max(block, axis=0, keepdims=True)
                top = block_top if top is None else jnp.maximum(top, block_top)
            total = jnp.zeros_like(top)
            for at, size in key_spans:
                block = jnp.exp2(scores[pl.ds(at, size), :] - top)
                total = total + jnp.sum(block, axis=0, keepdims=True)
                weights[pl.ds(at, size), :] = block.astype(jnp.bfloat16)
            lse[pl.ds(head, 1), :] = top + jnp.log2(total)
            own = pl.ds(pl.multiple_of(head * HEAD_DIM, HEAD_DIM), HEAD_DIM)
            mixed_t[own, :] = (dot(values_t[own, :], weights[...]) * (1.0 / total)).astype(
                jnp.bfloat16
            )
        return carry

    lax.fori_loop(0, q.shape[1] // 128, pair_step, 0)
    mixed[...] = mixed_t[...].T
    part[...] = dot_nt(mixed[...], wvo[1]).astype(jnp.bfloat16)


def dense_in_kernel(
    length, section, own_part, other_part, params, bias_hidden, w1, cotangent,
    section_new, hidden, act, slope, grad_low,
):
    count = section.shape[0]
    for at, size in spans(count, 64):
        rows = pl.ds(at, size)
        branch = own_part[rows, :].astype(jnp.float32) + other_part[rows, :].astype(jnp.float32)
        block = section[rows, :] + (branch + params[11:12, :])
        section_new[rows, :] = block
        hidden[rows, :] = norm_rows(block, params[4:5, :], params[5:6, :])
        row_ids = lax.broadcasted_iota(jnp.int32, (size, 1), 0) + at
        valid = (row_ids < length[0]).astype(jnp.float32)
        grad_low[rows, :] = (cotangent[rows, :].astype(jnp.float32) * valid).astype(jnp.bfloat16)

    def step(at, carry):
        cols = pl.ds(pl.multiple_of(at * 256, 256), 256)
        pre_act = dot(hidden[...], w1[:, cols]) + bias_hidden[:, cols]
        spread = 0.5 + 0.5 * lax.erf(pre_act * (2.0**-0.5))
        act[:, cols] = (pre_act * spread).astype(jnp.bfloat16)
        density = jnp.exp2(pre_act * pre_act * (-0.5 * LOG2E)) * 0.3989422804014327
        slope[:, cols] = (spread + pre_act * density).astype(jnp.bfloat16)
        return carry

    lax.fori_loop(0, act.shape[1] // 256, step, 0)


def dense_out_kernel(
    act, slope, grad_low, w1, w2,
    grad_pre, part, grad_hidden, grad_bias,
):
    def step(at, carry):
        cols = pl.ds(pl.multiple_of(at * 256, 256), 256)
        grad_act = dot(grad_low[...], w2[:, cols]).astype(jnp.bfloat16).astype(jnp.float32)
        grad_block = (grad_act * slope[:, cols].astype(jnp.float32)).astype(jnp.bfloat16)
        grad_pre[:, cols] = grad_block
        grad_bias[:, cols] = row_sum(grad_block)
        return carry

    lax.fori_loop(0, act.shape[1] // 256, step, 0)
    part[...] = dot_nt(act[...], w2[...]).astype(jnp.bfloat16)
    grad_hidden[...] = dot_nt(grad_pre[...], w1[...]).astype(jnp.bfloat16)


def put_relative(product, here, order, keep, send, which, cols):
    half = keep.shape[0]
    rows = keep.shape[2]
    for at, offset in enumerate(order):
        block = product[pl.ds(pl.multiple_of((here ^ offset) * rows, 16), rows), :]
        target = keep if at < half else send
        target[at % half, which, :, cols] = block.astype(jnp.bfloat16)


def weight_kernel(uses, lefts_count, orders, *refs):
    rights_count = 1 + max(right for _, right, _, _, _ in uses)
    lefts, rights = refs[1 : 1 + lefts_count], refs[1 + lefts_count : 1 + lefts_count + rights_count]
    outs = refs[1 + lefts_count + rights_count : -2]
    product, turned = refs[-2:]
    width = product.shape[1]
    me = refs[0][0]
    in_turned = None
    for left, right, first, group, which in uses:
        left_t, right = lefts[left], rights[right]
        if left_t.shape[0] != D:
            if in_turned != left:
                turned[...] = left_t[...].T
                in_turned = left
            left_t = turned

        def step(at, carry, left_t=left_t, right=right, first=first, group=group, which=which):
            cols = pl.ds(pl.multiple_of(at * width, width), width)
            taken = pl.ds(pl.multiple_of(first + at * width, width), width)
            product[...] = dot(left_t[...], right[:, taken])
            if orders is None:
                outs[group][which, :, cols] = product[...].astype(jnp.bfloat16)
            else:
                put_relative(
                    product, me, orders[group], outs[2 * group], outs[2 * group + 1], which, cols
                )
            return carry

        lax.fori_loop(0, outs[0].shape[-1] // width, step, 0)


def attention_pull(
    keys, values, keys_t, q, grad_mixed, grad_mixed_t, mixed_t, lse, allowed, step,
    grad_keys, grad_values, grad_q_t,
):
    masks = head_masks()
    key_spans = spans(keys.shape[0], step)

    def pair_step(pair, carry):
        cols = pl.ds(pl.multiple_of(pair * 128, 128), 128)
        queries = [q[:, cols] * mask for mask in masks]
        grads = [(grad_mixed[:, cols] * 0.125) * mask for mask in masks]
        heads = [pl.ds(pl.multiple_of(pair * 128 + p * 64, 64), 64) for p in range(2)]
        levels, deltas = [], []
        for parity in range(2):
            levels.append(lse[pl.ds(pair * 2 + parity, 1), :])
            product = grad_mixed_t[heads[parity], :].astype(jnp.float32) * mixed_t[
                heads[parity], :
            ].astype(jnp.float32)
            deltas.append(jnp.sum(product, axis=0, keepdims=True) * 0.125)
        sums = [None, None]
        for at, size in key_spans:
            rows = pl.ds(at, size)
            key_sum = value_sum = None
            for parity in range(2):
                scores = dot_nt(keys[rows, cols], queries[parity]) * (0.125 * LOG2E)
                weights = jnp.exp2(scores - levels[parity])
                if allowed is not None:
                    weights = jnp.where(allowed[rows, :] > 0.5, weights, 0.0)
                grad_soft = dot_nt(values[rows, cols], grads[parity])
                grad_raw = (weights * (grad_soft - deltas[parity])).astype(jnp.bfloat16)
                value_part = dot(weights.astype(jnp.bfloat16), grads[parity])
                key_part = dot(grad_raw, queries[parity])
                query_part = dot(keys_t[heads[parity], rows], grad_raw)
                value_sum = value_part if value_sum is None else value_sum + value_part
                key_sum = key_part if key_sum is None else key_sum + key_part
                sums[parity] = query_part if sums[parity] is None else sums[parity] + query_part
            grad_values[rows, cols] = (value_sum * 8.0).astype(jnp.bfloat16)
            grad_keys[rows, cols] = key_sum.astype(jnp.bfloat16)
        for parity in range(2):
            grad_q_t[heads[parity], :] = sums[parity].astype(jnp.bfloat16)
        return carry

    lax.fori_loop(0, q.shape[1] // 128, pair_step, 0)


def cross_backward_kernel(
    section, grad_part, grad_other, out_part, out_other, grad_top, params,
    wqk, wvo, q, keys, values, keys_t, mixed_t, lse,
    layer_out, grad_section, grad_z, grad_q, grad_keys, grad_values, grad_hidden, vectors, biases,
    grad_mixed, grad_mixed_t, grad_q_t,
):
    count = section.shape[0]
    sums = None
    for at, size in spans(count, 64):
        rows = pl.ds(at, size)
        block = section[rows, :]
        branch = out_part[rows, :].astype(jnp.float32) + out_other[rows, :].astype(jnp.float32)
        layer_out[rows, :] = (block + (branch + params[12:13, :])).astype(jnp.bfloat16)
        grad = grad_part[rows, :].astype(jnp.float32) + grad_other[rows, :].astype(jnp.float32)
        pulled, gain_sum, shift_sum = norm_pull(block, grad, params[4:5, :])
        top = grad_top[rows, :].astype(jnp.float32)
        total = top + pulled
        low = total.astype(jnp.bfloat16)
        grad_section[rows, :] = total
        grad_z[rows, :] = low
        parts = [gain_sum, shift_sum, row_sum(low), jnp.sum(top, axis=0, keepdims=True)]
        sums = parts if sums is None else [old + new for old, new in zip(sums, parts)]
    for at, value in enumerate(sums):
        vectors[at : at + 1, :] = value
    grad_mixed[...] = dot(grad_z[...], wvo[1]).astype(jnp.bfloat16)
    grad_mixed_t[...] = grad_mixed[...].T
    attention_pull(
        keys, values, keys_t, q, grad_mixed, grad_mixed_t, mixed_t, lse, None, 256,
        grad_keys, grad_values, grad_q_t,
    )
    grad_q[...] = grad_q_t[...].T
    grad_hidden[...] = dot_nt(grad_q[...], wqk[0]).astype(jnp.bfloat16)
    biases[0:1, :] = row_sum(grad_q[...])
    biases[1:2, :] = row_sum(grad_values[...])


def self_backward_kernel(
    length, section, grad_section, grad_part, grad_other, params,
    wqk, wvo, q, k, v, mixed_t, lse,
    grad_new, grad_z, grad_q, grad_keys, grad_values, grad_hidden, vectors, biases,
    grad_mixed, grad_mixed_t, grad_q_t, keys_t, allowed,
):
    count = section.shape[0]
    sums = None
    for at, size in spans(count, 64):
        rows = pl.ds(at, size)
        grad = grad_part[rows, :].astype(jnp.float32) + grad_other[rows, :].astype(jnp.float32)
        pulled, gain_sum, shift_sum = norm_pull(section[rows, :], grad, params[2:3, :])
        total = grad_section[rows, :] + pulled
        low = total.astype(jnp.bfloat16)
        grad_new[rows, :] = total
        grad_z[rows, :] = low
        parts = [gain_sum, shift_sum, row_sum(low)]
        sums = parts if sums is None else [old + new for old, new in zip(sums, parts)]
    for at, value in enumerate(sums):
        vectors[at : at + 1, :] = value
    grad_mixed[...] = dot(grad_z[...], wvo[1]).astype(jnp.bfloat16)
    grad_mixed_t[...] = grad_mixed[...].T
    keys_t[...] = k[...].T
    key_ids = lax.broadcasted_iota(jnp.int32, (count, count), 0)
    query_ids = lax.broadcasted_iota(jnp.int32, (count, count), 1)
    allowed[...] = ((key_ids <= query_ids) & (key_ids < length[0])).astype(jnp.float32)
    attention_pull(
        k, v, keys_t, q, grad_mixed, grad_mixed_t, mixed_t, lse, allowed, 256,
        grad_keys, grad_values, grad_q_t,
    )
    grad_q[...] = grad_q_t[...].T
    grad_hidden[...] = (
        dot_nt(grad_q[...], wqk[0])
        + dot_nt(grad_keys[...], wqk[1])
        + dot_nt(grad_values[...], wvo[0])
    ).astype(jnp.bfloat16)
    biases[0:1, :] = row_sum(grad_q[...])
    biases[1:2, :] = row_sum(grad_values[...])


def last_kernel(
    core, tokens, grad_section, grad_part, grad_other, params,
    vectors2, vectors3, biases_self, biases_cross, grad_b1,
    input_grad, vectors,
):
    sums = None
    for at, size in spans(tokens.shape[0], 64):
        rows = pl.ds(at, size)
        grad = grad_part[rows, :].astype(jnp.float32) + grad_other[rows, :].astype(jnp.float32)
        pulled, gain_sum, shift_sum = norm_pull(
            tokens[rows, :].astype(jnp.float32), grad, params[0:1, :]
        )
        input_grad[rows, :] = grad_section[rows, :] + pulled
        parts = [gain_sum, shift_sum]
        sums = parts if sums is None else [old + new for old, new in zip(sums, parts)]
    leader = (core[0] == 0).astype(jnp.float32)
    vectors[...] = jnp.zeros_like(vectors)
    shared = sums + [vectors2[0:1, :], vectors2[1:2, :], vectors3[0:1, :], vectors3[1:2, :]]
    shared = list(enumerate(shared)) + [(8, vectors2[2:3, :]), (11, vectors3[2:3, :]), (12, vectors3[3:4, :])]
    for at, value in shared:
        vectors[at : at + 1, :] = value * leader
    width = biases_self.shape[1]
    cols = pl.ds(pl.multiple_of(core[0] * width, 128), width)
    for at, ref in ((6, biases_self), (9, biases_cross)):
        vectors[at : at + 1, cols] = ref[0:1, :]
        vectors[at + 1 : at + 2, cols] = ref[1:2, :]
    held = grad_b1.shape[1] // D
    for at in range(held):
        vectors[pl.ds(13 + core[0] * held + at, 1), :] = grad_b1[:, at * D : at * D + D]


def enc_kernel(place, grad_keys, grad_values, wqk, wvo, *refs):
    own, out = refs[:-1], refs[-1]
    cols = pl.ds(pl.multiple_of(place[0] * wqk.shape[2], 128), wqk.shape[2])
    for at, size in spans(grad_keys.shape[0], 256):
        rows = pl.ds(at, size)
        total = dot_nt(grad_keys[rows, :], wqk[1, cols, :]) + dot_nt(
            grad_values[rows, :], wvo[0, cols, :]
        )
        if own:
            total = total + own[0][rows, :].astype(jnp.float32)
        if own:
            out[rows, 0, :] = total
        else:
            out[rows, :] = total.astype(out.dtype)


def swap(array, bit):
    count = lax.axis_size("dp")
    return lax.ppermute(array, "dp", [(i, i ^ bit) for i in range(count)])


def swap_core(array):
    return lax.ppermute(array, "mp", [(0, 1), (1, 0)])


def together(*values):
    return lax.optimization_barrier(values)


def sum_round(value, bits):
    me = lax.axis_index("dp")
    offsets = [0]
    for bit in bits:
        offsets = offsets + [offset ^ bit for offset in offsets]
    stack = [value] + [swap(value, offset) for offset in offsets[1:]]
    for bit in bits:
        flip = (me & bit) != 0
        pairs = [(stack[at], stack[at + 1]) for at in range(0, len(stack), 2)]
        stack = [jnp.where(flip, b, a) + jnp.where(flip, a, b) for a, b in pairs]
    return stack[0]


def sum_far(value):
    for bits in [(4, 8)] if lax.axis_size("dp") == 16 else high_bits():
        value = sum_round(value, bits)
    return value


def high_bits():
    return [(1 << k,) for k in range(2, lax.axis_size("dp").bit_length() - 1)]


def sum_near(value):
    value = sum_round(value, (1, 2))
    return value + swap_core(value)


FAR = [0, 4, 8, 12]


def join(stack, came):
    return jnp.concatenate([stack, came], axis=0)


def far_stack(piece):
    return jnp.concatenate([piece] + [swap(piece, offset) for offset in FAR[1:]], axis=0)


def near_first(halves_of):
    return [join(part, swap(part, bit)) for part, bit in zip(halves_of, (1, 2))]


def near_second(nears):
    return [swap(near, bit) for near, bit in zip(nears, (2, 1))]


def assemble_pair(nears, lasts):
    return [
        assemble([(near, first, 0), (last, second, 0)], 1)
        for near, last, (first, second) in zip(nears, lasts, map(near_offsets, (1, 2)))
    ]


def assemble_wide(nears, lasts):
    parts = []
    for half in range(2):
        first, second = near_offsets(half + 1)
        parts += [(nears[half], first, half), (lasts[half], second, half)]
    return assemble(parts, 2)[0]


def halves(stack, by_cols):
    at = 3 if by_cols else 1
    return jnp.split(stack, 2, axis=at)


def assemble(parts, split):
    wide, rows, cols = parts[0][0].shape[1:]

    def kernel(*refs):
        stacks, out, sems = refs[: len(parts)], refs[len(parts)], refs[-1]
        here = lax.axis_index("dp")
        copies = []
        for stack, (_, firsts, half) in zip(stacks, parts):
            for at in range(8):
                offset = firsts[at // 4] ^ FAR[at % 4]
                place = pl.multiple_of((here ^ offset) * rows, 16)
                target = out.at[:, pl.ds(place, rows), pl.ds(half * cols, cols)]
                copies.append(pltpu.make_async_copy(stack.at[at], target, sems.at[len(copies)]))
        for copy in copies:
            copy.start()
        for copy in copies:
            copy.wait()

    return pl.pallas_call(
        kernel,
        out_shape=array_of((wide, 16 * rows, split * cols)),
        in_specs=[pl.BlockSpec(memory_space=pl.ANY)] * len(parts),
        out_specs=pl.BlockSpec(memory_space=pltpu.VMEM),
        scratch_shapes=[pltpu.SemaphoreType.DMA((16 * split,))],
        compiler_params=pltpu.CompilerParams(vmem_limit_bytes=16 * 2**20),
        cost_estimate=pl.CostEstimate(flops=0, bytes_accessed=6_000_000, transcendentals=0),
    )(*[stack for stack, _, _ in parts])


def near_offsets(first):
    return (0, first), (3 ^ first, 3)


def weight_parts(uses, lefts, rights, wide, cols):
    count = lax.axis_size("dp")
    direct = count == 16
    orders = []
    for first in (2, 1):
        order = FAR
        for bit in (3 ^ first, first):
            order = order + [offset ^ bit for offset in order]
        orders.append(order)
    if direct:
        outs = [array_of((8, wide, D // 16, cols))] * 4
    else:
        outs = [array_of((wide, D, cols))] * 2
    return run_kernel(
        functools.partial(weight_kernel, uses, len(lefts), orders if direct else None),
        outs,
        lax.axis_index("dp")[None],
        *lefts,
        *rights,
        scratch=[pltpu.VMEM((D, 384), jnp.float32), pltpu.VMEM((D, BLOCK), jnp.bfloat16)],
        moved=12 * len(uses) * D * cols,
    )


def send_first(parts):
    _, send_a, _, send_b = parts
    return swap(send_a, 2), swap(send_b, 1)


def send_second(highs):
    return swap(highs[0], 1), swap(highs[1], 2)


def fold_both(parts, cames):
    keep_a, _, keep_b, _ = parts
    (low_a, high_a), (low_b, high_b) = fold(keep_a, cames[0]), fold(keep_b, cames[1])
    return (low_a, low_b), (high_a, high_b)


def fold(keep, came):
    half = keep.shape[0] // 2
    high = keep[half:].astype(jnp.float32) + came[half:].astype(jnp.float32)
    return (
        keep[:half].astype(jnp.float32) + came[:half].astype(jnp.float32),
        high.astype(jnp.bfloat16),
    )


def far_ready(lows, cames):
    total = jnp.concatenate(
        [low.astype(jnp.float32) + came.astype(jnp.float32) for low, came in zip(lows, cames)],
        axis=1,
    )
    return [total[0]] + [total[at].astype(jnp.bfloat16) for at in range(1, 4)]


def far_total(own, *cames):
    for came in cames:
        own = own + came.astype(jnp.float32)
    return own


def adamw(weight, gradient, first_moment, second, factor, decays, step_rate):
    clipped = gradient * factor
    first_new = decays[0] * first_moment + (1.0 - decays[0]) * clipped
    second_new = decays[1] * second + (1.0 - decays[1]) * clipped * clipped
    first_hat = first_new / (1.0 - decays[0] ** STEP)
    second_hat = second_new / (1.0 - decays[1] ** STEP)
    weight_new = weight - step_rate * (first_hat / (jnp.sqrt(second_hat) + 1e-08) + 0.1 * weight)
    return (weight_new, first_new, second_new, weight_new.astype(jnp.bfloat16))


def local(
    tokens,
    enc_states,
    lengths,
    cotangent,
    attn_master,
    attn_first,
    attn_second,
    dense_master,
    dense_first,
    dense_second,
    vector_params,
    vector_first,
    vector_second,
    decays,
):
    core = lax.axis_index("mp")
    attn_low = attn_master.astype(jnp.bfloat16)
    dense_low = dense_master.astype(jnp.bfloat16)
    device = lax.axis_index("dp") * lax.axis_size("mp") + core
    own_cols = vector_params.shape[1]
    placed = lax.dynamic_update_slice_in_dim(
        jnp.zeros((vector_params.shape[0], D), jnp.float32), vector_params, device * own_cols, 1
    )
    fast = lax.axis_size("dp") == 16
    head_cols = attn_master.shape[3]
    hidden_cols = dense_master.shape[2]
    head_rows = 2 * (head_cols // 128)
    count = tokens.shape[0]
    keys_count = enc_states.shape[1]
    enc = enc_states[0]
    rows_d = array_of((count, D))
    rows_f = array_of((count, D), jnp.float32)
    rows_h = array_of((count, head_cols))
    turned_h = array_of((head_cols, count))
    lse_shape = array_of((head_rows, count), jnp.float32)
    keys_h = array_of((keys_count, head_cols))
    keys_t_h = array_of((head_cols, keys_count))
    scratch_h = pltpu.VMEM((count, head_cols), jnp.bfloat16)
    scratch_t = pltpu.VMEM((head_cols, count), jnp.bfloat16)
    scratch_s = pltpu.VMEM((count, count), jnp.float32)

    def local_slice(bias_row, span_size):
        return lax.dynamic_slice_in_dim(bias_row, core * span_size, span_size)[None]

    if fast:
        low_self, low_cross = attn_low[0][None], attn_low[1][None]
        low_w1, low_w2 = dense_low[:1][None], dense_low[1:][None]
        self_far, params, low_cross = together(
            far_stack(low_self), sum_near(sum_far(placed)), low_cross
        )
    else:
        params = sum_near(sum_far(placed))
        attn_all = lax.all_gather(attn_low, "dp", axis=2, tiled=True)
        dense_all = lax.all_gather(dense_low, "dp", axis=1, tiled=True)
        self_qk, self_vo, cross_qk, cross_vo = (
            attn_all[0, :2], attn_all[0, 2:], attn_all[1, :2], attn_all[1, 2:],
        )
        w1, w2 = dense_all[0], dense_all[1]
    bias_q_self = local_slice(params[6], head_cols)
    bias_v_self = local_slice(params[7], head_cols)
    bias_q_cross = local_slice(params[9], head_cols)
    bias_v_cross = local_slice(params[10], head_cols)
    bias_hidden = local_slice(params[13:].reshape(FF), hidden_cols)
    length_in = lengths

    if fast:
        self_near, cross_far, low_w1 = together(
            near_first(halves(self_far, False)), far_stack(low_cross), low_w1
        )
        self_last, cross_near, w1_far, low_w2, length_in = together(
            near_second(self_near),
            near_first(halves(cross_far, False)),
            far_stack(low_w1),
            low_w2,
            lengths,
        )
        self_qk, self_vo = assemble_pair(self_near, self_last)
    hidden1, self_q, self_k, self_v, self_mixed, self_mixed_t, self_lse, self_part = run_kernel(
        self_forward_kernel,
        [rows_d, rows_h, rows_h, rows_h, rows_h, turned_h, lse_shape, rows_d],
        length_in, tokens, params, bias_q_self, bias_v_self, self_qk, self_vo,
        scratch=[scratch_t, scratch_s],
        moved=30_000_000,
    )
    if fast:
        cross_last, w1_near, w2_far, self_part, bias_v_cross = together(
            near_second(cross_near),
            near_first(halves(w1_far, True)),
            far_stack(low_w2),
            self_part,
            bias_v_cross,
        )
        cross_qk, cross_vo = assemble_pair(cross_near, cross_last)
    cross_k, cross_v, cross_k_t, cross_v_t, enc_t = run_kernel(
        cross_keys_kernel,
        [keys_h, keys_h, keys_t_h, keys_t_h, array_of((D, keys_count))],
        enc, cross_qk, cross_vo, bias_v_cross,
        moved=25_000_000,
    )
    section1, hidden2, cross_q, cross_mixed, cross_mixed_t, cross_lse, cross_part = run_kernel(
        cross_forward_kernel,
        [rows_f, rows_d, rows_h, rows_h, turned_h, lse_shape, rows_d],
        tokens, self_part, swap_core(self_part), params, bias_q_cross, cross_qk, cross_vo,
        cross_k, cross_v_t,
        scratch=[
            pltpu.VMEM((keys_count, count), jnp.float32),
            pltpu.VMEM((keys_count, count), jnp.bfloat16),
        ],
        moved=70_000_000,
    )
    if fast:
        w1_last, w2_near, cross_part = together(
            near_second(w1_near), near_first(halves(w2_far, True)), cross_part
        )
        w1 = assemble_wide(w1_near, w1_last)
    hidden_rows = array_of((count, hidden_cols))
    section2, hidden3, act, slope, grad_low = run_kernel(
        dense_in_kernel,
        [rows_f, rows_d, hidden_rows, hidden_rows, rows_d],
        lengths, section1, cross_part, swap_core(cross_part), params, bias_hidden, w1, cotangent,
        moved=30_000_000,
    )
    half_cols = hidden_cols // 2
    dense_uses = ((0, 0, 0, 0, 0), (0, 0, half_cols, 1, 0))
    w2_parts = weight_parts(dense_uses, (grad_low,), (act,), 1, half_cols)
    if fast:
        w2_last, w2_parts, slope = together(near_second(w2_near), w2_parts, slope)
        w2 = assemble_wide(w2_near, w2_last)
    grad_pre, out_part, grad_h3, grad_b1 = run_kernel(
        dense_out_kernel,
        [hidden_rows, rows_d, rows_d, array_of((1, hidden_cols), jnp.float32)],
        act, slope, grad_low, w1, w2,
        moved=30_000_000,
    )
    w1_parts = weight_parts(dense_uses, (hidden3,), (grad_pre,), 1, half_cols)
    grad_h3_other, out_other = swap_core(grad_h3), swap_core(out_part)
    if fast:
        w2_came, w1_parts, grad_h3_other, out_other = together(
            send_first(w2_parts), w1_parts, grad_h3_other, out_other
        )
        w2_lows, w2_highs = fold_both(w2_parts, w2_came)
    (
        layer_out, grad_section2, grad_z2, cross_dq, cross_dk, cross_dv, grad_h2, vectors3, biases_cross,
    ) = run_kernel(
        cross_backward_kernel,
        [rows_d, rows_f, rows_d, rows_h, keys_h, keys_h, rows_d,
         array_of((4, D), jnp.float32), array_of((2, head_cols), jnp.float32)],
        section2, grad_h3, grad_h3_other, out_part, out_other, grad_low, params,
        cross_qk, cross_vo, cross_q, cross_k, cross_v, cross_k_t, cross_mixed_t, cross_lse,
        scratch=[scratch_h, scratch_t, scratch_t],
        moved=120_000_000,
    )
    if fast:
        w2_came, w1_came, cross_dq, cross_dk, grad_h2 = together(
            send_second(w2_highs), send_first(w1_parts), cross_dq, cross_dk, grad_h2
        )
        w2_own, *w2_out = far_ready(w2_lows, w2_came)
        w1_lows, w1_highs = fold_both(w1_parts, w1_came)
    cross_parts = weight_parts(
        ((0, 0, 0, 0, 0), (1, 1, 0, 0, 1), (1, 2, 0, 1, 0), (2, 3, 0, 1, 1)),
        (hidden2, enc_t, grad_z2),
        (cross_dq, cross_dk, cross_dv, cross_mixed),
        2,
        head_cols,
    )
    grad_h2_other = swap_core(grad_h2)
    length_back = lengths
    if fast:
        w1_came, w2_in1, w2_in2, cross_parts, grad_h2_other, length_back = together(
            send_second(w1_highs), swap(w2_out[0], 4), swap(w2_out[1], 8),
            cross_parts, grad_h2_other, lengths,
        )
        w1_own, *w1_out = far_ready(w1_lows, w1_came)
    (
        grad_section1, grad_z1, self_dq, self_dk, self_dv, grad_h1, vectors2, biases_self,
    ) = run_kernel(
        self_backward_kernel,
        [rows_f, rows_d, rows_h, rows_h, rows_h, rows_d,
         array_of((3, D), jnp.float32), array_of((2, head_cols), jnp.float32)],
        length_back, section1, grad_section2, grad_h2, grad_h2_other, params,
        self_qk, self_vo, self_q, self_k, self_v, self_mixed_t, self_lse,
        scratch=[scratch_h, scratch_t, scratch_t, scratch_t, scratch_s],
        moved=60_000_000,
    )
    if fast:
        cross_came, w2_in3, w1_in1, self_dq, grad_h1 = together(
            send_first(cross_parts), swap(w2_out[2], 12), swap(w1_out[0], 4), self_dq, grad_h1
        )
        cross_lows, cross_highs = fold_both(cross_parts, cross_came)
    self_parts = weight_parts(
        ((0, 0, 0, 0, 0), (0, 1, 0, 0, 1), (0, 2, 0, 1, 0), (1, 3, 0, 1, 1)),
        (hidden1, grad_z1),
        (self_dq, self_dk, self_dv, self_mixed),
        2,
        head_cols,
    )
    grad_h1_other = swap_core(grad_h1)
    core_in = core[None]
    if fast:
        cross_came, w1_in2, self_parts, grad_h1_other, core_in = together(
            send_second(cross_highs), swap(w1_out[1], 8), self_parts, grad_h1_other, core_in
        )
        cross_own, *cross_out = far_ready(cross_lows, cross_came)
    input_grad, vector_grad = run_kernel(
        last_kernel,
        [rows_f, array_of(params.shape, jnp.float32)],
        core_in, tokens, grad_section1, grad_h1, grad_h1_other, params,
        vectors2, vectors3, biases_self, biases_cross, grad_b1,
        moved=12_000_000,
    )
    enc_other = run_kernel(
        enc_kernel,
        array_of((keys_count, head_cols)),
        1 - core_in, cross_dk, cross_dv, cross_qk, cross_vo,
        moved=15_000_000,
    )
    if fast:
        self_came, w1_in3, cross_in1, vector_grad, enc_other = together(
            send_first(self_parts), swap(w1_out[2], 12), swap(cross_out[0], 4),
            vector_grad, enc_other,
        )
        self_lows, self_highs = fold_both(self_parts, self_came)
        self_came, cross_in2, cross_in3, vector_all, enc_came = together(
            send_second(self_highs), swap(cross_out[1], 8), swap(cross_out[2], 12),
            sum_near(sum_far(vector_grad)), swap_core(enc_other),
        )
        self_own, *self_out = far_ready(self_lows, self_came)
    else:
        vector_all = sum_near(sum_far(vector_grad))
        enc_came = swap_core(enc_other)
    enc_grad = run_kernel(
        enc_kernel,
        array_of((keys_count, 1, head_cols), jnp.float32),
        core_in, cross_dk, cross_dv, cross_qk, cross_vo, enc_came,
        moved=20_000_000,
    )
    if fast:
        dense_sums = [
            far_total(own, *cames).transpose(1, 0, 2).reshape(D // 16, hidden_cols)
            for own, cames in (
                (w1_own, (w1_in1, w1_in2, w1_in3)),
                (w2_own, (w2_in1, w2_in2, w2_in3)),
            )
        ]
        dense_sum = jnp.stack(dense_sums)
        cross_sum = far_total(cross_own, cross_in1, cross_in2, cross_in3)
        early_squares = jnp.sum(dense_sum * dense_sum) + jnp.sum(cross_sum * cross_sum)
        self_ins, enc_grad, early_squares = together(
            [swap(out, offset) for out, offset in zip(self_out, FAR[1:])], enc_grad, early_squares
        )
        self_sum = far_total(self_own, *self_ins)
    else:
        self_sum, cross_sum, dense1, dense2 = [
            jnp.concatenate(
                [
                    lax.psum_scatter(
                        part.astype(jnp.float32), "dp", scatter_dimension=1, tiled=True
                    )
                    for part in parts
                ],
                axis=axis,
            )
            for parts, axis in ((self_parts, 0), (cross_parts, 0), (w1_parts, 2), (w2_parts, 2))
        ]
        dense_sum = jnp.concatenate([dense1, dense2], axis=0)
        early_squares = jnp.sum(dense_sum * dense_sum) + jnp.sum(cross_sum * cross_sum)
    enc_grad = enc_grad.transpose(1, 0, 2)
    vector_sum = lax.dynamic_slice_in_dim(vector_all, device * own_cols, own_cols, 1)
    vector_squares = jnp.sum(vector_all * vector_all)
    attn_sum = jnp.stack([self_sum, cross_sum])
    local_squares = jnp.sum(self_sum * self_sum) + early_squares
    square_total = sum_near(sum_far(jnp.full((8, 128), local_squares)))[0, 0] + vector_squares
    clip_norm = jnp.sqrt(square_total)
    factor = jnp.minimum(1.0, 1.0 / (clip_norm + 1e-06))
    bias_gradient = vector_sum[12] * factor
    attn_new, attn_first_new, attn_second_new, attn_copy = adamw(
        attn_master, attn_sum, attn_first, attn_second, factor, decays, attn_rate
    )
    dense_new, dense_first_new, dense_second_new, dense_copy = adamw(
        dense_master, dense_sum, dense_first, dense_second, factor, decays, dense_rate
    )
    vector_new, vector_first_new, vector_second_new, vector_copy = adamw(
        vector_params, vector_sum, vector_first, vector_second, factor, decays, vector_rate
    )
    return (
        layer_out,
        input_grad,
        enc_grad,
        clip_norm,
        attn_new,
        attn_first_new,
        attn_second_new,
        attn_copy,
        dense_new,
        dense_first_new,
        dense_second_new,
        dense_copy,
        vector_new,
        vector_first_new,
        vector_second_new,
        vector_copy,
        bias_gradient,
    )


def solution(mesh):
    return jax.shard_map(
        local,
        mesh=mesh,
        in_specs=(
            P("dp", None),
            P("dp", None, None),
            P("dp"),
            P("dp", None),
            P(None, None, "dp", "mp"),
            P(None, None, "dp", "mp"),
            P(None, None, "dp", "mp"),
            P(None, "dp", "mp"),
            P(None, "dp", "mp"),
            P(None, "dp", "mp"),
            P(None, ("dp", "mp")),
            P(None, ("dp", "mp")),
            P(None, ("dp", "mp")),
            P(),
        ),
        out_specs=(
            P("dp", None),
            P("dp", None),
            P("dp", None, "mp"),
            P(),
            P(None, None, "dp", "mp"),
            P(None, None, "dp", "mp"),
            P(None, None, "dp", "mp"),
            P(None, None, "dp", "mp"),
            P(None, "dp", "mp"),
            P(None, "dp", "mp"),
            P(None, "dp", "mp"),
            P(None, "dp", "mp"),
            P(None, ("dp", "mp")),
            P(None, ("dp", "mp")),
            P(None, ("dp", "mp")),
            P(None, ("dp", "mp")),
            P(("dp", "mp")),
        ),
        check_vma=False,
    )
```

```python
import functools

import jax
import jax.numpy as jnp
from jax import lax
from jax.experimental import pallas as pl
from jax.experimental.pallas import tpu as pltpu
from jax.sharding import PartitionSpec as P

D = 768
HEAD_DIM = 64
FF = 3072
BLOCK = 448
STEP = 3


attn_rate = 0.08
dense_rate = 0.03
vector_rate = 0.3
LOG2E = 1.4426950408889634


def dot(left_side, right_side):
    return jnp.dot(left_side, right_side, preferred_element_type=jnp.float32)


def dot_nt(left_side, right_side):
    return lax.dot_general(
        left_side, right_side, (((1,), (1,)), ((), ())), preferred_element_type=jnp.float32
    )


def spans(total, step):
    return [(at, min(step, total - at)) for at in range(0, total, step)]


def unit_norm(values):
    centred = values - jnp.mean(values, axis=-1, keepdims=True)
    inverse = lax.rsqrt(jnp.mean(centred * centred, axis=-1, keepdims=True) + 1e-05)
    return centred * inverse, inverse


def norm_rows(values, gain, shift):
    unit, _ = unit_norm(values)
    return (unit * gain + shift).astype(jnp.bfloat16)


def norm_pull(values, grad, gain):
    unit, inverse = unit_norm(values)
    scaled = grad * gain
    pulled = inverse * (
        scaled
        - jnp.mean(scaled, axis=-1, keepdims=True)
        - unit * jnp.mean(scaled * unit, axis=-1, keepdims=True)
    )
    return (
        pulled,
        jnp.sum(grad * unit, axis=0, keepdims=True),
        jnp.sum(grad, axis=0, keepdims=True),
    )


def head_masks():
    lane = lax.broadcasted_iota(jnp.int32, (1, 2 * HEAD_DIM), 1)
    return [(lane < HEAD_DIM).astype(jnp.bfloat16), (lane >= HEAD_DIM).astype(jnp.bfloat16)]


def row_sum(values):
    return jnp.sum(values.astype(jnp.float32), axis=0, keepdims=True)


def run_kernel(kernel, out_shapes, *operands, scratch=(), flops=0, moved=0):
    spaces = [
        pl.BlockSpec(
            memory_space=pltpu.SMEM if operand.dtype == jnp.int32 else pltpu.VMEM
        )
        for operand in operands
    ]
    return pl.pallas_call(
        kernel,
        out_shape=out_shapes,
        in_specs=spaces,
        out_specs=jax.tree.map(lambda _: pl.BlockSpec(memory_space=pltpu.VMEM), out_shapes),
        scratch_shapes=list(scratch),
        compiler_params=pltpu.CompilerParams(vmem_limit_bytes=56 * 2**20),
        cost_estimate=pl.CostEstimate(flops=flops, bytes_accessed=moved, transcendentals=0),
    )(*operands)


def array_of(shape, dtype=jnp.bfloat16):
    return jax.ShapeDtypeStruct(shape, dtype)


def cross_keys_kernel(enc, wqk, wvo, bias_v, keys, values, keys_t, values_t, enc_t):
    for at, size in spans(enc.shape[0], 256):
        rows = pl.ds(at, size)
        block = enc[rows, :]
        enc_t[:, rows] = block.T
        key_block = dot(block, wqk[1]).astype(jnp.bfloat16)
        value_block = (dot(block, wvo[0]) + bias_v[...]).astype(jnp.bfloat16)
        keys[rows, :] = key_block
        values[rows, :] = value_block
        keys_t[:, rows] = key_block.T
        values_t[:, rows] = value_block.T


def self_forward_kernel(
    length, tokens, params, bias_q, bias_v, wqk, wvo,
    hidden, q, k, v, mixed, mixed_t, lse, part,
    values_t, allowed,
):
    count = tokens.shape[0]
    for at, size in spans(count, 64):
        rows = pl.ds(at, size)
        hidden[rows, :] = norm_rows(
            tokens[rows, :].astype(jnp.float32), params[0:1, :], params[1:2, :]
        )
    q[...] = (dot(hidden[...], wqk[0]) + bias_q[...]).astype(jnp.bfloat16)
    k[...] = dot(hidden[...], wqk[1]).astype(jnp.bfloat16)
    v[...] = (dot(hidden[...], wvo[0]) + bias_v[...]).astype(jnp.bfloat16)
    values_t[...] = v[...].T
    key_ids = lax.broadcasted_iota(jnp.int32, (count, count), 0)
    query_ids = lax.broadcasted_iota(jnp.int32, (count, count), 1)
    allowed[...] = ((key_ids <= query_ids) & (key_ids < length[0])).astype(jnp.float32)
    masks = head_masks()

    def pair_step(pair, carry):
        cols = pl.ds(pl.multiple_of(pair * 128, 128), 128)
        for parity in range(2):
            head = pair * 2 + parity
            scores = dot_nt(k[:, cols], q[:, cols] * masks[parity]) * (0.125 * LOG2E)
            scores = jnp.where(allowed[...] > 0.5, scores, -1e30)
            top = jnp.max(scores, axis=0, keepdims=True)
            weights = jnp.exp2(scores - top)
            total = jnp.sum(weights, axis=0, keepdims=True)
            lse[pl.ds(head, 1), :] = top + jnp.log2(total)
            own = pl.ds(pl.multiple_of(head * HEAD_DIM, HEAD_DIM), HEAD_DIM)
            mixed_t[own, :] = (
                dot(values_t[own, :], weights.astype(jnp.bfloat16)) * (1.0 / total)
            ).astype(jnp.bfloat16)
        return carry

    lax.fori_loop(0, q.shape[1] // 128, pair_step, 0)
    mixed[...] = mixed_t[...].T
    part[...] = dot_nt(mixed[...], wvo[1]).astype(jnp.bfloat16)


def cross_forward_kernel(
    tokens, own_part, other_part, params, bias_q, wqk, wvo, keys, values_t,
    section, hidden, q, mixed, mixed_t, lse, part,
    scores, weights,
):
    count = tokens.shape[0]
    for at, size in spans(count, 64):
        rows = pl.ds(at, size)
        branch = own_part[rows, :].astype(jnp.float32) + other_part[rows, :].astype(jnp.float32)
        block = tokens[rows, :].astype(jnp.float32) + (branch + params[8:9, :])
        section[rows, :] = block
        hidden[rows, :] = norm_rows(block, params[2:3, :], params[3:4, :])
    q[...] = (dot(hidden[...], wqk[0]) + bias_q[...]).astype(jnp.bfloat16)
    masks = head_masks()
    key_spans = spans(keys.shape[0], 256)

    def pair_step(pair, carry):
        cols = pl.ds(pl.multiple_of(pair * 128, 128), 128)
        for parity in range(2):
            head = pair * 2 + parity
            queries = q[:, cols] * masks[parity]
            top = None
            for at, size in key_spans:
                block = dot_nt(keys[pl.ds(at, size), cols], queries) * (0.125 * LOG2E)
                scores[pl.ds(at, size), :] = block
                block_top = jnp.max(block, axis=0, keepdims=True)
                top = block_top if top is None else jnp.maximum(top, block_top)
            total = jnp.zeros_like(top)
            for at, size in key_spans:
                block = jnp.exp2(scores[pl.ds(at, size), :] - top)
                total = total + jnp.sum(block, axis=0, keepdims=True)
                weights[pl.ds(at, size), :] = block.astype(jnp.bfloat16)
            lse[pl.ds(head, 1), :] = top + jnp.log2(total)
            own = pl.ds(pl.multiple_of(head * HEAD_DIM, HEAD_DIM), HEAD_DIM)
            mixed_t[own, :] = (dot(values_t[own, :], weights[...]) * (1.0 / total)).astype(
                jnp.bfloat16
            )
        return carry

    lax.fori_loop(0, q.shape[1] // 128, pair_step, 0)
    mixed[...] = mixed_t[...].T
    part[...] = dot_nt(mixed[...], wvo[1]).astype(jnp.bfloat16)


def dense_in_kernel(
    length, section, own_part, other_part, params, bias_hidden, w1_low, w1_high, cotangent,
    section_new, hidden, act, slope, grad_low,
):
    count = section.shape[0]
    for at, size in spans(count, 64):
        rows = pl.ds(at, size)
        branch = own_part[rows, :].astype(jnp.float32) + other_part[rows, :].astype(jnp.float32)
        block = section[rows, :] + (branch + params[11:12, :])
        section_new[rows, :] = block
        hidden[rows, :] = norm_rows(block, params[4:5, :], params[5:6, :])
        row_ids = lax.broadcasted_iota(jnp.int32, (size, 1), 0) + at
        valid = (row_ids < length[0]).astype(jnp.float32)
        grad_low[rows, :] = (cotangent[rows, :].astype(jnp.float32) * valid).astype(jnp.bfloat16)

    width = w1_low.shape[2]
    for half, blocks in enumerate((w1_low, w1_high)):

        def step(at, carry, half=half, blocks=blocks):
            cols = pl.ds(pl.multiple_of((2 * half + at) * width, 128), width)
            pre_act = dot(hidden[...], blocks[at]) + bias_hidden[:, cols]
            spread = 0.5 + 0.5 * lax.erf(pre_act * (2.0**-0.5))
            act[:, cols] = (pre_act * spread).astype(jnp.bfloat16)
            density = jnp.exp2(pre_act * pre_act * (-0.5 * LOG2E)) * 0.3989422804014327
            slope[:, cols] = (spread + pre_act * density).astype(jnp.bfloat16)
            return carry

        lax.fori_loop(0, 2, step, 0)


def dense_out_kernel(
    act, slope, grad_low, w1_low, w1_high, w2_low, w2_high,
    grad_pre, part, grad_hidden, grad_bias,
):
    width = w1_low.shape[2]
    for half, blocks in enumerate((w2_low, w2_high)):

        def step(at, carry, half=half, blocks=blocks):
            cols = pl.ds(pl.multiple_of((2 * half + at) * width, 128), width)
            grad_act = dot(grad_low[...], blocks[at]).astype(jnp.bfloat16).astype(jnp.float32)
            grad_block = (grad_act * slope[:, cols].astype(jnp.float32)).astype(jnp.bfloat16)
            grad_pre[:, cols] = grad_block
            grad_bias[:, cols] = row_sum(grad_block)
            return carry

        lax.fori_loop(0, 2, step, 0)
    for left, low, high, out in (
        (act, w2_low, w2_high, part),
        (grad_pre, w1_low, w1_high, grad_hidden),
    ):
        total = None
        for at in range(4):
            product = dot_nt(left[:, at * width : at * width + width], (low, high)[at // 2][at % 2])
            total = product if total is None else total + product
        out[...] = total.astype(jnp.bfloat16)


def put_relative(product, here, order, keep, send, which, cols):
    half = keep.shape[0]
    rows = keep.shape[2]
    for at, offset in enumerate(order):
        block = product[pl.ds(pl.multiple_of((here ^ offset) * rows, 16), rows), :]
        target = keep if at < half else send
        target[at % half, which, :, cols] = block.astype(jnp.bfloat16)


def weight_kernel(uses, lefts_count, orders, *refs):
    rights_count = 1 + max(right for _, right, _, _, _ in uses)
    lefts, rights = refs[1 : 1 + lefts_count], refs[1 + lefts_count : 1 + lefts_count + rights_count]
    outs = refs[1 + lefts_count + rights_count : -2]
    product, turned = refs[-2:]
    width = product.shape[1]
    me = refs[0][0]
    in_turned = None
    for left, right, first, group, which in uses:
        left_t, right = lefts[left], rights[right]
        if left_t.shape[0] != D:
            if in_turned != left:
                turned[...] = left_t[...].T
                in_turned = left
            left_t = turned

        def step(at, carry, left_t=left_t, right=right, first=first, group=group, which=which):
            cols = pl.ds(pl.multiple_of(at * width, width), width)
            taken = pl.ds(pl.multiple_of(first + at * width, width), width)
            product[...] = dot(left_t[...], right[:, taken])
            if orders is None:
                outs[group][which, :, cols] = product[...].astype(jnp.bfloat16)
            else:
                put_relative(
                    product, me, orders[group], outs[2 * group], outs[2 * group + 1], which, cols
                )
            return carry

        lax.fori_loop(0, outs[0].shape[-1] // width, step, 0)


def attention_pull(
    keys, values, keys_t, q, grad_mixed, grad_mixed_t, mixed_t, lse, allowed, step,
    grad_keys, grad_values, grad_q_t,
):
    masks = head_masks()
    key_spans = spans(keys.shape[0], step)

    def pair_step(pair, carry):
        cols = pl.ds(pl.multiple_of(pair * 128, 128), 128)
        queries = [q[:, cols] * mask for mask in masks]
        grads = [(grad_mixed[:, cols] * 0.125) * mask for mask in masks]
        heads = [pl.ds(pl.multiple_of(pair * 128 + p * 64, 64), 64) for p in range(2)]
        levels, deltas = [], []
        for parity in range(2):
            levels.append(lse[pl.ds(pair * 2 + parity, 1), :])
            product = grad_mixed_t[heads[parity], :].astype(jnp.float32) * mixed_t[
                heads[parity], :
            ].astype(jnp.float32)
            deltas.append(jnp.sum(product, axis=0, keepdims=True) * 0.125)
        sums = [None, None]
        for at, size in key_spans:
            rows = pl.ds(at, size)
            key_sum = value_sum = None
            for parity in range(2):
                scores = dot_nt(keys[rows, cols], queries[parity]) * (0.125 * LOG2E)
                weights = jnp.exp2(scores - levels[parity])
                if allowed is not None:
                    weights = jnp.where(allowed[rows, :] > 0.5, weights, 0.0)
                grad_soft = dot_nt(values[rows, cols], grads[parity])
                grad_raw = (weights * (grad_soft - deltas[parity])).astype(jnp.bfloat16)
                value_part = dot(weights.astype(jnp.bfloat16), grads[parity])
                key_part = dot(grad_raw, queries[parity])
                query_part = dot(keys_t[heads[parity], rows], grad_raw)
                value_sum = value_part if value_sum is None else value_sum + value_part
                key_sum = key_part if key_sum is None else key_sum + key_part
                sums[parity] = query_part if sums[parity] is None else sums[parity] + query_part
            grad_values[rows, cols] = (value_sum * 8.0).astype(jnp.bfloat16)
            grad_keys[rows, cols] = key_sum.astype(jnp.bfloat16)
        for parity in range(2):
            grad_q_t[heads[parity], :] = sums[parity].astype(jnp.bfloat16)
        return carry

    lax.fori_loop(0, q.shape[1] // 128, pair_step, 0)


def cross_backward_kernel(
    section, grad_part, grad_other, out_part, out_other, grad_top, params,
    wqk, wvo, q, keys, values, keys_t, mixed_t, lse,
    layer_out, grad_section, grad_z, grad_q, grad_keys, grad_values, grad_hidden, vectors, biases,
    grad_mixed, grad_mixed_t, grad_q_t,
):
    count = section.shape[0]
    sums = None
    for at, size in spans(count, 64):
        rows = pl.ds(at, size)
        block = section[rows, :]
        branch = out_part[rows, :].astype(jnp.float32) + out_other[rows, :].astype(jnp.float32)
        layer_out[rows, :] = (block + (branch + params[12:13, :])).astype(jnp.bfloat16)
        grad = grad_part[rows, :].astype(jnp.float32) + grad_other[rows, :].astype(jnp.float32)
        pulled, gain_sum, shift_sum = norm_pull(block, grad, params[4:5, :])
        top = grad_top[rows, :].astype(jnp.float32)
        total = top + pulled
        low = total.astype(jnp.bfloat16)
        grad_section[rows, :] = total
        grad_z[rows, :] = low
        parts = [gain_sum, shift_sum, row_sum(low), jnp.sum(top, axis=0, keepdims=True)]
        sums = parts if sums is None else [old + new for old, new in zip(sums, parts)]
    for at, value in enumerate(sums):
        vectors[at : at + 1, :] = value
    grad_mixed[...] = dot(grad_z[...], wvo[1]).astype(jnp.bfloat16)
    grad_mixed_t[...] = grad_mixed[...].T
    attention_pull(
        keys, values, keys_t, q, grad_mixed, grad_mixed_t, mixed_t, lse, None, 256,
        grad_keys, grad_values, grad_q_t,
    )
    grad_q[...] = grad_q_t[...].T
    grad_hidden[...] = dot_nt(grad_q[...], wqk[0]).astype(jnp.bfloat16)
    biases[0:1, :] = row_sum(grad_q[...])
    biases[1:2, :] = row_sum(grad_values[...])


def self_backward_kernel(
    length, section, grad_section, grad_part, grad_other, params,
    wqk, wvo, q, k, v, mixed_t, lse,
    grad_new, grad_z, grad_q, grad_keys, grad_values, grad_hidden, vectors, biases,
    grad_mixed, grad_mixed_t, grad_q_t, keys_t, allowed,
):
    count = section.shape[0]
    sums = None
    for at, size in spans(count, 64):
        rows = pl.ds(at, size)
        grad = grad_part[rows, :].astype(jnp.float32) + grad_other[rows, :].astype(jnp.float32)
        pulled, gain_sum, shift_sum = norm_pull(section[rows, :], grad, params[2:3, :])
        total = grad_section[rows, :] + pulled
        low = total.astype(jnp.bfloat16)
        grad_new[rows, :] = total
        grad_z[rows, :] = low
        parts = [gain_sum, shift_sum, row_sum(low)]
        sums = parts if sums is None else [old + new for old, new in zip(sums, parts)]
    for at, value in enumerate(sums):
        vectors[at : at + 1, :] = value
    grad_mixed[...] = dot(grad_z[...], wvo[1]).astype(jnp.bfloat16)
    grad_mixed_t[...] = grad_mixed[...].T
    keys_t[...] = k[...].T
    key_ids = lax.broadcasted_iota(jnp.int32, (count, count), 0)
    query_ids = lax.broadcasted_iota(jnp.int32, (count, count), 1)
    allowed[...] = ((key_ids <= query_ids) & (key_ids < length[0])).astype(jnp.float32)
    attention_pull(
        k, v, keys_t, q, grad_mixed, grad_mixed_t, mixed_t, lse, allowed, 256,
        grad_keys, grad_values, grad_q_t,
    )
    grad_q[...] = grad_q_t[...].T
    grad_hidden[...] = (
        dot_nt(grad_q[...], wqk[0])
        + dot_nt(grad_keys[...], wqk[1])
        + dot_nt(grad_values[...], wvo[0])
    ).astype(jnp.bfloat16)
    biases[0:1, :] = row_sum(grad_q[...])
    biases[1:2, :] = row_sum(grad_values[...])


def last_kernel(
    core, tokens, grad_section, grad_part, grad_other, params,
    vectors2, vectors3, biases_self, biases_cross, grad_b1,
    input_grad, vectors,
):
    sums = None
    for at, size in spans(tokens.shape[0], 64):
        rows = pl.ds(at, size)
        grad = grad_part[rows, :].astype(jnp.float32) + grad_other[rows, :].astype(jnp.float32)
        pulled, gain_sum, shift_sum = norm_pull(
            tokens[rows, :].astype(jnp.float32), grad, params[0:1, :]
        )
        input_grad[rows, :] = grad_section[rows, :] + pulled
        parts = [gain_sum, shift_sum]
        sums = parts if sums is None else [old + new for old, new in zip(sums, parts)]
    leader = (core[0] == 0).astype(jnp.float32)
    vectors[...] = jnp.zeros_like(vectors)
    shared = sums + [vectors2[0:1, :], vectors2[1:2, :], vectors3[0:1, :], vectors3[1:2, :]]
    shared = list(enumerate(shared)) + [(8, vectors2[2:3, :]), (11, vectors3[2:3, :]), (12, vectors3[3:4, :])]
    for at, value in shared:
        vectors[at : at + 1, :] = value * leader
    width = biases_self.shape[1]
    cols = pl.ds(pl.multiple_of(core[0] * width, 128), width)
    for at, ref in ((6, biases_self), (9, biases_cross)):
        vectors[at : at + 1, cols] = ref[0:1, :]
        vectors[at + 1 : at + 2, cols] = ref[1:2, :]
    held = grad_b1.shape[1] // D
    for at in range(held):
        vectors[pl.ds(13 + core[0] * held + at, 1), :] = grad_b1[:, at * D : at * D + D]


def enc_kernel(place, grad_keys, grad_values, wqk, wvo, *refs):
    own, out = refs[:-1], refs[-1]
    cols = pl.ds(pl.multiple_of(place[0] * wqk.shape[2], 128), wqk.shape[2])
    for at, size in spans(grad_keys.shape[0], 256):
        rows = pl.ds(at, size)
        total = dot_nt(grad_keys[rows, :], wqk[1, cols, :]) + dot_nt(
            grad_values[rows, :], wvo[0, cols, :]
        )
        if own:
            total = total + own[0][rows, :].astype(jnp.float32)
        if own:
            out[rows, 0, :] = total
        else:
            out[rows, :] = total.astype(out.dtype)


def swap(array, bit):
    count = lax.axis_size("dp")
    return lax.ppermute(array, "dp", [(i, i ^ bit) for i in range(count)])


def swap_core(array):
    return lax.ppermute(array, "mp", [(0, 1), (1, 0)])


def together(*values):
    return lax.optimization_barrier(values)


def sum_round(value, bits):
    me = lax.axis_index("dp")
    offsets = [0]
    for bit in bits:
        offsets = offsets + [offset ^ bit for offset in offsets]
    stack = [value] + [swap(value, offset) for offset in offsets[1:]]
    for bit in bits:
        flip = (me & bit) != 0
        pairs = [(stack[at], stack[at + 1]) for at in range(0, len(stack), 2)]
        stack = [jnp.where(flip, b, a) + jnp.where(flip, a, b) for a, b in pairs]
    return stack[0]


def sum_far(value):
    for bits in [(4, 8)] if lax.axis_size("dp") == 16 else high_bits():
        value = sum_round(value, bits)
    return value


def high_bits():
    return [(1 << k,) for k in range(2, lax.axis_size("dp").bit_length() - 1)]


def sum_near(value):
    value = sum_round(value, (1, 2))
    return value + swap_core(value)


FAR = [0, 4, 8, 12]


def join(stack, came):
    return jnp.concatenate([stack, came], axis=0)


def far_stack(piece):
    return jnp.concatenate([piece] + [swap(piece, offset) for offset in FAR[1:]], axis=0)


def near_steps(first, second):
    parts = None if first is None else halves(first)
    onward = []
    for place, bit in enumerate((1, 2)):
        pieces = []
        if second is not None:
            pieces.append(second[1 - place])
        if first is not None:
            pieces.append(parts[place])
        onward.append(swap(jnp.concatenate(pieces, axis=0), bit))
    cut = 0 if second is None else 8
    nears = None if first is None else [join(part, came[cut:]) for part, came in zip(parts, onward)]
    lasts = None if second is None else onward[::-1]
    return nears, lasts


def assemble_pair(nears, lasts):
    return [
        assemble([(near, first), (last, second)])
        for near, last, (first, second) in zip(nears, lasts, map(near_offsets, (1, 2)))
    ]


def halves(stack):
    return jnp.split(stack, 2, axis=1)


def assemble(parts):
    wide, rows, cols = parts[0][0].shape[1:]

    def kernel(*refs):
        stacks, out, sems = refs[: len(parts)], refs[len(parts)], refs[-1]
        here = lax.axis_index("dp")
        copies = []
        for stack, (_, firsts) in zip(stacks, parts):
            for at in range(8):
                offset = firsts[at // 4] ^ FAR[at % 4]
                place = pl.multiple_of((here ^ offset) * rows, 16)
                target = out.at[:, pl.ds(place, rows), :]
                copies.append(pltpu.make_async_copy(stack.at[at], target, sems.at[len(copies)]))
        for copy in copies:
            copy.start()
        for copy in copies:
            copy.wait()

    return pl.pallas_call(
        kernel,
        out_shape=array_of((wide, 16 * rows, cols)),
        in_specs=[pl.BlockSpec(memory_space=pl.ANY)] * len(parts),
        out_specs=pl.BlockSpec(memory_space=pltpu.VMEM),
        scratch_shapes=[pltpu.SemaphoreType.DMA((16,))],
        compiler_params=pltpu.CompilerParams(vmem_limit_bytes=16 * 2**20),
    )(*[stack for stack, _ in parts])


def near_offsets(first):
    return (0, first), (3 ^ first, 3)


def weight_parts(uses, lefts, rights, wide, cols):
    count = lax.axis_size("dp")
    direct = count == 16
    orders = []
    for first in (2, 1):
        order = FAR
        for bit in (3 ^ first, first):
            order = order + [offset ^ bit for offset in order]
        orders.append(order)
    if direct:
        outs = [array_of((8, wide, D // 16, cols))] * 4
    else:
        outs = [array_of((wide, D, cols))] * 2
    return run_kernel(
        functools.partial(weight_kernel, uses, len(lefts), orders if direct else None),
        outs,
        lax.axis_index("dp")[None],
        *lefts,
        *rights,
        scratch=[pltpu.VMEM((D, 384), jnp.float32), pltpu.VMEM((D, BLOCK), jnp.bfloat16)],
        moved=12 * len(uses) * D * cols,
    )


def send_near(first, second):
    cames = []
    for place, bit in enumerate((1, 2)):
        pieces = []
        if second is not None:
            pieces.append(second[place])
        if first is not None:
            pieces.append(first[3 - 2 * place])
        cames.append(swap(pieces[0] if len(pieces) == 1 else jnp.concatenate(pieces), bit))
    cut = 0 if second is None else 4
    return [came[cut:] for came in cames[::-1]], [came[:cut] for came in cames]


def fold_both(parts, cames):
    keep_a, _, keep_b, _ = parts
    (low_a, high_a), (low_b, high_b) = fold(keep_a, cames[0]), fold(keep_b, cames[1])
    return (low_a, low_b), (high_a, high_b)


def fold(keep, came):
    half = keep.shape[0] // 2
    high = keep[half:].astype(jnp.float32) + came[half:].astype(jnp.float32)
    return (
        keep[:half].astype(jnp.float32) + came[:half].astype(jnp.float32),
        high.astype(jnp.bfloat16),
    )


def far_ready(lows, cames):
    total = jnp.concatenate(
        [low.astype(jnp.float32) + came.astype(jnp.float32) for low, came in zip(lows, cames)],
        axis=1,
    )
    return [total[0]] + [total[at].astype(jnp.bfloat16) for at in range(1, 4)]


def totals_kernel(groups, *refs):
    squares = None
    for at in range(groups):
        own, *cames = refs[4 * at : 4 * at + 4]
        total = own[...]
        for came in cames:
            total = total + came[...].astype(jnp.float32)
        refs[4 * groups + at][...] = total
        square = jnp.sum(total * total, axis=(0, 1), keepdims=True)[0]
        squares = square if squares is None else squares + square
    refs[5 * groups][...] = squares


def finish_kernel(
    decays, sums, vector_sum, self_sum, cross_sum, w1_sum, w2_sum,
    attn, attn_first, attn_second, dense, dense_first, dense_second,
    vector, vector_first, vector_second,
    norm, attn_new, attn_first_new, attn_second_new, attn_copy,
    dense_new, dense_first_new, dense_second_new, dense_copy,
    vector_new, vector_first_new, vector_second_new, vector_copy, bias_gradient,
):
    vectors = sums[0 : sums.shape[0] - 1, :]
    squares = jnp.sum(jnp.sum(vectors * vectors, axis=0, keepdims=True), axis=1, keepdims=True)
    clip_norm = jnp.sqrt(squares + sums[sums.shape[0] - 1 : sums.shape[0], 0:1])
    norm[...] = jnp.broadcast_to(clip_norm, norm.shape)
    factor = jnp.minimum(1.0, 1.0 / (clip_norm + 1e-06))
    first_rate, second_rate = decays[0:1, 0:1], decays[0:1, 1:2]
    first_scale = 1.0 / (1.0 - first_rate * first_rate * first_rate)
    second_scale = 1.0 / (1.0 - second_rate * second_rate * second_rate)

    def update(gradient, weight, first, second, step_rate):
        clipped = gradient * factor
        first_new = first_rate * first + (1.0 - first_rate) * clipped
        second_new = second_rate * second + (1.0 - second_rate) * clipped * clipped
        change = (first_new * first_scale) / (jnp.sqrt(second_new * second_scale) + 1e-08)
        return weight - step_rate * (change + 0.1 * weight), first_new, second_new

    for at, gradient in enumerate((self_sum, cross_sum)):
        for which in range(4):
            new, first, second = update(
                gradient[which],
                attn[at, which],
                attn_first[at, which],
                attn_second[at, which],
                attn_rate,
            )
            attn_new[at, which] = new
            attn_first_new[at, which] = first
            attn_second_new[at, which] = second
            attn_copy[at, which] = new.astype(jnp.bfloat16)
    width = w1_sum.shape[2]
    for at, gradient in enumerate((w1_sum, w2_sum)):
        for which in range(4):
            cols = slice(which * width, which * width + width)
            new, first, second = update(
                gradient[which],
                dense[at, :, cols],
                dense_first[at, :, cols],
                dense_second[at, :, cols],
                dense_rate,
            )
            dense_new[at, :, cols] = new
            dense_first_new[at, :, cols] = first
            dense_second_new[at, :, cols] = second
            dense_copy[at, :, cols] = new.astype(jnp.bfloat16)
    new, first, second = update(
        vector_sum[...], vector[...], vector_first[...], vector_second[...], vector_rate
    )
    vector_new[...] = new
    vector_first_new[...] = first
    vector_second_new[...] = second
    vector_copy[...] = new.astype(jnp.bfloat16)
    bias_gradient[...] = vector_sum[12:13, :] * factor


def local(
    tokens,
    enc_states,
    lengths,
    cotangent,
    attn_master,
    attn_first,
    attn_second,
    dense_master,
    dense_first,
    dense_second,
    vector_params,
    vector_first,
    vector_second,
    decays,
):
    core = lax.axis_index("mp")
    attn_low = attn_master.astype(jnp.bfloat16)
    dense_low = dense_master.astype(jnp.bfloat16)
    blocks = dense_master.shape[2] // attn_master.shape[3]
    dense_low = jnp.stack(jnp.split(dense_low, blocks, axis=2), axis=1)
    device = lax.axis_index("dp") * lax.axis_size("mp") + core
    own_cols = vector_params.shape[1]
    placed = lax.dynamic_update_slice_in_dim(
        jnp.zeros((vector_params.shape[0], D), jnp.float32), vector_params, device * own_cols, 1
    )
    fast = lax.axis_size("dp") == 16
    head_cols = attn_master.shape[3]
    hidden_cols = dense_master.shape[2]
    head_rows = 2 * (head_cols // 128)
    count = tokens.shape[0]
    keys_count = enc_states.shape[1]
    enc = enc_states[0]
    rows_d = array_of((count, D))
    rows_f = array_of((count, D), jnp.float32)
    rows_h = array_of((count, head_cols))
    turned_h = array_of((head_cols, count))
    lse_shape = array_of((head_rows, count), jnp.float32)
    keys_h = array_of((keys_count, head_cols))
    keys_t_h = array_of((head_cols, keys_count))
    scratch_h = pltpu.VMEM((count, head_cols), jnp.bfloat16)
    scratch_t = pltpu.VMEM((head_cols, count), jnp.bfloat16)
    scratch_s = pltpu.VMEM((count, count), jnp.float32)

    def local_slice(bias_row, span_size):
        return lax.dynamic_slice_in_dim(bias_row, core * span_size, span_size)[None]

    if fast:
        vector_low, low_self = together(sum_far(placed), attn_low[0][None])
        vector_low = vector_low + swap(vector_low, 1)
        vector_low = vector_low + swap(vector_low, 2)
        low_cross, low_w1, low_w2 = attn_low[1][None], dense_low[0][None], dense_low[1][None]
        self_far, params, low_cross = together(
            far_stack(low_self), vector_low + swap_core(vector_low), low_cross
        )
    else:
        params = sum_near(sum_far(placed))
        attn_all = lax.all_gather(attn_low, "dp", axis=2, tiled=True)
        dense_all = lax.all_gather(dense_low, "dp", axis=2, tiled=True)
        self_qk, self_vo, cross_qk, cross_vo = (
            attn_all[0, :2], attn_all[0, 2:], attn_all[1, :2], attn_all[1, 2:],
        )
        w1, w2 = [(whole[:2], whole[2:]) for whole in dense_all]
    bias_q_self = local_slice(params[6], head_cols)
    bias_v_self = local_slice(params[7], head_cols)
    bias_q_cross = local_slice(params[9], head_cols)
    bias_v_cross = local_slice(params[10], head_cols)
    bias_hidden = local_slice(params[13:].reshape(FF), hidden_cols)
    length_in = lengths

    if fast:
        (self_near, _), cross_far, low_w1 = together(
            near_steps(self_far, None), far_stack(low_cross), low_w1
        )
        (cross_near, self_last), w1_far, low_w2, length_in = together(
            near_steps(cross_far, self_near), far_stack(low_w1), low_w2, lengths
        )
        self_qk, self_vo = assemble_pair(self_near, self_last)
    hidden1, self_q, self_k, self_v, self_mixed, self_mixed_t, self_lse, self_part = run_kernel(
        self_forward_kernel,
        [rows_d, rows_h, rows_h, rows_h, rows_h, turned_h, lse_shape, rows_d],
        length_in, tokens, params, bias_q_self, bias_v_self, self_qk, self_vo,
        scratch=[scratch_t, scratch_s],
        moved=30_000_000,
    )
    if fast:
        (w1_near, cross_last), w2_far, self_part, bias_v_cross = together(
            near_steps(w1_far, cross_near), far_stack(low_w2), self_part, bias_v_cross
        )
        cross_qk, cross_vo = assemble_pair(cross_near, cross_last)
    cross_k, cross_v, cross_k_t, cross_v_t, enc_t = run_kernel(
        cross_keys_kernel,
        [keys_h, keys_h, keys_t_h, keys_t_h, array_of((D, keys_count))],
        enc, cross_qk, cross_vo, bias_v_cross,
        moved=25_000_000,
    )
    section1, hidden2, cross_q, cross_mixed, cross_mixed_t, cross_lse, cross_part = run_kernel(
        cross_forward_kernel,
        [rows_f, rows_d, rows_h, rows_h, turned_h, lse_shape, rows_d],
        tokens, self_part, swap_core(self_part), params, bias_q_cross, cross_qk, cross_vo,
        cross_k, cross_v_t,
        scratch=[
            pltpu.VMEM((keys_count, count), jnp.float32),
            pltpu.VMEM((keys_count, count), jnp.bfloat16),
        ],
        moved=70_000_000,
    )
    if fast:
        (w2_near, w1_last), cross_part = together(near_steps(w2_far, w1_near), cross_part)
        w1 = assemble_pair(w1_near, w1_last)
    hidden_rows = array_of((count, hidden_cols))
    section2, hidden3, act, slope, grad_low = run_kernel(
        dense_in_kernel,
        [rows_f, rows_d, hidden_rows, hidden_rows, rows_d],
        lengths, section1, cross_part, swap_core(cross_part), params, bias_hidden, *w1, cotangent,
        moved=30_000_000,
    )
    dense_uses = tuple((0, 0, at * head_cols, at // 2, at % 2) for at in range(4))
    w2_parts = weight_parts(dense_uses, (grad_low,), (act,), 2, head_cols)
    if fast:
        (_, w2_last), w2_parts, slope = together(near_steps(None, w2_near), w2_parts, slope)
        w2 = assemble_pair(w2_near, w2_last)
    grad_pre, out_part, grad_h3, grad_b1 = run_kernel(
        dense_out_kernel,
        [hidden_rows, rows_d, rows_d, array_of((1, hidden_cols), jnp.float32)],
        act, slope, grad_low, *w1, *w2,
        moved=30_000_000,
    )
    w1_parts = weight_parts(dense_uses, (hidden3,), (grad_pre,), 2, head_cols)
    if fast:
        (w2_came, _), w1_parts, grad_h3, out_part = together(
            send_near(w2_parts, None), w1_parts, grad_h3, out_part
        )
        w2_lows, w2_highs = fold_both(w2_parts, w2_came)
    grad_h3_other, out_other = swap_core(grad_h3), swap_core(out_part)
    (
        layer_out, grad_section2, grad_z2, cross_dq, cross_dk, cross_dv, grad_h2, vectors3, biases_cross,
    ) = run_kernel(
        cross_backward_kernel,
        [rows_d, rows_f, rows_d, rows_h, keys_h, keys_h, rows_d,
         array_of((4, D), jnp.float32), array_of((2, head_cols), jnp.float32)],
        section2, grad_h3, grad_h3_other, out_part, out_other, grad_low, params,
        cross_qk, cross_vo, cross_q, cross_k, cross_v, cross_k_t, cross_mixed_t, cross_lse,
        scratch=[scratch_h, scratch_t, scratch_t],
        moved=120_000_000,
    )
    if fast:
        (w1_came, w2_came), cross_dq, cross_dk, grad_h2 = together(
            send_near(w1_parts, w2_highs), cross_dq, cross_dk, grad_h2
        )
        w2_own, *w2_out = far_ready(w2_lows, w2_came)
        w1_lows, w1_highs = fold_both(w1_parts, w1_came)
    cross_parts = weight_parts(
        ((0, 0, 0, 0, 0), (1, 1, 0, 0, 1), (1, 2, 0, 1, 0), (2, 3, 0, 1, 1)),
        (hidden2, enc_t, grad_z2),
        (cross_dq, cross_dk, cross_dv, cross_mixed),
        2,
        head_cols,
    )
    grad_h2_other = swap_core(grad_h2)
    length_back = lengths
    if fast:
        (_, w1_came), w2_in1, w2_in2, cross_parts, grad_h2_other, length_back = together(
            send_near(None, w1_highs), swap(w2_out[0], 4), swap(w2_out[1], 8),
            cross_parts, grad_h2_other, lengths,
        )
        w1_own, *w1_out = far_ready(w1_lows, w1_came)
    (
        grad_section1, grad_z1, self_dq, self_dk, self_dv, grad_h1, vectors2, biases_self,
    ) = run_kernel(
        self_backward_kernel,
        [rows_f, rows_d, rows_h, rows_h, rows_h, rows_d,
         array_of((3, D), jnp.float32), array_of((2, head_cols), jnp.float32)],
        length_back, section1, grad_section2, grad_h2, grad_h2_other, params,
        self_qk, self_vo, self_q, self_k, self_v, self_mixed_t, self_lse,
        scratch=[scratch_h, scratch_t, scratch_t, scratch_t, scratch_s],
        moved=60_000_000,
    )
    if fast:
        (cross_came, _), w2_in3, w1_in1, w1_in2, self_dq, grad_h1 = together(
            send_near(cross_parts, None), swap(w2_out[2], 12), swap(w1_out[0], 4),
            swap(w1_out[1], 8), self_dq, grad_h1,
        )
        cross_lows, cross_highs = fold_both(cross_parts, cross_came)
    self_parts = weight_parts(
        ((0, 0, 0, 0, 0), (0, 1, 0, 0, 1), (0, 2, 0, 1, 0), (1, 3, 0, 1, 1)),
        (hidden1, grad_z1),
        (self_dq, self_dk, self_dv, self_mixed),
        2,
        head_cols,
    )
    grad_h1_other = swap_core(grad_h1)
    core_in = core[None]
    if fast:
        (_, cross_came), w1_in3, self_parts, grad_h1_other, core_in = together(
            send_near(None, cross_highs), swap(w1_out[2], 12), self_parts, grad_h1_other, core_in
        )
        cross_own, *cross_out = far_ready(cross_lows, cross_came)
    input_grad, vector_grad = run_kernel(
        last_kernel,
        [rows_f, array_of(params.shape, jnp.float32)],
        core_in, tokens, grad_section1, grad_h1, grad_h1_other, params,
        vectors2, vectors3, biases_self, biases_cross, grad_b1,
        moved=12_000_000,
    )
    enc_other = run_kernel(
        enc_kernel,
        array_of((keys_count, head_cols)),
        1 - core_in, cross_dk, cross_dv, cross_qk, cross_vo,
        moved=15_000_000,
    )
    if fast:
        (self_came, _), cross_ins, vector_grad, enc_other = together(
            send_near(self_parts, None),
            [swap(out, offset) for out, offset in zip(cross_out, FAR[1:])],
            vector_grad, enc_other,
        )
        self_lows, self_highs = fold_both(self_parts, self_came)
        (_, self_came), vector_grad, enc_came = together(
            send_near(None, self_highs), vector_grad, swap_core(enc_other)
        )
        self_own, *self_out = far_ready(self_lows, self_came)
    else:
        enc_came = swap_core(enc_other)
    enc_grad = run_kernel(
        enc_kernel,
        array_of((keys_count, 1, head_cols), jnp.float32),
        core_in, cross_dk, cross_dv, cross_qk, cross_vo, enc_came,
        moved=20_000_000,
    )
    group = array_of((4, D // lax.axis_size("dp"), head_cols), jnp.float32)
    square_row = array_of((1, head_cols), jnp.float32)
    if fast:
        w1_sum, w2_sum, cross_sum, early_squares = run_kernel(
            functools.partial(totals_kernel, 3),
            [group, group, group, square_row],
            w1_own, w1_in1, w1_in2, w1_in3, w2_own, w2_in1, w2_in2, w2_in3, cross_own, *cross_ins,
        )
        self_ins, enc_grad, early_squares = together(
            [swap(out, offset) for out, offset in zip(self_out, FAR[1:])], enc_grad, early_squares
        )
        self_sum, late_squares = run_kernel(
            functools.partial(totals_kernel, 1), [group, square_row], self_own, *self_ins
        )
    else:
        self_sum, cross_sum, w1_sum, w2_sum = [
            jnp.concatenate(
                [
                    lax.psum_scatter(
                        part.astype(jnp.float32), "dp", scatter_dimension=1, tiled=True
                    )
                    for part in parts
                ],
                axis=0,
            )
            for parts in (self_parts, cross_parts, w1_parts, w2_parts)
        ]
        early_squares, late_squares = [
            sum(jnp.sum(total * total, axis=(0, 1)) for total in sums)[None]
            for sums in ((cross_sum, w1_sum, w2_sum), (self_sum,))
        ]
    enc_grad = enc_grad.transpose(1, 0, 2)
    square = jnp.sum(early_squares + late_squares)
    sums = sum_near(
        sum_far(jnp.concatenate([vector_grad, jnp.full((1, D), square)], axis=0))
    )
    vector_sum = lax.dynamic_slice_in_dim(sums[:-1], device * own_cols, own_cols, 1)
    outs = [
        jax.ShapeDtypeStruct(master.shape, dtype)
        for master in (attn_master, dense_master, vector_params)
        for dtype in (jnp.float32, jnp.float32, jnp.float32, jnp.bfloat16)
    ]
    norm, *updated, bias_gradient = run_kernel(
        finish_kernel,
        [array_of((1, 128), jnp.float32), *outs, array_of((1, own_cols), jnp.float32)],
        decays[None], sums, vector_sum, self_sum, cross_sum, w1_sum, w2_sum,
        attn_master, attn_first, attn_second, dense_master, dense_first, dense_second,
        vector_params, vector_first, vector_second,
    )
    return (layer_out, input_grad, enc_grad, norm[0, 0], *updated, bias_gradient[0])


def solution(mesh):
    return jax.shard_map(
        local,
        mesh=mesh,
        in_specs=(
            P("dp", None),
            P("dp", None, None),
            P("dp"),
            P("dp", None),
            P(None, None, "dp", "mp"),
            P(None, None, "dp", "mp"),
            P(None, None, "dp", "mp"),
            P(None, "dp", "mp"),
            P(None, "dp", "mp"),
            P(None, "dp", "mp"),
            P(None, ("dp", "mp")),
            P(None, ("dp", "mp")),
            P(None, ("dp", "mp")),
            P(),
        ),
        out_specs=(
            P("dp", None),
            P("dp", None),
            P("dp", None, "mp"),
            P(),
            P(None, None, "dp", "mp"),
            P(None, None, "dp", "mp"),
            P(None, None, "dp", "mp"),
            P(None, None, "dp", "mp"),
            P(None, "dp", "mp"),
            P(None, "dp", "mp"),
            P(None, "dp", "mp"),
            P(None, "dp", "mp"),
            P(None, ("dp", "mp")),
            P(None, ("dp", "mp")),
            P(None, ("dp", "mp")),
            P(None, ("dp", "mp")),
            P(("dp", "mp")),
        ),
        check_vma=False,
    )
```

```python
import functools

import jax
import jax.numpy as jnp
from jax import lax
from jax.experimental import pallas as pl
from jax.experimental.pallas import tpu as pltpu
from jax.sharding import PartitionSpec as P

D = 768
HEAD_DIM = 64
FF = 3072
BLOCK = 448
STEP = 3


attn_rate = 0.08
dense_rate = 0.03
vector_rate = 0.3
LOG2E = 1.4426950408889634
FAR = [0, 4, 8, 12]


def dot(left_side, right_side):
    return jnp.dot(left_side, right_side, preferred_element_type=jnp.float32)


def dot_nt(left_side, right_side):
    return lax.dot_general(
        left_side, right_side, (((1,), (1,)), ((), ())), preferred_element_type=jnp.float32
    )


def spans(total, step):
    return [(at, min(step, total - at)) for at in range(0, total, step)]


def unit_norm(values):
    centred = values - jnp.mean(values, axis=-1, keepdims=True)
    inverse = lax.rsqrt(jnp.mean(centred * centred, axis=-1, keepdims=True) + 1e-05)
    return centred * inverse, inverse


def norm_rows(values, gain, shift):
    unit, _ = unit_norm(values)
    return (unit * gain + shift).astype(jnp.bfloat16)


def norm_pull(values, grad, gain):
    unit, inverse = unit_norm(values)
    scaled = grad * gain
    pulled = inverse * (
        scaled
        - jnp.mean(scaled, axis=-1, keepdims=True)
        - unit * jnp.mean(scaled * unit, axis=-1, keepdims=True)
    )
    return (
        pulled,
        jnp.sum(grad * unit, axis=0, keepdims=True),
        jnp.sum(grad, axis=0, keepdims=True),
    )


def head_masks():
    lane = lax.broadcasted_iota(jnp.int32, (1, 2 * HEAD_DIM), 1)
    return [(lane < HEAD_DIM).astype(jnp.bfloat16), (lane >= HEAD_DIM).astype(jnp.bfloat16)]


def row_sum(values):
    return jnp.sum(values.astype(jnp.float32), axis=0, keepdims=True)


HERE, CORE, LENGTH = range(3)


def run_kernel(kernel, out_shapes, *operands, scratch=(), weights=()):
    spaces = [
        pl.BlockSpec(memory_space=pltpu.SMEM if operand.dtype == jnp.int32 else pltpu.VMEM)
        for operand in operands
    ]
    held = [array for sources, _ in weights for array, _ in sources]
    single = not isinstance(out_shapes, (list, tuple))
    shapes = [out_shapes] if single else list(out_shapes)
    first_held, first_out = len(operands), len(operands) + len(held)
    buffers = [
        pltpu.VMEM((len(matrices),) + (D, sources[0][0].shape[-1]), jnp.bfloat16)
        for sources, matrices in weights
    ]
    copies_of = [
        sum(1 if offsets is None else 8 for _, offsets in sources) * len(matrices)
        for sources, matrices in weights
    ]
    semaphores = [pltpu.SemaphoreType.DMA((number,)) for number in copies_of]

    def body(*refs):
        refs = list(refs)
        if not weights:
            kernel(*refs)
            return
        info = refs[0]
        tail = len(refs) - 2 * len(weights)
        stacks = iter(refs[first_held:first_out])
        pending = []
        for at, (sources, matrices) in enumerate(weights):
            target, sems = refs[tail + at], refs[tail + len(weights) + at]
            copies = []
            for (_, offsets), stack in zip(sources, stacks):
                for which, matrix in enumerate(matrices):
                    if offsets is None:
                        pieces = [(stack.at[matrix], target.at[which])]
                    else:
                        rows = stack.shape[2]
                        pieces = []
                        for piece in range(8):
                            offset = offsets[piece // 4] ^ FAR[piece % 4]
                            place = pl.multiple_of((info[HERE] ^ offset) * rows, 16)
                            pieces.append(
                                (stack.at[piece, matrix], target.at[which, pl.ds(place, rows), :])
                            )
                    for source, place in pieces:
                        copies.append(pltpu.make_async_copy(source, place, sems.at[len(copies)]))
            for copy in copies:
                copy.start()
            pending.append((target, copies))

        def loaded(at):
            target, copies = pending[at]
            for copy in copies:
                copy.wait()
            return [target.at[which] for which in range(len(weights[at][1]))]

        kernel(loaded, *refs[:first_held], *refs[first_out:tail])

    outs = [pl.BlockSpec(memory_space=pltpu.VMEM) for _ in shapes]
    results = pl.pallas_call(
        body,
        out_shape=shapes,
        in_specs=spaces + [pl.BlockSpec(memory_space=pl.ANY) for _ in held],
        out_specs=outs,
        scratch_shapes=[*scratch, *buffers, *semaphores],
        compiler_params=pltpu.CompilerParams(vmem_limit_bytes=56 * 2**20),
    )(*operands, *held)
    return results[0] if single else results


def array_of(shape, dtype=jnp.bfloat16):
    return jax.ShapeDtypeStruct(shape, dtype)


def local_bias(params, row, core, width):
    return params[row : row + 1, pl.ds(pl.multiple_of(core * width, 128), width)]


def cross_keys_kernel(loaded, info, enc, params, keys, values, keys_t, values_t, enc_t):
    bias_v = local_bias(params, 10, info[CORE], keys.shape[1])
    for at, size in spans(enc.shape[0], 256):
        rows = pl.ds(at, size)
        enc_t[:, rows] = enc[rows, :].T
    (wk,), (wv,) = loaded(0), loaded(1)
    for at, size in spans(enc.shape[0], 256):
        rows = pl.ds(at, size)
        block = enc[rows, :]
        key_block = dot(block, wk[...]).astype(jnp.bfloat16)
        value_block = (dot(block, wv[...]) + bias_v).astype(jnp.bfloat16)
        keys[rows, :] = key_block
        values[rows, :] = value_block
        keys_t[:, rows] = key_block.T
        values_t[:, rows] = value_block.T


def self_forward_kernel(
    loaded, info, tokens, params,
    hidden, q, k, v, mixed, mixed_t, lse, part,
    values_t, allowed,
):
    count = tokens.shape[0]
    for at, size in spans(count, 64):
        rows = pl.ds(at, size)
        hidden[rows, :] = norm_rows(
            tokens[rows, :].astype(jnp.float32), params[0:1, :], params[1:2, :]
        )
    bias_q = local_bias(params, 6, info[CORE], q.shape[1])
    bias_v = local_bias(params, 7, info[CORE], q.shape[1])
    wq, wk = loaded(0)
    q[...] = (dot(hidden[...], wq[...]) + bias_q).astype(jnp.bfloat16)
    k[...] = dot(hidden[...], wk[...]).astype(jnp.bfloat16)
    wv, wo = loaded(1)
    v[...] = (dot(hidden[...], wv[...]) + bias_v).astype(jnp.bfloat16)
    values_t[...] = v[...].T
    key_ids = lax.broadcasted_iota(jnp.int32, (count, count), 0)
    query_ids = lax.broadcasted_iota(jnp.int32, (count, count), 1)
    allowed[...] = ((key_ids <= query_ids) & (key_ids < info[LENGTH])).astype(jnp.float32)
    masks = head_masks()

    def pair_step(pair, carry):
        cols = pl.ds(pl.multiple_of(pair * 128, 128), 128)
        for parity in range(2):
            head = pair * 2 + parity
            scores = dot_nt(k[:, cols], q[:, cols] * masks[parity]) * (0.125 * LOG2E)
            scores = jnp.where(allowed[...] > 0.5, scores, -1e30)
            top = jnp.max(scores, axis=0, keepdims=True)
            weights = jnp.exp2(scores - top)
            total = jnp.sum(weights, axis=0, keepdims=True)
            lse[pl.ds(head, 1), :] = top + jnp.log2(total)
            own = pl.ds(pl.multiple_of(head * HEAD_DIM, HEAD_DIM), HEAD_DIM)
            mixed_t[own, :] = (
                dot(values_t[own, :], weights.astype(jnp.bfloat16)) * (1.0 / total)
            ).astype(jnp.bfloat16)
        return carry

    lax.fori_loop(0, q.shape[1] // 128, pair_step, 0)
    mixed[...] = mixed_t[...].T
    part[...] = dot_nt(mixed[...], wo[...]).astype(jnp.bfloat16)


def cross_forward_kernel(
    loaded, info, tokens, own_part, other_part, params, keys, values_t,
    section, hidden, q, mixed, mixed_t, lse, part,
    scores, weights,
):
    count = tokens.shape[0]
    for at, size in spans(count, 64):
        rows = pl.ds(at, size)
        branch = own_part[rows, :].astype(jnp.float32) + other_part[rows, :].astype(jnp.float32)
        block = tokens[rows, :].astype(jnp.float32) + (branch + params[8:9, :])
        section[rows, :] = block
        hidden[rows, :] = norm_rows(block, params[2:3, :], params[3:4, :])
    (wq,), (wo,) = loaded(0), loaded(1)
    bias_q = local_bias(params, 9, info[CORE], q.shape[1])
    q[...] = (dot(hidden[...], wq[...]) + bias_q).astype(jnp.bfloat16)
    masks = head_masks()
    key_spans = spans(keys.shape[0], 256)

    def pair_step(pair, carry):
        cols = pl.ds(pl.multiple_of(pair * 128, 128), 128)
        for parity in range(2):
            head = pair * 2 + parity
            queries = q[:, cols] * masks[parity]
            top = None
            for at, size in key_spans:
                block = dot_nt(keys[pl.ds(at, size), cols], queries) * (0.125 * LOG2E)
                scores[pl.ds(at, size), :] = block
                block_top = jnp.max(block, axis=0, keepdims=True)
                top = block_top if top is None else jnp.maximum(top, block_top)
            total = jnp.zeros_like(top)
            for at, size in key_spans:
                block = jnp.exp2(scores[pl.ds(at, size), :] - top)
                total = total + jnp.sum(block, axis=0, keepdims=True)
                weights[pl.ds(at, size), :] = block.astype(jnp.bfloat16)
            lse[pl.ds(head, 1), :] = top + jnp.log2(total)
            own = pl.ds(pl.multiple_of(head * HEAD_DIM, HEAD_DIM), HEAD_DIM)
            mixed_t[own, :] = (dot(values_t[own, :], weights[...]) * (1.0 / total)).astype(
                jnp.bfloat16
            )
        return carry

    lax.fori_loop(0, q.shape[1] // 128, pair_step, 0)
    mixed[...] = mixed_t[...].T
    part[...] = dot_nt(mixed[...], wo[...]).astype(jnp.bfloat16)


def dense_in_kernel(
    loaded, info, section, own_part, other_part, params, cotangent,
    section_new, hidden, act, slope, grad_low,
):
    count = section.shape[0]
    for at, size in spans(count, 64):
        rows = pl.ds(at, size)
        branch = own_part[rows, :].astype(jnp.float32) + other_part[rows, :].astype(jnp.float32)
        block = section[rows, :] + (branch + params[11:12, :])
        section_new[rows, :] = block
        hidden[rows, :] = norm_rows(block, params[4:5, :], params[5:6, :])
        row_ids = lax.broadcasted_iota(jnp.int32, (size, 1), 0) + at
        valid = (row_ids < info[LENGTH]).astype(jnp.float32)
        grad_low[rows, :] = (cotangent[rows, :].astype(jnp.float32) * valid).astype(jnp.bfloat16)

    held = act.shape[1] // D
    for at in range(4):
        if at % 2 == 0:
            blocks = loaded(at // 2)
        width = blocks[0].shape[1]
        row = 13 + info[CORE] * held + at * width // D
        bias = params[pl.ds(row, 1), at * width % D : at * width % D + width]

        def step(part, carry, at=at, block=blocks[at % 2], bias=bias):
            cols = pl.ds(at * width, width)
            pre_act = dot(hidden[...], block[...]) + bias
            spread = 0.5 + 0.5 * lax.erf(pre_act * (2.0**-0.5))
            act[:, cols] = (pre_act * spread).astype(jnp.bfloat16)
            density = jnp.exp2(pre_act * pre_act * (-0.5 * LOG2E)) * 0.3989422804014327
            slope[:, cols] = (spread + pre_act * density).astype(jnp.bfloat16)
            return carry

        step(0, 0)


def dense_out_kernel(
    loaded, info, act, slope, grad_low,
    grad_pre, part, grad_hidden, grad_bias,
):
    w2 = loaded(0) + loaded(1)
    width = w2[0].shape[1]
    for at, block in enumerate(w2):
        cols = pl.ds(at * width, width)
        grad_act = dot(grad_low[...], block[...]).astype(jnp.bfloat16).astype(jnp.float32)
        grad_block = (grad_act * slope[:, cols].astype(jnp.float32)).astype(jnp.bfloat16)
        grad_pre[:, cols] = grad_block
        grad_bias[:, cols] = row_sum(grad_block)
    for left, blocks, out in (
        (act, w2, part),
        (grad_pre, loaded(2) + loaded(3), grad_hidden),
    ):
        total = None
        for at, block in enumerate(blocks):
            product = dot_nt(left[:, at * width : at * width + width], block[...])
            total = product if total is None else total + product
        out[...] = total.astype(jnp.bfloat16)


def put_relative(product, here, order, keep, send, which, cols):
    half = keep.shape[0]
    rows = keep.shape[2]
    for at, offset in enumerate(order):
        block = product[pl.ds(pl.multiple_of((here ^ offset) * rows, 16), rows), :]
        target = keep if at < half else send
        target[at % half, which, :, cols] = block.astype(jnp.bfloat16)


def weight_kernel(uses, lefts_count, orders, *refs):
    rights_count = 1 + max(right for _, right, _, _, _ in uses)
    lefts, rights = refs[1 : 1 + lefts_count], refs[1 + lefts_count : 1 + lefts_count + rights_count]
    outs = refs[1 + lefts_count + rights_count : -2]
    product, turned = refs[-2:]
    width = product.shape[1]
    me = refs[0][0]
    in_turned = None
    for left, right, first, group, which in uses:
        left_t, right = lefts[left], rights[right]
        if left_t.shape[0] != D:
            if in_turned != left:
                turned[...] = left_t[...].T
                in_turned = left
            left_t = turned

        def step(at, carry, left_t=left_t, right=right, first=first, group=group, which=which):
            cols = pl.ds(pl.multiple_of(at * width, width), width)
            taken = pl.ds(pl.multiple_of(first + at * width, width), width)
            product[...] = dot(left_t[...], right[:, taken])
            if orders is None:
                outs[group][which, :, cols] = product[...].astype(jnp.bfloat16)
            else:
                put_relative(
                    product, me, orders[group], outs[2 * group], outs[2 * group + 1], which, cols
                )
            return carry

        lax.fori_loop(0, outs[0].shape[-1] // width, step, 0)


def attention_pull(
    keys, values, keys_t, q, grad_mixed, grad_mixed_t, mixed_t, lse, allowed, step,
    grad_keys, grad_values, grad_q_t,
):
    masks = head_masks()
    key_spans = spans(keys.shape[0], step)

    def pair_step(pair, carry):
        cols = pl.ds(pl.multiple_of(pair * 128, 128), 128)
        queries = [q[:, cols] * mask for mask in masks]
        grads = [(grad_mixed[:, cols] * 0.125) * mask for mask in masks]
        heads = [pl.ds(pl.multiple_of(pair * 128 + p * 64, 64), 64) for p in range(2)]
        levels, deltas = [], []
        for parity in range(2):
            levels.append(lse[pl.ds(pair * 2 + parity, 1), :])
            product = grad_mixed_t[heads[parity], :].astype(jnp.float32) * mixed_t[
                heads[parity], :
            ].astype(jnp.float32)
            deltas.append(jnp.sum(product, axis=0, keepdims=True) * 0.125)
        sums = [None, None]
        for at, size in key_spans:
            rows = pl.ds(at, size)
            key_sum = value_sum = None
            for parity in range(2):
                scores = dot_nt(keys[rows, cols], queries[parity]) * (0.125 * LOG2E)
                weights = jnp.exp2(scores - levels[parity])
                if allowed is not None:
                    weights = jnp.where(allowed[rows, :] > 0.5, weights, 0.0)
                grad_soft = dot_nt(values[rows, cols], grads[parity])
                grad_raw = (weights * (grad_soft - deltas[parity])).astype(jnp.bfloat16)
                value_part = dot(weights.astype(jnp.bfloat16), grads[parity])
                key_part = dot(grad_raw, queries[parity])
                query_part = dot(keys_t[heads[parity], rows], grad_raw)
                value_sum = value_part if value_sum is None else value_sum + value_part
                key_sum = key_part if key_sum is None else key_sum + key_part
                sums[parity] = query_part if sums[parity] is None else sums[parity] + query_part
            grad_values[rows, cols] = (value_sum * 8.0).astype(jnp.bfloat16)
            grad_keys[rows, cols] = key_sum.astype(jnp.bfloat16)
        for parity in range(2):
            grad_q_t[heads[parity], :] = sums[parity].astype(jnp.bfloat16)
        return carry

    lax.fori_loop(0, q.shape[1] // 128, pair_step, 0)


def cross_backward_kernel(
    loaded, info, section, grad_part, grad_other, out_part, out_other, grad_top, params,
    q, keys, values, keys_t, mixed_t, lse,
    layer_out, grad_section, grad_z, grad_q, grad_keys, grad_values, grad_hidden, vectors, biases,
    grad_mixed, grad_mixed_t, grad_q_t,
):
    count = section.shape[0]
    sums = None
    for at, size in spans(count, 64):
        rows = pl.ds(at, size)
        block = section[rows, :]
        branch = out_part[rows, :].astype(jnp.float32) + out_other[rows, :].astype(jnp.float32)
        layer_out[rows, :] = (block + (branch + params[12:13, :])).astype(jnp.bfloat16)
        grad = grad_part[rows, :].astype(jnp.float32) + grad_other[rows, :].astype(jnp.float32)
        pulled, gain_sum, shift_sum = norm_pull(block, grad, params[4:5, :])
        top = grad_top[rows, :].astype(jnp.float32)
        total = top + pulled
        low = total.astype(jnp.bfloat16)
        grad_section[rows, :] = total
        grad_z[rows, :] = low
        parts = [gain_sum, shift_sum, row_sum(low), jnp.sum(top, axis=0, keepdims=True)]
        sums = parts if sums is None else [old + new for old, new in zip(sums, parts)]
    for at, value in enumerate(sums):
        vectors[at : at + 1, :] = value
    (wo,), (wq,) = loaded(1), loaded(0)
    grad_mixed[...] = dot(grad_z[...], wo[...]).astype(jnp.bfloat16)
    grad_mixed_t[...] = grad_mixed[...].T
    attention_pull(
        keys, values, keys_t, q, grad_mixed, grad_mixed_t, mixed_t, lse, None, 256,
        grad_keys, grad_values, grad_q_t,
    )
    grad_q[...] = grad_q_t[...].T
    grad_hidden[...] = dot_nt(grad_q[...], wq[...]).astype(jnp.bfloat16)
    biases[0:1, :] = row_sum(grad_q[...])
    biases[1:2, :] = row_sum(grad_values[...])


def self_backward_kernel(
    loaded, info, section, grad_section, grad_part, grad_other, params,
    q, k, v, mixed_t, lse,
    grad_new, grad_z, grad_q, grad_keys, grad_values, grad_hidden, vectors, biases,
    grad_mixed, grad_mixed_t, grad_q_t, keys_t, allowed,
):
    count = section.shape[0]
    sums = None
    for at, size in spans(count, 64):
        rows = pl.ds(at, size)
        grad = grad_part[rows, :].astype(jnp.float32) + grad_other[rows, :].astype(jnp.float32)
        pulled, gain_sum, shift_sum = norm_pull(section[rows, :], grad, params[2:3, :])
        total = grad_section[rows, :] + pulled
        low = total.astype(jnp.bfloat16)
        grad_new[rows, :] = total
        grad_z[rows, :] = low
        parts = [gain_sum, shift_sum, row_sum(low)]
        sums = parts if sums is None else [old + new for old, new in zip(sums, parts)]
    for at, value in enumerate(sums):
        vectors[at : at + 1, :] = value
    wv, wo = loaded(1)
    wq, wk = loaded(0)
    grad_mixed[...] = dot(grad_z[...], wo[...]).astype(jnp.bfloat16)
    grad_mixed_t[...] = grad_mixed[...].T
    keys_t[...] = k[...].T
    key_ids = lax.broadcasted_iota(jnp.int32, (count, count), 0)
    query_ids = lax.broadcasted_iota(jnp.int32, (count, count), 1)
    allowed[...] = ((key_ids <= query_ids) & (key_ids < info[LENGTH])).astype(jnp.float32)
    attention_pull(
        k, v, keys_t, q, grad_mixed, grad_mixed_t, mixed_t, lse, allowed, 256,
        grad_keys, grad_values, grad_q_t,
    )
    grad_q[...] = grad_q_t[...].T
    grad_hidden[...] = (
        dot_nt(grad_q[...], wq[...])
        + dot_nt(grad_keys[...], wk[...])
        + dot_nt(grad_values[...], wv[...])
    ).astype(jnp.bfloat16)
    biases[0:1, :] = row_sum(grad_q[...])
    biases[1:2, :] = row_sum(grad_values[...])


def last_kernel(
    info, tokens, grad_section, grad_part, grad_other, params,
    vectors2, vectors3, biases_self, biases_cross, grad_b1,
    input_grad, vectors,
):
    sums = None
    for at, size in spans(tokens.shape[0], 64):
        rows = pl.ds(at, size)
        grad = grad_part[rows, :].astype(jnp.float32) + grad_other[rows, :].astype(jnp.float32)
        pulled, gain_sum, shift_sum = norm_pull(
            tokens[rows, :].astype(jnp.float32), grad, params[0:1, :]
        )
        input_grad[rows, :] = grad_section[rows, :] + pulled
        parts = [gain_sum, shift_sum]
        sums = parts if sums is None else [old + new for old, new in zip(sums, parts)]
    leader = (info[CORE] == 0).astype(jnp.float32)
    vectors[...] = jnp.zeros_like(vectors)
    shared = sums + [vectors2[0:1, :], vectors2[1:2, :], vectors3[0:1, :], vectors3[1:2, :]]
    shared = list(enumerate(shared)) + [(8, vectors2[2:3, :]), (11, vectors3[2:3, :]), (12, vectors3[3:4, :])]
    for at, value in shared:
        vectors[at : at + 1, :] = value * leader
    width = biases_self.shape[1]
    cols = pl.ds(pl.multiple_of(info[CORE] * width, 128), width)
    for at, ref in ((6, biases_self), (9, biases_cross)):
        vectors[at : at + 1, cols] = ref[0:1, :]
        vectors[at + 1 : at + 2, cols] = ref[1:2, :]
    held = grad_b1.shape[1] // D
    for at in range(held):
        vectors[pl.ds(13 + info[CORE] * held + at, 1), :] = grad_b1[:, at * D : at * D + D]


def enc_kernel(loaded, info, grad_keys, grad_values, *refs):
    own, out = refs[:-1], refs[-1]
    width = grad_keys.shape[1]
    place = info[CORE] if own else 1 - info[CORE]
    cols = pl.ds(pl.multiple_of(place * width, 128), width)
    (wk,), (wv,) = loaded(0), loaded(1)
    for at, size in spans(grad_keys.shape[0], 256):
        rows = pl.ds(at, size)
        total = dot_nt(grad_keys[rows, :], wk[cols, :]) + dot_nt(grad_values[rows, :], wv[cols, :])
        if own:
            out[rows, 0, :] = total + own[0][rows, :].astype(jnp.float32)
        else:
            out[rows, :] = total.astype(out.dtype)


def swap(array, bit):
    count = lax.axis_size("dp")
    return lax.ppermute(array, "dp", [(i, i ^ bit) for i in range(count)])


def swap_core(array):
    return lax.ppermute(array, "mp", [(0, 1), (1, 0)])


def together(*values):
    return lax.optimization_barrier(values)


def sum_round(value, bits):
    me = lax.axis_index("dp")
    offsets = [0]
    for bit in bits:
        offsets = offsets + [offset ^ bit for offset in offsets]
    stack = [value] + [swap(value, offset) for offset in offsets[1:]]
    for bit in bits:
        flip = (me & bit) != 0
        pairs = [(stack[at], stack[at + 1]) for at in range(0, len(stack), 2)]
        stack = [jnp.where(flip, b, a) + jnp.where(flip, a, b) for a, b in pairs]
    return stack[0]


def sum_far(value):
    for bits in [(4, 8)] if lax.axis_size("dp") == 16 else high_bits():
        value = sum_round(value, bits)
    return value


def high_bits():
    return [(1 << k,) for k in range(2, lax.axis_size("dp").bit_length() - 1)]


def sum_near(value):
    value = sum_round(value, (1, 2))
    return value + swap_core(value)


def join(stack, came):
    return jnp.concatenate([stack, came], axis=0)


def far_stack(piece):
    return jnp.concatenate([piece] + [swap(piece, offset) for offset in FAR[1:]], axis=0)


def near_steps(first, second):
    parts = None if first is None else halves(first)
    onward = []
    for place, bit in enumerate((1, 2)):
        pieces = []
        if second is not None:
            pieces.append(second[1 - place])
        if first is not None:
            pieces.append(parts[place])
        onward.append(swap(jnp.concatenate(pieces, axis=0), bit))
    cut = 0 if second is None else 8
    nears = None if first is None else [join(part, came[cut:]) for part, came in zip(parts, onward)]
    lasts = None if second is None else onward[::-1]
    return nears, lasts


def near_parts(nears, lasts):
    return [
        [(near, (0, first)), (last, (3 ^ first, 3))]
        for near, last, first in zip(nears, lasts, (1, 2))
    ]


def halves(stack):
    return jnp.split(stack, 2, axis=1)


def weight_parts(uses, lefts, rights, wide, cols):
    count = lax.axis_size("dp")
    direct = count == 16
    orders = []
    for first in (2, 1):
        order = FAR
        for bit in (3 ^ first, first):
            order = order + [offset ^ bit for offset in order]
        orders.append(order)
    if direct:
        outs = [array_of((8, wide, D // 16, cols))] * 4
    else:
        outs = [array_of((wide, D, cols))] * 2
    return run_kernel(
        functools.partial(weight_kernel, uses, len(lefts), orders if direct else None),
        outs,
        lax.axis_index("dp")[None],
        *lefts,
        *rights,
        scratch=[pltpu.VMEM((D, 384), jnp.float32), pltpu.VMEM((D, BLOCK), jnp.bfloat16)],
    )


def send_near(first, second):
    cames = []
    for place, bit in enumerate((1, 2)):
        pieces = []
        if second is not None:
            pieces.append(second[place])
        if first is not None:
            pieces.append(first[3 - 2 * place])
        cames.append(swap(pieces[0] if len(pieces) == 1 else jnp.concatenate(pieces), bit))
    cut = 0 if second is None else 4
    return [came[cut:] for came in cames[::-1]], [came[:cut] for came in cames]


def fold_both(parts, cames):
    keep_a, _, keep_b, _ = parts
    (low_a, high_a), (low_b, high_b) = fold(keep_a, cames[0]), fold(keep_b, cames[1])
    return (low_a, low_b), (high_a, high_b)


def fold(keep, came):
    half = keep.shape[0] // 2
    high = keep[half:].astype(jnp.float32) + came[half:].astype(jnp.float32)
    return (
        keep[:half].astype(jnp.float32) + came[:half].astype(jnp.float32),
        high.astype(jnp.bfloat16),
    )


def far_ready(lows, cames):
    total = jnp.concatenate(
        [low.astype(jnp.float32) + came.astype(jnp.float32) for low, came in zip(lows, cames)],
        axis=1,
    )
    return [total[0]] + [total[at].astype(jnp.bfloat16) for at in range(1, 4)]


def totals_kernel(groups, *refs):
    squares = None
    outs = refs[-(groups + 1) :]
    for at in range(groups):
        own, *cames = refs[4 * at : 4 * at + 4]
        total = own[...]
        for came in cames:
            total = total + came[...].astype(jnp.float32)
        outs[at][...] = total
        square = jnp.sum(total * total, axis=(0, 1), keepdims=True)[0]
        squares = square if squares is None else squares + square
    if len(refs) == 5 * groups + 1:
        outs[groups][...] = squares
        return
    early, vectors = refs[4 * groups : 4 * groups + 2]
    count = vectors.shape[0]
    everything = jnp.sum(squares + early[...], axis=1, keepdims=True)
    outs[groups][0:count, :] = vectors[...]
    outs[groups][count : count + 1, :] = jnp.broadcast_to(everything, (1, vectors.shape[1]))


def finish_kernel(
    decays, sums, vector_sum, self_sum, cross_sum, w1_sum, w2_sum,
    attn, attn_first, attn_second, dense, dense_first, dense_second,
    vector, vector_first, vector_second,
    norm, attn_new, attn_first_new, attn_second_new, attn_copy,
    dense_new, dense_first_new, dense_second_new, dense_copy,
    vector_new, vector_first_new, vector_second_new, vector_copy, bias_gradient,
):
    vectors = sums[0 : sums.shape[0] - 1, :]
    squares = jnp.sum(jnp.sum(vectors * vectors, axis=0, keepdims=True), axis=1, keepdims=True)
    clip_norm = jnp.sqrt(squares + sums[sums.shape[0] - 1 : sums.shape[0], 0:1])
    norm[...] = jnp.broadcast_to(clip_norm, norm.shape)
    factor = jnp.minimum(1.0, 1.0 / (clip_norm + 1e-06))
    first_rate, second_rate = decays[0:1, 0:1], decays[0:1, 1:2]
    first_scale = 1.0 / (1.0 - first_rate * first_rate * first_rate)
    second_scale = 1.0 / (1.0 - second_rate * second_rate * second_rate)

    def update(gradient, weight, first, second, step_rate):
        clipped = gradient * factor
        first_new = first_rate * first + (1.0 - first_rate) * clipped
        second_new = second_rate * second + (1.0 - second_rate) * clipped * clipped
        change = (first_new * first_scale) / (jnp.sqrt(second_new * second_scale) + 1e-08)
        return weight - step_rate * (change + 0.1 * weight), first_new, second_new

    for at, gradient in enumerate((self_sum, cross_sum)):
        for which in range(4):
            new, first, second = update(
                gradient[which],
                attn[at, which],
                attn_first[at, which],
                attn_second[at, which],
                attn_rate,
            )
            attn_new[at, which] = new
            attn_first_new[at, which] = first
            attn_second_new[at, which] = second
            attn_copy[at, which] = new.astype(jnp.bfloat16)
    width = w1_sum.shape[2]
    for at, gradient in enumerate((w1_sum, w2_sum)):
        for which in range(4):
            cols = slice(which * width, which * width + width)
            new, first, second = update(
                gradient[which],
                dense[at, :, cols],
                dense_first[at, :, cols],
                dense_second[at, :, cols],
                dense_rate,
            )
            dense_new[at, :, cols] = new
            dense_first_new[at, :, cols] = first
            dense_second_new[at, :, cols] = second
            dense_copy[at, :, cols] = new.astype(jnp.bfloat16)
    new, first, second = update(
        vector_sum[...], vector[...], vector_first[...], vector_second[...], vector_rate
    )
    vector_new[...] = new
    vector_first_new[...] = first
    vector_second_new[...] = second
    vector_copy[...] = new.astype(jnp.bfloat16)
    bias_gradient[...] = vector_sum[12:13, :] * factor


def local(
    tokens,
    enc_states,
    lengths,
    cotangent,
    attn_master,
    attn_first,
    attn_second,
    dense_master,
    dense_first,
    dense_second,
    vector_params,
    vector_first,
    vector_second,
    decays,
):
    core = lax.axis_index("mp")
    attn_low = attn_master.astype(jnp.bfloat16)
    dense_low = dense_master.astype(jnp.bfloat16)
    blocks = dense_master.shape[2] // attn_master.shape[3]
    dense_low = jnp.stack(jnp.split(dense_low, blocks, axis=2), axis=1)
    device = lax.axis_index("dp") * lax.axis_size("mp") + core
    own_cols = vector_params.shape[1]
    placed = lax.dynamic_update_slice_in_dim(
        jnp.zeros((vector_params.shape[0], D), jnp.float32), vector_params, device * own_cols, 1
    )
    fast = lax.axis_size("dp") == 16
    head_cols = attn_master.shape[3]
    hidden_cols = dense_master.shape[2]
    head_rows = 2 * (head_cols // 128)
    count = tokens.shape[0]
    keys_count = enc_states.shape[1]
    enc = enc_states[0]
    rows_d = array_of((count, D))
    rows_f = array_of((count, D), jnp.float32)
    rows_h = array_of((count, head_cols))
    turned_h = array_of((head_cols, count))
    lse_shape = array_of((head_rows, count), jnp.float32)
    keys_h = array_of((keys_count, head_cols))
    keys_t_h = array_of((head_cols, keys_count))
    scratch_h = pltpu.VMEM((count, head_cols), jnp.bfloat16)
    scratch_t = pltpu.VMEM((head_cols, count), jnp.bfloat16)
    scratch_s = pltpu.VMEM((count, count), jnp.float32)

    here = lax.axis_index("dp")
    info = jnp.stack([here, core, lengths[0]]).astype(jnp.int32)
    if fast:
        low_self, low_cross = attn_low[0][None], attn_low[1][None]
        low_w1, low_w2 = dense_low[0][None], dense_low[1][None]
        vector_low = placed + swap(placed, 1)
        vector_low = vector_low + swap(vector_low, 2)
        self_far, vector_low = together(far_stack(low_self), vector_low + swap_core(vector_low))
        (self_near, _), params, low_cross = together(
            near_steps(self_far, None), sum_far(vector_low), low_cross
        )
        (_, self_last), cross_far, low_w1, info = together(
            near_steps(None, self_near), far_stack(low_cross), low_w1, info
        )
        self_a, self_b = near_parts(self_near, self_last)
    else:
        params = sum_near(sum_far(placed))
        attn_all = lax.all_gather(attn_low, "dp", axis=2, tiled=True)
        dense_all = lax.all_gather(dense_low, "dp", axis=2, tiled=True)
        (self_a, self_b), (cross_a, cross_b), (w1_a, w1_b), (w2_a, w2_b) = [
            [[(whole[:2], None)], [(whole[2:], None)]] for whole in (*attn_all, *dense_all)
        ]
    both = (0, 1)
    hidden1, self_q, self_k, self_v, self_mixed, self_mixed_t, self_lse, self_part = run_kernel(
        self_forward_kernel,
        [rows_d, rows_h, rows_h, rows_h, rows_h, turned_h, lse_shape, rows_d],
        info, tokens, params,
        scratch=[scratch_t, scratch_s],
        weights=[(self_a, both), (self_b, both)],
    )
    if fast:
        (cross_near, _), self_part = together(near_steps(cross_far, None), self_part)
    self_other = swap_core(self_part)
    if fast:
        (_, cross_last), w1_far, self_other, info, low_w2 = together(
            near_steps(None, cross_near), far_stack(low_w1), self_other, info, low_w2
        )
        cross_a, cross_b = near_parts(cross_near, cross_last)
    cross_k, cross_v, cross_k_t, cross_v_t, enc_t = run_kernel(
        cross_keys_kernel,
        [keys_h, keys_h, keys_t_h, keys_t_h, array_of((D, keys_count))],
        info, enc, params,
        weights=[(cross_a, (1,)), (cross_b, (0,))],
    )
    if fast:
        (w1_near, _), w2_far, cross_k, info = together(
            near_steps(w1_far, None), far_stack(low_w2), cross_k, info
        )
    section1, hidden2, cross_q, cross_mixed, cross_mixed_t, cross_lse, cross_part = run_kernel(
        cross_forward_kernel,
        [rows_f, rows_d, rows_h, rows_h, turned_h, lse_shape, rows_d],
        info, tokens, self_part, self_other, params, cross_k, cross_v_t,
        scratch=[
            pltpu.VMEM((keys_count, count), jnp.float32),
            pltpu.VMEM((keys_count, count), jnp.bfloat16),
        ],
        weights=[(cross_a, (0,)), (cross_b, (1,))],
    )
    if fast:
        (w2_near, w1_last), cross_part, info = together(
            near_steps(w2_far, w1_near), cross_part, info
        )
        w1_a, w1_b = near_parts(w1_near, w1_last)
    hidden_rows = array_of((count, hidden_cols))
    section2, hidden3, act, slope, grad_low = run_kernel(
        dense_in_kernel,
        [rows_f, rows_d, hidden_rows, hidden_rows, rows_d],
        info, section1, cross_part, swap_core(cross_part), params, cotangent,
        weights=[(w1_a, both), (w1_b, both)],
    )
    dense_uses = tuple((0, 0, at * head_cols, at // 2, at % 2) for at in range(4))
    w2_parts = weight_parts(dense_uses, (grad_low,), (act,), 2, head_cols)
    if fast:
        (_, w2_last), w2_parts, slope, info = together(
            near_steps(None, w2_near), w2_parts, slope, info
        )
        w2_a, w2_b = near_parts(w2_near, w2_last)
    grad_pre, out_part, grad_h3, grad_b1 = run_kernel(
        dense_out_kernel,
        [hidden_rows, rows_d, rows_d, array_of((1, hidden_cols), jnp.float32)],
        info, act, slope, grad_low,
        weights=[(w2_a, both), (w2_b, both), (w1_a, both), (w1_b, both)],
    )
    w1_parts = weight_parts(dense_uses, (hidden3,), (grad_pre,), 2, head_cols)
    if fast:
        (w2_came, _), w1_parts, grad_h3, out_part = together(
            send_near(w2_parts, None), w1_parts, grad_h3, out_part
        )
        w2_lows, w2_highs = fold_both(w2_parts, w2_came)
    grad_h3_other, out_other = swap_core(grad_h3), swap_core(out_part)
    (
        layer_out, grad_section2, grad_z2, cross_dq, cross_dk, cross_dv, grad_h2, vectors3, biases_cross,
    ) = run_kernel(
        cross_backward_kernel,
        [rows_d, rows_f, rows_d, rows_h, keys_h, keys_h, rows_d,
         array_of((4, D), jnp.float32), array_of((2, head_cols), jnp.float32)],
        info, section2, grad_h3, grad_h3_other, out_part, out_other, grad_low, params,
        cross_q, cross_k, cross_v, cross_k_t, cross_mixed_t, cross_lse,
        scratch=[scratch_h, scratch_t, scratch_t],
        weights=[(cross_a, (0,)), (cross_b, (1,))],
    )
    if fast:
        (w1_came, w2_came), cross_dq, cross_dk, grad_h2 = together(
            send_near(w1_parts, w2_highs), cross_dq, cross_dk, grad_h2
        )
        w2_own, *w2_out = far_ready(w2_lows, w2_came)
        w1_lows, w1_highs = fold_both(w1_parts, w1_came)
    cross_parts = weight_parts(
        ((0, 0, 0, 0, 0), (1, 1, 0, 0, 1), (1, 2, 0, 1, 0), (2, 3, 0, 1, 1)),
        (hidden2, enc_t, grad_z2),
        (cross_dq, cross_dk, cross_dv, cross_mixed),
        2,
        head_cols,
    )
    grad_h2_other = swap_core(grad_h2)
    if fast:
        (_, w1_came), w2_in1, w2_in2, cross_parts, grad_h2_other, info = together(
            send_near(None, w1_highs), swap(w2_out[0], 4), swap(w2_out[1], 8),
            cross_parts, grad_h2_other, info,
        )
        w1_own, *w1_out = far_ready(w1_lows, w1_came)
    (
        grad_section1, grad_z1, self_dq, self_dk, self_dv, grad_h1, vectors2, biases_self,
    ) = run_kernel(
        self_backward_kernel,
        [rows_f, rows_d, rows_h, rows_h, rows_h, rows_d,
         array_of((3, D), jnp.float32), array_of((2, head_cols), jnp.float32)],
        info, section1, grad_section2, grad_h2, grad_h2_other, params,
        self_q, self_k, self_v, self_mixed_t, self_lse,
        scratch=[scratch_h, scratch_t, scratch_t, scratch_t, scratch_s],
        weights=[(self_a, both), (self_b, both)],
    )
    if fast:
        (cross_came, _), w2_in3, w1_in1, w1_in2, self_dq, grad_h1 = together(
            send_near(cross_parts, None), swap(w2_out[2], 12), swap(w1_out[0], 4),
            swap(w1_out[1], 8), self_dq, grad_h1,
        )
        cross_lows, cross_highs = fold_both(cross_parts, cross_came)
    self_parts = weight_parts(
        ((0, 0, 0, 0, 0), (0, 1, 0, 0, 1), (0, 2, 0, 1, 0), (1, 3, 0, 1, 1)),
        (hidden1, grad_z1),
        (self_dq, self_dk, self_dv, self_mixed),
        2,
        head_cols,
    )
    grad_h1_other = swap_core(grad_h1)
    if fast:
        (_, cross_came), w1_in3, self_parts, grad_h1_other, info = together(
            send_near(None, cross_highs), swap(w1_out[2], 12), self_parts, grad_h1_other, info
        )
        cross_own, *cross_out = far_ready(cross_lows, cross_came)
    input_grad, vector_grad = run_kernel(
        last_kernel,
        [rows_f, array_of(params.shape, jnp.float32)],
        info, tokens, grad_section1, grad_h1, grad_h1_other, params,
        vectors2, vectors3, biases_self, biases_cross, grad_b1,
    )
    enc_other = run_kernel(
        enc_kernel,
        array_of((keys_count, head_cols)),
        info, cross_dk, cross_dv,
        weights=[(cross_a, (1,)), (cross_b, (0,))],
    )
    if fast:
        (self_came, _), cross_ins, vector_grad, enc_other = together(
            send_near(self_parts, None),
            [swap(out, offset) for out, offset in zip(cross_out, FAR[1:])],
            vector_grad, enc_other,
        )
        self_lows, self_highs = fold_both(self_parts, self_came)
        (_, self_came), vector_grad, enc_came = together(
            send_near(None, self_highs), vector_grad, swap_core(enc_other)
        )
        self_own, *self_out = far_ready(self_lows, self_came)
    else:
        enc_came = swap_core(enc_other)
    enc_grad = run_kernel(
        enc_kernel,
        array_of((keys_count, 1, head_cols), jnp.float32),
        info, cross_dk, cross_dv, enc_came,
        weights=[(cross_a, (1,)), (cross_b, (0,))],
    )
    group = array_of((4, D // lax.axis_size("dp"), head_cols), jnp.float32)
    square_row = array_of((1, head_cols), jnp.float32)
    if fast:
        w1_sum, w2_sum, cross_sum, early_squares = run_kernel(
            functools.partial(totals_kernel, 3),
            [group, group, group, square_row],
            w1_own, w1_in1, w1_in2, w1_in3, w2_own, w2_in1, w2_in2, w2_in3, cross_own, *cross_ins,
        )
        self_ins, enc_grad, early_squares = together(
            [swap(out, offset) for out, offset in zip(self_out, FAR[1:])], enc_grad, early_squares
        )
        self_sum, payload = run_kernel(
            functools.partial(totals_kernel, 1),
            [group, array_of((params.shape[0] + 1, D), jnp.float32)],
            self_own, *self_ins, early_squares, vector_grad,
        )
    else:
        self_sum, cross_sum, w1_sum, w2_sum = [
            jnp.concatenate(
                [
                    lax.psum_scatter(
                        part.astype(jnp.float32), "dp", scatter_dimension=1, tiled=True
                    )
                    for part in parts
                ],
                axis=0,
            )
            for parts in (self_parts, cross_parts, w1_parts, w2_parts)
        ]
        square = sum(jnp.sum(total * total) for total in (cross_sum, w1_sum, w2_sum, self_sum))
        payload = jnp.concatenate([vector_grad, jnp.full((1, D), square)], axis=0)
    enc_grad = enc_grad.transpose(1, 0, 2)
    sums = sum_near(sum_far(payload))
    vector_sum = lax.dynamic_slice_in_dim(sums[:-1], device * own_cols, own_cols, 1)
    outs = [
        jax.ShapeDtypeStruct(master.shape, dtype)
        for master in (attn_master, dense_master, vector_params)
        for dtype in (jnp.float32, jnp.float32, jnp.float32, jnp.bfloat16)
    ]
    norm, *updated, bias_gradient = run_kernel(
        finish_kernel,
        [array_of((1, 128), jnp.float32), *outs, array_of((1, own_cols), jnp.float32)],
        decays[None], sums, vector_sum, self_sum, cross_sum, w1_sum, w2_sum,
        attn_master, attn_first, attn_second, dense_master, dense_first, dense_second,
        vector_params, vector_first, vector_second,
    )
    return (layer_out, input_grad, enc_grad, norm[0, 0], *updated, bias_gradient[0])


def solution(mesh):
    return jax.shard_map(
        local,
        mesh=mesh,
        in_specs=(
            P("dp", None),
            P("dp", None, None),
            P("dp"),
            P("dp", None),
            P(None, None, "dp", "mp"),
            P(None, None, "dp", "mp"),
            P(None, None, "dp", "mp"),
            P(None, "dp", "mp"),
            P(None, "dp", "mp"),
            P(None, "dp", "mp"),
            P(None, ("dp", "mp")),
            P(None, ("dp", "mp")),
            P(None, ("dp", "mp")),
            P(),
        ),
        out_specs=(
            P("dp", None),
            P("dp", None),
            P("dp", None, "mp"),
            P(),
            P(None, None, "dp", "mp"),
            P(None, None, "dp", "mp"),
            P(None, None, "dp", "mp"),
            P(None, None, "dp", "mp"),
            P(None, "dp", "mp"),
            P(None, "dp", "mp"),
            P(None, "dp", "mp"),
            P(None, "dp", "mp"),
            P(None, ("dp", "mp")),
            P(None, ("dp", "mp")),
            P(None, ("dp", "mp")),
            P(None, ("dp", "mp")),
            P(("dp", "mp")),
        ),
        check_vma=False,
    )
```

```python
import functools

import jax
import jax.numpy as jnp
from jax import lax
from jax.experimental import pallas as pl
from jax.experimental.pallas import tpu as pltpu
from jax.sharding import PartitionSpec as P

D = 768
HEAD_DIM = 64
FF = 3072
BLOCK = 448
STEP = 3


attn_rate = 0.08
dense_rate = 0.03
vector_rate = 0.3
LOG2E = 1.4426950408889634
FAR = [0, 4, 8, 12]


def dot(left_side, right_side):
    return jnp.dot(left_side, right_side, preferred_element_type=jnp.float32)


def dot_nt(left_side, right_side):
    return lax.dot_general(
        left_side, right_side, (((1,), (1,)), ((), ())), preferred_element_type=jnp.float32
    )


def spans(total, step):
    return [(at, min(step, total - at)) for at in range(0, total, step)]


def unit_norm(values):
    centred = values - jnp.mean(values, axis=-1, keepdims=True)
    inverse = lax.rsqrt(jnp.mean(centred * centred, axis=-1, keepdims=True) + 1e-05)
    return centred * inverse, inverse


def norm_rows(values, gain, shift):
    unit, _ = unit_norm(values)
    return (unit * gain + shift).astype(jnp.bfloat16)


def norm_pull(values, grad, gain):
    unit, inverse = unit_norm(values)
    scaled = grad * gain
    pulled = inverse * (
        scaled
        - jnp.mean(scaled, axis=-1, keepdims=True)
        - unit * jnp.mean(scaled * unit, axis=-1, keepdims=True)
    )
    return (
        pulled,
        jnp.sum(grad * unit, axis=0, keepdims=True),
        jnp.sum(grad, axis=0, keepdims=True),
    )


def head_masks():
    lane = lax.broadcasted_iota(jnp.int32, (1, 2 * HEAD_DIM), 1)
    return [(lane < HEAD_DIM).astype(jnp.bfloat16), (lane >= HEAD_DIM).astype(jnp.bfloat16)]


def row_sum(values):
    return jnp.sum(values.astype(jnp.float32), axis=0, keepdims=True)


HERE, CORE, LENGTH = range(3)


def held_bytes(shape, dtype):
    *lead, rows, cols = (1, 1, *shape)
    count = -(-rows // 16) * 16 * (-(-cols // 128) * 128)
    for size in lead:
        count *= size
    return count * jnp.dtype(dtype).itemsize


def run_kernel(kernel, out_shapes, *operands, scratch=(), weights=()):
    spaces = [
        pl.BlockSpec(memory_space=pltpu.SMEM if operand.dtype == jnp.int32 else pltpu.VMEM)
        for operand in operands
    ]
    held = [array for sources, _ in weights for array, _ in sources]
    single = not isinstance(out_shapes, (list, tuple))
    shapes = [out_shapes] if single else list(out_shapes)
    first_held, first_out = len(operands), len(operands) + len(held)
    buffers = [
        pltpu.VMEM((len(matrices),) + (D, sources[0][0].shape[-1]), jnp.bfloat16)
        for sources, matrices in weights
    ]
    copies_of = [
        sum(1 if offsets is None else 8 for _, offsets in sources) * len(matrices)
        for sources, matrices in weights
    ]
    semaphores = [pltpu.SemaphoreType.DMA((number,)) for number in copies_of]

    def body(*refs):
        refs = list(refs)
        if not weights:
            kernel(*refs)
            return
        info = refs[0]
        tail = len(refs) - 2 * len(weights)
        stacks = iter(refs[first_held:first_out])
        pending = []
        for at, (sources, matrices) in enumerate(weights):
            target, sems = refs[tail + at], refs[tail + len(weights) + at]
            copies = []
            for (_, offsets), stack in zip(sources, stacks):
                for which, matrix in enumerate(matrices):
                    if offsets is None:
                        pieces = [(stack.at[matrix], target.at[which])]
                    else:
                        rows = stack.shape[2]
                        pieces = []
                        for piece in range(8):
                            offset = offsets[piece // 4] ^ FAR[piece % 4]
                            place = pl.multiple_of((info[HERE] ^ offset) * rows, 16)
                            pieces.append(
                                (stack.at[piece, matrix], target.at[which, pl.ds(place, rows), :])
                            )
                    for source, place in pieces:
                        copies.append(pltpu.make_async_copy(source, place, sems.at[len(copies)]))
            for copy in copies:
                copy.start()
            pending.append((target, copies))

        def loaded(at):
            target, copies = pending[at]
            for copy in copies:
                copy.wait()
            return [target.at[which] for which in range(len(weights[at][1]))]

        kernel(loaded, *refs[:first_held], *refs[first_out:tail])

    sizes = [(array.shape, array.dtype) for array in (*operands, *shapes)]
    sizes += [(array.shape, array.dtype) for array in (*scratch, *buffers)]
    needed = sum(held_bytes(shape, dtype) for shape, dtype in sizes)
    outs = [pl.BlockSpec(memory_space=pltpu.VMEM) for _ in shapes]
    results = pl.pallas_call(
        body,
        out_shape=shapes,
        in_specs=spaces + [pl.BlockSpec(memory_space=pl.ANY) for _ in held],
        out_specs=outs,
        scratch_shapes=[*scratch, *buffers, *semaphores],
        compiler_params=pltpu.CompilerParams(vmem_limit_bytes=needed + 8 * 2**20),
    )(*operands, *held)
    return results[0] if single else results


def array_of(shape, dtype=jnp.bfloat16):
    return jax.ShapeDtypeStruct(shape, dtype)


def local_bias(params, row, core, width):
    return params[row : row + 1, pl.ds(pl.multiple_of(core * width, 128), width)]


def cross_keys_kernel(loaded, info, enc, params, keys, values, keys_t, values_t, enc_t):
    bias_v = local_bias(params, 10, info[CORE], keys.shape[1])
    for at, size in spans(enc.shape[0], 256):
        rows = pl.ds(at, size)
        enc_t[:, rows] = enc[rows, :].T
    (wk,), (wv,) = loaded(0), loaded(1)
    for at, size in spans(enc.shape[0], 256):
        rows = pl.ds(at, size)
        block = enc[rows, :]
        key_block = dot(block, wk[...]).astype(jnp.bfloat16)
        value_block = (dot(block, wv[...]) + bias_v).astype(jnp.bfloat16)
        keys[rows, :] = key_block
        values[rows, :] = value_block
        keys_t[:, rows] = key_block.T
        values_t[:, rows] = value_block.T


def self_forward_kernel(
    loaded, info, tokens, params,
    hidden, q, k, v, mixed, mixed_t, lse, part,
    values_t, allowed,
):
    count = tokens.shape[0]
    for at, size in spans(count, 64):
        rows = pl.ds(at, size)
        hidden[rows, :] = norm_rows(
            tokens[rows, :].astype(jnp.float32), params[0:1, :], params[1:2, :]
        )
    bias_q = local_bias(params, 6, info[CORE], q.shape[1])
    bias_v = local_bias(params, 7, info[CORE], q.shape[1])
    wq, wk = loaded(0)
    q[...] = (dot(hidden[...], wq[...]) + bias_q).astype(jnp.bfloat16)
    k[...] = dot(hidden[...], wk[...]).astype(jnp.bfloat16)
    wv, wo = loaded(1)
    v[...] = (dot(hidden[...], wv[...]) + bias_v).astype(jnp.bfloat16)
    values_t[...] = v[...].T
    key_ids = lax.broadcasted_iota(jnp.int32, (count, count), 0)
    query_ids = lax.broadcasted_iota(jnp.int32, (count, count), 1)
    allowed[...] = ((key_ids <= query_ids) & (key_ids < info[LENGTH])).astype(jnp.float32)
    masks = head_masks()

    def pair_step(pair, carry):
        cols = pl.ds(pl.multiple_of(pair * 128, 128), 128)
        for parity in range(2):
            head = pair * 2 + parity
            scores = dot_nt(k[:, cols], q[:, cols] * masks[parity]) * (0.125 * LOG2E)
            scores = jnp.where(allowed[...] > 0.5, scores, -1e30)
            top = jnp.max(scores, axis=0, keepdims=True)
            weights = jnp.exp2(scores - top)
            total = jnp.sum(weights, axis=0, keepdims=True)
            lse[pl.ds(head, 1), :] = top + jnp.log2(total)
            own = pl.ds(pl.multiple_of(head * HEAD_DIM, HEAD_DIM), HEAD_DIM)
            mixed_t[own, :] = (
                dot(values_t[own, :], weights.astype(jnp.bfloat16)) * (1.0 / total)
            ).astype(jnp.bfloat16)
        return carry

    lax.fori_loop(0, q.shape[1] // 128, pair_step, 0)
    mixed[...] = mixed_t[...].T
    part[...] = dot_nt(mixed[...], wo[...]).astype(jnp.bfloat16)


def cross_forward_kernel(
    loaded, info, tokens, own_part, other_part, params, keys, values_t,
    section, hidden, q, mixed, mixed_t, lse, part,
    scores, weights,
):
    count = tokens.shape[0]
    for at, size in spans(count, 64):
        rows = pl.ds(at, size)
        branch = own_part[rows, :].astype(jnp.float32) + other_part[rows, :].astype(jnp.float32)
        block = tokens[rows, :].astype(jnp.float32) + (branch + params[8:9, :])
        section[rows, :] = block
        hidden[rows, :] = norm_rows(block, params[2:3, :], params[3:4, :])
    (wq,), (wo,) = loaded(0), loaded(1)
    bias_q = local_bias(params, 9, info[CORE], q.shape[1])
    q[...] = (dot(hidden[...], wq[...]) + bias_q).astype(jnp.bfloat16)
    masks = head_masks()
    key_spans = spans(keys.shape[0], 256)

    def pair_step(pair, carry):
        cols = pl.ds(pl.multiple_of(pair * 128, 128), 128)
        for parity in range(2):
            head = pair * 2 + parity
            queries = q[:, cols] * masks[parity]
            top = None
            for at, size in key_spans:
                block = dot_nt(keys[pl.ds(at, size), cols], queries) * (0.125 * LOG2E)
                scores[pl.ds(at, size), :] = block
                block_top = jnp.max(block, axis=0, keepdims=True)
                top = block_top if top is None else jnp.maximum(top, block_top)
            total = jnp.zeros_like(top)
            for at, size in key_spans:
                block = jnp.exp2(scores[pl.ds(at, size), :] - top)
                total = total + jnp.sum(block, axis=0, keepdims=True)
                weights[pl.ds(at, size), :] = block.astype(jnp.bfloat16)
            lse[pl.ds(head, 1), :] = top + jnp.log2(total)
            own = pl.ds(pl.multiple_of(head * HEAD_DIM, HEAD_DIM), HEAD_DIM)
            mixed_t[own, :] = (dot(values_t[own, :], weights[...]) * (1.0 / total)).astype(
                jnp.bfloat16
            )
        return carry

    lax.fori_loop(0, q.shape[1] // 128, pair_step, 0)
    mixed[...] = mixed_t[...].T
    part[...] = dot_nt(mixed[...], wo[...]).astype(jnp.bfloat16)


def dense_in_kernel(
    loaded, info, section, own_part, other_part, params, cotangent,
    section_new, hidden, act, slope, grad_low,
):
    count = section.shape[0]
    for at, size in spans(count, 64):
        rows = pl.ds(at, size)
        branch = own_part[rows, :].astype(jnp.float32) + other_part[rows, :].astype(jnp.float32)
        block = section[rows, :] + (branch + params[11:12, :])
        section_new[rows, :] = block
        hidden[rows, :] = norm_rows(block, params[4:5, :], params[5:6, :])
        row_ids = lax.broadcasted_iota(jnp.int32, (size, 1), 0) + at
        valid = (row_ids < info[LENGTH]).astype(jnp.float32)
        grad_low[rows, :] = (cotangent[rows, :].astype(jnp.float32) * valid).astype(jnp.bfloat16)

    held = act.shape[1] // D
    for at in range(4):
        if at % 2 == 0:
            blocks = loaded(at // 2)
        width = blocks[0].shape[1]
        row = 13 + info[CORE] * held + at * width // D
        bias = params[pl.ds(row, 1), at * width % D : at * width % D + width]

        def step(part, carry, at=at, block=blocks[at % 2], bias=bias):
            cols = pl.ds(at * width, width)
            pre_act = dot(hidden[...], block[...]) + bias
            spread = 0.5 + 0.5 * lax.erf(pre_act * (2.0**-0.5))
            act[:, cols] = (pre_act * spread).astype(jnp.bfloat16)
            density = jnp.exp2(pre_act * pre_act * (-0.5 * LOG2E)) * 0.3989422804014327
            slope[:, cols] = (spread + pre_act * density).astype(jnp.bfloat16)
            return carry

        step(0, 0)


def dense_out_kernel(
    loaded, info, act, slope, grad_low,
    grad_pre, part, grad_hidden, grad_bias,
):
    w2 = loaded(0) + loaded(1)
    width = w2[0].shape[1]
    for at, block in enumerate(w2):
        cols = pl.ds(at * width, width)
        grad_act = dot(grad_low[...], block[...]).astype(jnp.bfloat16).astype(jnp.float32)
        grad_block = (grad_act * slope[:, cols].astype(jnp.float32)).astype(jnp.bfloat16)
        grad_pre[:, cols] = grad_block
        grad_bias[:, cols] = row_sum(grad_block)
    for left, blocks, out in (
        (act, w2, part),
        (grad_pre, loaded(2) + loaded(3), grad_hidden),
    ):
        total = None
        for at, block in enumerate(blocks):
            product = dot_nt(left[:, at * width : at * width + width], block[...])
            total = product if total is None else total + product
        out[...] = total.astype(jnp.bfloat16)


def put_relative(product, here, order, keep, send, which, cols):
    half = keep.shape[0]
    rows = keep.shape[2]
    for at, offset in enumerate(order):
        block = product[pl.ds(pl.multiple_of((here ^ offset) * rows, 16), rows), :]
        target = keep if at < half else send
        target[at % half, which, :, cols] = block.astype(jnp.bfloat16)


def weight_kernel(uses, lefts_count, orders, *refs):
    rights_count = 1 + max(right for _, right, _, _, _ in uses)
    lefts, rights = refs[1 : 1 + lefts_count], refs[1 + lefts_count : 1 + lefts_count + rights_count]
    outs = refs[1 + lefts_count + rights_count : -2]
    product, turned = refs[-2:]
    width = product.shape[1]
    me = refs[0][0]
    in_turned = None
    for left, right, first, group, which in uses:
        left_t, right = lefts[left], rights[right]
        if left_t.shape[0] != D:
            if in_turned != left:
                turned[...] = left_t[...].T
                in_turned = left
            left_t = turned

        def step(at, carry, left_t=left_t, right=right, first=first, group=group, which=which):
            cols = pl.ds(pl.multiple_of(at * width, width), width)
            taken = pl.ds(pl.multiple_of(first + at * width, width), width)
            product[...] = dot(left_t[...], right[:, taken])
            if orders is None:
                outs[group][which, :, cols] = product[...].astype(jnp.bfloat16)
            else:
                put_relative(
                    product, me, orders[group], outs[2 * group], outs[2 * group + 1], which, cols
                )
            return carry

        lax.fori_loop(0, outs[0].shape[-1] // width, step, 0)


def attention_pull(
    keys, values, keys_t, q, grad_mixed, grad_mixed_t, mixed_t, lse, allowed, step,
    grad_keys, grad_values, grad_q_t,
):
    masks = head_masks()
    key_spans = spans(keys.shape[0], step)

    def pair_step(pair, carry):
        cols = pl.ds(pl.multiple_of(pair * 128, 128), 128)
        queries = [q[:, cols] * mask for mask in masks]
        grads = [(grad_mixed[:, cols] * 0.125) * mask for mask in masks]
        heads = [pl.ds(pl.multiple_of(pair * 128 + p * 64, 64), 64) for p in range(2)]
        levels, deltas = [], []
        for parity in range(2):
            levels.append(lse[pl.ds(pair * 2 + parity, 1), :])
            product = grad_mixed_t[heads[parity], :].astype(jnp.float32) * mixed_t[
                heads[parity], :
            ].astype(jnp.float32)
            deltas.append(jnp.sum(product, axis=0, keepdims=True) * 0.125)
        sums = [None, None]
        for at, size in key_spans:
            rows = pl.ds(at, size)
            key_sum = value_sum = None
            for parity in range(2):
                scores = dot_nt(keys[rows, cols], queries[parity]) * (0.125 * LOG2E)
                weights = jnp.exp2(scores - levels[parity])
                if allowed is not None:
                    weights = jnp.where(allowed[rows, :] > 0.5, weights, 0.0)
                grad_soft = dot_nt(values[rows, cols], grads[parity])
                grad_raw = (weights * (grad_soft - deltas[parity])).astype(jnp.bfloat16)
                value_part = dot(weights.astype(jnp.bfloat16), grads[parity])
                key_part = dot(grad_raw, queries[parity])
                query_part = dot(keys_t[heads[parity], rows], grad_raw)
                value_sum = value_part if value_sum is None else value_sum + value_part
                key_sum = key_part if key_sum is None else key_sum + key_part
                sums[parity] = query_part if sums[parity] is None else sums[parity] + query_part
            grad_values[rows, cols] = (value_sum * 8.0).astype(jnp.bfloat16)
            grad_keys[rows, cols] = key_sum.astype(jnp.bfloat16)
        for parity in range(2):
            grad_q_t[heads[parity], :] = sums[parity].astype(jnp.bfloat16)
        return carry

    lax.fori_loop(0, q.shape[1] // 128, pair_step, 0)


def cross_backward_kernel(
    loaded, info, section, grad_part, grad_other, out_part, out_other, grad_top, params,
    q, keys, values, keys_t, mixed_t, lse,
    layer_out, grad_section, grad_z, grad_q, grad_keys, grad_values, grad_hidden, vectors, biases,
    grad_mixed, grad_mixed_t, grad_q_t,
):
    count = section.shape[0]
    sums = None
    for at, size in spans(count, 64):
        rows = pl.ds(at, size)
        block = section[rows, :]
        branch = out_part[rows, :].astype(jnp.float32) + out_other[rows, :].astype(jnp.float32)
        layer_out[rows, :] = (block + (branch + params[12:13, :])).astype(jnp.bfloat16)
        grad = grad_part[rows, :].astype(jnp.float32) + grad_other[rows, :].astype(jnp.float32)
        pulled, gain_sum, shift_sum = norm_pull(block, grad, params[4:5, :])
        top = grad_top[rows, :].astype(jnp.float32)
        total = top + pulled
        low = total.astype(jnp.bfloat16)
        grad_section[rows, :] = total
        grad_z[rows, :] = low
        parts = [gain_sum, shift_sum, row_sum(low), jnp.sum(top, axis=0, keepdims=True)]
        sums = parts if sums is None else [old + new for old, new in zip(sums, parts)]
    for at, value in enumerate(sums):
        vectors[at : at + 1, :] = value
    (wo,), (wq,) = loaded(1), loaded(0)
    grad_mixed[...] = dot(grad_z[...], wo[...]).astype(jnp.bfloat16)
    grad_mixed_t[...] = grad_mixed[...].T
    attention_pull(
        keys, values, keys_t, q, grad_mixed, grad_mixed_t, mixed_t, lse, None, 256,
        grad_keys, grad_values, grad_q_t,
    )
    grad_q[...] = grad_q_t[...].T
    grad_hidden[...] = dot_nt(grad_q[...], wq[...]).astype(jnp.bfloat16)
    biases[0:1, :] = row_sum(grad_q[...])
    biases[1:2, :] = row_sum(grad_values[...])


def self_backward_kernel(
    loaded, info, section, grad_section, grad_part, grad_other, params,
    q, k, v, mixed_t, lse,
    grad_new, grad_z, grad_q, grad_keys, grad_values, grad_hidden, vectors, biases,
    grad_mixed, grad_mixed_t, grad_q_t, keys_t, allowed,
):
    count = section.shape[0]
    sums = None
    for at, size in spans(count, 64):
        rows = pl.ds(at, size)
        grad = grad_part[rows, :].astype(jnp.float32) + grad_other[rows, :].astype(jnp.float32)
        pulled, gain_sum, shift_sum = norm_pull(section[rows, :], grad, params[2:3, :])
        total = grad_section[rows, :] + pulled
        low = total.astype(jnp.bfloat16)
        grad_new[rows, :] = total
        grad_z[rows, :] = low
        parts = [gain_sum, shift_sum, row_sum(low)]
        sums = parts if sums is None else [old + new for old, new in zip(sums, parts)]
    for at, value in enumerate(sums):
        vectors[at : at + 1, :] = value
    wv, wo = loaded(1)
    wq, wk = loaded(0)
    grad_mixed[...] = dot(grad_z[...], wo[...]).astype(jnp.bfloat16)
    grad_mixed_t[...] = grad_mixed[...].T
    keys_t[...] = k[...].T
    key_ids = lax.broadcasted_iota(jnp.int32, (count, count), 0)
    query_ids = lax.broadcasted_iota(jnp.int32, (count, count), 1)
    allowed[...] = ((key_ids <= query_ids) & (key_ids < info[LENGTH])).astype(jnp.float32)
    attention_pull(
        k, v, keys_t, q, grad_mixed, grad_mixed_t, mixed_t, lse, allowed, 256,
        grad_keys, grad_values, grad_q_t,
    )
    grad_q[...] = grad_q_t[...].T
    grad_hidden[...] = (
        dot_nt(grad_q[...], wq[...])
        + dot_nt(grad_keys[...], wk[...])
        + dot_nt(grad_values[...], wv[...])
    ).astype(jnp.bfloat16)
    biases[0:1, :] = row_sum(grad_q[...])
    biases[1:2, :] = row_sum(grad_values[...])


def last_kernel(
    info, tokens, grad_section, grad_part, grad_other, params,
    vectors2, vectors3, biases_self, biases_cross, grad_b1,
    input_grad, vectors,
):
    sums = None
    for at, size in spans(tokens.shape[0], 64):
        rows = pl.ds(at, size)
        grad = grad_part[rows, :].astype(jnp.float32) + grad_other[rows, :].astype(jnp.float32)
        pulled, gain_sum, shift_sum = norm_pull(
            tokens[rows, :].astype(jnp.float32), grad, params[0:1, :]
        )
        input_grad[rows, :] = grad_section[rows, :] + pulled
        parts = [gain_sum, shift_sum]
        sums = parts if sums is None else [old + new for old, new in zip(sums, parts)]
    leader = (info[CORE] == 0).astype(jnp.float32)
    vectors[...] = jnp.zeros_like(vectors)
    shared = sums + [vectors2[0:1, :], vectors2[1:2, :], vectors3[0:1, :], vectors3[1:2, :]]
    shared = list(enumerate(shared)) + [(8, vectors2[2:3, :]), (11, vectors3[2:3, :]), (12, vectors3[3:4, :])]
    for at, value in shared:
        vectors[at : at + 1, :] = value * leader
    width = biases_self.shape[1]
    cols = pl.ds(pl.multiple_of(info[CORE] * width, 128), width)
    for at, ref in ((6, biases_self), (9, biases_cross)):
        vectors[at : at + 1, cols] = ref[0:1, :]
        vectors[at + 1 : at + 2, cols] = ref[1:2, :]
    held = grad_b1.shape[1] // D
    for at in range(held):
        vectors[pl.ds(13 + info[CORE] * held + at, 1), :] = grad_b1[:, at * D : at * D + D]


def enc_kernel(loaded, info, grad_keys, grad_values, *refs):
    own, out = refs[:-1], refs[-1]
    width = grad_keys.shape[1]
    place = info[CORE] if own else 1 - info[CORE]
    cols = pl.ds(pl.multiple_of(place * width, 128), width)
    (wk,), (wv,) = loaded(0), loaded(1)
    for at, size in spans(grad_keys.shape[0], 256):
        rows = pl.ds(at, size)
        total = dot_nt(grad_keys[rows, :], wk[cols, :]) + dot_nt(grad_values[rows, :], wv[cols, :])
        if own:
            out[rows, 0, :] = total + own[0][rows, :].astype(jnp.float32)
        else:
            out[rows, :] = total.astype(out.dtype)


def swap(array, bit):
    count = lax.axis_size("dp")
    return lax.ppermute(array, "dp", [(i, i ^ bit) for i in range(count)])


def swap_core(array):
    return lax.ppermute(array, "mp", [(0, 1), (1, 0)])


def together(*values):
    return lax.optimization_barrier(values)


def sum_round(value, bits):
    me = lax.axis_index("dp")
    offsets = [0]
    for bit in bits:
        offsets = offsets + [offset ^ bit for offset in offsets]
    stack = [value] + [swap(value, offset) for offset in offsets[1:]]
    for bit in bits:
        flip = (me & bit) != 0
        pairs = [(stack[at], stack[at + 1]) for at in range(0, len(stack), 2)]
        stack = [jnp.where(flip, b, a) + jnp.where(flip, a, b) for a, b in pairs]
    return stack[0]


def sum_far(value):
    for bits in [(4, 8)] if lax.axis_size("dp") == 16 else high_bits():
        value = sum_round(value, bits)
    return value


def high_bits():
    return [(1 << k,) for k in range(2, lax.axis_size("dp").bit_length() - 1)]


def sum_near(value):
    value = sum_round(value, (1, 2))
    return value + swap_core(value)


def join(stack, came):
    return jnp.concatenate([stack, came], axis=0)


def far_stack(piece):
    return jnp.concatenate([piece] + [swap(piece, offset) for offset in FAR[1:]], axis=0)


def near_steps(first, second):
    parts = None if first is None else halves(first)
    onward = []
    for place, bit in enumerate((1, 2)):
        pieces = []
        if second is not None:
            pieces.append(second[1 - place])
        if first is not None:
            pieces.append(parts[place])
        onward.append(swap(jnp.concatenate(pieces, axis=0), bit))
    cut = 0 if second is None else 8
    nears = None if first is None else [join(part, came[cut:]) for part, came in zip(parts, onward)]
    lasts = None if second is None else onward[::-1]
    return nears, lasts


def near_parts(nears, lasts):
    return [
        [(near, (0, first)), (last, (3 ^ first, 3))]
        for near, last, first in zip(nears, lasts, (1, 2))
    ]


def halves(stack):
    return jnp.split(stack, 2, axis=1)


def weight_parts(uses, lefts, rights, wide, cols):
    count = lax.axis_size("dp")
    direct = count == 16
    orders = []
    for first in (2, 1):
        order = FAR
        for bit in (3 ^ first, first):
            order = order + [offset ^ bit for offset in order]
        orders.append(order)
    if direct:
        outs = [array_of((8, wide, D // 16, cols))] * 4
    else:
        outs = [array_of((wide, D, cols))] * 2
    return run_kernel(
        functools.partial(weight_kernel, uses, len(lefts), orders if direct else None),
        outs,
        lax.axis_index("dp")[None],
        *lefts,
        *rights,
        scratch=[pltpu.VMEM((D, 384), jnp.float32), pltpu.VMEM((D, BLOCK), jnp.bfloat16)],
    )


def send_near(first, second):
    cames = []
    for place, bit in enumerate((1, 2)):
        pieces = []
        if second is not None:
            pieces.append(second[place])
        if first is not None:
            pieces.append(first[3 - 2 * place])
        cames.append(swap(pieces[0] if len(pieces) == 1 else jnp.concatenate(pieces), bit))
    cut = 0 if second is None else 4
    return [came[cut:] for came in cames[::-1]], [came[:cut] for came in cames]


def fold_both(parts, cames):
    keep_a, _, keep_b, _ = parts
    (low_a, high_a), (low_b, high_b) = fold(keep_a, cames[0]), fold(keep_b, cames[1])
    return (low_a, low_b), (high_a, high_b)


def fold(keep, came):
    half = keep.shape[0] // 2
    high = keep[half:].astype(jnp.float32) + came[half:].astype(jnp.float32)
    return (
        keep[:half].astype(jnp.float32) + came[:half].astype(jnp.float32),
        high.astype(jnp.bfloat16),
    )


def far_ready(lows, cames):
    total = jnp.concatenate(
        [low.astype(jnp.float32) + came.astype(jnp.float32) for low, came in zip(lows, cames)],
        axis=1,
    )
    return [total[0]] + [total[at].astype(jnp.bfloat16) for at in range(1, 4)]


def totals_kernel(groups, *refs):
    squares = None
    outs = refs[-(groups + 1) :]
    for at in range(groups):
        own, *cames = refs[4 * at : 4 * at + 4]
        total = own[...]
        for came in cames:
            total = total + came[...].astype(jnp.float32)
        outs[at][...] = total
        square = jnp.sum(total * total, axis=(0, 1), keepdims=True)[0]
        squares = square if squares is None else squares + square
    if len(refs) == 5 * groups + 1:
        outs[groups][...] = squares
        return
    early, vectors = refs[4 * groups : 4 * groups + 2]
    count = vectors.shape[0]
    everything = jnp.sum(squares + early[...], axis=1, keepdims=True)
    outs[groups][0:count, :] = vectors[...]
    outs[groups][count : count + 1, :] = jnp.broadcast_to(everything, (1, vectors.shape[1]))


def finish_kernel(
    decays, sums, vector_sum, self_sum, cross_sum, w1_sum, w2_sum,
    attn, attn_first, attn_second, dense, dense_first, dense_second,
    vector, vector_first, vector_second,
    norm, attn_new, attn_first_new, attn_second_new, attn_copy,
    dense_new, dense_first_new, dense_second_new, dense_copy,
    vector_new, vector_first_new, vector_second_new, vector_copy, bias_gradient,
):
    vectors = sums[0 : sums.shape[0] - 1, :]
    squares = jnp.sum(jnp.sum(vectors * vectors, axis=0, keepdims=True), axis=1, keepdims=True)
    clip_norm = jnp.sqrt(squares + sums[sums.shape[0] - 1 : sums.shape[0], 0:1])
    norm[...] = jnp.broadcast_to(clip_norm, norm.shape)
    factor = jnp.minimum(1.0, 1.0 / (clip_norm + 1e-06))
    first_rate, second_rate = decays[0:1, 0:1], decays[0:1, 1:2]
    first_scale = 1.0 / (1.0 - first_rate * first_rate * first_rate)
    second_scale = 1.0 / (1.0 - second_rate * second_rate * second_rate)

    def update(gradient, weight, first, second, step_rate):
        clipped = gradient * factor
        first_new = first_rate * first + (1.0 - first_rate) * clipped
        second_new = second_rate * second + (1.0 - second_rate) * clipped * clipped
        change = (first_new * first_scale) / (jnp.sqrt(second_new * second_scale) + 1e-08)
        return weight - step_rate * (change + 0.1 * weight), first_new, second_new

    for at, gradient in enumerate((self_sum, cross_sum)):
        for which in range(4):
            new, first, second = update(
                gradient[which],
                attn[at, which],
                attn_first[at, which],
                attn_second[at, which],
                attn_rate,
            )
            attn_new[at, which] = new
            attn_first_new[at, which] = first
            attn_second_new[at, which] = second
            attn_copy[at, which] = new.astype(jnp.bfloat16)
    width = w1_sum.shape[2]
    for at, gradient in enumerate((w1_sum, w2_sum)):
        for which in range(4):
            cols = slice(which * width, which * width + width)
            new, first, second = update(
                gradient[which],
                dense[at, :, cols],
                dense_first[at, :, cols],
                dense_second[at, :, cols],
                dense_rate,
            )
            dense_new[at, :, cols] = new
            dense_first_new[at, :, cols] = first
            dense_second_new[at, :, cols] = second
            dense_copy[at, :, cols] = new.astype(jnp.bfloat16)
    new, first, second = update(
        vector_sum[...], vector[...], vector_first[...], vector_second[...], vector_rate
    )
    vector_new[...] = new
    vector_first_new[...] = first
    vector_second_new[...] = second
    vector_copy[...] = new.astype(jnp.bfloat16)
    bias_gradient[...] = vector_sum[12:13, :] * factor


def local(
    tokens,
    enc_states,
    lengths,
    cotangent,
    attn_master,
    attn_first,
    attn_second,
    dense_master,
    dense_first,
    dense_second,
    vector_params,
    vector_first,
    vector_second,
    decays,
):
    core = lax.axis_index("mp")
    attn_low = attn_master.astype(jnp.bfloat16)
    dense_low = dense_master.astype(jnp.bfloat16)
    blocks = dense_master.shape[2] // attn_master.shape[3]
    dense_low = jnp.stack(jnp.split(dense_low, blocks, axis=2), axis=1)
    device = lax.axis_index("dp") * lax.axis_size("mp") + core
    own_cols = vector_params.shape[1]
    placed = lax.dynamic_update_slice_in_dim(
        jnp.zeros((vector_params.shape[0], D), jnp.float32), vector_params, device * own_cols, 1
    )
    fast = lax.axis_size("dp") == 16
    head_cols = attn_master.shape[3]
    hidden_cols = dense_master.shape[2]
    head_rows = 2 * (head_cols // 128)
    count = tokens.shape[0]
    keys_count = enc_states.shape[1]
    enc = enc_states[0]
    rows_d = array_of((count, D))
    rows_f = array_of((count, D), jnp.float32)
    rows_h = array_of((count, head_cols))
    turned_h = array_of((head_cols, count))
    lse_shape = array_of((head_rows, count), jnp.float32)
    keys_h = array_of((keys_count, head_cols))
    keys_t_h = array_of((head_cols, keys_count))
    scratch_h = pltpu.VMEM((count, head_cols), jnp.bfloat16)
    scratch_t = pltpu.VMEM((head_cols, count), jnp.bfloat16)
    scratch_s = pltpu.VMEM((count, count), jnp.float32)

    here = lax.axis_index("dp")
    info = jnp.stack([here, core, lengths[0]]).astype(jnp.int32)
    if fast:
        low_self, low_cross = attn_low[0][None], attn_low[1][None]
        low_w1, low_w2 = dense_low[0][None], dense_low[1][None]
        vector_low = placed + swap(placed, 1)
        vector_low = vector_low + swap(vector_low, 2)
        self_far, vector_low = together(far_stack(low_self), vector_low + swap_core(vector_low))
        (self_near, _), params, low_cross = together(
            near_steps(self_far, None), sum_far(vector_low), low_cross
        )
        (_, self_last), cross_far, low_w1, info = together(
            near_steps(None, self_near), far_stack(low_cross), low_w1, info
        )
        self_a, self_b = near_parts(self_near, self_last)
    else:
        params = sum_near(sum_far(placed))
        attn_all = lax.all_gather(attn_low, "dp", axis=2, tiled=True)
        dense_all = lax.all_gather(dense_low, "dp", axis=2, tiled=True)
        (self_a, self_b), (cross_a, cross_b), (w1_a, w1_b), (w2_a, w2_b) = [
            [[(whole[:2], None)], [(whole[2:], None)]] for whole in (*attn_all, *dense_all)
        ]
    both = (0, 1)
    hidden1, self_q, self_k, self_v, self_mixed, self_mixed_t, self_lse, self_part = run_kernel(
        self_forward_kernel,
        [rows_d, rows_h, rows_h, rows_h, rows_h, turned_h, lse_shape, rows_d],
        info, tokens, params,
        scratch=[scratch_t, scratch_s],
        weights=[(self_a, both), (self_b, both)],
    )
    if fast:
        (cross_near, _), self_part = together(near_steps(cross_far, None), self_part)
    self_other = swap_core(self_part)
    if fast:
        (_, cross_last), w1_far, self_other, info, low_w2 = together(
            near_steps(None, cross_near), far_stack(low_w1), self_other, info, low_w2
        )
        cross_a, cross_b = near_parts(cross_near, cross_last)
    cross_k, cross_v, cross_k_t, cross_v_t, enc_t = run_kernel(
        cross_keys_kernel,
        [keys_h, keys_h, keys_t_h, keys_t_h, array_of((D, keys_count))],
        info, enc, params,
        weights=[(cross_a, (1,)), (cross_b, (0,))],
    )
    if fast:
        (w1_near, _), w2_far, cross_k, info = together(
            near_steps(w1_far, None), far_stack(low_w2), cross_k, info
        )
    section1, hidden2, cross_q, cross_mixed, cross_mixed_t, cross_lse, cross_part = run_kernel(
        cross_forward_kernel,
        [rows_f, rows_d, rows_h, rows_h, turned_h, lse_shape, rows_d],
        info, tokens, self_part, self_other, params, cross_k, cross_v_t,
        scratch=[
            pltpu.VMEM((keys_count, count), jnp.float32),
            pltpu.VMEM((keys_count, count), jnp.bfloat16),
        ],
        weights=[(cross_a, (0,)), (cross_b, (1,))],
    )
    if fast:
        (w2_near, w1_last), cross_part, info = together(
            near_steps(w2_far, w1_near), cross_part, info
        )
        w1_a, w1_b = near_parts(w1_near, w1_last)
    hidden_rows = array_of((count, hidden_cols))
    section2, hidden3, act, slope, grad_low = run_kernel(
        dense_in_kernel,
        [rows_f, rows_d, hidden_rows, hidden_rows, rows_d],
        info, section1, cross_part, swap_core(cross_part), params, cotangent,
        weights=[(w1_a, both), (w1_b, both)],
    )
    dense_uses = tuple((0, 0, at * head_cols, at // 2, at % 2) for at in range(4))
    w2_parts = weight_parts(dense_uses, (grad_low,), (act,), 2, head_cols)
    if fast:
        (_, w2_last), w2_parts, slope, info = together(
            near_steps(None, w2_near), w2_parts, slope, info
        )
        w2_a, w2_b = near_parts(w2_near, w2_last)
    grad_pre, out_part, grad_h3, grad_b1 = run_kernel(
        dense_out_kernel,
        [hidden_rows, rows_d, rows_d, array_of((1, hidden_cols), jnp.float32)],
        info, act, slope, grad_low,
        weights=[(w2_a, both), (w2_b, both), (w1_a, both), (w1_b, both)],
    )
    w1_parts = weight_parts(dense_uses, (hidden3,), (grad_pre,), 2, head_cols)
    if fast:
        (w2_came, _), w1_parts, grad_h3, out_part = together(
            send_near(w2_parts, None), w1_parts, grad_h3, out_part
        )
        w2_lows, w2_highs = fold_both(w2_parts, w2_came)
    grad_h3_other, out_other = swap_core(grad_h3), swap_core(out_part)
    (
        layer_out, grad_section2, grad_z2, cross_dq, cross_dk, cross_dv, grad_h2, vectors3, biases_cross,
    ) = run_kernel(
        cross_backward_kernel,
        [rows_d, rows_f, rows_d, rows_h, keys_h, keys_h, rows_d,
         array_of((4, D), jnp.float32), array_of((2, head_cols), jnp.float32)],
        info, section2, grad_h3, grad_h3_other, out_part, out_other, grad_low, params,
        cross_q, cross_k, cross_v, cross_k_t, cross_mixed_t, cross_lse,
        scratch=[scratch_h, scratch_t, scratch_t],
        weights=[(cross_a, (0,)), (cross_b, (1,))],
    )
    if fast:
        (w1_came, w2_came), cross_dq, cross_dk, grad_h2 = together(
            send_near(w1_parts, w2_highs), cross_dq, cross_dk, grad_h2
        )
        w2_own, *w2_out = far_ready(w2_lows, w2_came)
        w1_lows, w1_highs = fold_both(w1_parts, w1_came)
    cross_parts = weight_parts(
        ((0, 0, 0, 0, 0), (1, 1, 0, 0, 1), (1, 2, 0, 1, 0), (2, 3, 0, 1, 1)),
        (hidden2, enc_t, grad_z2),
        (cross_dq, cross_dk, cross_dv, cross_mixed),
        2,
        head_cols,
    )
    grad_h2_other = swap_core(grad_h2)
    if fast:
        (_, w1_came), w2_in1, w2_in2, cross_parts, grad_h2_other, info = together(
            send_near(None, w1_highs), swap(w2_out[0], 4), swap(w2_out[1], 8),
            cross_parts, grad_h2_other, info,
        )
        w1_own, *w1_out = far_ready(w1_lows, w1_came)
    (
        grad_section1, grad_z1, self_dq, self_dk, self_dv, grad_h1, vectors2, biases_self,
    ) = run_kernel(
        self_backward_kernel,
        [rows_f, rows_d, rows_h, rows_h, rows_h, rows_d,
         array_of((3, D), jnp.float32), array_of((2, head_cols), jnp.float32)],
        info, section1, grad_section2, grad_h2, grad_h2_other, params,
        self_q, self_k, self_v, self_mixed_t, self_lse,
        scratch=[scratch_h, scratch_t, scratch_t, scratch_t, scratch_s],
        weights=[(self_a, both), (self_b, both)],
    )
    if fast:
        (cross_came, _), w2_in3, w1_in1, w1_in2, self_dq, grad_h1 = together(
            send_near(cross_parts, None), swap(w2_out[2], 12), swap(w1_out[0], 4),
            swap(w1_out[1], 8), self_dq, grad_h1,
        )
        cross_lows, cross_highs = fold_both(cross_parts, cross_came)
    self_parts = weight_parts(
        ((0, 0, 0, 0, 0), (0, 1, 0, 0, 1), (0, 2, 0, 1, 0), (1, 3, 0, 1, 1)),
        (hidden1, grad_z1),
        (self_dq, self_dk, self_dv, self_mixed),
        2,
        head_cols,
    )
    grad_h1_other = swap_core(grad_h1)
    if fast:
        (_, cross_came), w1_in3, self_parts, grad_h1_other, info = together(
            send_near(None, cross_highs), swap(w1_out[2], 12), self_parts, grad_h1_other, info
        )
        cross_own, *cross_out = far_ready(cross_lows, cross_came)
    input_grad, vector_grad = run_kernel(
        last_kernel,
        [rows_f, array_of(params.shape, jnp.float32)],
        info, tokens, grad_section1, grad_h1, grad_h1_other, params,
        vectors2, vectors3, biases_self, biases_cross, grad_b1,
    )
    enc_other = run_kernel(
        enc_kernel,
        array_of((keys_count, head_cols)),
        info, cross_dk, cross_dv,
        weights=[(cross_a, (1,)), (cross_b, (0,))],
    )
    if fast:
        (self_came, _), cross_ins, vector_grad, enc_other = together(
            send_near(self_parts, None),
            [swap(out, offset) for out, offset in zip(cross_out, FAR[1:])],
            vector_grad, enc_other,
        )
        self_lows, self_highs = fold_both(self_parts, self_came)
        (_, self_came), vector_grad, enc_came = together(
            send_near(None, self_highs), vector_grad, swap_core(enc_other)
        )
        self_own, *self_out = far_ready(self_lows, self_came)
    else:
        enc_came = swap_core(enc_other)
    enc_grad = run_kernel(
        enc_kernel,
        array_of((keys_count, 1, head_cols), jnp.float32),
        info, cross_dk, cross_dv, enc_came,
        weights=[(cross_a, (1,)), (cross_b, (0,))],
    )
    group = array_of((4, D // lax.axis_size("dp"), head_cols), jnp.float32)
    square_row = array_of((1, head_cols), jnp.float32)
    if fast:
        w1_sum, w2_sum, cross_sum, early_squares = run_kernel(
            functools.partial(totals_kernel, 3),
            [group, group, group, square_row],
            w1_own, w1_in1, w1_in2, w1_in3, w2_own, w2_in1, w2_in2, w2_in3, cross_own, *cross_ins,
        )
        self_ins, enc_grad, early_squares = together(
            [swap(out, offset) for out, offset in zip(self_out, FAR[1:])], enc_grad, early_squares
        )
        self_sum, payload = run_kernel(
            functools.partial(totals_kernel, 1),
            [group, array_of((params.shape[0] + 1, D), jnp.float32)],
            self_own, *self_ins, early_squares, vector_grad,
        )
    else:
        self_sum, cross_sum, w1_sum, w2_sum = [
            jnp.concatenate(
                [
                    lax.psum_scatter(
                        part.astype(jnp.float32), "dp", scatter_dimension=1, tiled=True
                    )
                    for part in parts
                ],
                axis=0,
            )
            for parts in (self_parts, cross_parts, w1_parts, w2_parts)
        ]
        square = sum(jnp.sum(total * total) for total in (cross_sum, w1_sum, w2_sum, self_sum))
        payload = jnp.concatenate([vector_grad, jnp.full((1, D), square)], axis=0)
    enc_grad = enc_grad.transpose(1, 0, 2)
    sums = sum_near(sum_far(payload))
    vector_sum = lax.dynamic_slice_in_dim(sums[:-1], device * own_cols, own_cols, 1)
    outs = [
        jax.ShapeDtypeStruct(master.shape, dtype)
        for master in (attn_master, dense_master, vector_params)
        for dtype in (jnp.float32, jnp.float32, jnp.float32, jnp.bfloat16)
    ]
    norm, *updated, bias_gradient = run_kernel(
        finish_kernel,
        [array_of((1, 128), jnp.float32), *outs, array_of((1, own_cols), jnp.float32)],
        decays[None], sums, vector_sum, self_sum, cross_sum, w1_sum, w2_sum,
        attn_master, attn_first, attn_second, dense_master, dense_first, dense_second,
        vector_params, vector_first, vector_second,
    )
    return (layer_out, input_grad, enc_grad, norm[0, 0], *updated, bias_gradient[0])


def solution(mesh):
    return jax.shard_map(
        local,
        mesh=mesh,
        in_specs=(
            P("dp", None),
            P("dp", None, None),
            P("dp"),
            P("dp", None),
            P(None, None, "dp", "mp"),
            P(None, None, "dp", "mp"),
            P(None, None, "dp", "mp"),
            P(None, "dp", "mp"),
            P(None, "dp", "mp"),
            P(None, "dp", "mp"),
            P(None, ("dp", "mp")),
            P(None, ("dp", "mp")),
            P(None, ("dp", "mp")),
            P(),
        ),
        out_specs=(
            P("dp", None),
            P("dp", None),
            P("dp", None, "mp"),
            P(),
            P(None, None, "dp", "mp"),
            P(None, None, "dp", "mp"),
            P(None, None, "dp", "mp"),
            P(None, None, "dp", "mp"),
            P(None, "dp", "mp"),
            P(None, "dp", "mp"),
            P(None, "dp", "mp"),
            P(None, "dp", "mp"),
            P(None, ("dp", "mp")),
            P(None, ("dp", "mp")),
            P(None, ("dp", "mp")),
            P(None, ("dp", "mp")),
            P(("dp", "mp")),
        ),
        check_vma=False,
    )
```

```python
import functools

import jax
import jax.numpy as jnp
from jax import lax
from jax.experimental import pallas as pl
from jax.experimental.pallas import tpu as pltpu
from jax.sharding import PartitionSpec as P

D = 768
HEAD_DIM = 64
FF = 3072
BLOCK = 448
STEP = 3


attn_rate = 0.08
dense_rate = 0.03
vector_rate = 0.3
LOG2E = 1.4426950408889634
FAR = [0, 4, 8, 12]


def dot(left_side, right_side):
    return jnp.dot(left_side, right_side, preferred_element_type=jnp.float32)


def dot_nt(left_side, right_side):
    return lax.dot_general(
        left_side, right_side, (((1,), (1,)), ((), ())), preferred_element_type=jnp.float32
    )


def spans(total, step):
    return [(at, min(step, total - at)) for at in range(0, total, step)]


def unit_norm(values):
    centred = values - jnp.mean(values, axis=-1, keepdims=True)
    inverse = lax.rsqrt(jnp.mean(centred * centred, axis=-1, keepdims=True) + 1e-05)
    return centred * inverse, inverse


def norm_rows(values, gain, shift):
    unit, _ = unit_norm(values)
    return (unit * gain + shift).astype(jnp.bfloat16)


def norm_pull(values, grad, gain):
    unit, inverse = unit_norm(values)
    scaled = grad * gain
    pulled = inverse * (
        scaled
        - jnp.mean(scaled, axis=-1, keepdims=True)
        - unit * jnp.mean(scaled * unit, axis=-1, keepdims=True)
    )
    return (
        pulled,
        jnp.sum(grad * unit, axis=0, keepdims=True),
        jnp.sum(grad, axis=0, keepdims=True),
    )


def head_masks():
    lane = lax.broadcasted_iota(jnp.int32, (1, 2 * HEAD_DIM), 1)
    return [(lane < HEAD_DIM).astype(jnp.bfloat16), (lane >= HEAD_DIM).astype(jnp.bfloat16)]


def row_sum(values):
    return jnp.sum(values.astype(jnp.float32), axis=0, keepdims=True)


HERE, CORE, LENGTH = range(3)


def held_bytes(shape, dtype):
    *lead, rows, cols = (1, 1, *shape)
    count = -(-rows // 16) * 16 * (-(-cols // 128) * 128)
    for size in lead:
        count *= size
    return count * jnp.dtype(dtype).itemsize


def run_kernel(kernel, out_shapes, *operands, scratch=(), weights=()):
    spaces = [
        pl.BlockSpec(memory_space=pltpu.SMEM if operand.dtype == jnp.int32 else pltpu.VMEM)
        for operand in operands
    ]
    held = [array for sources, _ in weights for array, _ in sources]
    single = not isinstance(out_shapes, (list, tuple))
    shapes = [out_shapes] if single else list(out_shapes)
    first_held, first_out = len(operands), len(operands) + len(held)
    buffers = [
        pltpu.VMEM((len(matrices),) + (D, sources[0][0].shape[-1]), jnp.bfloat16)
        for sources, matrices in weights
    ]

    def body(*refs):
        if not weights:
            kernel(*refs)
            return
        info = refs[0]
        tail = len(refs) - len(weights)
        stacks = iter(refs[first_held:first_out])
        groups = [[(next(stacks), offsets) for _, offsets in sources] for sources, _ in weights]

        def loaded(at):
            target = refs[tail + at]
            for stack, offsets in groups[at]:
                for which, matrix in enumerate(weights[at][1]):
                    if offsets is None:
                        target[which] = stack[matrix]
                        continue
                    rows = stack.shape[2]
                    for piece in range(8):
                        offset = offsets[piece // 4] ^ FAR[piece % 4]
                        place = pl.multiple_of((info[HERE] ^ offset) * rows, 16)
                        target[which, pl.ds(place, rows), :] = stack[piece, matrix]
            return [target.at[which] for which in range(len(weights[at][1]))]

        kernel(loaded, *refs[:first_held], *refs[first_out:tail])

    sizes = [(array.shape, array.dtype) for array in (*operands, *held, *shapes)]
    sizes += [(array.shape, array.dtype) for array in (*scratch, *buffers)]
    needed = sum(held_bytes(shape, dtype) for shape, dtype in sizes)
    outs = [pl.BlockSpec(memory_space=pltpu.VMEM) for _ in shapes]
    results = pl.pallas_call(
        body,
        out_shape=shapes,
        in_specs=spaces + [pl.BlockSpec(memory_space=pltpu.VMEM) for _ in held],
        out_specs=outs,
        scratch_shapes=[*scratch, *buffers],
        compiler_params=pltpu.CompilerParams(vmem_limit_bytes=needed + 8 * 2**20),
    )(*operands, *held)
    return results[0] if single else results


def array_of(shape, dtype=jnp.bfloat16):
    return jax.ShapeDtypeStruct(shape, dtype)


def local_bias(params, row, core, width):
    return params[row : row + 1, pl.ds(pl.multiple_of(core * width, 128), width)]


def cross_keys_kernel(loaded, info, enc, params, keys, values, keys_t, values_t, enc_t):
    bias_v = local_bias(params, 10, info[CORE], keys.shape[1])
    for at, size in spans(enc.shape[0], 256):
        rows = pl.ds(at, size)
        enc_t[:, rows] = enc[rows, :].T
    (wk,), (wv,) = loaded(0), loaded(1)
    for at, size in spans(enc.shape[0], 256):
        rows = pl.ds(at, size)
        block = enc[rows, :]
        key_block = dot(block, wk[...]).astype(jnp.bfloat16)
        value_block = (dot(block, wv[...]) + bias_v).astype(jnp.bfloat16)
        keys[rows, :] = key_block
        values[rows, :] = value_block
        keys_t[:, rows] = key_block.T
        values_t[:, rows] = value_block.T


def self_forward_kernel(
    loaded, info, tokens, params,
    hidden, q, k, v, mixed, mixed_t, lse, part,
    values_t, allowed,
):
    count = tokens.shape[0]
    for at, size in spans(count, 64):
        rows = pl.ds(at, size)
        hidden[rows, :] = norm_rows(
            tokens[rows, :].astype(jnp.float32), params[0:1, :], params[1:2, :]
        )
    bias_q = local_bias(params, 6, info[CORE], q.shape[1])
    bias_v = local_bias(params, 7, info[CORE], q.shape[1])
    wq, wk = loaded(0)
    q[...] = (dot(hidden[...], wq[...]) + bias_q).astype(jnp.bfloat16)
    k[...] = dot(hidden[...], wk[...]).astype(jnp.bfloat16)
    wv, wo = loaded(1)
    v[...] = (dot(hidden[...], wv[...]) + bias_v).astype(jnp.bfloat16)
    values_t[...] = v[...].T
    key_ids = lax.broadcasted_iota(jnp.int32, (count, count), 0)
    query_ids = lax.broadcasted_iota(jnp.int32, (count, count), 1)
    allowed[...] = ((key_ids <= query_ids) & (key_ids < info[LENGTH])).astype(jnp.float32)
    masks = head_masks()

    def pair_step(pair, carry):
        cols = pl.ds(pl.multiple_of(pair * 128, 128), 128)
        for parity in range(2):
            head = pair * 2 + parity
            scores = dot_nt(k[:, cols], q[:, cols] * masks[parity]) * (0.125 * LOG2E)
            scores = jnp.where(allowed[...] > 0.5, scores, -1e30)
            top = jnp.max(scores, axis=0, keepdims=True)
            weights = jnp.exp2(scores - top)
            total = jnp.sum(weights, axis=0, keepdims=True)
            lse[pl.ds(head, 1), :] = top + jnp.log2(total)
            own = pl.ds(pl.multiple_of(head * HEAD_DIM, HEAD_DIM), HEAD_DIM)
            mixed_t[own, :] = (
                dot(values_t[own, :], weights.astype(jnp.bfloat16)) * (1.0 / total)
            ).astype(jnp.bfloat16)
        return carry

    lax.fori_loop(0, q.shape[1] // 128, pair_step, 0)
    mixed[...] = mixed_t[...].T
    part[...] = dot_nt(mixed[...], wo[...]).astype(jnp.bfloat16)


def cross_forward_kernel(
    loaded, info, tokens, own_part, other_part, params, keys, values_t,
    section, hidden, q, mixed, mixed_t, lse, part,
    scores, weights,
):
    count = tokens.shape[0]
    for at, size in spans(count, 64):
        rows = pl.ds(at, size)
        branch = own_part[rows, :].astype(jnp.float32) + other_part[rows, :].astype(jnp.float32)
        block = tokens[rows, :].astype(jnp.float32) + (branch + params[8:9, :])
        section[rows, :] = block
        hidden[rows, :] = norm_rows(block, params[2:3, :], params[3:4, :])
    (wq,), (wo,) = loaded(0), loaded(1)
    bias_q = local_bias(params, 9, info[CORE], q.shape[1])
    q[...] = (dot(hidden[...], wq[...]) + bias_q).astype(jnp.bfloat16)
    masks = head_masks()
    key_spans = spans(keys.shape[0], 256)

    def pair_step(pair, carry):
        cols = pl.ds(pl.multiple_of(pair * 128, 128), 128)
        for parity in range(2):
            head = pair * 2 + parity
            queries = q[:, cols] * masks[parity]
            top = None
            for at, size in key_spans:
                block = dot_nt(keys[pl.ds(at, size), cols], queries) * (0.125 * LOG2E)
                scores[pl.ds(at, size), :] = block
                block_top = jnp.max(block, axis=0, keepdims=True)
                top = block_top if top is None else jnp.maximum(top, block_top)
            total = jnp.zeros_like(top)
            for at, size in key_spans:
                block = jnp.exp2(scores[pl.ds(at, size), :] - top)
                total = total + jnp.sum(block, axis=0, keepdims=True)
                weights[pl.ds(at, size), :] = block.astype(jnp.bfloat16)
            lse[pl.ds(head, 1), :] = top + jnp.log2(total)
            own = pl.ds(pl.multiple_of(head * HEAD_DIM, HEAD_DIM), HEAD_DIM)
            mixed_t[own, :] = (dot(values_t[own, :], weights[...]) * (1.0 / total)).astype(
                jnp.bfloat16
            )
        return carry

    lax.fori_loop(0, q.shape[1] // 128, pair_step, 0)
    mixed[...] = mixed_t[...].T
    part[...] = dot_nt(mixed[...], wo[...]).astype(jnp.bfloat16)


def dense_in_kernel(
    loaded, info, section, own_part, other_part, params, cotangent,
    section_new, hidden, act, slope, grad_low,
):
    count = section.shape[0]
    for at, size in spans(count, 64):
        rows = pl.ds(at, size)
        branch = own_part[rows, :].astype(jnp.float32) + other_part[rows, :].astype(jnp.float32)
        block = section[rows, :] + (branch + params[11:12, :])
        section_new[rows, :] = block
        hidden[rows, :] = norm_rows(block, params[4:5, :], params[5:6, :])
        row_ids = lax.broadcasted_iota(jnp.int32, (size, 1), 0) + at
        valid = (row_ids < info[LENGTH]).astype(jnp.float32)
        grad_low[rows, :] = (cotangent[rows, :].astype(jnp.float32) * valid).astype(jnp.bfloat16)

    held = act.shape[1] // D
    for at in range(4):
        if at % 2 == 0:
            blocks = loaded(at // 2)
        width = blocks[0].shape[1]
        row = 13 + info[CORE] * held + at * width // D
        bias = params[pl.ds(row, 1), at * width % D : at * width % D + width]

        def step(part, carry, at=at, block=blocks[at % 2], bias=bias):
            cols = pl.ds(at * width, width)
            pre_act = dot(hidden[...], block[...]) + bias
            spread = 0.5 + 0.5 * lax.erf(pre_act * (2.0**-0.5))
            act[:, cols] = (pre_act * spread).astype(jnp.bfloat16)
            density = jnp.exp2(pre_act * pre_act * (-0.5 * LOG2E)) * 0.3989422804014327
            slope[:, cols] = (spread + pre_act * density).astype(jnp.bfloat16)
            return carry

        step(0, 0)


def dense_out_kernel(
    loaded, info, act, slope, grad_low,
    grad_pre, part, grad_hidden, grad_bias,
):
    w2 = loaded(0) + loaded(1)
    width = w2[0].shape[1]
    for at, block in enumerate(w2):
        cols = pl.ds(at * width, width)
        grad_act = dot(grad_low[...], block[...]).astype(jnp.bfloat16).astype(jnp.float32)
        grad_block = (grad_act * slope[:, cols].astype(jnp.float32)).astype(jnp.bfloat16)
        grad_pre[:, cols] = grad_block
        grad_bias[:, cols] = row_sum(grad_block)
    for left, blocks, out in (
        (act, w2, part),
        (grad_pre, loaded(2) + loaded(3), grad_hidden),
    ):
        total = None
        for at, block in enumerate(blocks):
            product = dot_nt(left[:, at * width : at * width + width], block[...])
            total = product if total is None else total + product
        out[...] = total.astype(jnp.bfloat16)


def put_relative(product, here, order, keep, send, which, cols):
    half = keep.shape[0]
    rows = keep.shape[2]
    for at, offset in enumerate(order):
        block = product[pl.ds(pl.multiple_of((here ^ offset) * rows, 16), rows), :]
        target = keep if at < half else send
        target[at % half, which, :, cols] = block.astype(jnp.bfloat16)


def weight_kernel(uses, lefts_count, orders, *refs):
    rights_count = 1 + max(right for _, right, _, _, _ in uses)
    lefts, rights = refs[1 : 1 + lefts_count], refs[1 + lefts_count : 1 + lefts_count + rights_count]
    outs = refs[1 + lefts_count + rights_count : -2]
    product, turned = refs[-2:]
    width = product.shape[1]
    me = refs[0][0]
    in_turned = None
    for left, right, first, group, which in uses:
        left_t, right = lefts[left], rights[right]
        if left_t.shape[0] != D:
            if in_turned != left:
                turned[...] = left_t[...].T
                in_turned = left
            left_t = turned

        def step(at, carry, left_t=left_t, right=right, first=first, group=group, which=which):
            cols = pl.ds(pl.multiple_of(at * width, width), width)
            taken = pl.ds(pl.multiple_of(first + at * width, width), width)
            product[...] = dot(left_t[...], right[:, taken])
            if orders is None:
                outs[group][which, :, cols] = product[...].astype(jnp.bfloat16)
            else:
                put_relative(
                    product, me, orders[group], outs[2 * group], outs[2 * group + 1], which, cols
                )
            return carry

        lax.fori_loop(0, outs[0].shape[-1] // width, step, 0)


def attention_pull(
    keys, values, keys_t, q, grad_mixed, grad_mixed_t, mixed_t, lse, allowed, step,
    grad_keys, grad_values, grad_q_t,
):
    masks = head_masks()
    key_spans = spans(keys.shape[0], step)

    def pair_step(pair, carry):
        cols = pl.ds(pl.multiple_of(pair * 128, 128), 128)
        queries = [q[:, cols] * mask for mask in masks]
        grads = [(grad_mixed[:, cols] * 0.125) * mask for mask in masks]
        heads = [pl.ds(pl.multiple_of(pair * 128 + p * 64, 64), 64) for p in range(2)]
        levels, deltas = [], []
        for parity in range(2):
            levels.append(lse[pl.ds(pair * 2 + parity, 1), :])
            product = grad_mixed_t[heads[parity], :].astype(jnp.float32) * mixed_t[
                heads[parity], :
            ].astype(jnp.float32)
            deltas.append(jnp.sum(product, axis=0, keepdims=True) * 0.125)
        sums = [None, None]
        for at, size in key_spans:
            rows = pl.ds(at, size)
            key_sum = value_sum = None
            for parity in range(2):
                scores = dot_nt(keys[rows, cols], queries[parity]) * (0.125 * LOG2E)
                weights = jnp.exp2(scores - levels[parity])
                if allowed is not None:
                    weights = jnp.where(allowed[rows, :] > 0.5, weights, 0.0)
                grad_soft = dot_nt(values[rows, cols], grads[parity])
                grad_raw = (weights * (grad_soft - deltas[parity])).astype(jnp.bfloat16)
                value_part = dot(weights.astype(jnp.bfloat16), grads[parity])
                key_part = dot(grad_raw, queries[parity])
                query_part = dot(keys_t[heads[parity], rows], grad_raw)
                value_sum = value_part if value_sum is None else value_sum + value_part
                key_sum = key_part if key_sum is None else key_sum + key_part
                sums[parity] = query_part if sums[parity] is None else sums[parity] + query_part
            grad_values[rows, cols] = (value_sum * 8.0).astype(jnp.bfloat16)
            grad_keys[rows, cols] = key_sum.astype(jnp.bfloat16)
        for parity in range(2):
            grad_q_t[heads[parity], :] = sums[parity].astype(jnp.bfloat16)
        return carry

    lax.fori_loop(0, q.shape[1] // 128, pair_step, 0)


def cross_backward_kernel(
    loaded, info, section, grad_part, grad_other, out_part, out_other, grad_top, params,
    q, keys, values, keys_t, mixed_t, lse,
    layer_out, grad_section, grad_z, grad_q, grad_keys, grad_values, grad_hidden, vectors, biases,
    grad_mixed, grad_mixed_t, grad_q_t,
):
    count = section.shape[0]
    sums = None
    for at, size in spans(count, 64):
        rows = pl.ds(at, size)
        block = section[rows, :]
        branch = out_part[rows, :].astype(jnp.float32) + out_other[rows, :].astype(jnp.float32)
        layer_out[rows, :] = (block + (branch + params[12:13, :])).astype(jnp.bfloat16)
        grad = grad_part[rows, :].astype(jnp.float32) + grad_other[rows, :].astype(jnp.float32)
        pulled, gain_sum, shift_sum = norm_pull(block, grad, params[4:5, :])
        top = grad_top[rows, :].astype(jnp.float32)
        total = top + pulled
        low = total.astype(jnp.bfloat16)
        grad_section[rows, :] = total
        grad_z[rows, :] = low
        parts = [gain_sum, shift_sum, row_sum(low), jnp.sum(top, axis=0, keepdims=True)]
        sums = parts if sums is None else [old + new for old, new in zip(sums, parts)]
    for at, value in enumerate(sums):
        vectors[at : at + 1, :] = value
    (wo,), (wq,) = loaded(1), loaded(0)
    grad_mixed[...] = dot(grad_z[...], wo[...]).astype(jnp.bfloat16)
    grad_mixed_t[...] = grad_mixed[...].T
    attention_pull(
        keys, values, keys_t, q, grad_mixed, grad_mixed_t, mixed_t, lse, None, 256,
        grad_keys, grad_values, grad_q_t,
    )
    grad_q[...] = grad_q_t[...].T
    grad_hidden[...] = dot_nt(grad_q[...], wq[...]).astype(jnp.bfloat16)
    biases[0:1, :] = row_sum(grad_q[...])
    biases[1:2, :] = row_sum(grad_values[...])


def self_backward_kernel(
    loaded, info, section, grad_section, grad_part, grad_other, params,
    q, k, v, mixed_t, lse,
    grad_new, grad_z, grad_q, grad_keys, grad_values, grad_hidden, vectors, biases,
    grad_mixed, grad_mixed_t, grad_q_t, keys_t, allowed,
):
    count = section.shape[0]
    sums = None
    for at, size in spans(count, 64):
        rows = pl.ds(at, size)
        grad = grad_part[rows, :].astype(jnp.float32) + grad_other[rows, :].astype(jnp.float32)
        pulled, gain_sum, shift_sum = norm_pull(section[rows, :], grad, params[2:3, :])
        total = grad_section[rows, :] + pulled
        low = total.astype(jnp.bfloat16)
        grad_new[rows, :] = total
        grad_z[rows, :] = low
        parts = [gain_sum, shift_sum, row_sum(low)]
        sums = parts if sums is None else [old + new for old, new in zip(sums, parts)]
    for at, value in enumerate(sums):
        vectors[at : at + 1, :] = value
    wv, wo = loaded(1)
    wq, wk = loaded(0)
    grad_mixed[...] = dot(grad_z[...], wo[...]).astype(jnp.bfloat16)
    grad_mixed_t[...] = grad_mixed[...].T
    keys_t[...] = k[...].T
    key_ids = lax.broadcasted_iota(jnp.int32, (count, count), 0)
    query_ids = lax.broadcasted_iota(jnp.int32, (count, count), 1)
    allowed[...] = ((key_ids <= query_ids) & (key_ids < info[LENGTH])).astype(jnp.float32)
    attention_pull(
        k, v, keys_t, q, grad_mixed, grad_mixed_t, mixed_t, lse, allowed, 256,
        grad_keys, grad_values, grad_q_t,
    )
    grad_q[...] = grad_q_t[...].T
    grad_hidden[...] = (
        dot_nt(grad_q[...], wq[...])
        + dot_nt(grad_keys[...], wk[...])
        + dot_nt(grad_values[...], wv[...])
    ).astype(jnp.bfloat16)
    biases[0:1, :] = row_sum(grad_q[...])
    biases[1:2, :] = row_sum(grad_values[...])


def last_kernel(
    info, tokens, grad_section, grad_part, grad_other, params,
    vectors2, vectors3, biases_self, biases_cross, grad_b1,
    input_grad, vectors,
):
    sums = None
    for at, size in spans(tokens.shape[0], 64):
        rows = pl.ds(at, size)
        grad = grad_part[rows, :].astype(jnp.float32) + grad_other[rows, :].astype(jnp.float32)
        pulled, gain_sum, shift_sum = norm_pull(
            tokens[rows, :].astype(jnp.float32), grad, params[0:1, :]
        )
        input_grad[rows, :] = grad_section[rows, :] + pulled
        parts = [gain_sum, shift_sum]
        sums = parts if sums is None else [old + new for old, new in zip(sums, parts)]
    leader = (info[CORE] == 0).astype(jnp.float32)
    vectors[...] = jnp.zeros_like(vectors)
    shared = sums + [vectors2[0:1, :], vectors2[1:2, :], vectors3[0:1, :], vectors3[1:2, :]]
    shared = list(enumerate(shared)) + [(8, vectors2[2:3, :]), (11, vectors3[2:3, :]), (12, vectors3[3:4, :])]
    for at, value in shared:
        vectors[at : at + 1, :] = value * leader
    width = biases_self.shape[1]
    cols = pl.ds(pl.multiple_of(info[CORE] * width, 128), width)
    for at, ref in ((6, biases_self), (9, biases_cross)):
        vectors[at : at + 1, cols] = ref[0:1, :]
        vectors[at + 1 : at + 2, cols] = ref[1:2, :]
    held = grad_b1.shape[1] // D
    for at in range(held):
        vectors[pl.ds(13 + info[CORE] * held + at, 1), :] = grad_b1[:, at * D : at * D + D]


def enc_kernel(loaded, info, grad_keys, grad_values, *refs):
    own, out = refs[:-1], refs[-1]
    width = grad_keys.shape[1]
    place = info[CORE] if own else 1 - info[CORE]
    cols = pl.ds(pl.multiple_of(place * width, 128), width)
    (wk,), (wv,) = loaded(0), loaded(1)
    for at, size in spans(grad_keys.shape[0], 256):
        rows = pl.ds(at, size)
        total = dot_nt(grad_keys[rows, :], wk[cols, :]) + dot_nt(grad_values[rows, :], wv[cols, :])
        if own:
            out[rows, 0, :] = total + own[0][rows, :].astype(jnp.float32)
        else:
            out[rows, :] = total.astype(out.dtype)


def swap(array, bit):
    count = lax.axis_size("dp")
    return lax.ppermute(array, "dp", [(i, i ^ bit) for i in range(count)])


def swap_core(array):
    return lax.ppermute(array, "mp", [(0, 1), (1, 0)])


def together(*values):
    return lax.optimization_barrier(values)


def sum_round(value, bits):
    me = lax.axis_index("dp")
    offsets = [0]
    for bit in bits:
        offsets = offsets + [offset ^ bit for offset in offsets]
    stack = [value] + [swap(value, offset) for offset in offsets[1:]]
    for bit in bits:
        flip = (me & bit) != 0
        pairs = [(stack[at], stack[at + 1]) for at in range(0, len(stack), 2)]
        stack = [jnp.where(flip, b, a) + jnp.where(flip, a, b) for a, b in pairs]
    return stack[0]


def sum_far(value):
    for bits in [(4, 8)] if lax.axis_size("dp") == 16 else high_bits():
        value = sum_round(value, bits)
    return value


def high_bits():
    return [(1 << k,) for k in range(2, lax.axis_size("dp").bit_length() - 1)]


def sum_near(value):
    value = sum_round(value, (1, 2))
    return value + swap_core(value)


def join(stack, came):
    return jnp.concatenate([stack, came], axis=0)


def far_stack(piece):
    return jnp.concatenate([piece] + [swap(piece, offset) for offset in FAR[1:]], axis=0)


def near_steps(first, second):
    parts = None if first is None else halves(first)
    onward = []
    for place, bit in enumerate((1, 2)):
        pieces = []
        if second is not None:
            pieces.append(second[1 - place])
        if first is not None:
            pieces.append(parts[place])
        onward.append(swap(jnp.concatenate(pieces, axis=0), bit))
    cut = 0 if second is None else 8
    nears = None if first is None else [join(part, came[cut:]) for part, came in zip(parts, onward)]
    lasts = None if second is None else onward[::-1]
    return nears, lasts


def near_parts(nears, lasts):
    return [
        [(near, (0, first)), (last, (3 ^ first, 3))]
        for near, last, first in zip(nears, lasts, (1, 2))
    ]


def halves(stack):
    return jnp.split(stack, 2, axis=1)


def weight_parts(uses, lefts, rights, wide, cols):
    count = lax.axis_size("dp")
    direct = count == 16
    orders = []
    for first in (2, 1):
        order = FAR
        for bit in (3 ^ first, first):
            order = order + [offset ^ bit for offset in order]
        orders.append(order)
    if direct:
        outs = [array_of((8, wide, D // 16, cols))] * 4
    else:
        outs = [array_of((wide, D, cols))] * 2
    return run_kernel(
        functools.partial(weight_kernel, uses, len(lefts), orders if direct else None),
        outs,
        lax.axis_index("dp")[None],
        *lefts,
        *rights,
        scratch=[pltpu.VMEM((D, 384), jnp.float32), pltpu.VMEM((D, BLOCK), jnp.bfloat16)],
    )


def send_near(first, second):
    cames = []
    for place, bit in enumerate((1, 2)):
        pieces = []
        if second is not None:
            pieces.append(second[place])
        if first is not None:
            pieces.append(first[3 - 2 * place])
        cames.append(swap(pieces[0] if len(pieces) == 1 else jnp.concatenate(pieces), bit))
    cut = 0 if second is None else 4
    return [came[cut:] for came in cames[::-1]], [came[:cut] for came in cames]


def fold_both(parts, cames):
    keep_a, _, keep_b, _ = parts
    (low_a, high_a), (low_b, high_b) = fold(keep_a, cames[0]), fold(keep_b, cames[1])
    return (low_a, low_b), (high_a, high_b)


def fold(keep, came):
    half = keep.shape[0] // 2
    high = keep[half:].astype(jnp.float32) + came[half:].astype(jnp.float32)
    return (
        keep[:half].astype(jnp.float32) + came[:half].astype(jnp.float32),
        high.astype(jnp.bfloat16),
    )


def far_ready(lows, cames):
    total = jnp.concatenate(
        [low.astype(jnp.float32) + came.astype(jnp.float32) for low, came in zip(lows, cames)],
        axis=1,
    )
    return [total[0]] + [total[at].astype(jnp.bfloat16) for at in range(1, 4)]


def totals_kernel(groups, *refs):
    squares = None
    outs = refs[-(groups + 1) :]
    for at in range(groups):
        own, *cames = refs[4 * at : 4 * at + 4]
        total = own[...]
        for came in cames:
            total = total + came[...].astype(jnp.float32)
        outs[at][...] = total
        square = jnp.sum(total * total, axis=(0, 1), keepdims=True)[0]
        squares = square if squares is None else squares + square
    if len(refs) == 5 * groups + 1:
        outs[groups][...] = squares
        return
    everything = jnp.sum(squares + refs[4 * groups][...], axis=1, keepdims=True)
    outs[groups][...] = jnp.broadcast_to(everything, outs[groups].shape)


def prepare_kernel(decays, attn, attn_first, attn_second, dense, dense_first, dense_second, *outs):
    scales = (None, decays[0:1, 0:1], decays[0:1, 1:2])
    arrays = ((attn, attn_first, attn_second), (dense, dense_first, dense_second))
    for at, (group, rate) in enumerate(zip(arrays, (attn_rate, dense_rate))):
        for which, ref in enumerate(group):
            scale = 1.0 - 0.1 * rate if which == 0 else scales[which]
            outs[3 * at + which][...] = ref[...] * scale


def finish_kernel(
    decays, sums, norm_rows, vector_sum, self_sum, cross_sum, w1_sum, w2_sum,
    attn, attn_first, attn_second, dense, dense_first, dense_second,
    vector, vector_first, vector_second,
    norm, attn_new, attn_first_new, attn_second_new, attn_copy,
    dense_new, dense_first_new, dense_second_new, dense_copy,
    vector_new, vector_first_new, vector_second_new, vector_copy, bias_gradient,
):
    vectors = sums[...]
    squares = jnp.sum(jnp.sum(vectors * vectors, axis=0, keepdims=True), axis=1, keepdims=True)
    clip_norm = jnp.sqrt(squares + norm_rows[0:1, 0:1])
    norm[...] = jnp.broadcast_to(clip_norm, norm.shape)
    factor = jnp.minimum(1.0, 1.0 / (clip_norm + 1e-06))
    first_rate, second_rate = decays[0:1, 0:1], decays[0:1, 1:2]
    first_scale = 1.0 / (1.0 - first_rate * first_rate * first_rate)
    second_scale = 1.0 / (1.0 - second_rate * second_rate * second_rate)
    first_part = (1.0 - first_rate) * factor
    second_part = (1.0 - second_rate) * factor * factor

    def update(gradient, weight, first, second, step_rate):
        first_new = first + first_part * gradient
        second_new = second + second_part * gradient * gradient
        change = (first_new * first_scale) / (jnp.sqrt(second_new * second_scale) + 1e-08)
        return weight - step_rate * change, first_new, second_new

    for at, gradient in enumerate((self_sum, cross_sum)):
        for which in range(4):
            new, first, second = update(
                gradient[which],
                attn[at, which],
                attn_first[at, which],
                attn_second[at, which],
                attn_rate,
            )
            attn_new[at, which] = new
            attn_first_new[at, which] = first
            attn_second_new[at, which] = second
            attn_copy[at, which] = new.astype(jnp.bfloat16)
    width = w1_sum.shape[2]
    for at, gradient in enumerate((w1_sum, w2_sum)):
        for which in range(4):
            cols = slice(which * width, which * width + width)
            new, first, second = update(
                gradient[which],
                dense[at, :, cols],
                dense_first[at, :, cols],
                dense_second[at, :, cols],
                dense_rate,
            )
            dense_new[at, :, cols] = new
            dense_first_new[at, :, cols] = first
            dense_second_new[at, :, cols] = second
            dense_copy[at, :, cols] = new.astype(jnp.bfloat16)
    new, first, second = update(
        vector_sum[...],
        vector[...] * (1.0 - 0.1 * vector_rate),
        vector_first[...] * first_rate,
        vector_second[...] * second_rate,
        vector_rate,
    )
    vector_new[...] = new
    vector_first_new[...] = first
    vector_second_new[...] = second
    vector_copy[...] = new.astype(jnp.bfloat16)
    bias_gradient[...] = vector_sum[12:13, :] * factor


def local(
    tokens,
    enc_states,
    lengths,
    cotangent,
    attn_master,
    attn_first,
    attn_second,
    dense_master,
    dense_first,
    dense_second,
    vector_params,
    vector_first,
    vector_second,
    decays,
):
    core = lax.axis_index("mp")
    attn_low = attn_master.astype(jnp.bfloat16)
    dense_low = dense_master.astype(jnp.bfloat16)
    blocks = dense_master.shape[2] // attn_master.shape[3]
    dense_low = jnp.stack(jnp.split(dense_low, blocks, axis=2), axis=1)
    device = lax.axis_index("dp") * lax.axis_size("mp") + core
    own_cols = vector_params.shape[1]
    placed = lax.dynamic_update_slice_in_dim(
        jnp.zeros((vector_params.shape[0], D), jnp.float32), vector_params, device * own_cols, 1
    )
    fast = lax.axis_size("dp") == 16
    head_cols = attn_master.shape[3]
    hidden_cols = dense_master.shape[2]
    head_rows = 2 * (head_cols // 128)
    count = tokens.shape[0]
    keys_count = enc_states.shape[1]
    enc = enc_states[0]
    rows_d = array_of((count, D))
    rows_f = array_of((count, D), jnp.float32)
    rows_h = array_of((count, head_cols))
    turned_h = array_of((head_cols, count))
    lse_shape = array_of((head_rows, count), jnp.float32)
    keys_h = array_of((keys_count, head_cols))
    keys_t_h = array_of((head_cols, keys_count))
    scratch_h = pltpu.VMEM((count, head_cols), jnp.bfloat16)
    scratch_t = pltpu.VMEM((head_cols, count), jnp.bfloat16)
    scratch_s = pltpu.VMEM((count, count), jnp.float32)

    here = lax.axis_index("dp")
    info = jnp.stack([here, core, lengths[0]]).astype(jnp.int32)
    if fast:
        low_self, low_cross = attn_low[0][None], attn_low[1][None]
        low_w1, low_w2 = dense_low[0][None], dense_low[1][None]
        vector_low = placed + swap(placed, 1)
        vector_low = vector_low + swap(vector_low, 2)
        self_far, vector_low = together(far_stack(low_self), vector_low + swap_core(vector_low))
        (self_near, _), params, low_cross = together(
            near_steps(self_far, None), sum_far(vector_low), low_cross
        )
        (_, self_last), cross_far, low_w1, info = together(
            near_steps(None, self_near), far_stack(low_cross), low_w1, info
        )
        self_a, self_b = near_parts(self_near, self_last)
    else:
        params = sum_near(sum_far(placed))
        attn_all = lax.all_gather(attn_low, "dp", axis=2, tiled=True)
        dense_all = lax.all_gather(dense_low, "dp", axis=2, tiled=True)
        (self_a, self_b), (cross_a, cross_b), (w1_a, w1_b), (w2_a, w2_b) = [
            [[(whole[:2], None)], [(whole[2:], None)]] for whole in (*attn_all, *dense_all)
        ]
    both = (0, 1)
    hidden1, self_q, self_k, self_v, self_mixed, self_mixed_t, self_lse, self_part = run_kernel(
        self_forward_kernel,
        [rows_d, rows_h, rows_h, rows_h, rows_h, turned_h, lse_shape, rows_d],
        info, tokens, params,
        scratch=[scratch_t, scratch_s],
        weights=[(self_a, both), (self_b, both)],
    )
    if fast:
        (cross_near, _), self_part = together(near_steps(cross_far, None), self_part)
    self_other = swap_core(self_part)
    if fast:
        (_, cross_last), w1_far, self_other, info, low_w2 = together(
            near_steps(None, cross_near), far_stack(low_w1), self_other, info, low_w2
        )
        cross_a, cross_b = near_parts(cross_near, cross_last)
    cross_k, cross_v, cross_k_t, cross_v_t, enc_t = run_kernel(
        cross_keys_kernel,
        [keys_h, keys_h, keys_t_h, keys_t_h, array_of((D, keys_count))],
        info, enc, params,
        weights=[(cross_a, (1,)), (cross_b, (0,))],
    )
    if fast:
        (w1_near, _), w2_far, cross_k, info = together(
            near_steps(w1_far, None), far_stack(low_w2), cross_k, info
        )
    section1, hidden2, cross_q, cross_mixed, cross_mixed_t, cross_lse, cross_part = run_kernel(
        cross_forward_kernel,
        [rows_f, rows_d, rows_h, rows_h, turned_h, lse_shape, rows_d],
        info, tokens, self_part, self_other, params, cross_k, cross_v_t,
        scratch=[
            pltpu.VMEM((keys_count, count), jnp.float32),
            pltpu.VMEM((keys_count, count), jnp.bfloat16),
        ],
        weights=[(cross_a, (0,)), (cross_b, (1,))],
    )
    if fast:
        (w2_near, w1_last), cross_part, info = together(
            near_steps(w2_far, w1_near), cross_part, info
        )
        w1_a, w1_b = near_parts(w1_near, w1_last)
    hidden_rows = array_of((count, hidden_cols))
    section2, hidden3, act, slope, grad_low = run_kernel(
        dense_in_kernel,
        [rows_f, rows_d, hidden_rows, hidden_rows, rows_d],
        info, section1, cross_part, swap_core(cross_part), params, cotangent,
        weights=[(w1_a, both), (w1_b, both)],
    )
    dense_uses = tuple((0, 0, at * head_cols, at // 2, at % 2) for at in range(4))
    w2_parts = weight_parts(dense_uses, (grad_low,), (act,), 2, head_cols)
    if fast:
        (_, w2_last), w2_parts, slope, info = together(
            near_steps(None, w2_near), w2_parts, slope, info
        )
        w2_a, w2_b = near_parts(w2_near, w2_last)
    grad_pre, out_part, grad_h3, grad_b1 = run_kernel(
        dense_out_kernel,
        [hidden_rows, rows_d, rows_d, array_of((1, hidden_cols), jnp.float32)],
        info, act, slope, grad_low,
        weights=[(w2_a, both), (w2_b, both), (w1_a, both), (w1_b, both)],
    )
    w1_parts = weight_parts(dense_uses, (hidden3,), (grad_pre,), 2, head_cols)
    if fast:
        (w2_came, _), w1_parts, grad_h3, out_part = together(
            send_near(w2_parts, None), w1_parts, grad_h3, out_part
        )
        w2_lows, w2_highs = fold_both(w2_parts, w2_came)
    grad_h3_other, out_other = swap_core(grad_h3), swap_core(out_part)
    (
        layer_out, grad_section2, grad_z2, cross_dq, cross_dk, cross_dv, grad_h2, vectors3, biases_cross,
    ) = run_kernel(
        cross_backward_kernel,
        [rows_d, rows_f, rows_d, rows_h, keys_h, keys_h, rows_d,
         array_of((4, D), jnp.float32), array_of((2, head_cols), jnp.float32)],
        info, section2, grad_h3, grad_h3_other, out_part, out_other, grad_low, params,
        cross_q, cross_k, cross_v, cross_k_t, cross_mixed_t, cross_lse,
        scratch=[scratch_h, scratch_t, scratch_t],
        weights=[(cross_a, (0,)), (cross_b, (1,))],
    )
    if fast:
        (w1_came, w2_came), cross_dq, cross_dk, grad_h2 = together(
            send_near(w1_parts, w2_highs), cross_dq, cross_dk, grad_h2
        )
        w2_own, *w2_out = far_ready(w2_lows, w2_came)
        w1_lows, w1_highs = fold_both(w1_parts, w1_came)
    cross_parts = weight_parts(
        ((0, 0, 0, 0, 0), (1, 1, 0, 0, 1), (1, 2, 0, 1, 0), (2, 3, 0, 1, 1)),
        (hidden2, enc_t, grad_z2),
        (cross_dq, cross_dk, cross_dv, cross_mixed),
        2,
        head_cols,
    )
    grad_h2_other = swap_core(grad_h2)
    if fast:
        (_, w1_came), w2_in1, w2_in2, cross_parts, grad_h2_other, info = together(
            send_near(None, w1_highs), swap(w2_out[0], 4), swap(w2_out[1], 8),
            cross_parts, grad_h2_other, info,
        )
        w1_own, *w1_out = far_ready(w1_lows, w1_came)
    (
        grad_section1, grad_z1, self_dq, self_dk, self_dv, grad_h1, vectors2, biases_self,
    ) = run_kernel(
        self_backward_kernel,
        [rows_f, rows_d, rows_h, rows_h, rows_h, rows_d,
         array_of((3, D), jnp.float32), array_of((2, head_cols), jnp.float32)],
        info, section1, grad_section2, grad_h2, grad_h2_other, params,
        self_q, self_k, self_v, self_mixed_t, self_lse,
        scratch=[scratch_h, scratch_t, scratch_t, scratch_t, scratch_s],
        weights=[(self_a, both), (self_b, both)],
    )
    if fast:
        (cross_came, _), w2_in3, w1_in1, w1_in2, self_dq, grad_h1 = together(
            send_near(cross_parts, None), swap(w2_out[2], 12), swap(w1_out[0], 4),
            swap(w1_out[1], 8), self_dq, grad_h1,
        )
        cross_lows, cross_highs = fold_both(cross_parts, cross_came)
    self_parts = weight_parts(
        ((0, 0, 0, 0, 0), (0, 1, 0, 0, 1), (0, 2, 0, 1, 0), (1, 3, 0, 1, 1)),
        (hidden1, grad_z1),
        (self_dq, self_dk, self_dv, self_mixed),
        2,
        head_cols,
    )
    grad_h1_other = swap_core(grad_h1)
    if fast:
        (_, cross_came), w1_in3, self_parts, grad_h1_other, info = together(
            send_near(None, cross_highs), swap(w1_out[2], 12), self_parts, grad_h1_other, info
        )
        cross_own, *cross_out = far_ready(cross_lows, cross_came)
    input_grad, vector_grad = run_kernel(
        last_kernel,
        [rows_f, array_of(params.shape, jnp.float32)],
        info, tokens, grad_section1, grad_h1, grad_h1_other, params,
        vectors2, vectors3, biases_self, biases_cross, grad_b1,
    )
    enc_other = run_kernel(
        enc_kernel,
        array_of((keys_count, head_cols)),
        info, cross_dk, cross_dv,
        weights=[(cross_a, (1,)), (cross_b, (0,))],
    )
    if fast:
        (self_came, _), cross_ins, vector_grad, enc_other = together(
            send_near(self_parts, None),
            [swap(out, offset) for out, offset in zip(cross_out, FAR[1:])],
            vector_grad, enc_other,
        )
        self_lows, self_highs = fold_both(self_parts, self_came)
        vector_far = sum_round(sum_round(vector_grad, (4,)), (8,))
        (_, self_came), vector_far, enc_came = together(
            send_near(None, self_highs), vector_far, swap_core(enc_other)
        )
        self_own, *self_out = far_ready(self_lows, self_came)
    else:
        enc_came = swap_core(enc_other)
    enc_grad = run_kernel(
        enc_kernel,
        array_of((keys_count, 1, head_cols), jnp.float32),
        info, cross_dk, cross_dv, enc_came,
        weights=[(cross_a, (1,)), (cross_b, (0,))],
    )
    group = array_of((4, D // lax.axis_size("dp"), head_cols), jnp.float32)
    masters = (attn_master, attn_first, attn_second, dense_master, dense_first, dense_second)
    prepared = run_kernel(
        prepare_kernel,
        [array_of(master.shape, jnp.float32) for master in masters],
        *lax.optimization_barrier((decays[None], enc_came))[:1], *masters,
    )
    square_row = array_of((1, head_cols), jnp.float32)
    if fast:
        w1_sum, w2_sum, cross_sum, early_squares = run_kernel(
            functools.partial(totals_kernel, 3),
            [group, group, group, square_row],
            w1_own, w1_in1, w1_in2, w1_in3, w2_own, w2_in1, w2_in2, w2_in3, cross_own, *cross_ins,
        )
        vector_far, prepared = together(vector_far, prepared)
        vector_near = sum_round(sum_round(vector_far, (1,)), (2,))
        self_ins, sums, enc_grad, early_squares, prepared = together(
            [swap(out, offset) for out, offset in zip(self_out, FAR[1:])],
            vector_near + swap_core(vector_near), enc_grad, early_squares, prepared,
        )
        self_sum, square_all = run_kernel(
            functools.partial(totals_kernel, 1),
            [group, array_of((8, 128), jnp.float32)],
            self_own, *self_ins, early_squares,
        )
    else:
        self_sum, cross_sum, w1_sum, w2_sum = [
            jnp.concatenate(
                [
                    lax.psum_scatter(
                        part.astype(jnp.float32), "dp", scatter_dimension=1, tiled=True
                    )
                    for part in parts
                ],
                axis=0,
            )
            for parts in (self_parts, cross_parts, w1_parts, w2_parts)
        ]
        square = sum(jnp.sum(total * total) for total in (cross_sum, w1_sum, w2_sum, self_sum))
        square_all = jnp.full((8, 128), square)
        sums = sum_near(sum_far(vector_grad))
    enc_grad = enc_grad.transpose(1, 0, 2)
    vector_sum = lax.dynamic_slice_in_dim(sums, device * own_cols, own_cols, 1)
    outs = [
        jax.ShapeDtypeStruct(master.shape, dtype)
        for master in (attn_master, dense_master, vector_params)
        for dtype in (jnp.float32, jnp.float32, jnp.float32, jnp.bfloat16)
    ]
    norm, *updated, bias_gradient = run_kernel(
        finish_kernel,
        [array_of((1, 128), jnp.float32), *outs, array_of((1, own_cols), jnp.float32)],
        decays[None], sums, sum_near(sum_far(square_all)), vector_sum,
        self_sum, cross_sum, w1_sum, w2_sum, *prepared,
        vector_params, vector_first, vector_second,
    )
    return (layer_out, input_grad, enc_grad, norm[0, 0], *updated, bias_gradient[0])


def solution(mesh):
    return jax.shard_map(
        local,
        mesh=mesh,
        in_specs=(
            P("dp", None),
            P("dp", None, None),
            P("dp"),
            P("dp", None),
            P(None, None, "dp", "mp"),
            P(None, None, "dp", "mp"),
            P(None, None, "dp", "mp"),
            P(None, "dp", "mp"),
            P(None, "dp", "mp"),
            P(None, "dp", "mp"),
            P(None, ("dp", "mp")),
            P(None, ("dp", "mp")),
            P(None, ("dp", "mp")),
            P(),
        ),
        out_specs=(
            P("dp", None),
            P("dp", None),
            P("dp", None, "mp"),
            P(),
            P(None, None, "dp", "mp"),
            P(None, None, "dp", "mp"),
            P(None, None, "dp", "mp"),
            P(None, None, "dp", "mp"),
            P(None, "dp", "mp"),
            P(None, "dp", "mp"),
            P(None, "dp", "mp"),
            P(None, "dp", "mp"),
            P(None, ("dp", "mp")),
            P(None, ("dp", "mp")),
            P(None, ("dp", "mp")),
            P(None, ("dp", "mp")),
            P(("dp", "mp")),
        ),
        check_vma=False,
    )
```

```python
import functools

import jax
import jax.numpy as jnp
from jax import lax
from jax.experimental import pallas as pl
from jax.experimental.pallas import tpu as pltpu
from jax.sharding import PartitionSpec as P

D = 768
HEAD_DIM = 64
FF = 3072
BLOCK = 448
STEP = 3


attn_rate = 0.08
dense_rate = 0.03
vector_rate = 0.3
LOG2E = 1.4426950408889634
FAR = [0, 4, 8, 12]


def dot(left_side, right_side):
    return jnp.dot(left_side, right_side, preferred_element_type=jnp.float32)


def dot_nt(left_side, right_side):
    return lax.dot_general(
        left_side, right_side, (((1,), (1,)), ((), ())), preferred_element_type=jnp.float32
    )


def spans(total, step):
    return [(at, min(step, total - at)) for at in range(0, total, step)]


def row_loop(count, step, carry):
    def body(at, carry):
        first = pl.multiple_of(at * 64, 64)
        return step(pl.ds(first, 64), first, carry)

    return lax.fori_loop(0, count // 64, body, carry)


def add_rows(old, new):
    return [a + b for a, b in zip(old, new)]


def zero_rows(number):
    return [jnp.zeros((1, D), jnp.float32)] * number


def unit_norm(values):
    centred = values - jnp.mean(values, axis=-1, keepdims=True)
    inverse = lax.rsqrt(jnp.mean(centred * centred, axis=-1, keepdims=True) + 1e-05)
    return centred * inverse, inverse


def norm_rows(values, gain, shift):
    unit, _ = unit_norm(values)
    return (unit * gain + shift).astype(jnp.bfloat16)


def norm_pull(values, grad, gain):
    unit, inverse = unit_norm(values)
    scaled = grad * gain
    pulled = inverse * (
        scaled
        - jnp.mean(scaled, axis=-1, keepdims=True)
        - unit * jnp.mean(scaled * unit, axis=-1, keepdims=True)
    )
    return (
        pulled,
        jnp.sum(grad * unit, axis=0, keepdims=True),
        jnp.sum(grad, axis=0, keepdims=True),
    )


def head_masks():
    lane = lax.broadcasted_iota(jnp.int32, (1, 2 * HEAD_DIM), 1)
    return [(lane < HEAD_DIM).astype(jnp.bfloat16), (lane >= HEAD_DIM).astype(jnp.bfloat16)]


def row_sum(values):
    return jnp.sum(values.astype(jnp.float32), axis=0, keepdims=True)


HERE, CORE, LENGTH = range(3)


def held_bytes(shape, dtype):
    *lead, rows, cols = (1, 1, *shape)
    count = -(-rows // 16) * 16 * (-(-cols // 128) * 128)
    for size in lead:
        count *= size
    return count * jnp.dtype(dtype).itemsize


def run_kernel(kernel, out_shapes, *operands, scratch=(), weights=(), keep=False):
    spaces = [
        pl.BlockSpec(memory_space=pltpu.SMEM if operand.dtype == jnp.int32 else pltpu.VMEM)
        for operand in operands
    ]
    held = [array for sources, _ in weights for array, _ in sources]
    single = not isinstance(out_shapes, (list, tuple))
    shapes = [out_shapes] if single else list(out_shapes)
    cut = [sources[0][1] is not None for sources, _ in weights]
    joined = [
        array_of((len(matrices), D, sources[0][0].shape[-1]))
        for (sources, matrices), pieces in zip(weights, cut)
        if pieces
    ]
    results_count = len(shapes)
    if keep:
        shapes = shapes + joined
        buffers = []
    else:
        buffers = [pltpu.VMEM(shape.shape, shape.dtype) for shape in joined]
    first_held, first_out = len(operands), len(operands) + len(held)
    first_scratch = first_out + len(shapes)

    def body(*refs):
        if not weights:
            kernel(*refs)
            return
        info = refs[0]
        stacks = iter(refs[first_held:first_out])
        groups = [[(next(stacks), offsets) for _, offsets in sources] for sources, _ in weights]
        if keep:
            targets = refs[first_out + results_count : first_scratch]
            scratch_refs = refs[first_scratch:]
        else:
            targets = refs[len(refs) - len(joined) :]
            scratch_refs = refs[first_scratch : len(refs) - len(joined)]

        def loaded(at):
            matrices = weights[at][1]
            if not cut[at]:
                return [groups[at][0][0].at[matrix] for matrix in matrices]
            target = targets[sum(cut[:at])]
            for stack, offsets in groups[at]:
                for which, matrix in enumerate(matrices):
                    rows = stack.shape[2]
                    for piece in range(8):
                        offset = offsets[piece // 4] ^ FAR[piece % 4]
                        place = pl.multiple_of((info[HERE] ^ offset) * rows, 16)
                        target[which, pl.ds(place, rows), :] = stack[piece, matrix]
            return [target.at[which] for which in range(len(matrices))]

        outs = refs[first_out : first_out + results_count]
        kernel(loaded, *refs[:first_held], *outs, *scratch_refs)

    sizes = [(array.shape, array.dtype) for array in (*operands, *held, *shapes)]
    sizes += [(array.shape, array.dtype) for array in (*scratch, *buffers)]
    needed = sum(held_bytes(shape, dtype) for shape, dtype in sizes)
    results = pl.pallas_call(
        body,
        out_shape=shapes,
        in_specs=spaces + [pl.BlockSpec(memory_space=pltpu.VMEM) for _ in held],
        out_specs=[pl.BlockSpec(memory_space=pltpu.VMEM) for _ in shapes],
        scratch_shapes=[*scratch, *buffers],
        compiler_params=pltpu.CompilerParams(vmem_limit_bytes=needed + 4 * 2**20),
    )(*operands, *held)
    if keep:
        wholes = iter(results[results_count:])
        sources = [[(next(wholes), None)] if pieces else given for pieces, (given, _) in zip(cut, weights)]
        return [*results[:results_count], *sources]
    return results[0] if single else results


def array_of(shape, dtype=jnp.bfloat16):
    return jax.ShapeDtypeStruct(shape, dtype)


def local_bias(params, row, core, width):
    return params[row : row + 1, pl.ds(pl.multiple_of(core * width, 128), width)]


def cross_keys_kernel(loaded, info, enc, params, keys, values, keys_t, values_t, enc_t):
    bias_v = local_bias(params, 10, info[CORE], keys.shape[1])
    for at, size in spans(enc.shape[0], 256):
        rows = pl.ds(at, size)
        enc_t[:, rows] = enc[rows, :].T
    (wk,), (wv,) = loaded(0), loaded(1)
    for at, size in spans(enc.shape[0], 256):
        rows = pl.ds(at, size)
        block = enc[rows, :]
        key_block = dot(block, wk[...]).astype(jnp.bfloat16)
        value_block = (dot(block, wv[...]) + bias_v).astype(jnp.bfloat16)
        keys[rows, :] = key_block
        values[rows, :] = value_block
        keys_t[:, rows] = key_block.T
        values_t[:, rows] = value_block.T


def self_forward_kernel(
    loaded, info, tokens, params,
    hidden, q, k, v, mixed, mixed_t, lse, part,
    values_t, allowed,
):
    count = tokens.shape[0]

    def block_step(rows, at, carry):
        hidden[rows, :] = norm_rows(
            tokens[rows, :].astype(jnp.float32), params[0:1, :], params[1:2, :]
        )
        return carry

    row_loop(count, block_step, 0)
    bias_q = local_bias(params, 6, info[CORE], q.shape[1])
    bias_v = local_bias(params, 7, info[CORE], q.shape[1])
    wq, wk = loaded(0)
    q[...] = (dot(hidden[...], wq[...]) + bias_q).astype(jnp.bfloat16)
    k[...] = dot(hidden[...], wk[...]).astype(jnp.bfloat16)
    wv, wo = loaded(1)
    v[...] = (dot(hidden[...], wv[...]) + bias_v).astype(jnp.bfloat16)
    values_t[...] = v[...].T
    key_ids = lax.broadcasted_iota(jnp.int32, (count, count), 0)
    query_ids = lax.broadcasted_iota(jnp.int32, (count, count), 1)
    allowed[...] = ((key_ids <= query_ids) & (key_ids < info[LENGTH])).astype(jnp.float32)
    masks = head_masks()

    def pair_step(pair, carry):
        cols = pl.ds(pl.multiple_of(pair * 128, 128), 128)
        for parity in range(2):
            head = pair * 2 + parity
            scores = dot_nt(k[:, cols], q[:, cols] * masks[parity]) * (0.125 * LOG2E)
            scores = jnp.where(allowed[...] > 0.5, scores, -1e30)
            top = jnp.max(scores, axis=0, keepdims=True)
            weights = jnp.exp2(scores - top)
            total = jnp.sum(weights, axis=0, keepdims=True)
            lse[pl.ds(head, 1), :] = top + jnp.log2(total)
            own = pl.ds(pl.multiple_of(head * HEAD_DIM, HEAD_DIM), HEAD_DIM)
            mixed_t[own, :] = (
                dot(values_t[own, :], weights.astype(jnp.bfloat16)) * (1.0 / total)
            ).astype(jnp.bfloat16)
        return carry

    lax.fori_loop(0, q.shape[1] // 128, pair_step, 0)
    mixed[...] = mixed_t[...].T
    part[...] = dot_nt(mixed[...], wo[...]).astype(jnp.bfloat16)


def cross_forward_kernel(
    loaded, info, tokens, own_part, other_part, params, keys, values_t,
    section, hidden, q, mixed, mixed_t, lse, part,
    scores, weights,
):
    count = tokens.shape[0]

    def block_step(rows, at, carry):
        branch = own_part[rows, :].astype(jnp.float32) + other_part[rows, :].astype(jnp.float32)
        block = tokens[rows, :].astype(jnp.float32) + (branch + params[8:9, :])
        section[rows, :] = block
        hidden[rows, :] = norm_rows(block, params[2:3, :], params[3:4, :])
        return carry

    row_loop(count, block_step, 0)
    (wq,), (wo,) = loaded(0), loaded(1)
    bias_q = local_bias(params, 9, info[CORE], q.shape[1])
    q[...] = (dot(hidden[...], wq[...]) + bias_q).astype(jnp.bfloat16)
    masks = head_masks()
    key_spans = spans(keys.shape[0], 256)

    def pair_step(pair, carry):
        cols = pl.ds(pl.multiple_of(pair * 128, 128), 128)
        for parity in range(2):
            head = pair * 2 + parity
            queries = q[:, cols] * masks[parity]
            top = None
            for at, size in key_spans:
                block = dot_nt(keys[pl.ds(at, size), cols], queries) * (0.125 * LOG2E)
                scores[pl.ds(at, size), :] = block
                block_top = jnp.max(block, axis=0, keepdims=True)
                top = block_top if top is None else jnp.maximum(top, block_top)
            total = jnp.zeros_like(top)
            for at, size in key_spans:
                block = jnp.exp2(scores[pl.ds(at, size), :] - top)
                total = total + jnp.sum(block, axis=0, keepdims=True)
                weights[pl.ds(at, size), :] = block.astype(jnp.bfloat16)
            lse[pl.ds(head, 1), :] = top + jnp.log2(total)
            own = pl.ds(pl.multiple_of(head * HEAD_DIM, HEAD_DIM), HEAD_DIM)
            mixed_t[own, :] = (dot(values_t[own, :], weights[...]) * (1.0 / total)).astype(
                jnp.bfloat16
            )
        return carry

    lax.fori_loop(0, q.shape[1] // 128, pair_step, 0)
    mixed[...] = mixed_t[...].T
    part[...] = dot_nt(mixed[...], wo[...]).astype(jnp.bfloat16)


def dense_in_kernel(
    loaded, info, section, own_part, other_part, params, cotangent,
    section_new, hidden, act, slope, grad_low,
):
    count = section.shape[0]

    def block_step(rows, at, carry):
        branch = own_part[rows, :].astype(jnp.float32) + other_part[rows, :].astype(jnp.float32)
        block = section[rows, :] + (branch + params[11:12, :])
        section_new[rows, :] = block
        hidden[rows, :] = norm_rows(block, params[4:5, :], params[5:6, :])
        row_ids = lax.broadcasted_iota(jnp.int32, (64, 1), 0) + at
        valid = (row_ids < info[LENGTH]).astype(jnp.float32)
        grad_low[rows, :] = (cotangent[rows, :].astype(jnp.float32) * valid).astype(jnp.bfloat16)
        return carry

    row_loop(count, block_step, 0)

    held = act.shape[1] // D
    for at in range(4):
        if at % 2 == 0:
            blocks = loaded(at // 2)
        width = blocks[0].shape[1]
        row = 13 + info[CORE] * held + at * width // D
        bias = params[pl.ds(row, 1), at * width % D : at * width % D + width]

        def step(part, carry, at=at, block=blocks[at % 2], bias=bias):
            cols = pl.ds(at * width, width)
            pre_act = dot(hidden[...], block[...]) + bias
            spread = 0.5 + 0.5 * lax.erf(pre_act * (2.0**-0.5))
            act[:, cols] = (pre_act * spread).astype(jnp.bfloat16)
            density = jnp.exp2(pre_act * pre_act * (-0.5 * LOG2E)) * 0.3989422804014327
            slope[:, cols] = (spread + pre_act * density).astype(jnp.bfloat16)
            return carry

        step(0, 0)


def dense_out_kernel(
    loaded, info, act, slope, grad_low,
    grad_pre, part, grad_hidden, grad_bias,
):
    w2 = loaded(0) + loaded(1)
    width = w2[0].shape[1]
    for at, block in enumerate(w2):
        cols = pl.ds(at * width, width)
        grad_act = dot(grad_low[...], block[...]).astype(jnp.bfloat16).astype(jnp.float32)
        grad_block = (grad_act * slope[:, cols].astype(jnp.float32)).astype(jnp.bfloat16)
        grad_pre[:, cols] = grad_block
        grad_bias[:, cols] = row_sum(grad_block)
    for left, blocks, out in (
        (act, w2, part),
        (grad_pre, loaded(2) + loaded(3), grad_hidden),
    ):
        total = None
        for at, block in enumerate(blocks):
            product = dot_nt(left[:, at * width : at * width + width], block[...])
            total = product if total is None else total + product
        out[...] = total.astype(jnp.bfloat16)


def put_relative(product, here, order, keep, send, which, cols):
    half = keep.shape[0]
    rows = keep.shape[2]
    for at, offset in enumerate(order):
        block = product[pl.ds(pl.multiple_of((here ^ offset) * rows, 16), rows), :]
        target = keep if at < half else send
        target[at % half, which, :, cols] = block.astype(jnp.bfloat16)


def weight_kernel(uses, lefts_count, orders, *refs):
    rights_count = 1 + max(right for _, right, _, _, _ in uses)
    lefts, rights = refs[1 : 1 + lefts_count], refs[1 + lefts_count : 1 + lefts_count + rights_count]
    outs = refs[1 + lefts_count + rights_count : -2]
    product, turned = refs[-2:]
    width = product.shape[1]
    me = refs[0][0]
    in_turned = None
    for left, right, first, group, which in uses:
        left_t, right = lefts[left], rights[right]
        if left_t.shape[0] != D:
            if in_turned != left:
                turned[...] = left_t[...].T
                in_turned = left
            left_t = turned

        def step(at, carry, left_t=left_t, right=right, first=first, group=group, which=which):
            cols = pl.ds(pl.multiple_of(at * width, width), width)
            taken = pl.ds(pl.multiple_of(first + at * width, width), width)
            product[...] = dot(left_t[...], right[:, taken])
            if orders is None:
                outs[group][which, :, cols] = product[...].astype(jnp.bfloat16)
            else:
                put_relative(
                    product, me, orders[group], outs[2 * group], outs[2 * group + 1], which, cols
                )
            return carry

        lax.fori_loop(0, outs[0].shape[-1] // width, step, 0)


def attention_pull(
    keys, values, keys_t, q, grad_mixed, grad_mixed_t, mixed_t, lse, allowed, step,
    grad_keys, grad_values, grad_q_t, first, last,
):
    masks = head_masks()
    key_spans = spans(keys.shape[0], step)

    def pair_step(pair, carry):
        cols = pl.ds(pl.multiple_of(pair * 128, 128), 128)
        queries = [q[:, cols] * mask for mask in masks]
        grads = [(grad_mixed[:, cols] * 0.125) * mask for mask in masks]
        heads = [pl.ds(pl.multiple_of(pair * 128 + p * 64, 64), 64) for p in range(2)]
        levels, deltas = [], []
        for parity in range(2):
            levels.append(lse[pl.ds(pair * 2 + parity, 1), :])
            product = grad_mixed_t[heads[parity], :].astype(jnp.float32) * mixed_t[
                heads[parity], :
            ].astype(jnp.float32)
            deltas.append(jnp.sum(product, axis=0, keepdims=True) * 0.125)
        def block_step(rows, sums):
            key_sum = value_sum = None
            added = []
            for parity in range(2):
                scores = dot_nt(keys[rows, cols], queries[parity]) * (0.125 * LOG2E)
                weights = jnp.exp2(scores - levels[parity])
                if allowed is not None:
                    weights = jnp.where(allowed[rows, :] > 0.5, weights, 0.0)
                grad_soft = dot_nt(values[rows, cols], grads[parity])
                grad_raw = (weights * (grad_soft - deltas[parity])).astype(jnp.bfloat16)
                value_part = dot(weights.astype(jnp.bfloat16), grads[parity])
                key_part = dot(grad_raw, queries[parity])
                added.append(dot(keys_t[heads[parity], rows], grad_raw))
                value_sum = value_part if value_sum is None else value_sum + value_part
                key_sum = key_part if key_sum is None else key_sum + key_part
            grad_values[rows, cols] = (value_sum * 8.0).astype(jnp.bfloat16)
            grad_keys[rows, cols] = key_sum.astype(jnp.bfloat16)
            return added if sums is None else add_rows(sums, added)

        full = keys.shape[0] // step
        if full > 1:

            def looped(at, sums):
                return block_step(pl.ds(pl.multiple_of(at * step, step), step), sums)

            zero = jnp.zeros((HEAD_DIM, q.shape[0]), jnp.float32)
            sums = lax.fori_loop(0, full, looped, [zero, zero])
            rest = [(full * step, keys.shape[0] - full * step)]
        else:
            sums, rest = None, key_spans
        for at, size in rest:
            if size:
                sums = block_step(pl.ds(at, size), sums)
        for parity in range(2):
            grad_q_t[heads[parity], :] = sums[parity].astype(jnp.bfloat16)
        return carry

    lax.fori_loop(first, last, pair_step, 0)


def output_kernel(section, out_part, out_other, params, layer_out):

    def block_step(rows, at, carry):
        branch = out_part[rows, :].astype(jnp.float32) + out_other[rows, :].astype(jnp.float32)
        layer_out[rows, :] = (section[rows, :] + (branch + params[12:13, :])).astype(jnp.bfloat16)
        return carry

    row_loop(section.shape[0], block_step, 0)


def cross_backward_kernel(
    loaded, info, section, grad_part, grad_other, grad_top, params,
    q, keys, values, keys_t, mixed_t, lse,
    grad_section, grad_z, vectors, grad_mixed, grad_mixed_t,
    grad_keys, grad_values, grad_q_t,
):
    count = section.shape[0]

    def block_step(rows, at, sums):
        block = section[rows, :]
        grad = grad_part[rows, :].astype(jnp.float32) + grad_other[rows, :].astype(jnp.float32)
        pulled, gain_sum, shift_sum = norm_pull(block, grad, params[4:5, :])
        top = grad_top[rows, :].astype(jnp.float32)
        total = top + pulled
        low = total.astype(jnp.bfloat16)
        grad_section[rows, :] = total
        grad_z[rows, :] = low
        parts = [gain_sum, shift_sum, row_sum(low), jnp.sum(top, axis=0, keepdims=True)]
        return add_rows(sums, parts)

    sums = row_loop(count, block_step, zero_rows(4))
    for at, value in enumerate(sums):
        vectors[at : at + 1, :] = value
    (wo,) = loaded(0)
    grad_mixed[...] = dot(grad_z[...], wo[...]).astype(jnp.bfloat16)
    grad_mixed_t[...] = grad_mixed[...].T
    attention_pull(
        keys, values, keys_t, q, grad_mixed, grad_mixed_t, mixed_t, lse, None, 512,
        grad_keys, grad_values, grad_q_t, 0, q.shape[1] // 128 - 1,
    )


def cross_rest_kernel(
    loaded, info, q, keys, values, keys_t, mixed_t, lse, grad_mixed, grad_mixed_t,
    keys_begun, values_begun, q_t_begun,
    grad_q, grad_keys, grad_values, grad_hidden, biases,
    grad_q_t,
):
    pairs = q.shape[1] // 128
    attention_pull(
        keys, values, keys_t, q, grad_mixed, grad_mixed_t, mixed_t, lse, None, 512,
        grad_keys, grad_values, grad_q_t, pairs - 1, pairs,
    )
    begun = (pairs - 1) * 128
    grad_keys[:, :begun] = keys_begun[:, :begun]
    grad_values[:, :begun] = values_begun[:, :begun]
    grad_q_t[:begun, :] = q_t_begun[:begun, :]
    grad_q[...] = grad_q_t[...].T
    (wq,) = loaded(0)
    grad_hidden[...] = dot_nt(grad_q[...], wq[...]).astype(jnp.bfloat16)
    biases[0:1, :] = row_sum(grad_q[...])
    biases[1:2, :] = row_sum(grad_values[...])


def self_backward_kernel(
    loaded, info, section, grad_section, grad_part, grad_other, params,
    q, k, v, mixed_t, lse,
    grad_new, grad_z, grad_q, grad_keys, grad_values, grad_hidden, vectors, biases,
    grad_mixed, grad_mixed_t, grad_q_t, keys_t, allowed,
):
    count = section.shape[0]

    def block_step(rows, at, sums):
        grad = grad_part[rows, :].astype(jnp.float32) + grad_other[rows, :].astype(jnp.float32)
        pulled, gain_sum, shift_sum = norm_pull(section[rows, :], grad, params[2:3, :])
        total = grad_section[rows, :] + pulled
        low = total.astype(jnp.bfloat16)
        grad_new[rows, :] = total
        grad_z[rows, :] = low
        parts = [gain_sum, shift_sum, row_sum(low)]
        return add_rows(sums, parts)

    sums = row_loop(count, block_step, zero_rows(3))
    for at, value in enumerate(sums):
        vectors[at : at + 1, :] = value
    wv, wo = loaded(1)
    wq, wk = loaded(0)
    grad_mixed[...] = dot(grad_z[...], wo[...]).astype(jnp.bfloat16)
    grad_mixed_t[...] = grad_mixed[...].T
    keys_t[...] = k[...].T
    key_ids = lax.broadcasted_iota(jnp.int32, (count, count), 0)
    query_ids = lax.broadcasted_iota(jnp.int32, (count, count), 1)
    allowed[...] = ((key_ids <= query_ids) & (key_ids < info[LENGTH])).astype(jnp.float32)
    attention_pull(
        k, v, keys_t, q, grad_mixed, grad_mixed_t, mixed_t, lse, allowed, 256,
        grad_keys, grad_values, grad_q_t, 0, q.shape[1] // 128,
    )
    grad_q[...] = grad_q_t[...].T
    grad_hidden[...] = (
        dot_nt(grad_q[...], wq[...])
        + dot_nt(grad_keys[...], wk[...])
        + dot_nt(grad_values[...], wv[...])
    ).astype(jnp.bfloat16)
    biases[0:1, :] = row_sum(grad_q[...])
    biases[1:2, :] = row_sum(grad_values[...])


def last_kernel(
    info, tokens, grad_section, grad_part, grad_other, params,
    vectors2, vectors3, biases_self, biases_cross, grad_b1,
    input_grad, vectors,
):

    def block_step(rows, at, sums):
        grad = grad_part[rows, :].astype(jnp.float32) + grad_other[rows, :].astype(jnp.float32)
        pulled, gain_sum, shift_sum = norm_pull(
            tokens[rows, :].astype(jnp.float32), grad, params[0:1, :]
        )
        input_grad[rows, :] = grad_section[rows, :] + pulled
        parts = [gain_sum, shift_sum]
        return add_rows(sums, parts)

    sums = row_loop(tokens.shape[0], block_step, zero_rows(2))
    leader = (info[CORE] == 0).astype(jnp.float32)
    vectors[...] = jnp.zeros_like(vectors)
    shared = sums + [vectors2[0:1, :], vectors2[1:2, :], vectors3[0:1, :], vectors3[1:2, :]]
    shared = list(enumerate(shared)) + [(8, vectors2[2:3, :]), (11, vectors3[2:3, :]), (12, vectors3[3:4, :])]
    for at, value in shared:
        vectors[at : at + 1, :] = value * leader
    width = biases_self.shape[1]
    cols = pl.ds(pl.multiple_of(info[CORE] * width, 128), width)
    for at, ref in ((6, biases_self), (9, biases_cross)):
        vectors[at : at + 1, cols] = ref[0:1, :]
        vectors[at + 1 : at + 2, cols] = ref[1:2, :]
    held = grad_b1.shape[1] // D
    for at in range(held):
        vectors[pl.ds(13 + info[CORE] * held + at, 1), :] = grad_b1[:, at * D : at * D + D]


def enc_kernel(loaded, info, grad_keys, grad_values, *refs):
    own, out = refs[:-1], refs[-1]
    width = grad_keys.shape[1]
    place = info[CORE] if own else 1 - info[CORE]
    cols = pl.ds(pl.multiple_of(place * width, 128), width)
    (wk,), (wv,) = loaded(0), loaded(1)
    for at, size in spans(grad_keys.shape[0], 256):
        rows = pl.ds(at, size)
        total = dot_nt(grad_keys[rows, :], wk[cols, :]) + dot_nt(grad_values[rows, :], wv[cols, :])
        if own:
            out[rows, 0, :] = total + own[0][rows, :].astype(jnp.float32)
        else:
            out[rows, :] = total.astype(out.dtype)


def swap(array, bit):
    count = lax.axis_size("dp")
    return lax.ppermute(array, "dp", [(i, i ^ bit) for i in range(count)])


def swap_core(array):
    return lax.ppermute(array, "mp", [(0, 1), (1, 0)])


def together(*values):
    return lax.optimization_barrier(values)


def sum_round(value, bits):
    me = lax.axis_index("dp")
    offsets = [0]
    for bit in bits:
        offsets = offsets + [offset ^ bit for offset in offsets]
    stack = [value] + [swap(value, offset) for offset in offsets[1:]]
    for bit in bits:
        flip = (me & bit) != 0
        pairs = [(stack[at], stack[at + 1]) for at in range(0, len(stack), 2)]
        stack = [jnp.where(flip, b, a) + jnp.where(flip, a, b) for a, b in pairs]
    return stack[0]


def sum_far(value):
    for bits in [(4, 8)] if lax.axis_size("dp") == 16 else high_bits():
        value = sum_round(value, bits)
    return value


def high_bits():
    return [(1 << k,) for k in range(2, lax.axis_size("dp").bit_length() - 1)]


def sum_near(value):
    value = sum_round(value, (1, 2))
    return value + swap_core(value)


def join(stack, came):
    return jnp.concatenate([stack, came], axis=0)


def far_stack(piece):
    return jnp.concatenate([piece] + [swap(piece, offset) for offset in FAR[1:]], axis=0)


def near_steps(first, second):
    parts = None if first is None else halves(first)
    onward = []
    for place, bit in enumerate((1, 2)):
        pieces = []
        if second is not None:
            pieces.append(second[1 - place])
        if first is not None:
            pieces.append(parts[place])
        onward.append(swap(jnp.concatenate(pieces, axis=0), bit))
    cut = 0 if second is None else 8
    nears = None if first is None else [join(part, came[cut:]) for part, came in zip(parts, onward)]
    lasts = None if second is None else onward[::-1]
    return nears, lasts


def near_parts(nears, lasts):
    return [
        [(near, (0, first)), (last, (3 ^ first, 3))]
        for near, last, first in zip(nears, lasts, (1, 2))
    ]


def halves(stack):
    return jnp.split(stack, 2, axis=1)


def weight_parts(uses, lefts, rights, wide, cols):
    count = lax.axis_size("dp")
    direct = count == 16
    orders = []
    for first in (2, 1):
        order = FAR
        for bit in (3 ^ first, first):
            order = order + [offset ^ bit for offset in order]
        orders.append(order)
    if direct:
        outs = [array_of((8, wide, D // 16, cols))] * 4
    else:
        outs = [array_of((wide, D, cols))] * 2
    return run_kernel(
        functools.partial(weight_kernel, uses, len(lefts), orders if direct else None),
        outs,
        lax.axis_index("dp")[None],
        *lefts,
        *rights,
        scratch=[pltpu.VMEM((D, 384), jnp.float32), pltpu.VMEM((D, BLOCK), jnp.bfloat16)],
    )


def send_near(first, second):
    cames = []
    for place, bit in enumerate((1, 2)):
        pieces = []
        if second is not None:
            pieces.append(second[place])
        if first is not None:
            pieces.append(first[3 - 2 * place])
        cames.append(swap(pieces[0] if len(pieces) == 1 else jnp.concatenate(pieces), bit))
    cut = 0 if second is None else 4
    return [came[cut:] for came in cames[::-1]], [came[:cut] for came in cames]


def fold_both(parts, cames):
    keep_a, _, keep_b, _ = parts
    (low_a, high_a), (low_b, high_b) = fold(keep_a, cames[0]), fold(keep_b, cames[1])
    return (low_a, low_b), (high_a, high_b)


def fold(keep, came):
    half = keep.shape[0] // 2
    high = keep[half:].astype(jnp.float32) + came[half:].astype(jnp.float32)
    return (
        keep[:half].astype(jnp.float32) + came[:half].astype(jnp.float32),
        high.astype(jnp.bfloat16),
    )


def far_ready(lows, cames):
    total = jnp.concatenate(
        [low.astype(jnp.float32) + came.astype(jnp.float32) for low, came in zip(lows, cames)],
        axis=1,
    )
    return [total[0]] + [total[at].astype(jnp.bfloat16) for at in range(1, 4)]


def totals_kernel(groups, *refs):
    squares = None
    outs = refs[-(groups + 1) :]
    for at in range(groups):
        own, *cames = refs[4 * at : 4 * at + 4]
        total = own[...]
        for came in cames:
            total = total + came[...].astype(jnp.float32)
        outs[at][...] = total
        square = jnp.sum(total * total, axis=(0, 1), keepdims=True)[0]
        squares = square if squares is None else squares + square
    if len(refs) == 5 * groups + 1:
        outs[groups][...] = squares
        return
    early, vectors = refs[4 * groups : 4 * groups + 2]
    count = vectors.shape[0]
    everything = jnp.sum(squares + early[...], axis=1, keepdims=True)
    outs[groups][0:count, :] = vectors[...]
    outs[groups][count : count + 1, :] = jnp.broadcast_to(everything, (1, vectors.shape[1]))


def prepare_kernel(decays, attn, attn_first, attn_second, dense, dense_first, dense_second, *outs):
    scales = (None, decays[0:1, 0:1], decays[0:1, 1:2])
    arrays = ((attn, attn_first, attn_second), (dense, dense_first, dense_second))
    for at, (group, rate) in enumerate(zip(arrays, (attn_rate, dense_rate))):
        for which, ref in enumerate(group):
            scale = 1.0 - 0.1 * rate if which == 0 else scales[which]
            outs[3 * at + which][...] = ref[...] * scale


def finish_kernel(
    decays, sums, vector_sum, self_sum, cross_sum, w1_sum, w2_sum,
    attn, attn_first, attn_second, dense, dense_first, dense_second,
    vector, vector_first, vector_second,
    norm, attn_new, attn_first_new, attn_second_new, attn_copy,
    dense_new, dense_first_new, dense_second_new, dense_copy,
    vector_new, vector_first_new, vector_second_new, vector_copy, bias_gradient,
):
    last = sums.shape[0] - 1
    vectors = sums[0:last, :]
    squares = jnp.sum(jnp.sum(vectors * vectors, axis=0, keepdims=True), axis=1, keepdims=True)
    clip_norm = jnp.sqrt(squares + sums[last : last + 1, 0:1])
    norm[...] = jnp.broadcast_to(clip_norm, norm.shape)
    factor = jnp.minimum(1.0, 1.0 / (clip_norm + 1e-06))
    first_rate, second_rate = decays[0:1, 0:1], decays[0:1, 1:2]
    first_scale = 1.0 / (1.0 - first_rate * first_rate * first_rate)
    second_scale = 1.0 / (1.0 - second_rate * second_rate * second_rate)
    first_part = (1.0 - first_rate) * factor
    second_part = (1.0 - second_rate) * factor * factor

    def update(gradient, weight, first, second, step_rate):
        first_new = first + first_part * gradient
        second_new = second + second_part * gradient * gradient
        change = (first_new * first_scale) / (jnp.sqrt(second_new * second_scale) + 1e-08)
        return weight - step_rate * change, first_new, second_new

    for at, gradient in enumerate((self_sum, cross_sum)):
        for which in range(4):
            new, first, second = update(
                gradient[which],
                attn[at, which],
                attn_first[at, which],
                attn_second[at, which],
                attn_rate,
            )
            attn_new[at, which] = new
            attn_first_new[at, which] = first
            attn_second_new[at, which] = second
            attn_copy[at, which] = new.astype(jnp.bfloat16)
    width = w1_sum.shape[2]
    for at, gradient in enumerate((w1_sum, w2_sum)):
        for which in range(4):
            cols = slice(which * width, which * width + width)
            new, first, second = update(
                gradient[which],
                dense[at, :, cols],
                dense_first[at, :, cols],
                dense_second[at, :, cols],
                dense_rate,
            )
            dense_new[at, :, cols] = new
            dense_first_new[at, :, cols] = first
            dense_second_new[at, :, cols] = second
            dense_copy[at, :, cols] = new.astype(jnp.bfloat16)
    new, first, second = update(
        vector_sum[...],
        vector[...] * (1.0 - 0.1 * vector_rate),
        vector_first[...] * first_rate,
        vector_second[...] * second_rate,
        vector_rate,
    )
    vector_new[...] = new
    vector_first_new[...] = first
    vector_second_new[...] = second
    vector_copy[...] = new.astype(jnp.bfloat16)
    bias_gradient[...] = vector_sum[12:13, :] * factor


def local(
    tokens,
    enc_states,
    lengths,
    cotangent,
    attn_master,
    attn_first,
    attn_second,
    dense_master,
    dense_first,
    dense_second,
    vector_params,
    vector_first,
    vector_second,
    decays,
):
    core = lax.axis_index("mp")
    attn_low = attn_master.astype(jnp.bfloat16)
    dense_low = dense_master.astype(jnp.bfloat16)
    blocks = dense_master.shape[2] // attn_master.shape[3]
    dense_low = jnp.stack(jnp.split(dense_low, blocks, axis=2), axis=1)
    device = lax.axis_index("dp") * lax.axis_size("mp") + core
    own_cols = vector_params.shape[1]
    attn_low, vector_in = together(attn_low, vector_params)
    placed = lax.dynamic_update_slice_in_dim(
        jnp.zeros((vector_params.shape[0], D), jnp.float32), vector_in, device * own_cols, 1
    )
    fast = lax.axis_size("dp") == 16
    head_cols = attn_master.shape[3]
    hidden_cols = dense_master.shape[2]
    head_rows = 2 * (head_cols // 128)
    count = tokens.shape[0]
    keys_count = enc_states.shape[1]
    enc = enc_states[0]
    rows_d = array_of((count, D))
    rows_f = array_of((count, D), jnp.float32)
    rows_h = array_of((count, head_cols))
    turned_h = array_of((head_cols, count))
    lse_shape = array_of((head_rows, count), jnp.float32)
    keys_h = array_of((keys_count, head_cols))
    keys_t_h = array_of((head_cols, keys_count))
    scratch_h = pltpu.VMEM((count, head_cols), jnp.bfloat16)
    scratch_t = pltpu.VMEM((head_cols, count), jnp.bfloat16)
    scratch_s = pltpu.VMEM((count, count), jnp.float32)

    here = lax.axis_index("dp")
    info = jnp.stack([here, core, lengths[0]]).astype(jnp.int32)
    if fast:
        low_self, low_cross = attn_low[0][None], attn_low[1][None]
        low_w1, low_w2 = dense_low[0][None], dense_low[1][None]
        vector_low = placed + swap(placed, 1)
        vector_low = vector_low + swap(vector_low, 2)
        self_far, vector_low = together(far_stack(low_self), vector_low + swap_core(vector_low))
        (self_near, _), params, low_cross = together(
            near_steps(self_far, None), sum_far(vector_low), low_cross
        )
        (_, self_last), cross_far, low_w1, info = together(
            near_steps(None, self_near), far_stack(low_cross), low_w1, info
        )
        self_a, self_b = near_parts(self_near, self_last)
    else:
        params = sum_near(sum_far(placed))
        attn_all = lax.all_gather(attn_low, "dp", axis=2, tiled=True)
        dense_all = lax.all_gather(dense_low, "dp", axis=2, tiled=True)
        (self_a, self_b), (cross_a, cross_b), (w1_a, w1_b), (w2_a, w2_b) = [
            [[(whole[:2], None)], [(whole[2:], None)]] for whole in (*attn_all, *dense_all)
        ]
    both = (0, 1)
    cross_uses = ((0,), (0,), (0,), (0,)) if fast else ((0,), (1,), (1,), (0,))
    (
        hidden1, self_q, self_k, self_v, self_mixed, self_mixed_t, self_lse, self_part, self_a, self_b,
    ) = run_kernel(
        self_forward_kernel,
        [rows_d, rows_h, rows_h, rows_h, rows_h, turned_h, lse_shape, rows_d],
        info, tokens, params,
        scratch=[scratch_t, scratch_s],
        weights=[(self_a, both), (self_b, both)],
        keep=True,
    )
    if fast:
        (cross_near, _), self_part = together(near_steps(cross_far, None), self_part)
    self_other = swap_core(self_part)
    if fast:
        (_, cross_last), w1_far, self_other, info, low_w2 = together(
            near_steps(None, cross_near), far_stack(low_w1), self_other, info, low_w2
        )
        cross_a, cross_b = near_parts(cross_near, cross_last)
    cross_k, cross_v, cross_k_t, cross_v_t, enc_t, cross_wk, cross_wv = run_kernel(
        cross_keys_kernel,
        [keys_h, keys_h, keys_t_h, keys_t_h, array_of((D, keys_count))],
        info, enc, params,
        weights=[(cross_a, (1,)), (cross_b, (0,))],
        keep=True,
    )
    if fast:
        (w1_near, _), w2_far, cross_k, info = together(
            near_steps(w1_far, None), far_stack(low_w2), cross_k, info
        )
    (
        section1, hidden2, cross_q, cross_mixed, cross_mixed_t, cross_lse, cross_part, cross_wq, cross_wo,
    ) = run_kernel(
        cross_forward_kernel,
        [rows_f, rows_d, rows_h, rows_h, turned_h, lse_shape, rows_d],
        info, tokens, self_part, self_other, params, cross_k, cross_v_t,
        scratch=[
            pltpu.VMEM((keys_count, count), jnp.float32),
            pltpu.VMEM((keys_count, count), jnp.bfloat16),
        ],
        weights=[(cross_a, (0,)), (cross_b, (1,))],
        keep=True,
    )
    if fast:
        (w2_near, w1_last), cross_part, info = together(
            near_steps(w2_far, w1_near), cross_part, info
        )
        w1_a, w1_b = near_parts(w1_near, w1_last)
    hidden_rows = array_of((count, hidden_cols))
    section2, hidden3, act, slope, grad_low, w1_a, w1_b = run_kernel(
        dense_in_kernel,
        [rows_f, rows_d, hidden_rows, hidden_rows, rows_d],
        info, section1, cross_part, swap_core(cross_part), params, cotangent,
        weights=[(w1_a, both), (w1_b, both)],
        keep=True,
    )
    dense_uses = tuple((0, 0, at * head_cols, at // 2, at % 2) for at in range(4))
    w2_parts = weight_parts(dense_uses, (grad_low,), (act,), 2, head_cols)
    if fast:
        (_, w2_last), w2_parts, slope, info = together(
            near_steps(None, w2_near), w2_parts, slope, info
        )
        w2_a, w2_b = near_parts(w2_near, w2_last)
    grad_pre, out_part, grad_h3, grad_b1 = run_kernel(
        dense_out_kernel,
        [hidden_rows, rows_d, rows_d, array_of((1, hidden_cols), jnp.float32)],
        info, act, slope, grad_low,
        weights=[(w2_a, both), (w2_b, both), (w1_a, both), (w1_b, both)],
    )
    w1_parts = weight_parts(dense_uses, (hidden3,), (grad_pre,), 2, head_cols)
    if fast:
        (w2_came, _), w1_parts, grad_h3, out_part = together(
            send_near(w2_parts, None), w1_parts, grad_h3, out_part
        )
        w2_lows, w2_highs = fold_both(w2_parts, w2_came)
    grad_h3_other, out_other = swap_core(grad_h3), swap_core(out_part)
    (
        grad_section2, grad_z2, vectors3, grad_cross, grad_cross_t, dk_begun, dv_begun, dq_begun,
    ) = run_kernel(
        cross_backward_kernel,
        [rows_f, rows_d, array_of((4, D), jnp.float32), rows_h, turned_h,
         keys_h, keys_h, turned_h],
        info, section2, grad_h3, grad_h3_other, grad_low, params,
        cross_q, cross_k, cross_v, cross_k_t, cross_mixed_t, cross_lse,
        weights=[(cross_wo, cross_uses[1])],
    )
    if fast:
        (w1_came, w2_came), dk_begun, info = together(
            send_near(w1_parts, w2_highs), dk_begun, info
        )
        w2_own, *w2_out = far_ready(w2_lows, w2_came)
        w1_lows, w1_highs = fold_both(w1_parts, w1_came)
    layer_out = run_kernel(output_kernel, rows_d, section2, out_part, out_other, params)
    cross_dq, cross_dk, cross_dv, grad_h2, biases_cross = run_kernel(
        cross_rest_kernel,
        [rows_h, keys_h, keys_h, rows_d, array_of((2, head_cols), jnp.float32)],
        info, cross_q, cross_k, cross_v, cross_k_t, cross_mixed_t, cross_lse,
        grad_cross, grad_cross_t, dk_begun, dv_begun, dq_begun,
        scratch=[scratch_t],
        weights=[(cross_wq, cross_uses[0])],
    )
    cross_parts = weight_parts(
        ((0, 0, 0, 0, 0), (1, 1, 0, 0, 1), (1, 2, 0, 1, 0), (2, 3, 0, 1, 1)),
        (hidden2, enc_t, grad_z2),
        (cross_dq, cross_dk, cross_dv, cross_mixed),
        2,
        head_cols,
    )
    grad_h2_other = swap_core(grad_h2)
    if fast:
        (_, w1_came), w2_in1, w2_in2, cross_parts, grad_h2_other, info = together(
            send_near(None, w1_highs), swap(w2_out[0], 4), swap(w2_out[1], 8),
            cross_parts, grad_h2_other, info,
        )
        w1_own, *w1_out = far_ready(w1_lows, w1_came)
    (
        grad_section1, grad_z1, self_dq, self_dk, self_dv, grad_h1, vectors2, biases_self,
    ) = run_kernel(
        self_backward_kernel,
        [rows_f, rows_d, rows_h, rows_h, rows_h, rows_d,
         array_of((3, D), jnp.float32), array_of((2, head_cols), jnp.float32)],
        info, section1, grad_section2, grad_h2, grad_h2_other, params,
        self_q, self_k, self_v, self_mixed_t, self_lse,
        scratch=[scratch_h, scratch_t, scratch_t, scratch_t, scratch_s],
        weights=[(self_a, both), (self_b, both)],
    )
    if fast:
        (cross_came, _), w2_in3, w1_in1, w1_in2, self_dq, grad_h1 = together(
            send_near(cross_parts, None), swap(w2_out[2], 12), swap(w1_out[0], 4),
            swap(w1_out[1], 8), self_dq, grad_h1,
        )
        cross_lows, cross_highs = fold_both(cross_parts, cross_came)
    self_parts = weight_parts(
        ((0, 0, 0, 0, 0), (0, 1, 0, 0, 1), (0, 2, 0, 1, 0), (1, 3, 0, 1, 1)),
        (hidden1, grad_z1),
        (self_dq, self_dk, self_dv, self_mixed),
        2,
        head_cols,
    )
    grad_h1_other = swap_core(grad_h1)
    if fast:
        (_, cross_came), w1_in3, self_parts, grad_h1_other, info = together(
            send_near(None, cross_highs), swap(w1_out[2], 12), self_parts, grad_h1_other, info
        )
        cross_own, *cross_out = far_ready(cross_lows, cross_came)
    input_grad, vector_grad = run_kernel(
        last_kernel,
        [rows_f, array_of(params.shape, jnp.float32)],
        info, tokens, grad_section1, grad_h1, grad_h1_other, params,
        vectors2, vectors3, biases_self, biases_cross, grad_b1,
    )
    enc_other = run_kernel(
        enc_kernel,
        array_of((keys_count, head_cols)),
        info, cross_dk, cross_dv,
        weights=[(cross_wk, cross_uses[2]), (cross_wv, cross_uses[3])],
    )
    if fast:
        (self_came, _), cross_ins, vector_grad, enc_other = together(
            send_near(self_parts, None),
            [swap(out, offset) for out, offset in zip(cross_out, FAR[1:])],
            vector_grad, enc_other,
        )
        self_lows, self_highs = fold_both(self_parts, self_came)
        (_, self_came), enc_came = together(send_near(None, self_highs), swap_core(enc_other))
        self_own, *self_out = far_ready(self_lows, self_came)
    else:
        enc_came = swap_core(enc_other)
    enc_grad = run_kernel(
        enc_kernel,
        array_of((keys_count, 1, head_cols), jnp.float32),
        info, cross_dk, cross_dv, enc_came,
        weights=[(cross_wk, cross_uses[2]), (cross_wv, cross_uses[3])],
    )
    group = array_of((4, D // lax.axis_size("dp"), head_cols), jnp.float32)
    masters = (attn_master, attn_first, attn_second, dense_master, dense_first, dense_second)
    prepared = run_kernel(
        prepare_kernel,
        [array_of(master.shape, jnp.float32) for master in masters],
        *lax.optimization_barrier((decays[None], enc_came))[:1], *masters,
    )
    square_row = array_of((1, head_cols), jnp.float32)
    if fast:
        w1_sum, w2_sum, cross_sum, early_squares = run_kernel(
            functools.partial(totals_kernel, 3),
            [group, group, group, square_row],
            w1_own, w1_in1, w1_in2, w1_in3, w2_own, w2_in1, w2_in2, w2_in3, cross_own, *cross_ins,
        )
        self_ins, enc_grad, early_squares, prepared = together(
            [swap(out, offset) for out, offset in zip(self_out, FAR[1:])],
            enc_grad, early_squares, prepared,
        )
        self_sum, payload = run_kernel(
            functools.partial(totals_kernel, 1),
            [group, array_of((params.shape[0] + 1, D), jnp.float32)],
            self_own, *self_ins, early_squares, vector_grad,
        )
    else:
        self_sum, cross_sum, w1_sum, w2_sum = [
            jnp.concatenate(
                [
                    lax.psum_scatter(
                        part.astype(jnp.float32), "dp", scatter_dimension=1, tiled=True
                    )
                    for part in parts
                ],
                axis=0,
            )
            for parts in (self_parts, cross_parts, w1_parts, w2_parts)
        ]
        square = sum(jnp.sum(total * total) for total in (cross_sum, w1_sum, w2_sum, self_sum))
        payload = jnp.concatenate([vector_grad, jnp.full((1, D), square)], axis=0)
    enc_grad = enc_grad.transpose(1, 0, 2)
    sums = sum_near(sum_far(payload))
    vector_sum = lax.dynamic_slice_in_dim(sums[:-1], device * own_cols, own_cols, 1)
    outs = [
        jax.ShapeDtypeStruct(master.shape, dtype)
        for master in (attn_master, dense_master, vector_params)
        for dtype in (jnp.float32, jnp.float32, jnp.float32, jnp.bfloat16)
    ]
    norm, *updated, bias_gradient = run_kernel(
        finish_kernel,
        [array_of((1, 128), jnp.float32), *outs, array_of((1, own_cols), jnp.float32)],
        decays[None], sums, vector_sum,
        self_sum, cross_sum, w1_sum, w2_sum, *prepared,
        vector_params, vector_first, vector_second,
    )
    return (layer_out, input_grad, enc_grad, norm[0, 0], *updated, bias_gradient[0])


def solution(mesh):
    return jax.shard_map(
        local,
        mesh=mesh,
        in_specs=(
            P("dp", None),
            P("dp", None, None),
            P("dp"),
            P("dp", None),
            P(None, None, "dp", "mp"),
            P(None, None, "dp", "mp"),
            P(None, None, "dp", "mp"),
            P(None, "dp", "mp"),
            P(None, "dp", "mp"),
            P(None, "dp", "mp"),
            P(None, ("dp", "mp")),
            P(None, ("dp", "mp")),
            P(None, ("dp", "mp")),
            P(),
        ),
        out_specs=(
            P("dp", None),
            P("dp", None),
            P("dp", None, "mp"),
            P(),
            P(None, None, "dp", "mp"),
            P(None, None, "dp", "mp"),
            P(None, None, "dp", "mp"),
            P(None, None, "dp", "mp"),
            P(None, "dp", "mp"),
            P(None, "dp", "mp"),
            P(None, "dp", "mp"),
            P(None, "dp", "mp"),
            P(None, ("dp", "mp")),
            P(None, ("dp", "mp")),
            P(None, ("dp", "mp")),
            P(None, ("dp", "mp")),
            P(("dp", "mp")),
        ),
        check_vma=False,
    )
```

```python
import functools

import jax
import jax.numpy as jnp
from jax import lax
from jax.experimental import pallas as pl
from jax.experimental.pallas import tpu as pltpu
from jax.sharding import PartitionSpec as P

D = 768
HEAD_DIM = 64
FF = 3072
BLOCK = 448
STEP = 3


attn_rate = 0.08
dense_rate = 0.03
vector_rate = 0.3
LOG2E = 1.4426950408889634
FAR = [0, 4, 8, 12]


def dot(left_side, right_side):
    return jnp.dot(left_side, right_side, preferred_element_type=jnp.float32)


def dot_nt(left_side, right_side):
    return lax.dot_general(
        left_side, right_side, (((1,), (1,)), ((), ())), preferred_element_type=jnp.float32
    )


def spans(total, step):
    return [(at, min(step, total - at)) for at in range(0, total, step)]


def row_loop(count, step, carry):
    def body(at, carry):
        first = pl.multiple_of(at * 64, 64)
        return step(pl.ds(first, 64), first, carry)

    return lax.fori_loop(0, count // 64, body, carry)


def add_rows(old, new):
    return [a + b for a, b in zip(old, new)]


def zero_rows(number):
    return [jnp.zeros((1, D), jnp.float32)] * number


def unit_norm(values):
    centred = values - jnp.mean(values, axis=-1, keepdims=True)
    inverse = lax.rsqrt(jnp.mean(centred * centred, axis=-1, keepdims=True) + 1e-05)
    return centred * inverse, inverse


def norm_rows(values, gain, shift):
    unit, _ = unit_norm(values)
    return (unit * gain + shift).astype(jnp.bfloat16)


def norm_pull(values, grad, gain):
    unit, inverse = unit_norm(values)
    scaled = grad * gain
    pulled = inverse * (
        scaled
        - jnp.mean(scaled, axis=-1, keepdims=True)
        - unit * jnp.mean(scaled * unit, axis=-1, keepdims=True)
    )
    return (
        pulled,
        jnp.sum(grad * unit, axis=0, keepdims=True),
        jnp.sum(grad, axis=0, keepdims=True),
    )


def head_masks():
    lane = lax.broadcasted_iota(jnp.int32, (1, 2 * HEAD_DIM), 1)
    return [(lane < HEAD_DIM).astype(jnp.bfloat16), (lane >= HEAD_DIM).astype(jnp.bfloat16)]


def row_sum(values):
    return jnp.sum(values.astype(jnp.float32), axis=0, keepdims=True)


HERE, CORE, LENGTH = range(3)


def held_bytes(shape, dtype):
    *lead, rows, cols = (1, 1, *shape)
    count = -(-rows // 16) * 16 * (-(-cols // 128) * 128)
    for size in lead:
        count *= size
    return count * jnp.dtype(dtype).itemsize


def run_kernel(kernel, out_shapes, *operands, scratch=(), weights=(), keep=False):
    spaces = [
        pl.BlockSpec(memory_space=pltpu.SMEM if operand.dtype == jnp.int32 else pltpu.VMEM)
        for operand in operands
    ]
    held = [array for sources, _ in weights for array, _ in sources]
    single = not isinstance(out_shapes, (list, tuple))
    shapes = [out_shapes] if single else list(out_shapes)
    cut = [sources[0][1] is not None for sources, _ in weights]
    joined = [
        array_of((len(matrices), D, sources[0][0].shape[-1]))
        for (sources, matrices), pieces in zip(weights, cut)
        if pieces
    ]
    results_count = len(shapes)
    if keep:
        shapes = shapes + joined
        buffers = []
    else:
        buffers = [pltpu.VMEM(shape.shape, shape.dtype) for shape in joined]
    first_held, first_out = len(operands), len(operands) + len(held)
    first_scratch = first_out + len(shapes)

    def body(*refs):
        if not weights:
            kernel(*refs)
            return
        info = refs[0]
        stacks = iter(refs[first_held:first_out])
        groups = [[(next(stacks), offsets) for _, offsets in sources] for sources, _ in weights]
        if keep:
            targets = refs[first_out + results_count : first_scratch]
            scratch_refs = refs[first_scratch:]
        else:
            targets = refs[len(refs) - len(joined) :]
            scratch_refs = refs[first_scratch : len(refs) - len(joined)]

        def loaded(at):
            matrices = weights[at][1]
            if not cut[at]:
                return [groups[at][0][0].at[matrix] for matrix in matrices]
            target = targets[sum(cut[:at])]
            for stack, offsets in groups[at]:
                for which, matrix in enumerate(matrices):
                    rows = stack.shape[2]
                    for piece in range(8):
                        offset = offsets[piece // 4] ^ FAR[piece % 4]
                        place = pl.multiple_of((info[HERE] ^ offset) * rows, 16)
                        target[which, pl.ds(place, rows), :] = stack[piece, matrix]
            return [target.at[which] for which in range(len(matrices))]

        outs = refs[first_out : first_out + results_count]
        kernel(loaded, *refs[:first_held], *outs, *scratch_refs)

    sizes = [(array.shape, array.dtype) for array in (*operands, *held, *shapes)]
    sizes += [(array.shape, array.dtype) for array in (*scratch, *buffers)]
    needed = sum(held_bytes(shape, dtype) for shape, dtype in sizes)
    results = pl.pallas_call(
        body,
        out_shape=shapes,
        in_specs=spaces + [pl.BlockSpec(memory_space=pltpu.VMEM) for _ in held],
        out_specs=[pl.BlockSpec(memory_space=pltpu.VMEM) for _ in shapes],
        scratch_shapes=[*scratch, *buffers],
        compiler_params=pltpu.CompilerParams(vmem_limit_bytes=needed + 4 * 2**20),
    )(*operands, *held)
    if keep:
        wholes = iter(results[results_count:])
        sources = [[(next(wholes), None)] if pieces else given for pieces, (given, _) in zip(cut, weights)]
        return [*results[:results_count], *sources]
    return results[0] if single else results


def array_of(shape, dtype=jnp.bfloat16):
    return jax.ShapeDtypeStruct(shape, dtype)


def local_bias(params, row, core, width):
    return params[row : row + 1, pl.ds(pl.multiple_of(core * width, 128), width)]


def cross_keys_kernel(loaded, info, enc, params, keys, values, keys_t, values_t, enc_t):
    bias_v = local_bias(params, 10, info[CORE], keys.shape[1])
    for at, size in spans(enc.shape[0], 256):
        rows = pl.ds(at, size)
        enc_t[:, rows] = enc[rows, :].T
    (wk,), (wv,) = loaded(0), loaded(1)
    for at, size in spans(enc.shape[0], 256):
        rows = pl.ds(at, size)
        block = enc[rows, :]
        key_block = dot(block, wk[...]).astype(jnp.bfloat16)
        value_block = (dot(block, wv[...]) + bias_v).astype(jnp.bfloat16)
        keys[rows, :] = key_block
        values[rows, :] = value_block
        keys_t[:, rows] = key_block.T
        values_t[:, rows] = value_block.T


def self_forward_kernel(
    loaded, info, tokens, params,
    hidden, q, k, v, mixed, mixed_t, lse, part,
    values_t, allowed,
):
    count = tokens.shape[0]

    def block_step(rows, at, carry):
        hidden[rows, :] = norm_rows(
            tokens[rows, :].astype(jnp.float32), params[0:1, :], params[1:2, :]
        )
        return carry

    row_loop(count, block_step, 0)
    bias_q = local_bias(params, 6, info[CORE], q.shape[1])
    bias_v = local_bias(params, 7, info[CORE], q.shape[1])
    wq, wk = loaded(0)
    q[...] = (dot(hidden[...], wq[...]) + bias_q).astype(jnp.bfloat16)
    k[...] = dot(hidden[...], wk[...]).astype(jnp.bfloat16)
    wv, wo = loaded(1)
    v[...] = (dot(hidden[...], wv[...]) + bias_v).astype(jnp.bfloat16)
    values_t[...] = v[...].T
    key_ids = lax.broadcasted_iota(jnp.int32, (count, count), 0)
    query_ids = lax.broadcasted_iota(jnp.int32, (count, count), 1)
    allowed[...] = ((key_ids <= query_ids) & (key_ids < info[LENGTH])).astype(jnp.float32)
    masks = head_masks()

    def pair_step(pair, carry):
        cols = pl.ds(pl.multiple_of(pair * 128, 128), 128)
        for parity in range(2):
            head = pair * 2 + parity
            scores = dot_nt(k[:, cols], q[:, cols] * masks[parity]) * (0.125 * LOG2E)
            scores = jnp.where(allowed[...] > 0.5, scores, -1e30)
            top = jnp.max(scores, axis=0, keepdims=True)
            weights = jnp.exp2(scores - top)
            total = jnp.sum(weights, axis=0, keepdims=True)
            lse[pl.ds(head, 1), :] = top + jnp.log2(total)
            own = pl.ds(pl.multiple_of(head * HEAD_DIM, HEAD_DIM), HEAD_DIM)
            mixed_t[own, :] = (
                dot(values_t[own, :], weights.astype(jnp.bfloat16)) * (1.0 / total)
            ).astype(jnp.bfloat16)
        return carry

    lax.fori_loop(0, q.shape[1] // 128, pair_step, 0)
    mixed[...] = mixed_t[...].T
    part[...] = dot_nt(mixed[...], wo[...]).astype(jnp.bfloat16)


def cross_forward_kernel(
    loaded, info, tokens, own_part, other_part, params, keys, values_t,
    section, hidden, q, mixed, mixed_t, lse, part,
    scores, weights,
):
    count = tokens.shape[0]

    def block_step(rows, at, carry):
        branch = own_part[rows, :].astype(jnp.float32) + other_part[rows, :].astype(jnp.float32)
        block = tokens[rows, :].astype(jnp.float32) + (branch + params[8:9, :])
        section[rows, :] = block
        hidden[rows, :] = norm_rows(block, params[2:3, :], params[3:4, :])
        return carry

    row_loop(count, block_step, 0)
    (wq,), (wo,) = loaded(0), loaded(1)
    bias_q = local_bias(params, 9, info[CORE], q.shape[1])
    q[...] = (dot(hidden[...], wq[...]) + bias_q).astype(jnp.bfloat16)
    masks = head_masks()
    key_spans = spans(keys.shape[0], 256)

    def pair_step(pair, carry):
        cols = pl.ds(pl.multiple_of(pair * 128, 128), 128)
        for parity in range(2):
            head = pair * 2 + parity
            queries = q[:, cols] * masks[parity]
            top = None
            for at, size in key_spans:
                block = dot_nt(keys[pl.ds(at, size), cols], queries) * (0.125 * LOG2E)
                scores[pl.ds(at, size), :] = block
                block_top = jnp.max(block, axis=0, keepdims=True)
                top = block_top if top is None else jnp.maximum(top, block_top)
            total = jnp.zeros_like(top)
            for at, size in key_spans:
                block = jnp.exp2(scores[pl.ds(at, size), :] - top)
                total = total + jnp.sum(block, axis=0, keepdims=True)
                weights[pl.ds(at, size), :] = block.astype(jnp.bfloat16)
            lse[pl.ds(head, 1), :] = top + jnp.log2(total)
            own = pl.ds(pl.multiple_of(head * HEAD_DIM, HEAD_DIM), HEAD_DIM)
            mixed_t[own, :] = (dot(values_t[own, :], weights[...]) * (1.0 / total)).astype(
                jnp.bfloat16
            )
        return carry

    lax.fori_loop(0, q.shape[1] // 128, pair_step, 0)
    mixed[...] = mixed_t[...].T
    part[...] = dot_nt(mixed[...], wo[...]).astype(jnp.bfloat16)


def dense_in_kernel(
    loaded, info, section, own_part, other_part, params, cotangent,
    section_new, hidden, act, slope, grad_low,
):
    count = section.shape[0]

    def block_step(rows, at, carry):
        branch = own_part[rows, :].astype(jnp.float32) + other_part[rows, :].astype(jnp.float32)
        block = section[rows, :] + (branch + params[11:12, :])
        section_new[rows, :] = block
        hidden[rows, :] = norm_rows(block, params[4:5, :], params[5:6, :])
        row_ids = lax.broadcasted_iota(jnp.int32, (64, 1), 0) + at
        valid = (row_ids < info[LENGTH]).astype(jnp.float32)
        grad_low[rows, :] = (cotangent[rows, :].astype(jnp.float32) * valid).astype(jnp.bfloat16)
        return carry

    row_loop(count, block_step, 0)

    held = act.shape[1] // D
    for at in range(4):
        if at % 2 == 0:
            blocks = loaded(at // 2)
        width = blocks[0].shape[1]
        row = 13 + info[CORE] * held + at * width // D
        bias = params[pl.ds(row, 1), at * width % D : at * width % D + width]

        def step(part, carry, at=at, block=blocks[at % 2], bias=bias):
            cols = pl.ds(at * width, width)
            pre_act = dot(hidden[...], block[...]) + bias
            spread = 0.5 + 0.5 * lax.erf(pre_act * (2.0**-0.5))
            act[:, cols] = (pre_act * spread).astype(jnp.bfloat16)
            density = jnp.exp2(pre_act * pre_act * (-0.5 * LOG2E)) * 0.3989422804014327
            slope[:, cols] = (spread + pre_act * density).astype(jnp.bfloat16)
            return carry

        step(0, 0)


def dense_out_kernel(
    loaded, info, act, slope, grad_low,
    grad_pre, part, grad_hidden, grad_bias,
):
    w2 = loaded(0) + loaded(1)
    width = w2[0].shape[1]
    for at, block in enumerate(w2):
        cols = pl.ds(at * width, width)
        grad_act = dot(grad_low[...], block[...]).astype(jnp.bfloat16).astype(jnp.float32)
        grad_block = (grad_act * slope[:, cols].astype(jnp.float32)).astype(jnp.bfloat16)
        grad_pre[:, cols] = grad_block
        grad_bias[:, cols] = row_sum(grad_block)
    for left, blocks, out in (
        (act, w2, part),
        (grad_pre, loaded(2) + loaded(3), grad_hidden),
    ):
        total = None
        for at, block in enumerate(blocks):
            product = dot_nt(left[:, at * width : at * width + width], block[...])
            total = product if total is None else total + product
        out[...] = total.astype(jnp.bfloat16)


def put_relative(product, here, order, keep, send, which, cols):
    half = keep.shape[0]
    rows = keep.shape[2]
    for at, offset in enumerate(order):
        block = product[pl.ds(pl.multiple_of((here ^ offset) * rows, 16), rows), :]
        target = keep if at < half else send
        target[at % half, which, :, cols] = block.astype(jnp.bfloat16)


def weight_kernel(uses, lefts_count, orders, *refs):
    rights_count = 1 + max(right for _, right, _, _, _ in uses)
    lefts, rights = refs[1 : 1 + lefts_count], refs[1 + lefts_count : 1 + lefts_count + rights_count]
    outs = refs[1 + lefts_count + rights_count : -2]
    product, turned = refs[-2:]
    width = product.shape[1]
    me = refs[0][0]
    in_turned = None
    for left, right, first, group, which in uses:
        left_t, right = lefts[left], rights[right]
        if left_t.shape[0] != D:
            if in_turned != left:
                turned[...] = left_t[...].T
                in_turned = left
            left_t = turned

        def step(at, carry, left_t=left_t, right=right, first=first, group=group, which=which):
            cols = pl.ds(pl.multiple_of(at * width, width), width)
            taken = pl.ds(pl.multiple_of(first + at * width, width), width)
            product[...] = dot(left_t[...], right[:, taken])
            if orders is None:
                outs[group][which, :, cols] = product[...].astype(jnp.bfloat16)
            else:
                put_relative(
                    product, me, orders[group], outs[2 * group], outs[2 * group + 1], which, cols
                )
            return carry

        lax.fori_loop(0, outs[0].shape[-1] // width, step, 0)


def attention_pull(
    keys, values, keys_t, q, grad_mixed, grad_mixed_t, mixed_t, lse, allowed, step,
    grad_keys, grad_values, grad_q_t, first, last,
):
    masks = head_masks()
    key_spans = spans(keys.shape[0], step)

    def pair_step(pair, carry):
        cols = pl.ds(pl.multiple_of(pair * 128, 128), 128)
        queries = [q[:, cols] * mask for mask in masks]
        grads = [(grad_mixed[:, cols] * 0.125) * mask for mask in masks]
        heads = [pl.ds(pl.multiple_of(pair * 128 + p * 64, 64), 64) for p in range(2)]
        levels, deltas = [], []
        for parity in range(2):
            levels.append(lse[pl.ds(pair * 2 + parity, 1), :])
            product = grad_mixed_t[heads[parity], :].astype(jnp.float32) * mixed_t[
                heads[parity], :
            ].astype(jnp.float32)
            deltas.append(jnp.sum(product, axis=0, keepdims=True) * 0.125)
        def block_step(rows, sums):
            key_sum = value_sum = None
            added = []
            for parity in range(2):
                scores = dot_nt(keys[rows, cols], queries[parity]) * (0.125 * LOG2E)
                weights = jnp.exp2(scores - levels[parity])
                if allowed is not None:
                    weights = jnp.where(allowed[rows, :] > 0.5, weights, 0.0)
                grad_soft = dot_nt(values[rows, cols], grads[parity])
                grad_raw = (weights * (grad_soft - deltas[parity])).astype(jnp.bfloat16)
                value_part = dot(weights.astype(jnp.bfloat16), grads[parity])
                key_part = dot(grad_raw, queries[parity])
                added.append(dot(keys_t[heads[parity], rows], grad_raw))
                value_sum = value_part if value_sum is None else value_sum + value_part
                key_sum = key_part if key_sum is None else key_sum + key_part
            grad_values[rows, cols] = (value_sum * 8.0).astype(jnp.bfloat16)
            grad_keys[rows, cols] = key_sum.astype(jnp.bfloat16)
            return added if sums is None else add_rows(sums, added)

        full = keys.shape[0] // step
        if full > 1:

            def looped(at, sums):
                return block_step(pl.ds(pl.multiple_of(at * step, step), step), sums)

            zero = jnp.zeros((HEAD_DIM, q.shape[0]), jnp.float32)
            sums = lax.fori_loop(0, full, looped, [zero, zero])
            rest = [(full * step, keys.shape[0] - full * step)]
        else:
            sums, rest = None, key_spans
        for at, size in rest:
            if size:
                sums = block_step(pl.ds(at, size), sums)
        for parity in range(2):
            grad_q_t[heads[parity], :] = sums[parity].astype(jnp.bfloat16)
        return carry

    lax.fori_loop(first, last, pair_step, 0)


def output_kernel(section, out_part, out_other, params, layer_out):

    def block_step(rows, at, carry):
        branch = out_part[rows, :].astype(jnp.float32) + out_other[rows, :].astype(jnp.float32)
        layer_out[rows, :] = (section[rows, :] + (branch + params[12:13, :])).astype(jnp.bfloat16)
        return carry

    row_loop(section.shape[0], block_step, 0)


def cross_backward_kernel(
    loaded, info, section, grad_part, grad_other, grad_top, params,
    q, keys, values, keys_t, mixed_t, lse,
    grad_section, grad_z, vectors, grad_mixed, grad_mixed_t,
    grad_keys, grad_values, grad_q_t,
):
    count = section.shape[0]

    def block_step(rows, at, sums):
        block = section[rows, :]
        grad = grad_part[rows, :].astype(jnp.float32) + grad_other[rows, :].astype(jnp.float32)
        pulled, gain_sum, shift_sum = norm_pull(block, grad, params[4:5, :])
        top = grad_top[rows, :].astype(jnp.float32)
        total = top + pulled
        low = total.astype(jnp.bfloat16)
        grad_section[rows, :] = total
        grad_z[rows, :] = low
        parts = [gain_sum, shift_sum, row_sum(low), jnp.sum(top, axis=0, keepdims=True)]
        return add_rows(sums, parts)

    sums = row_loop(count, block_step, zero_rows(4))
    for at, value in enumerate(sums):
        vectors[at : at + 1, :] = value
    (wo,) = loaded(0)
    grad_mixed[...] = dot(grad_z[...], wo[...]).astype(jnp.bfloat16)
    grad_mixed_t[...] = grad_mixed[...].T
    attention_pull(
        keys, values, keys_t, q, grad_mixed, grad_mixed_t, mixed_t, lse, None, 256,
        grad_keys, grad_values, grad_q_t, 0, q.shape[1] // 128 - 1,
    )


def cross_rest_kernel(
    loaded, info, q, keys, values, keys_t, mixed_t, lse, grad_mixed, grad_mixed_t,
    keys_begun, values_begun, q_t_begun,
    grad_q, grad_keys, grad_values, grad_hidden, biases,
    grad_q_t,
):
    pairs = q.shape[1] // 128
    attention_pull(
        keys, values, keys_t, q, grad_mixed, grad_mixed_t, mixed_t, lse, None, 256,
        grad_keys, grad_values, grad_q_t, pairs - 1, pairs,
    )
    begun = (pairs - 1) * 128
    grad_keys[:, :begun] = keys_begun[:, :begun]
    grad_values[:, :begun] = values_begun[:, :begun]
    grad_q_t[:begun, :] = q_t_begun[:begun, :]
    grad_q[...] = grad_q_t[...].T
    (wq,) = loaded(0)
    grad_hidden[...] = dot_nt(grad_q[...], wq[...]).astype(jnp.bfloat16)
    biases[0:1, :] = row_sum(grad_q[...])
    biases[1:2, :] = row_sum(grad_values[...])


def self_backward_kernel(
    loaded, info, section, grad_section, grad_part, grad_other, params,
    q, k, v, mixed_t, lse,
    grad_new, grad_z, grad_q, grad_keys, grad_values, grad_hidden, vectors, biases,
    grad_mixed, grad_mixed_t, grad_q_t, keys_t, allowed,
):
    count = section.shape[0]

    def block_step(rows, at, sums):
        grad = grad_part[rows, :].astype(jnp.float32) + grad_other[rows, :].astype(jnp.float32)
        pulled, gain_sum, shift_sum = norm_pull(section[rows, :], grad, params[2:3, :])
        total = grad_section[rows, :] + pulled
        low = total.astype(jnp.bfloat16)
        grad_new[rows, :] = total
        grad_z[rows, :] = low
        parts = [gain_sum, shift_sum, row_sum(low)]
        return add_rows(sums, parts)

    sums = row_loop(count, block_step, zero_rows(3))
    for at, value in enumerate(sums):
        vectors[at : at + 1, :] = value
    wv, wo = loaded(1)
    wq, wk = loaded(0)
    grad_mixed[...] = dot(grad_z[...], wo[...]).astype(jnp.bfloat16)
    grad_mixed_t[...] = grad_mixed[...].T
    keys_t[...] = k[...].T
    key_ids = lax.broadcasted_iota(jnp.int32, (count, count), 0)
    query_ids = lax.broadcasted_iota(jnp.int32, (count, count), 1)
    allowed[...] = ((key_ids <= query_ids) & (key_ids < info[LENGTH])).astype(jnp.float32)
    attention_pull(
        k, v, keys_t, q, grad_mixed, grad_mixed_t, mixed_t, lse, allowed, 256,
        grad_keys, grad_values, grad_q_t, 0, q.shape[1] // 128,
    )
    grad_q[...] = grad_q_t[...].T
    grad_hidden[...] = (
        dot_nt(grad_q[...], wq[...])
        + dot_nt(grad_keys[...], wk[...])
        + dot_nt(grad_values[...], wv[...])
    ).astype(jnp.bfloat16)
    biases[0:1, :] = row_sum(grad_q[...])
    biases[1:2, :] = row_sum(grad_values[...])


def last_kernel(
    info, tokens, grad_section, grad_part, grad_other, params,
    vectors2, vectors3, biases_self, biases_cross, grad_b1,
    input_grad, vectors,
):

    def block_step(rows, at, sums):
        grad = grad_part[rows, :].astype(jnp.float32) + grad_other[rows, :].astype(jnp.float32)
        pulled, gain_sum, shift_sum = norm_pull(
            tokens[rows, :].astype(jnp.float32), grad, params[0:1, :]
        )
        input_grad[rows, :] = grad_section[rows, :] + pulled
        parts = [gain_sum, shift_sum]
        return add_rows(sums, parts)

    sums = row_loop(tokens.shape[0], block_step, zero_rows(2))
    leader = (info[CORE] == 0).astype(jnp.float32)
    vectors[...] = jnp.zeros_like(vectors)
    shared = sums + [vectors2[0:1, :], vectors2[1:2, :], vectors3[0:1, :], vectors3[1:2, :]]
    shared = list(enumerate(shared)) + [(8, vectors2[2:3, :]), (11, vectors3[2:3, :]), (12, vectors3[3:4, :])]
    for at, value in shared:
        vectors[at : at + 1, :] = value * leader
    width = biases_self.shape[1]
    cols = pl.ds(pl.multiple_of(info[CORE] * width, 128), width)
    for at, ref in ((6, biases_self), (9, biases_cross)):
        vectors[at : at + 1, cols] = ref[0:1, :]
        vectors[at + 1 : at + 2, cols] = ref[1:2, :]
    held = grad_b1.shape[1] // D
    for at in range(held):
        vectors[pl.ds(13 + info[CORE] * held + at, 1), :] = grad_b1[:, at * D : at * D + D]


def enc_kernel(loaded, info, grad_keys, grad_values, *refs):
    own, out = refs[:-1], refs[-1]
    width = grad_keys.shape[1]
    place = info[CORE] if own else 1 - info[CORE]
    cols = pl.ds(pl.multiple_of(place * width, 128), width)
    (wk,), (wv,) = loaded(0), loaded(1)
    for at, size in spans(grad_keys.shape[0], 256):
        rows = pl.ds(at, size)
        total = dot_nt(grad_keys[rows, :], wk[cols, :]) + dot_nt(grad_values[rows, :], wv[cols, :])
        if own:
            out[rows, 0, :] = total + own[0][rows, :].astype(jnp.float32)
        else:
            out[rows, :] = total.astype(out.dtype)


def swap(array, bit):
    count = lax.axis_size("dp")
    return lax.ppermute(array, "dp", [(i, i ^ bit) for i in range(count)])


def swap_core(array):
    return lax.ppermute(array, "mp", [(0, 1), (1, 0)])


def together(*values):
    return lax.optimization_barrier(values)


def sum_round(value, bits):
    me = lax.axis_index("dp")
    offsets = [0]
    for bit in bits:
        offsets = offsets + [offset ^ bit for offset in offsets]
    stack = [value] + [swap(value, offset) for offset in offsets[1:]]
    for bit in bits:
        flip = (me & bit) != 0
        pairs = [(stack[at], stack[at + 1]) for at in range(0, len(stack), 2)]
        stack = [jnp.where(flip, b, a) + jnp.where(flip, a, b) for a, b in pairs]
    return stack[0]


def sum_far(value):
    for bits in [(4, 8)] if lax.axis_size("dp") == 16 else high_bits():
        value = sum_round(value, bits)
    return value


def high_bits():
    return [(1 << k,) for k in range(2, lax.axis_size("dp").bit_length() - 1)]


def sum_near(value):
    value = sum_round(value, (1, 2))
    return value + swap_core(value)


def join(stack, came):
    return jnp.concatenate([stack, came], axis=0)


def far_stack(piece):
    return jnp.concatenate([piece] + [swap(piece, offset) for offset in FAR[1:]], axis=0)


def near_steps(first, second):
    parts = None if first is None else halves(first)
    onward = []
    for place, bit in enumerate((1, 2)):
        pieces = []
        if second is not None:
            pieces.append(second[1 - place])
        if first is not None:
            pieces.append(parts[place])
        onward.append(swap(jnp.concatenate(pieces, axis=0), bit))
    cut = 0 if second is None else 8
    nears = None if first is None else [join(part, came[cut:]) for part, came in zip(parts, onward)]
    lasts = None if second is None else onward[::-1]
    return nears, lasts


def near_parts(nears, lasts):
    return [
        [(near, (0, first)), (last, (3 ^ first, 3))]
        for near, last, first in zip(nears, lasts, (1, 2))
    ]


def halves(stack):
    return jnp.split(stack, 2, axis=1)


def weight_parts(uses, lefts, rights, wide, cols):
    count = lax.axis_size("dp")
    direct = count == 16
    orders = []
    for first in (2, 1):
        order = FAR
        for bit in (3 ^ first, first):
            order = order + [offset ^ bit for offset in order]
        orders.append(order)
    if direct:
        outs = [array_of((8, wide, D // 16, cols))] * 4
    else:
        outs = [array_of((wide, D, cols))] * 2
    return run_kernel(
        functools.partial(weight_kernel, uses, len(lefts), orders if direct else None),
        outs,
        lax.axis_index("dp")[None],
        *lefts,
        *rights,
        scratch=[pltpu.VMEM((D, 384), jnp.float32), pltpu.VMEM((D, BLOCK), jnp.bfloat16)],
    )


def send_near(first, second):
    cames = []
    for place, bit in enumerate((1, 2)):
        pieces = []
        if second is not None:
            pieces.append(second[place])
        if first is not None:
            pieces.append(first[3 - 2 * place])
        cames.append(swap(pieces[0] if len(pieces) == 1 else jnp.concatenate(pieces), bit))
    cut = 0 if second is None else 4
    return [came[cut:] for came in cames[::-1]], [came[:cut] for came in cames]


def fold_both(parts, cames):
    keep_a, _, keep_b, _ = parts
    (low_a, high_a), (low_b, high_b) = fold(keep_a, cames[0]), fold(keep_b, cames[1])
    return (low_a, low_b), (high_a, high_b)


def fold(keep, came):
    half = keep.shape[0] // 2
    high = keep[half:].astype(jnp.float32) + came[half:].astype(jnp.float32)
    return (
        keep[:half].astype(jnp.float32) + came[:half].astype(jnp.float32),
        high.astype(jnp.bfloat16),
    )


def far_ready(lows, cames):
    total = jnp.concatenate(
        [low.astype(jnp.float32) + came.astype(jnp.float32) for low, came in zip(lows, cames)],
        axis=1,
    )
    return [total[0]] + [total[at].astype(jnp.bfloat16) for at in range(1, 4)]


def totals_kernel(groups, *refs):
    squares = None
    outs = refs[-(groups + 1) :]
    for at in range(groups):
        own, *cames = refs[4 * at : 4 * at + 4]
        total = own[...]
        for came in cames:
            total = total + came[...].astype(jnp.float32)
        outs[at][...] = total
        square = jnp.sum(total * total, axis=(0, 1), keepdims=True)[0]
        squares = square if squares is None else squares + square
    if len(refs) == 5 * groups + 1:
        outs[groups][...] = squares
        return
    early, vectors = refs[4 * groups : 4 * groups + 2]
    count = vectors.shape[0]
    everything = jnp.sum(squares + early[...], axis=1, keepdims=True)
    outs[groups][0:count, :] = vectors[...]
    outs[groups][count : count + 1, :] = jnp.broadcast_to(everything, (1, vectors.shape[1]))


def prepare_kernel(decays, attn, attn_first, attn_second, dense, dense_first, dense_second, *outs):
    scales = (None, decays[0:1, 0:1], decays[0:1, 1:2])
    arrays = ((attn, attn_first, attn_second), (dense, dense_first, dense_second))
    for at, (group, rate) in enumerate(zip(arrays, (attn_rate, dense_rate))):
        for which, ref in enumerate(group):
            scale = 1.0 - 0.1 * rate if which == 0 else scales[which]
            outs[3 * at + which][...] = ref[...] * scale


def finish_kernel(
    decays, sums, vector_sum, self_sum, cross_sum, w1_sum, w2_sum,
    attn, attn_first, attn_second, dense, dense_first, dense_second,
    vector, vector_first, vector_second,
    norm, attn_new, attn_first_new, attn_second_new, attn_copy,
    dense_new, dense_first_new, dense_second_new, dense_copy,
    vector_new, vector_first_new, vector_second_new, vector_copy, bias_gradient,
):
    last = sums.shape[0] - 1
    vectors = sums[0:last, :]
    squares = jnp.sum(jnp.sum(vectors * vectors, axis=0, keepdims=True), axis=1, keepdims=True)
    clip_norm = jnp.sqrt(squares + sums[last : last + 1, 0:1])
    norm[...] = jnp.broadcast_to(clip_norm, norm.shape)
    factor = jnp.minimum(1.0, 1.0 / (clip_norm + 1e-06))
    first_rate, second_rate = decays[0:1, 0:1], decays[0:1, 1:2]
    first_scale = 1.0 / (1.0 - first_rate * first_rate * first_rate)
    second_scale = 1.0 / (1.0 - second_rate * second_rate * second_rate)
    first_part = (1.0 - first_rate) * factor
    second_part = (1.0 - second_rate) * factor * factor

    def update(gradient, weight, first, second, step_rate):
        first_new = first + first_part * gradient
        second_new = second + second_part * gradient * gradient
        change = (first_new * first_scale) / (jnp.sqrt(second_new * second_scale) + 1e-08)
        return weight - step_rate * change, first_new, second_new

    for at, gradient in enumerate((self_sum, cross_sum)):
        for which in range(4):
            new, first, second = update(
                gradient[which],
                attn[at, which],
                attn_first[at, which],
                attn_second[at, which],
                attn_rate,
            )
            attn_new[at, which] = new
            attn_first_new[at, which] = first
            attn_second_new[at, which] = second
            attn_copy[at, which] = new.astype(jnp.bfloat16)
    width = w1_sum.shape[2]
    for at, gradient in enumerate((w1_sum, w2_sum)):
        for which in range(4):
            cols = slice(which * width, which * width + width)
            new, first, second = update(
                gradient[which],
                dense[at, :, cols],
                dense_first[at, :, cols],
                dense_second[at, :, cols],
                dense_rate,
            )
            dense_new[at, :, cols] = new
            dense_first_new[at, :, cols] = first
            dense_second_new[at, :, cols] = second
            dense_copy[at, :, cols] = new.astype(jnp.bfloat16)
    new, first, second = update(
        vector_sum[...],
        vector[...] * (1.0 - 0.1 * vector_rate),
        vector_first[...] * first_rate,
        vector_second[...] * second_rate,
        vector_rate,
    )
    vector_new[...] = new
    vector_first_new[...] = first
    vector_second_new[...] = second
    vector_copy[...] = new.astype(jnp.bfloat16)
    bias_gradient[...] = vector_sum[12:13, :] * factor


def local(
    tokens,
    enc_states,
    lengths,
    cotangent,
    attn_master,
    attn_first,
    attn_second,
    dense_master,
    dense_first,
    dense_second,
    vector_params,
    vector_first,
    vector_second,
    decays,
):
    core = lax.axis_index("mp")
    attn_low = attn_master.astype(jnp.bfloat16)
    dense_low = dense_master.astype(jnp.bfloat16)
    blocks = dense_master.shape[2] // attn_master.shape[3]
    dense_low = jnp.stack(jnp.split(dense_low, blocks, axis=2), axis=1)
    device = lax.axis_index("dp") * lax.axis_size("mp") + core
    own_cols = vector_params.shape[1]
    attn_low, vector_in = together(attn_low, vector_params)
    placed = lax.dynamic_update_slice_in_dim(
        jnp.zeros((vector_params.shape[0], D), jnp.float32), vector_in, device * own_cols, 1
    )
    fast = lax.axis_size("dp") == 16
    head_cols = attn_master.shape[3]
    hidden_cols = dense_master.shape[2]
    head_rows = 2 * (head_cols // 128)
    count = tokens.shape[0]
    keys_count = enc_states.shape[1]
    enc = enc_states[0]
    rows_d = array_of((count, D))
    rows_f = array_of((count, D), jnp.float32)
    rows_h = array_of((count, head_cols))
    turned_h = array_of((head_cols, count))
    lse_shape = array_of((head_rows, count), jnp.float32)
    keys_h = array_of((keys_count, head_cols))
    keys_t_h = array_of((head_cols, keys_count))
    scratch_h = pltpu.VMEM((count, head_cols), jnp.bfloat16)
    scratch_t = pltpu.VMEM((head_cols, count), jnp.bfloat16)
    scratch_s = pltpu.VMEM((count, count), jnp.float32)

    here = lax.axis_index("dp")
    info = jnp.stack([here, core, lengths[0]]).astype(jnp.int32)
    if fast:
        low_self, low_cross = attn_low[0][None], attn_low[1][None]
        low_w1, low_w2 = dense_low[0][None], dense_low[1][None]
        vector_low = placed + swap(placed, 1)
        vector_low = vector_low + swap(vector_low, 2)
        self_far, vector_low = together(far_stack(low_self), vector_low + swap_core(vector_low))
        (self_near, _), params, low_cross = together(
            near_steps(self_far, None), sum_far(vector_low), low_cross
        )
        (_, self_last), cross_far, low_w1, info = together(
            near_steps(None, self_near), far_stack(low_cross), low_w1, info
        )
        self_a, self_b = near_parts(self_near, self_last)
    else:
        params = sum_near(sum_far(placed))
        attn_all = lax.all_gather(attn_low, "dp", axis=2, tiled=True)
        dense_all = lax.all_gather(dense_low, "dp", axis=2, tiled=True)
        (self_a, self_b), (cross_a, cross_b), (w1_a, w1_b), (w2_a, w2_b) = [
            [[(whole[:2], None)], [(whole[2:], None)]] for whole in (*attn_all, *dense_all)
        ]
    both = (0, 1)
    cross_uses = ((0,), (0,), (0,), (0,)) if fast else ((0,), (1,), (1,), (0,))
    (
        hidden1, self_q, self_k, self_v, self_mixed, self_mixed_t, self_lse, self_part, self_a, self_b,
    ) = run_kernel(
        self_forward_kernel,
        [rows_d, rows_h, rows_h, rows_h, rows_h, turned_h, lse_shape, rows_d],
        info, tokens, params,
        scratch=[scratch_t, scratch_s],
        weights=[(self_a, both), (self_b, both)],
        keep=True,
    )
    if fast:
        (cross_near, _), self_part = together(near_steps(cross_far, None), self_part)
    self_other = swap_core(self_part)
    if fast:
        (_, cross_last), w1_far, self_other, info, low_w2 = together(
            near_steps(None, cross_near), far_stack(low_w1), self_other, info, low_w2
        )
        cross_a, cross_b = near_parts(cross_near, cross_last)
    cross_k, cross_v, cross_k_t, cross_v_t, enc_t, cross_wk, cross_wv = run_kernel(
        cross_keys_kernel,
        [keys_h, keys_h, keys_t_h, keys_t_h, array_of((D, keys_count))],
        info, enc, params,
        weights=[(cross_a, (1,)), (cross_b, (0,))],
        keep=True,
    )
    if fast:
        (w1_near, _), w2_far, cross_k, info = together(
            near_steps(w1_far, None), far_stack(low_w2), cross_k, info
        )
    (
        section1, hidden2, cross_q, cross_mixed, cross_mixed_t, cross_lse, cross_part, cross_wq, cross_wo,
    ) = run_kernel(
        cross_forward_kernel,
        [rows_f, rows_d, rows_h, rows_h, turned_h, lse_shape, rows_d],
        info, tokens, self_part, self_other, params, cross_k, cross_v_t,
        scratch=[
            pltpu.VMEM((keys_count, count), jnp.float32),
            pltpu.VMEM((keys_count, count), jnp.bfloat16),
        ],
        weights=[(cross_a, (0,)), (cross_b, (1,))],
        keep=True,
    )
    if fast:
        (w2_near, w1_last), cross_part, info = together(
            near_steps(w2_far, w1_near), cross_part, info
        )
        w1_a, w1_b = near_parts(w1_near, w1_last)
    hidden_rows = array_of((count, hidden_cols))
    section2, hidden3, act, slope, grad_low, w1_a, w1_b = run_kernel(
        dense_in_kernel,
        [rows_f, rows_d, hidden_rows, hidden_rows, rows_d],
        info, section1, cross_part, swap_core(cross_part), params, cotangent,
        weights=[(w1_a, both), (w1_b, both)],
        keep=True,
    )
    dense_uses = tuple((0, 0, at * head_cols, at // 2, at % 2) for at in range(4))
    w2_parts = weight_parts(dense_uses, (grad_low,), (act,), 2, head_cols)
    if fast:
        (_, w2_last), w2_parts, slope, info = together(
            near_steps(None, w2_near), w2_parts, slope, info
        )
        w2_a, w2_b = near_parts(w2_near, w2_last)
    grad_pre, out_part, grad_h3, grad_b1 = run_kernel(
        dense_out_kernel,
        [hidden_rows, rows_d, rows_d, array_of((1, hidden_cols), jnp.float32)],
        info, act, slope, grad_low,
        weights=[(w2_a, both), (w2_b, both), (w1_a, both), (w1_b, both)],
    )
    w1_parts = weight_parts(dense_uses, (hidden3,), (grad_pre,), 2, head_cols)
    if fast:
        (w2_came, _), w1_parts, grad_h3, out_part = together(
            send_near(w2_parts, None), w1_parts, grad_h3, out_part
        )
        w2_lows, w2_highs = fold_both(w2_parts, w2_came)
    grad_h3_other, out_other = swap_core(grad_h3), swap_core(out_part)
    (
        grad_section2, grad_z2, vectors3, grad_cross, grad_cross_t, dk_begun, dv_begun, dq_begun,
    ) = run_kernel(
        cross_backward_kernel,
        [rows_f, rows_d, array_of((4, D), jnp.float32), rows_h, turned_h,
         keys_h, keys_h, turned_h],
        info, section2, grad_h3, grad_h3_other, grad_low, params,
        cross_q, cross_k, cross_v, cross_k_t, cross_mixed_t, cross_lse,
        weights=[(cross_wo, cross_uses[1])],
    )
    if fast:
        (w1_came, w2_came), dk_begun, info = together(
            send_near(w1_parts, w2_highs), dk_begun, info
        )
        w2_own, *w2_out = far_ready(w2_lows, w2_came)
        w1_lows, w1_highs = fold_both(w1_parts, w1_came)
    layer_out = run_kernel(output_kernel, rows_d, section2, out_part, out_other, params)
    cross_dq, cross_dk, cross_dv, grad_h2, biases_cross = run_kernel(
        cross_rest_kernel,
        [rows_h, keys_h, keys_h, rows_d, array_of((2, head_cols), jnp.float32)],
        info, cross_q, cross_k, cross_v, cross_k_t, cross_mixed_t, cross_lse,
        grad_cross, grad_cross_t, dk_begun, dv_begun, dq_begun,
        scratch=[scratch_t],
        weights=[(cross_wq, cross_uses[0])],
    )
    cross_parts = weight_parts(
        ((0, 0, 0, 0, 0), (1, 1, 0, 0, 1), (1, 2, 0, 1, 0), (2, 3, 0, 1, 1)),
        (hidden2, enc_t, grad_z2),
        (cross_dq, cross_dk, cross_dv, cross_mixed),
        2,
        head_cols,
    )
    grad_h2_other = swap_core(grad_h2)
    if fast:
        (_, w1_came), w2_in1, w2_in2, cross_parts, grad_h2_other, info = together(
            send_near(None, w1_highs), swap(w2_out[0], 4), swap(w2_out[1], 8),
            cross_parts, grad_h2_other, info,
        )
        w1_own, *w1_out = far_ready(w1_lows, w1_came)
    (
        grad_section1, grad_z1, self_dq, self_dk, self_dv, grad_h1, vectors2, biases_self,
    ) = run_kernel(
        self_backward_kernel,
        [rows_f, rows_d, rows_h, rows_h, rows_h, rows_d,
         array_of((3, D), jnp.float32), array_of((2, head_cols), jnp.float32)],
        info, section1, grad_section2, grad_h2, grad_h2_other, params,
        self_q, self_k, self_v, self_mixed_t, self_lse,
        scratch=[scratch_h, scratch_t, scratch_t, scratch_t, scratch_s],
        weights=[(self_a, both), (self_b, both)],
    )
    if fast:
        (cross_came, _), w2_in3, w1_in1, w1_in2, self_dq, grad_h1 = together(
            send_near(cross_parts, None), swap(w2_out[2], 12), swap(w1_out[0], 4),
            swap(w1_out[1], 8), self_dq, grad_h1,
        )
        cross_lows, cross_highs = fold_both(cross_parts, cross_came)
    self_parts = weight_parts(
        ((0, 0, 0, 0, 0), (0, 1, 0, 0, 1), (0, 2, 0, 1, 0), (1, 3, 0, 1, 1)),
        (hidden1, grad_z1),
        (self_dq, self_dk, self_dv, self_mixed),
        2,
        head_cols,
    )
    grad_h1_other = swap_core(grad_h1)
    if fast:
        (_, cross_came), w1_in3, self_parts, grad_h1_other, info = together(
            send_near(None, cross_highs), swap(w1_out[2], 12), self_parts, grad_h1_other, info
        )
        cross_own, *cross_out = far_ready(cross_lows, cross_came)
    input_grad, vector_grad = run_kernel(
        last_kernel,
        [rows_f, array_of(params.shape, jnp.float32)],
        info, tokens, grad_section1, grad_h1, grad_h1_other, params,
        vectors2, vectors3, biases_self, biases_cross, grad_b1,
    )
    enc_other = run_kernel(
        enc_kernel,
        array_of((keys_count, head_cols)),
        info, cross_dk, cross_dv,
        weights=[(cross_wk, cross_uses[2]), (cross_wv, cross_uses[3])],
    )
    if fast:
        (self_came, _), cross_ins, vector_grad, enc_other = together(
            send_near(self_parts, None),
            [swap(out, offset) for out, offset in zip(cross_out, FAR[1:])],
            vector_grad, enc_other,
        )
        self_lows, self_highs = fold_both(self_parts, self_came)
        (_, self_came), enc_came = together(send_near(None, self_highs), swap_core(enc_other))
        self_own, *self_out = far_ready(self_lows, self_came)
    else:
        enc_came = swap_core(enc_other)
    enc_grad = run_kernel(
        enc_kernel,
        array_of((keys_count, 1, head_cols), jnp.float32),
        info, cross_dk, cross_dv, enc_came,
        weights=[(cross_wk, cross_uses[2]), (cross_wv, cross_uses[3])],
    )
    group = array_of((4, D // lax.axis_size("dp"), head_cols), jnp.float32)
    masters = (attn_master, attn_first, attn_second, dense_master, dense_first, dense_second)
    prepared = run_kernel(
        prepare_kernel,
        [array_of(master.shape, jnp.float32) for master in masters],
        *lax.optimization_barrier((decays[None], enc_came))[:1], *masters,
    )
    square_row = array_of((1, head_cols), jnp.float32)
    if fast:
        w1_sum, w2_sum, cross_sum, early_squares = run_kernel(
            functools.partial(totals_kernel, 3),
            [group, group, group, square_row],
            w1_own, w1_in1, w1_in2, w1_in3, w2_own, w2_in1, w2_in2, w2_in3, cross_own, *cross_ins,
        )
        self_ins, enc_grad, early_squares, prepared = together(
            [swap(out, offset) for out, offset in zip(self_out, FAR[1:])],
            enc_grad, early_squares, prepared,
        )
        self_sum, payload = run_kernel(
            functools.partial(totals_kernel, 1),
            [group, array_of((params.shape[0] + 1, D), jnp.float32)],
            self_own, *self_ins, early_squares, vector_grad,
        )
    else:
        self_sum, cross_sum, w1_sum, w2_sum = [
            jnp.concatenate(
                [
                    lax.psum_scatter(
                        part.astype(jnp.float32), "dp", scatter_dimension=1, tiled=True
                    )
                    for part in parts
                ],
                axis=0,
            )
            for parts in (self_parts, cross_parts, w1_parts, w2_parts)
        ]
        square = sum(jnp.sum(total * total) for total in (cross_sum, w1_sum, w2_sum, self_sum))
        payload = jnp.concatenate([vector_grad, jnp.full((1, D), square)], axis=0)
    enc_grad = enc_grad.transpose(1, 0, 2)
    sums = sum_near(sum_far(payload))
    vector_sum = lax.dynamic_slice_in_dim(sums[:-1], device * own_cols, own_cols, 1)
    outs = [
        jax.ShapeDtypeStruct(master.shape, dtype)
        for master in (attn_master, dense_master, vector_params)
        for dtype in (jnp.float32, jnp.float32, jnp.float32, jnp.bfloat16)
    ]
    norm, *updated, bias_gradient = run_kernel(
        finish_kernel,
        [array_of((1, 128), jnp.float32), *outs, array_of((1, own_cols), jnp.float32)],
        decays[None], sums, vector_sum,
        self_sum, cross_sum, w1_sum, w2_sum, *prepared,
        vector_params, vector_first, vector_second,
    )
    return (layer_out, input_grad, enc_grad, norm[0, 0], *updated, bias_gradient[0])


def solution(mesh):
    return jax.shard_map(
        local,
        mesh=mesh,
        in_specs=(
            P("dp", None),
            P("dp", None, None),
            P("dp"),
            P("dp", None),
            P(None, None, "dp", "mp"),
            P(None, None, "dp", "mp"),
            P(None, None, "dp", "mp"),
            P(None, "dp", "mp"),
            P(None, "dp", "mp"),
            P(None, "dp", "mp"),
            P(None, ("dp", "mp")),
            P(None, ("dp", "mp")),
            P(None, ("dp", "mp")),
            P(),
        ),
        out_specs=(
            P("dp", None),
            P("dp", None),
            P("dp", None, "mp"),
            P(),
            P(None, None, "dp", "mp"),
            P(None, None, "dp", "mp"),
            P(None, None, "dp", "mp"),
            P(None, None, "dp", "mp"),
            P(None, "dp", "mp"),
            P(None, "dp", "mp"),
            P(None, "dp", "mp"),
            P(None, "dp", "mp"),
            P(None, ("dp", "mp")),
            P(None, ("dp", "mp")),
            P(None, ("dp", "mp")),
            P(None, ("dp", "mp")),
            P(("dp", "mp")),
        ),
        check_vma=False,
    )
```
